32 devices in a mesh: dp: 4 (over y, x), seq: 2 (over core), mp: 4 (over z).
Axes of the slice: x: 2, y: 2, z: 4, core: 2. Of those that a mesh axis runs over, the one named last changes fastest.
Arguments:
- x_in: bfloat16 [3, 4, 2048, 2048], P(None, 'dp', 'seq', 'mp'), may hold values from -6 to 6
- cotangent: bfloat16 [3, 4, 2048, 2048], P(None, 'dp', 'seq', 'mp'), may hold values from -6 to 6
- lengths: int32 [3, 4], P(None, 'dp'), may hold values from 512 to 2048, as said below
- adapter_ids: int32 [3, 4], P(None, 'dp'), may hold values from 0 to 7
- norm_gain: float32 [2048], replicated, may hold values from 0.5 to 1.5
- w_zx: bfloat16 [2048, 2, 4096], P(('dp', 'seq'), None, 'mp'), may hold values from -0.125 to 0.125
- w_bc: bfloat16 [2048, 256], P(('dp', 'seq')), may hold values from -0.125 to 0.125
- w_dt: bfloat16 [2048, 64], P(('dp', 'seq'), 'mp'), may hold values from -0.19921875 to 0.19921875
- dt_bias: float32 [64], P('mp'), may hold values from -9.5 to -4.5
- a_log: float32 [64], P('mp'), may hold values from 0 to 0.7
- d_skip: float32 [64], P('mp'), may hold values from 0.5 to 1.5
- conv_x: float32 [4, 4096], P(None, 'mp'), may hold values from -3 to 3
- conv_bc: float32 [4, 256], replicated, may hold values from -3 to 3
- gate_gain: float32 [4096], P('mp'), may hold values from 0.5 to 1.5
- w_out: bfloat16 [4096, 2048], P('mp', ('dp', 'seq')), may hold values from -0.09375 to 0.09375
- in_down: bfloat16 [8, 2048, 16], P(None, ('dp', 'seq', 'mp')), may hold values from -0.125 to 0.125
- in_up: bfloat16 [128, 2, 4096], P(('dp', 'seq'), None, 'mp'), may hold values from -0.75 to 0.75
- out_down: bfloat16 [4096, 128], P('mp', ('dp', 'seq')), may hold values from -0.09375 to 0.09375
- out_up: bfloat16 [128, 2048], P(None, ('dp', 'seq', 'mp')), may hold values from -0.75 to 0.75
Outputs:
- out: bfloat16 [3, 4, 2048, 2048], P(None, 'dp', 'seq', 'mp')
- x_grad: float32 [3, 4, 2048, 2048], P(None, 'dp', 'seq', 'mp')
- in_down_grad: float32 [8, 2048, 16], P(None, ('dp', 'seq', 'mp'))
- in_up_grad: float32 [128, 2, 4096], P(('dp', 'seq'), None, 'mp')
- out_down_grad: float32 [4096, 128], P('mp', ('dp', 'seq'))
- out_up_grad: float32 [128, 2048], P(None, ('dp', 'seq', 'mp'))
The draws below stay inside these ranges and needn't reach their ends.
Inputs may be any that keep to these rules, and one draw needn't show every extreme that they name: `lengths`: each slot holds its sequence from its first position; the rest is padding. For every slot column, one of the 3 micro-batches fills it to 2048.
All inputs are finite; a program needn't handle non-finite values.
Results may differ from the reference program's by a relative error of at most 0.0029.
The reference program's roundings to bfloat16 on the way count: a program that leaves them out, or rounds other values in their place, can miss the bound.
Values may be sent and summed in bfloat16 or wider, within the bound.
A program may use at most 832 MiB of HBM per device.

```python
import jax
import jax.numpy as jnp
from jax import lax

D = 2048
H = 64
P_SIZE = 64
NS = 128
KC = 4
Q = 256
R = 16
ADAPT = 8
MB = 3
DI = 4096
SLOT_LEN = 2048
SLOTS = 4


def draw_lengths(key, part):
    key = jax.random.fold_in(key, 11)
    length_key, choice_key = jax.random.split(key)
    random_lengths = jax.random.randint(length_key, (MB, SLOTS), SLOT_LEN // 4, SLOT_LEN + 1)
    full_batch = jax.random.randint(choice_key, (SLOTS,), 0, MB)
    full_rows = jnp.arange(MB)[:, None] == full_batch[None, :]
    return jnp.where(full_rows, SLOT_LEN, random_lengths).astype(jnp.int32)


def draw_dt_bias(key, part):
    key = jax.random.fold_in(key, 23)
    pick_key, fast_key, slow_key = jax.random.split(key, 3)
    slow_share = 0.5
    slow_heads = jax.random.uniform(pick_key, (H,)) < slow_share
    fast_value = jax.random.uniform(fast_key, (H,), jnp.float32, -5.5, -4.5)
    slow_value = jax.random.uniform(slow_key, (H,), jnp.float32, -9.5, -8.5)
    return jnp.where(slow_heads, slow_value, fast_value).astype(jnp.float32)


def with_ends(values, rng, least, high):
    shape = values.shape
    index_at = [jax.random.randint(jax.random.fold_in(rng, axis), (), 0, shape[axis]) for axis in range(len(shape))]
    values = values.at[tuple(index_at)].set(least)
    longest = shape.index(max(shape))
    index_at[longest] = (index_at[longest] + 1) % shape[longest]
    return values.at[tuple(index_at)].set(high)


def block_scale(rng, dims, shards, smallest, largest):
    loudness = 1.0
    for position, parts in shards:
        steps = jax.random.uniform(jax.random.fold_in(jax.random.fold_in(rng, 6), position), (parts,), jnp.float32, smallest / len(shards), largest / len(shards))
        loudness = loudness * jnp.repeat(jnp.exp(steps), dims[position] // parts).reshape((-1,) + (1,) * (len(dims) - 1 - position))
    return loudness


def gaussian(rng, dims, scale, most, cuts=(), kind=jnp.bfloat16):
    loudness = block_scale(rng, dims, cuts, -0.22, 0.18) if cuts else 1.0
    values = jax.random.normal(rng, dims, jnp.float32) * scale * loudness
    return jnp.minimum(jnp.maximum(values, -most), most).astype(kind)


def setup_inputs(seed: int = 0) -> dict:
    key_list = jax.random.split(jax.random.key(seed), 20)
    x_in = gaussian(key_list[0], (MB, SLOTS, SLOT_LEN, D), 1.0, 6.0, ((1, 4), (2, 2), (3, 4)))
    cotangent = gaussian(key_list[1], (MB, SLOTS, SLOT_LEN, D), 1.0, 6.0, ((1, 4), (2, 2), (3, 4)))
    lengths = draw_lengths(jax.random.fold_in(key_list[19], 71), 0)
    adapter_ids = with_ends(jax.random.randint(key_list[3], (MB, SLOTS), 0, ADAPT), jax.random.fold_in(key_list[3], 1), 0, ADAPT - 1).astype(jnp.int32)
    norm_gain = jnp.clip(1.0 + 0.1 * jax.random.normal(key_list[4], (D,), jnp.float32), 0.5, 1.5)
    w_zx = gaussian(key_list[5], (D, 2, DI), D ** -0.5, 0.125, ((0, 8), (2, 4)))
    w_bc = gaussian(key_list[6], (D, 2 * NS), D ** -0.5, 0.125, ((0, 8),))
    w_dt = gaussian(key_list[7], (D, H), 0.033, 0.19921875, ((0, 8), (1, 4)))
    dt_bias = draw_dt_bias(jax.random.fold_in(key_list[19], 71), 0)
    a_log = jnp.clip(0.7 * jax.random.uniform(key_list[9], (H,), jnp.float32) ** block_scale(key_list[9], (H,), ((0, 4),), -0.2, 0.2), 0.0, 0.7)
    d_skip = jnp.clip(0.5 + 1.0 * jax.random.uniform(key_list[10], (H,), jnp.float32) ** block_scale(key_list[10], (H,), ((0, 4),), -0.2, 0.2), 0.5, 1.5)
    conv_x = gaussian(key_list[11], (KC, DI), KC ** -0.5, 3.0, ((1, 4),), jnp.float32)
    conv_bc = gaussian(key_list[12], (KC, 2 * NS), KC ** -0.5, 3.0, (), jnp.float32)
    gate_gain = jnp.clip(1.0 + 0.1 * jax.random.normal(key_list[13], (DI,), jnp.float32), 0.5, 1.5)
    w_out = gaussian(key_list[14], (DI, D), DI ** -0.5, 0.09375, ((0, 4), (1, 8)))
    in_down = gaussian(key_list[15], (ADAPT, D, R), D ** -0.5, 0.125, ((1, 32),))
    in_up = gaussian(key_list[16], (ADAPT * R, 2, DI), 0.125, 0.75, ((0, 8), (2, 4)))
    out_down = gaussian(key_list[17], (DI, ADAPT * R), DI ** -0.5, 0.09375, ((0, 4), (1, 8)))
    out_up = gaussian(key_list[18], (ADAPT * R, D), 0.125, 0.75, ((1, 32),))
    return dict(x_in=x_in, cotangent=cotangent, lengths=lengths, adapter_ids=adapter_ids, norm_gain=norm_gain, w_zx=w_zx, w_bc=w_bc, w_dt=w_dt, dt_bias=dt_bias, a_log=a_log, d_skip=d_skip, conv_x=conv_x, conv_bc=conv_bc, gate_gain=gate_gain, w_out=w_out, in_down=in_down, in_up=in_up, out_down=out_down, out_up=out_up)


eps = 1e-05
precise = lax.Precision.HIGHEST

@jax.custom_vjp
def low(v):
    return lax.optimization_barrier(v.astype(jnp.bfloat16)).astype(jnp.float32)

@jax.custom_vjp
def low_back(v):
    return v

def low_keep(v):
    return (low(v), None)

def low_pass(kept, grad):
    return (grad,)

def back_keep(v):
    return (v, None)

def back_low(kept, grad):
    return (low(grad),)
low.defvjp(low_keep, low_pass)
low_back.defvjp(back_keep, back_low)

def block_step(carry_state, pieces):
    x_part, b_part, c_part, log_part, step_part = pieces
    length = log_part.shape[0]
    cumulative = jnp.cumsum(log_part, axis=0)
    causal = jnp.arange(length)[:, None] >= jnp.arange(length)[None, :]
    spread = cumulative[:, None, :] - cumulative[None, :, :]
    decay_mat = jnp.exp(jnp.where(causal[:, :, None], spread, -10000.0))
    scores = jnp.dot(c_part, b_part.T, precision=precise)
    mixing = scores[:, :, None] * decay_mat * step_part[None, :, :]
    inner_out = jnp.einsum('tsh,shp->thp', mixing, x_part, precision=precise)
    carried = jnp.exp(cumulative)[:, :, None] * jnp.einsum('tn,hpn->thp', c_part, carry_state, precision=precise)
    weights = jnp.exp(cumulative[-1][None, :] - cumulative) * step_part
    update = jnp.einsum('sh,shp,sn->hpn', weights, x_part, b_part, precision=precise)
    new_state = jnp.exp(cumulative[-1])[:, None, None] * carry_state + update
    return (new_state, inner_out + carried)

def ssd_scan(x_heads, b_rows, c_rows, log_rows, step_rows):
    length = x_heads.shape[0]
    blocks = length // Q

    def blocked(tensor):
        return tensor.reshape((blocks, Q) + tensor.shape[1:])
    init_state = jnp.zeros((H, P_SIZE, NS), jnp.float32)
    final_state, outputs = lax.scan(jax.checkpoint(block_step), init_state, (blocked(x_heads), blocked(b_rows), blocked(c_rows), blocked(log_rows), blocked(step_rows)))
    return outputs.reshape(length, H, P_SIZE)

def mamba_layer(x_rows, adapters, length, adapter_id, frozen):
    norm_gain, w_zx, w_bc, w_dt, dt_bias, a_log, d_skip, conv_x, conv_bc, gate_gain, w_out = frozen
    in_down, in_up, out_down, out_up = adapters
    row_count = x_rows.shape[0]
    mask_rows = (jnp.arange(row_count) < length).astype(jnp.float32)
    select = jax.nn.one_hot(adapter_id, ADAPT, dtype=jnp.float32)
    normed = x_rows * lax.rsqrt(lax.optimization_barrier(jnp.mean(x_rows * x_rows, axis=-1, keepdims=True)) + eps) * norm_gain
    normed_low = low(normed)
    down_sel = jnp.einsum('a,adr->dr', select, in_down, precision=precise)
    up_sel = jnp.einsum('a,arf->rf', select, in_up.reshape(ADAPT, R, 2 * DI), precision=precise)
    low_rank = jnp.dot(normed_low, down_sel, precision=precise)
    proj_zx = jnp.dot(normed_low, w_zx.reshape(D, 2 * DI), precision=precise) + jnp.dot(low_rank, up_sel, precision=precise)
    proj_zx = low_back(proj_zx)
    proj_bc = low(low_back(jnp.dot(normed_low, w_bc, precision=precise)))
    proj_dt = low_back(jnp.dot(normed_low, w_dt, precision=precise))
    gate_in = proj_zx[:, :DI]
    conv_in = jnp.concatenate([low(proj_zx[:, DI:]), proj_bc], axis=1)
    conv_taps = jnp.concatenate([conv_x, conv_bc], axis=1)
    padded = jnp.pad(conv_in, ((KC - 1, 0), (0, 0)))
    conv_pre = sum((conv_taps[tap_index] * padded[tap_index:tap_index + row_count] for tap_index in range(KC)))
    conv_out = jax.nn.silu(conv_pre)
    x_heads = conv_out[:, :DI].reshape(row_count, H, P_SIZE)
    b_rows = conv_out[:, DI:DI + NS]
    c_rows = conv_out[:, DI + NS:]
    step_rows = jax.nn.softplus(proj_dt + dt_bias) * mask_rows[:, None]
    log_rows = step_rows * -jnp.exp(a_log)
    mixed_out = ssd_scan(x_heads, b_rows, c_rows, log_rows, step_rows) + d_skip[:, None] * x_heads
    gated_out = mixed_out.reshape(row_count, DI) * jax.nn.silu(gate_in)
    scaled = gated_out * lax.rsqrt(lax.optimization_barrier(jnp.mean(gated_out * gated_out, axis=-1, keepdims=True)) + eps) * gate_gain
    scaled_low = low(scaled)
    out_sel = jnp.einsum('a,far->fr', select, out_down.reshape(DI, ADAPT, R), precision=precise)
    up_out = jnp.einsum('a,ard->rd', select, out_up.reshape(ADAPT, R, D), precision=precise)
    rank_out = jnp.dot(scaled_low, out_sel, precision=precise)
    branch = jnp.dot(scaled_low, w_out, precision=precise) + jnp.dot(rank_out, up_out, precision=precise)
    return x_rows + mask_rows[:, None] * branch

def reference(x_in, cotangent, lengths, adapter_ids, norm_gain, w_zx, w_bc, w_dt, dt_bias, a_log, d_skip, conv_x, conv_bc, gate_gain, w_out, in_down, in_up, out_down, out_up):
    frozen = tuple((tensor.astype(jnp.float32) for tensor in (norm_gain, w_zx, w_bc, w_dt, dt_bias, a_log, d_skip, conv_x, conv_bc, gate_gain, w_out)))
    adapters = tuple((tensor.astype(jnp.float32) for tensor in (in_down, in_up, out_down, out_up)))
    seq_count = MB * SLOTS
    rows_all = x_in.reshape(seq_count, SLOT_LEN, D).astype(jnp.float32)
    cot_all = cotangent.reshape(seq_count, SLOT_LEN, D).astype(jnp.float32)

    def one_sequence(totals, seq_items):
        x_rows, cot_rows, length, adapter_id = seq_items

        def forward(x_value, adapter_value):
            return mamba_layer(x_value, adapter_value, length, adapter_id, frozen)
        result, pullback = jax.vjp(forward, x_rows, adapters)
        x_grad, adapter_grads = pullback(cot_rows)
        totals = jax.tree.map(jnp.add, totals, adapter_grads)
        return (totals, (result.astype(jnp.bfloat16), x_grad))
    zero_grads = tuple((jnp.zeros(tensor.shape, jnp.float32) for tensor in adapters))
    totals, (outputs, x_grads) = lax.scan(one_sequence, zero_grads, (rows_all, cot_all, lengths.reshape(seq_count), adapter_ids.reshape(seq_count)))
    return (outputs.reshape(x_in.shape), x_grads.reshape(x_in.shape), totals[0], totals[1], totals[2], totals[3])
```

```python
import functools

import jax
import jax.numpy as jnp
from jax import lax
from jax.experimental import pallas as pl
from jax.experimental.pallas import tpu as pltpu
from jax.sharding import PartitionSpec as P

D = 2048
P_SIZE = 64
NS = 128
KC = 4
Q = 256
R = 16
ADAPT = 8
DI = 4096
HG = 4
HALO = 16


eps = 1e-05
precise = lax.Precision.HIGHEST
VMEM_LIMIT = 56 * 1024 * 1024


def shifted(array, axis, by):
    size = lax.axis_size(axis)
    pairs = [(i, i + by) for i in range(size) if 0 <= i + by < size]
    return lax.ppermute(array, axis, pairs)


def entering(part, axis, combine, identity, reverse):
    count = lax.axis_size(axis)
    place = lax.axis_index(axis)
    ahead = count - 1 - place if reverse else place
    gathered = jax.tree.map(lambda a: lax.all_gather(a, axis), part)
    state = jax.tree.map(lambda a, e: jnp.zeros_like(a) + jnp.asarray(e, a.dtype), part, identity)

    def one(hop, state):
        source = count - 1 - hop if reverse else hop
        return combine(
            state, jax.tree.map(lambda a: lax.dynamic_index_in_dim(a, source, 0, False), gathered)
        )

    return lax.fori_loop(0, ahead, one, state)


def silu_grad(value):
    sigmoid_val = jax.nn.sigmoid(value)
    return sigmoid_val * (1.0 + value * (1.0 - sigmoid_val))


def block_step(carry_state, pieces):
    x_part, b_part, c_part, log_part, step_part = pieces
    length = log_part.shape[0]
    cumulative = jnp.cumsum(log_part, axis=0)
    causal = jnp.arange(length)[:, None] >= jnp.arange(length)[None, :]
    spread = cumulative[:, None, :] - cumulative[None, :, :]
    decay_mat = jnp.exp(jnp.where(causal[:, :, None], spread, -10000.0))
    scores = jnp.dot(c_part, b_part.T, precision=precise)
    mixing = scores[:, :, None] * decay_mat * step_part[None, :, :]
    inner_out = jnp.einsum("tsh,shp->thp", mixing, x_part, precision=precise)
    carried = jnp.exp(cumulative)[:, :, None] * jnp.einsum(
        "tn,hpn->thp", c_part, carry_state, precision=precise
    )
    weights = jnp.exp(cumulative[-1][None, :] - cumulative) * step_part
    update = jnp.einsum("sh,shp,sn->hpn", weights, x_part, b_part, precision=precise)
    new_state = jnp.exp(cumulative[-1])[:, None, None] * carry_state + update
    return (new_state, inner_out + carried)


def local_scan(x_heads, b_rows, c_rows, log_rows, step_rows):
    seg_rows = x_heads.shape[0]
    blocks = seg_rows // Q

    def blocked(tensor):
        return tensor.reshape((blocks, Q) + tensor.shape[1:])

    init_state = jnp.zeros((x_heads.shape[1], x_heads.shape[2], b_rows.shape[1]), jnp.float32)
    final_state, outputs = lax.scan(
        block_step,
        init_state,
        (blocked(x_heads), blocked(b_rows), blocked(c_rows), blocked(log_rows), blocked(step_rows)),
    )
    return (outputs.reshape(x_heads.shape), final_state, jnp.sum(log_rows, axis=0))


def incoming(c_rows, log_rows, state_in):
    cumulative = jnp.cumsum(log_rows, axis=0)
    return jnp.exp(cumulative)[:, :, None] * jnp.einsum(
        "tn,hpn->thp", c_rows, state_in, precision=precise
    )


def compose(earlier, later):
    return (later[0] * earlier[0], later[1] + later[0][..., None, None] * earlier[1])


def fetch_weights(w_zx, w_bc, w_dt, w_out, in_up, out_down):
    return (
        lax.all_gather(w_zx, ("dp", "seq"), axis=0, tiled=True),
        lax.all_gather(w_bc, ("dp", "seq"), axis=0, tiled=True),
        lax.all_gather(w_dt, ("dp", "seq"), axis=0, tiled=True),
        lax.all_gather(w_out, ("dp", "seq"), axis=1, tiled=True),
        lax.all_gather(in_up, ("dp", "seq"), axis=0, tiled=True),
        lax.all_gather(out_down, ("dp", "seq"), axis=1, tiled=True),
    )


def reduce_adapters(grads):
    near_sums = (
        lax.psum_scatter(grads[1], ("dp", "seq"), scatter_dimension=0, tiled=True),
        lax.psum_scatter(grads[2], ("dp", "seq"), scatter_dimension=1, tiled=True),
    )
    wide_sums = (
        lax.psum_scatter(grads[0], ("dp", "seq", "mp"), scatter_dimension=1, tiled=True),
        lax.psum_scatter(grads[3], ("dp", "seq", "mp"), scatter_dimension=1, tiled=True),
    )
    return (wide_sums[0], near_sums[0], near_sums[1], wide_sums[1])


def body(
    x_in,
    cotangent,
    lengths,
    adapter_ids,
    norm_gain,
    w_zx,
    w_bc,
    w_dt,
    dt_bias,
    a_log,
    d_skip,
    conv_x,
    conv_bc,
    gate_gain,
    w_out,
    in_down,
    in_up,
    out_down,
    out_up,
):
    micro_count, slot_count, seg_len, model_part = x_in.shape
    head_local = dt_bias.shape[0]
    inner_local = head_local * P_SIZE
    wide_down, wide_up = (
        lax.all_gather(in_down, ("dp", "seq", "mp"), axis=1, tiled=True),
        lax.all_gather(out_up, ("dp", "seq", "mp"), axis=1, tiled=True),
    )
    wide_down = wide_down.astype(jnp.float32)
    wide_up = wide_up.astype(jnp.float32)
    conv_taps = jnp.concatenate([conv_x, conv_bc], axis=1)
    decay_rate = -jnp.exp(a_log)
    positions = lax.axis_index("seq") * seg_len + jnp.arange(seg_len)
    feature_start = lax.axis_index("mp") * model_part
    scan_local = jax.vmap(local_scan)
    incoming_map = jax.vmap(incoming)
    gathered = None
    outputs = []
    x_grads = []
    running = None
    for batch_index in range(micro_count):
        gathered = fetch_weights(w_zx, w_bc, w_dt, w_out, in_up, out_down)
        zx_weight, bc_weight, dt_weight, out_weight, up_in, down_out = gathered
        rows_own = x_in[batch_index]
        cot_own = cotangent[batch_index]
        rows_full, cot_full = (
            lax.all_gather(rows_own, "mp", axis=2, tiled=True),
            lax.all_gather(cot_own, "mp", axis=2, tiled=True),
        )
        rows_value = rows_full.astype(jnp.float32)
        inv_rms = lax.rsqrt(jnp.mean(rows_value * rows_value, axis=-1, keepdims=True) + eps)
        normed = rows_value * inv_rms * norm_gain
        normed_low = normed.astype(jnp.bfloat16)
        normed_value = normed_low.astype(jnp.float32)
        select = jax.nn.one_hot(adapter_ids[batch_index], ADAPT, dtype=jnp.float32)
        down_sel = jnp.einsum("sa,adr->sdr", select, wide_down, precision=precise)
        up_sel = jnp.einsum(
            "sa,arcf->srcf",
            select,
            up_in.astype(jnp.float32).reshape(ADAPT, R, 2, inner_local),
            precision=precise,
        )
        low_rank = jnp.einsum("std,sdr->str", normed_value, down_sel, precision=precise)
        proj_zx = jnp.einsum(
            "std,dcf->stcf", normed_low, zx_weight, preferred_element_type=jnp.float32
        )
        proj_zx = proj_zx + jnp.einsum("str,srcf->stcf", low_rank, up_sel, precision=precise)
        proj_bc = jnp.einsum(
            "std,dn->stn", normed_low, bc_weight, preferred_element_type=jnp.float32
        )
        proj_dt = jnp.einsum(
            "std,dh->sth", normed_low, dt_weight, preferred_element_type=jnp.float32
        )
        gate_in = proj_zx[:, :, 0]
        conv_in = jnp.concatenate(
            [proj_zx[:, :, 1].astype(jnp.bfloat16), proj_bc.astype(jnp.bfloat16)], axis=-1
        )
        earlier_rows = shifted(conv_in[:, seg_len - (KC - 1) :], "seq", 1)
        extended = jnp.concatenate([earlier_rows, conv_in], axis=1).astype(jnp.float32)
        conv_pre = sum(
            (
                conv_taps[tap_index] * extended[:, tap_index : tap_index + seg_len]
                for tap_index in range(KC)
            )
        )
        conv_out = jax.nn.silu(conv_pre)
        x_heads = conv_out[..., :inner_local].reshape(slot_count, seg_len, head_local, P_SIZE)
        b_rows = conv_out[..., inner_local : inner_local + NS]
        c_rows = conv_out[..., inner_local + NS :]
        mask_rows = (positions[None, :] < lengths[batch_index][:, None]).astype(jnp.float32)
        rate_in = proj_dt + dt_bias
        step_rows = jax.nn.softplus(rate_in) * mask_rows[..., None]
        log_rows = step_rows * decay_rate
        (plain_out, state_local, log_total), scan_back = jax.vjp(
            scan_local, x_heads, b_rows, c_rows, log_rows, step_rows
        )
        factor = jnp.exp(log_total)
        identity = (jnp.ones_like(factor), jnp.zeros_like(state_local))
        state_in = entering((factor, state_local), "seq", compose, identity, False)[1]
        from_state, state_back = jax.vjp(incoming_map, c_rows, log_rows, state_in)
        mixed_heads = plain_out + from_state + d_skip[:, None] * x_heads
        mixed_flat = mixed_heads.reshape(slot_count, seg_len, inner_local)
        gate_act = jax.nn.silu(gate_in)
        gated_out = mixed_flat * gate_act
        square_sum = lax.psum(jnp.sum(gated_out * gated_out, axis=-1), "mp")
        inv_gate = lax.rsqrt(square_sum / DI + eps)
        scaled = gated_out * inv_gate[..., None] * gate_gain
        scaled_low = scaled.astype(jnp.bfloat16)
        scaled_value = scaled_low.astype(jnp.float32)
        out_sel = jnp.einsum(
            "sa,far->sfr",
            select,
            down_out.astype(jnp.float32).reshape(inner_local, ADAPT, R),
            precision=precise,
        )
        up_out = jnp.einsum("sa,ard->srd", select, wide_up.reshape(ADAPT, R, D), precision=precise)
        rank_out = jnp.einsum("stf,sfr->str", scaled_value, out_sel, precision=precise)
        partial_out = jnp.einsum(
            "stf,fd->std", scaled_low, out_weight, preferred_element_type=jnp.float32
        )
        partial_out = partial_out + jnp.einsum("str,srd->std", rank_out, up_out, precision=precise)
        branch = lax.psum_scatter(partial_out, "mp", scatter_dimension=2, tiled=True)
        outputs.append(
            (rows_own.astype(jnp.float32) + mask_rows[..., None] * branch).astype(jnp.bfloat16)
        )
        branch_grad = cot_full * mask_rows[..., None].astype(jnp.bfloat16)
        branch_value = branch_grad.astype(jnp.float32)
        rank_grad = jnp.einsum("std,srd->str", branch_value, up_out, precision=precise)
        grad_up_out = jnp.einsum("str,std->srd", rank_out, branch_value, precision=precise)
        grad_out_sel = jnp.einsum("stf,str->sfr", scaled_value, rank_grad, precision=precise)
        scaled_grad = jnp.einsum(
            "std,fd->stf", branch_grad, out_weight, preferred_element_type=jnp.float32
        )
        scaled_grad = scaled_grad + jnp.einsum(
            "str,sfr->stf", rank_grad, out_sel, precision=precise
        )
        weighted = scaled_grad * gate_gain
        dot_sum = lax.psum(jnp.sum(weighted * gated_out, axis=-1), "mp")
        gated_grad = (
            weighted * inv_gate[..., None] - gated_out * (inv_gate**3 * dot_sum / DI)[..., None]
        )
        mixed_grad = (gated_grad * gate_act).reshape(slot_count, seg_len, head_local, P_SIZE)
        gate_grad = gated_grad * mixed_flat * silu_grad(gate_in)
        c_grad_in, log_grad_in, state_in_grad = state_back(mixed_grad)
        later_grads = entering((factor, state_in_grad), "seq", compose, identity, True)[1]
        total_grad = jnp.sum(later_grads * state_in, axis=(2, 3)) * factor
        x_heads_grad, b_grad, c_grad, log_grad, step_grad = scan_back(
            (mixed_grad, later_grads, total_grad)
        )
        x_heads_grad = x_heads_grad + d_skip[:, None] * mixed_grad
        c_grad = c_grad + c_grad_in
        step_grad = step_grad + (log_grad + log_grad_in) * decay_rate
        rate_grad = step_grad * mask_rows[..., None] * jax.nn.sigmoid(rate_in)
        conv_out_grad = jnp.concatenate(
            [x_heads_grad.reshape(slot_count, seg_len, inner_local), b_grad, c_grad], axis=-1
        )
        pre_grad = conv_out_grad * silu_grad(conv_pre)
        padded_grad = jnp.pad(pre_grad, ((0, 0), (KC - 1, KC - 1), (0, 0)))
        ext_grad = sum(
            (
                conv_taps[tap_index]
                * padded_grad[:, KC - 1 - tap_index : KC - 1 - tap_index + seg_len + KC - 1]
                for tap_index in range(KC)
            )
        )
        returned = shifted(ext_grad[:, : KC - 1], "seq", -1)
        in_grad = ext_grad[:, KC - 1 :]
        in_grad = in_grad.at[:, seg_len - (KC - 1) :].add(returned)
        zx_grad = jnp.stack([gate_grad, in_grad[..., :inner_local]], axis=2).astype(jnp.bfloat16)
        dt_grad_low = rate_grad.astype(jnp.bfloat16)
        zx_grad_value = zx_grad.astype(jnp.float32)
        rank_in_grad = jnp.einsum("stcf,srcf->str", zx_grad_value, up_sel, precision=precise)
        grad_up_sel = jnp.einsum("str,stcf->srcf", low_rank, zx_grad_value, precision=precise)
        grad_down_sel = jnp.einsum("std,str->sdr", normed_value, rank_in_grad, precision=precise)
        normed_part = jnp.einsum(
            "stcf,dcf->std", zx_grad, zx_weight, preferred_element_type=jnp.float32
        )
        normed_part = normed_part + jnp.einsum(
            "sth,dh->std", dt_grad_low, dt_weight, preferred_element_type=jnp.float32
        )
        normed_part = normed_part + jnp.einsum(
            "str,sdr->std", rank_in_grad, down_sel, precision=precise
        )
        bc_partial = in_grad[..., inner_local:]
        normed_sum, bc_sum = lax.psum((normed_part, bc_partial), "mp")
        normed_grad = normed_sum + jnp.einsum(
            "stn,dn->std",
            bc_sum.astype(jnp.bfloat16),
            bc_weight,
            preferred_element_type=jnp.float32,
        )
        scaled_in = normed_grad * norm_gain
        row_grad = inv_rms * scaled_in - rows_value * inv_rms**3 * jnp.mean(
            scaled_in * rows_value, axis=-1, keepdims=True
        )
        own_slice = lax.dynamic_slice_in_dim(row_grad, feature_start, model_part, 2)
        x_grads.append(cot_own.astype(jnp.float32) + own_slice)
        local_grads = (
            jnp.einsum("sa,sdr->adr", select, grad_down_sel, precision=precise),
            jnp.einsum("sa,srcf->arcf", select, grad_up_sel, precision=precise).reshape(
                ADAPT * R, 2, inner_local
            ),
            jnp.einsum("sa,sfr->far", select, grad_out_sel, precision=precise).reshape(
                inner_local, ADAPT * R
            ),
            jnp.einsum("sa,srd->ard", select, grad_up_out, precision=precise).reshape(ADAPT * R, D),
        )
        running = local_grads if running is None else jax.tree.map(jnp.add, running, local_grads)
    running = reduce_adapters(running)
    return (jnp.stack(outputs), jnp.stack(x_grads), running[0], running[1], running[2], running[3])


def split(v):
    hi = v.astype(jnp.bfloat16)
    return hi, (v - hi.astype(jnp.float32)).astype(jnp.bfloat16)


def mm(a, b):
    return lax.dot_general(a, b, (((1,), (0,)), ((), ())), preferred_element_type=jnp.float32)


def mm_t(a, b):
    return lax.dot_general(a, b, (((1,), (1,)), ((), ())), preferred_element_type=jnp.float32)


def mm3(a, b):
    return mm(a[0], b[0]) + mm(a[0], b[1]) + mm(a[1], b[0])


def mm3_t(a, b):
    return mm_t(a[0], b[0]) + mm_t(a[0], b[1]) + mm_t(a[1], b[0])


def conv_rows(rows, halo, taps):
    count = rows.shape[0]
    ext = jnp.concatenate([halo, rows], axis=0).astype(jnp.float32)
    total = taps[0:1] * ext[HALO - 3 : HALO - 3 + count]
    for j in range(1, KC):
        total = total + taps[j : j + 1] * ext[HALO - 3 + j : HALO - 3 + j + count]
    return total


def conv_rows_back(grad, taps):
    count, width = grad.shape
    zero = jnp.zeros((8, width), jnp.float32)
    ext = jnp.concatenate([zero, grad, zero], axis=0)
    total = taps[0:1] * ext[3 : 3 + count + 8]
    for j in range(1, KC):
        total = total + taps[j : j + 1] * ext[3 - j : 3 - j + count + 8]
    return total


def widen(columns, first):
    rows = columns.shape[0]
    lane = lax.broadcasted_iota(jnp.int32, (rows, 2 * P_SIZE), 1)
    return jnp.where(lane < P_SIZE, columns[:, first : first + 1], columns[:, first + 1 : first + 2])


def widen_all(columns):
    return jnp.concatenate([widen(columns, h) for h in range(0, HG, 2)], axis=1)


def head_sums(prod, group):
    rows = prod.shape[1]
    row = lax.broadcasted_iota(jnp.int32, (rows, 128), 0) // P_SIZE + group * HG
    lane = lax.broadcasted_iota(jnp.int32, (rows, 128), 1)
    pick = (row == lane).astype(jnp.float32).astype(jnp.bfloat16)
    hi, lo = split(prod)
    return mm(hi, pick) + mm(lo, pick)


def local_kernel(
    xin_ref, halo_ref, taps_ref, bcin_ref, bchalo_ref, bctaps_ref, cum_ref, cumt_ref, stept_ref, wt_ref, ec_ref,
    dec_ref, skip_ref, y_ref, state_ref, bc_ref, scores_ref, bt_ref
):
    rows = xin_ref.shape[1]
    blocks = rows // Q

    @pl.when(pl.program_id(1) == 0)
    def _():
        pre = conv_rows(bcin_ref[0], bchalo_ref[0], bctaps_ref[...])
        bc = pre * jax.nn.sigmoid(pre)
        bc_ref[0] = bc
        for b in range(blocks):
            part = bc[b * Q : (b + 1) * Q]
            b_part = split(part[:, :NS])
            c_part = split(part[:, NS:])
            scores_ref[b] = mm3_t(c_part, b_part)
            hi, lo = split(part[:, :NS].T)
            bt_ref[0, b] = hi
            bt_ref[1, b] = lo

    pre = conv_rows(xin_ref[0], halo_ref[0], taps_ref[...])
    x = pre * jax.nn.sigmoid(pre)
    lane = lax.broadcasted_iota(jnp.int32, (Q, 2 * P_SIZE), 1)
    causal = lax.broadcasted_iota(jnp.int32, (Q, Q), 0) >= lax.broadcasted_iota(jnp.int32, (Q, Q), 1)
    state = None
    for b in range(blocks):
        at = slice(b * Q, (b + 1) * Q)
        scores = scores_ref[b]
        xb = x[at]
        if b > 0:
            carried = widen_all(ec_ref[0, 0, at]) * mm3(split(bc_ref[0, at, NS:]), split(state))
        for h in range(0, HG, 2):
            pair = xb[:, h * P_SIZE : (h + 2) * P_SIZE]
            x_hi, x_lo = split(pair)
            both = jnp.concatenate([x_hi, x_lo], axis=1)
            halves = []
            for k in (h, h + 1):
                spread = cum_ref[0, 0, at, k : k + 1] - cumt_ref[0, 0, k : k + 1, at]
                decay = jnp.exp(jnp.where(causal, spread, -10000.0))
                m_hi, m_lo = split(scores * decay * stept_ref[0, 0, k : k + 1, at])
                first = mm(m_hi, both)
                halves.append(first[:, : 2 * P_SIZE] + first[:, 2 * P_SIZE :] + mm(m_lo, x_hi))
            skip = skip_ref[0:1, h * P_SIZE : (h + 2) * P_SIZE]
            y_pair = jnp.where(lane < P_SIZE, halves[0], halves[1]) + skip * pair
            if b > 0:
                y_pair = y_pair + carried[:, h * P_SIZE : (h + 2) * P_SIZE]
            y_ref[0, at, h * P_SIZE : (h + 2) * P_SIZE] = y_pair
        wx = xb * widen_all(wt_ref[0, 0, at])
        update = mm3((bt_ref[0, b], bt_ref[1, b]), split(wx))
        state = update if state is None else dec_ref[0, b : b + 1] * state + update
    state_ref[0] = state


def carry_kernel(y_ref, state_ref, bc_ref, el_ref, z_ref, mixed_ref, sum_ref):
    group = pl.program_id(1)
    c_part = split(bc_ref[0, :, NS:])
    mixed = y_ref[0] + widen_all(el_ref[0, 0]) * mm3(c_part, split(state_ref[0]))
    mixed_ref[0] = mixed
    z = z_ref[0]
    gated = mixed * (z * jax.nn.sigmoid(z))
    square = gated * gated
    part = square[:, :128]
    for k in range(1, square.shape[1] // 128):
        part = part + square[:, k * 128 : (k + 1) * 128]

    @pl.when(group == 0)
    def _():
        sum_ref[0] = part

    @pl.when(group > 0)
    def _():
        sum_ref[0] += part


def gate_back_kernel(
    gs_ref, mixed_ref, z_ref, inv_ref, coef_ref, gain_ref, bc_ref, el_ref, dy_ref, gz_ref, lam_ref, q_ref, ct_ref
):
    group = pl.program_id(1)

    @pl.when(group == 0)
    def _():
        hi, lo = split(bc_ref[0, :, NS:].T)
        ct_ref[0] = hi
        ct_ref[1] = lo

    z = z_ref[0]
    mixed = mixed_ref[0]
    sig = jax.nn.sigmoid(z)
    act = z * sig
    g_gated = gs_ref[0] * gain_ref[...] * inv_ref[0] - (mixed * act) * coef_ref[0]
    dy = g_gated * act
    dy_ref[0] = dy
    gz_ref[0] = (g_gated * mixed * (sig * (1.0 + z * (1.0 - sig)))).astype(jnp.bfloat16)
    lam_ref[0] = mm3((ct_ref[0], ct_ref[1]), split(dy * widen_all(el_ref[0, 0])))
    q = head_sums(dy * mixed, group)

    @pl.when(group == 0)
    def _():
        q_ref[0] = q

    @pl.when(group > 0)
    def _():
        q_ref[0] += q


def scan_back_kernel(
    dy_ref, xin_ref, halo_ref, taps_ref, bc_ref, cum_ref, cumt_ref, step_ref, wt0_ref, ec_ref, dec_ref, skip_ref,
    state_ref, lam_ref, gx_ref, head_ref, tail_ref, gbc_ref, xu_ref, dx_ref, scorest_ref, dscorest_ref, bt_ref, ct_ref
):
    group = pl.program_id(1)
    rows = xin_ref.shape[1]
    blocks = rows // Q

    @pl.when(group == 0)
    def _():
        for b in range(blocks):
            part = bc_ref[0, b * Q : (b + 1) * Q]
            scorest_ref[b] = mm3_t(split(part[:, :NS]), split(part[:, NS:]))
            dscorest_ref[b] = jnp.zeros((Q, Q), jnp.float32)
            hi, lo = split(part[:, :NS].T)
            bt_ref[0, b] = hi
            bt_ref[1, b] = lo
            hi, lo = split(part[:, NS:].T)
            ct_ref[0, b] = hi
            ct_ref[1, b] = lo
        gbc_ref[0] = jnp.zeros((rows, 2 * NS), jnp.float32)
        xu_ref[0] = jnp.zeros((rows, 128), jnp.float32)
        dx_ref[0] = jnp.zeros((rows, 128), jnp.float32)

    pre = conv_rows(xin_ref[0], halo_ref[0], taps_ref[...])
    sig = jax.nn.sigmoid(pre)
    x = pre * sig
    lane = lax.broadcasted_iota(jnp.int32, (Q, 2 * P_SIZE), 1)
    causal = lax.broadcasted_iota(jnp.int32, (Q, Q), 0) <= lax.broadcasted_iota(jnp.int32, (Q, Q), 1)
    states = [state_ref[0]]
    for b in range(blocks - 1):
        at = slice(b * Q, (b + 1) * Q)
        wx = x[at] * widen_all(wt0_ref[0, 0, at] * step_ref[0, 0, at])
        states.append(dec_ref[0, b : b + 1] * states[b] + mm3((bt_ref[0, b], bt_ref[1, b]), split(wx)))
    lam = lam_ref[0]
    g_parts = [None] * blocks
    for b in reversed(range(blocks)):
        at = slice(b * Q, (b + 1) * Q)
        xb = x[at]
        dy = dy_ref[0, at]
        scores = scorest_ref[b]
        dscores = dscorest_ref[b]
        u_parts = []
        for h in range(0, HG, 2):
            pair = slice(h * P_SIZE, (h + 2) * P_SIZE)
            x_hi, x_lo = split(xb[:, pair])
            d_hi, d_lo = split(dy[:, pair])
            both = jnp.concatenate([d_hi, d_lo], axis=1)
            halves = []
            for k in (h, h + 1):
                mine = (lane < P_SIZE) if k == h else (lane >= P_SIZE)
                spread = cumt_ref[0, 0, k : k + 1, at] - cum_ref[0, 0, at, k : k + 1]
                decay = jnp.exp(jnp.where(causal, spread, -10000.0))
                zero = jnp.zeros_like(x_hi)
                xm_hi = jnp.where(mine, x_hi, zero)
                xm_lo = jnp.where(mine, x_lo, zero)
                dm = mm_t(xm_hi, d_hi) + mm_t(xm_hi, d_lo) + mm_t(xm_lo, d_hi)
                dscores = dscores + dm * decay * step_ref[0, 0, at, k : k + 1]
                m_hi, m_lo = split(scores * decay)
                first = mm(m_hi, both)
                halves.append(first[:, : 2 * P_SIZE] + first[:, 2 * P_SIZE :] + mm(m_lo, d_hi))
            u_parts.append(jnp.where(lane < P_SIZE, halves[0], halves[1]))
        dscorest_ref[b] = dscores
        wt0 = widen_all(wt0_ref[0, 0, at])
        step = widen_all(step_ref[0, 0, at])
        lam_s = split(lam)
        part = bc_ref[0, at]
        u = jnp.concatenate(u_parts, axis=1) + wt0 * mm3(split(part[:, :NS]), lam_s)
        ev = split(widen_all(ec_ref[0, 0, at]) * dy)
        gbc_ref[0, at, :NS] += mm3_t(split(wt0 * step * xb), lam_s)
        gbc_ref[0, at, NS:] += mm3_t(ev, split(states[b]))
        if b > 0:
            lam = dec_ref[0, b : b + 1] * lam + mm3((ct_ref[0, b], ct_ref[1, b]), ev)
        xu_ref[0, at] += head_sums(xb * u, group)
        dx_ref[0, at] += head_sums(xb * dy * skip_ref[0:1], group)
        g_parts[b] = step * u + skip_ref[0:1] * dy
    g_pre = jnp.concatenate(g_parts, axis=0) * (sig * (1.0 + pre * (1.0 - sig)))
    g_ext = conv_rows_back(g_pre, taps_ref[...])
    gx_ref[0] = g_ext[8:].astype(jnp.bfloat16)
    head_ref[0] = g_ext[:8]
    tail_ref[0] = g_ext[rows:]

    @pl.when(group == pl.num_programs(1) - 1)
    def _():
        for b in range(blocks):
            at = slice(b * Q, (b + 1) * Q)
            part = bc_ref[0, at]
            ds = dscorest_ref[b]
            gbc_ref[0, at, :NS] += mm3(split(ds), split(part[:, NS:]))
            gbc_ref[0, at, NS:] += mm3(split(ds.T), split(part[:, :NS]))


def bc_back_kernel(g_ref, in_ref, halo_ref, taps_ref, out_ref, head_ref, tail_ref):
    rows = in_ref.shape[1]
    pre = conv_rows(in_ref[0], halo_ref[0], taps_ref[...])
    sig = jax.nn.sigmoid(pre)
    g_ext = conv_rows_back(g_ref[0] * (sig * (1.0 + pre * (1.0 - sig))), taps_ref[...])
    out_ref[0] = g_ext[8:]
    head_ref[0] = g_ext[:8]
    tail_ref[0] = g_ext[rows:]


def block(shape, index):
    return pl.BlockSpec(shape, index)


def call(kernel, name, groups, ins, outs, scratch, flops, size):
    return pl.pallas_call(
        kernel,
        name=name,
        grid=(1, groups),
        in_specs=[s for _, s in ins],
        out_specs=[s for _, s in outs],
        out_shape=[s for s, _ in outs],
        scratch_shapes=scratch,
        compiler_params=pltpu.CompilerParams(vmem_limit_bytes=VMEM_LIMIT),
        cost_estimate=pl.CostEstimate(flops=flops, bytes_accessed=size, transcendentals=0),
    )(*[a for a, _ in ins])


def split_low(v):
    hi = lax.reduce_precision(v, 8, 7)
    return jnp.concatenate([hi.astype(jnp.bfloat16), (v - hi).astype(jnp.bfloat16)], axis=-1)


def dot32(a, b, dims=((1,), (0,))):
    return lax.dot_general(a, b, (dims, ((), ())), preferred_element_type=jnp.float32)


def fold(v):
    half = v.shape[-1] // 2
    return v[..., :half] + v[..., half:]


def fast_body(
    x_in, cotangent, lengths, adapter_ids, norm_gain, w_zx, w_bc, w_dt, dt_bias, a_log, d_skip, conv_x, conv_bc,
    gate_gain, w_out, in_down, in_up, out_down, out_up
):
    bf16, f32 = jnp.bfloat16, jnp.float32
    micros, _, seg, feats = x_in.shape
    nz, nd = lax.axis_size("mp"), lax.axis_size("dp")
    core, z = lax.axis_index("seq"), lax.axis_index("mp")
    own = seg // nz
    tokens = 2 * own
    heads = dt_bias.shape[0] * nz // 2
    chan = heads * P_SIZE
    part = chan // nz
    groups = heads // HG
    wide = HG * P_SIZE
    blocks = tokens // Q
    swap = [(0, 1), (1, 0)]

    def other(v):
        return lax.ppermute(v, "seq", swap)

    def pair_cat(mine, theirs, axis):
        return jnp.where(
            core == 0, jnp.concatenate([mine, theirs], axis), jnp.concatenate([theirs, mine], axis)
        )

    def halves(v, axis, parts=2):
        shape = v.shape[:axis] + (parts, v.shape[axis] // parts) + v.shape[axis + 1 :]
        v = v.reshape(shape)
        return (
            lax.dynamic_index_in_dim(v, core, axis, False),
            lax.dynamic_index_in_dim(v, 1 - core, axis, False),
        )

    zx_mine, zx_theirs = halves(w_zx, 2)
    out_mine, out_theirs = halves(w_out, 0)
    up_mine, up_theirs = halves(in_up, 2)
    down_mine, down_theirs = halves(out_down, 0)
    dt_mine, dt_theirs = halves(w_dt, 1)
    bc_piece = lax.dynamic_slice_in_dim(w_bc, z * (w_bc.shape[0] // nz), w_bc.shape[0] // nz, 0)
    same = (bc_piece, in_down, out_up)
    small = [up_mine, down_mine, dt_mine, *same]
    small_shapes = [v.shape for v in small]
    pack_mine = jnp.concatenate([v.reshape(-1) for v in small])
    pack_theirs = jnp.concatenate([v.reshape(-1) for v in (up_theirs, down_theirs, dt_theirs, *same)])
    zx_pair = pair_cat(zx_mine, other(zx_theirs), 0)
    out_pair = pair_cat(out_mine, other(out_theirs), 1)
    pack_pair = pair_cat(pack_mine[None], other(pack_theirs)[None], 0)
    params = jnp.concatenate([dt_bias, a_log, d_skip, gate_gain, conv_x.reshape(-1)])
    params = lax.all_gather(params, "mp")
    packs = lax.all_gather(pack_pair, ("dp", "mp")).reshape(nd, nz, 2, -1)
    zx_all = lax.all_gather(zx_pair, ("dp", "mp")).reshape((nd, nz) + zx_pair.shape)
    out_all = lax.all_gather(out_pair, ("dp", "mp")).reshape((nd, nz) + out_pair.shape)
    zx_weight = jnp.transpose(zx_all, (3, 0, 2, 1, 4)).reshape(2, D, chan)
    out_weight = jnp.transpose(out_all, (1, 2, 0, 3)).reshape(chan, D)
    pieces = []
    at = 0
    for shape in small_shapes:
        size = 1
        for n in shape:
            size *= n
        pieces.append(packs[..., at : at + size].reshape((nd, nz, 2) + shape))
        at += size
    up_in = jnp.transpose(pieces[0], (0, 2, 3, 4, 1, 5)).reshape(ADAPT, R, 2 * chan)
    down_out = jnp.transpose(pieces[1], (0, 2, 4, 1, 3)).reshape(ADAPT, R, chan)
    dt_weight = jnp.transpose(pieces[2], (0, 2, 3, 1, 4)).reshape(D, heads)
    bc_weight = jnp.transpose(pieces[3], (0, 2, 1, 3, 4)).reshape(D, 2 * NS)
    wide_down = jnp.transpose(pieces[4], (3, 5, 0, 2, 1, 4)).reshape(ADAPT, R, D)
    wide_up = jnp.transpose(pieces[5], (3, 0, 2, 1, 4)).reshape(ADAPT, R, D)

    hl = dt_bias.shape[0]
    def own_part(v):
        v = v.reshape(v.shape[0], 2, v.shape[1] // 2)
        return lax.dynamic_index_in_dim(v, core, 1, False).reshape(-1)
    bias = own_part(params[:, :hl])
    rate = -jnp.exp(own_part(params[:, hl : 2 * hl]))
    skip = jnp.repeat(own_part(params[:, 2 * hl : 3 * hl]), P_SIZE)[None]
    width = gate_gain.shape[0]
    gain = own_part(params[:, 3 * hl : 3 * hl + width])[None]
    taps = params[:, 3 * hl + width :].reshape(nz, KC, 2, part)
    taps = jnp.transpose(lax.dynamic_index_in_dim(taps, core, 2, False), (1, 0, 2)).reshape(KC, chan)

    chunk = nz // 2
    mine = (z % chunk) * 2 + core

    def flat(c, zz):
        return c * nz + zz

    def route(step):
        pairs = []
        for c in range(2):
            for zz in range(nz):
                q = zz ^ step
                pairs.append((flat(c, zz), flat(q % 2, c * chunk + q // 2)))
        return pairs

    def to_rows(v):
        got = [
            lax.ppermute(lax.dynamic_slice_in_dim(v, (z ^ step) * own, own, 1), ("seq", "mp"), route(step))
            for step in range(nz)
        ]
        full = jnp.zeros(v.shape[:1] + (own, nz * feats), v.dtype)
        for step in range(nz):
            full = lax.dynamic_update_slice_in_dim(full, got[step], (mine ^ step) * feats, 2)
        return full

    def to_features(v):
        full = jnp.zeros(v.shape[:1] + (seg, feats), v.dtype)
        for step in range(nz):
            piece = lax.dynamic_slice_in_dim(v, (mine ^ step) * feats, feats, 2)
            got = lax.ppermute(piece, ("seq", "mp"), [(b, a) for a, b in route(step)])
            full = lax.dynamic_update_slice_in_dim(full, got, (z ^ step) * own, 1)
        return full

    x_rows = to_rows(x_in[:, 0])
    cot_rows = to_rows(cotangent[:, 0])
    start = z * tokens
    own_pos = start + core * own + jnp.arange(own)
    all_pos = start + jnp.arange(tokens)
    tri = (jnp.arange(Q)[:, None] >= jnp.arange(Q)[None, :]).astype(f32)
    tri_all = (jnp.arange(tokens)[:, None] <= jnp.arange(tokens)[None, :]).astype(f32)
    forward_edge = [(i, i + 1) for i in range(nz - 1)]
    backward_edge = [(i + 1, i) for i in range(nz - 1)]

    m3 = lambda m, g: (0, 0, g)
    m0 = lambda m, g: (0, 0, 0)
    g4 = lambda m, g: (0, g, 0, 0)
    g2 = lambda m, g: (0, g)
    z2 = lambda m, g: (0, 0)
    col = block((1, 1, tokens, HG), g4)
    row = block((1, 1, HG, tokens), g4)
    chan_block = block((1, tokens, wide), m3)
    halo_block = block((1, HALO, wide), m3)
    taps_block = block((KC, wide), g2)
    line_block = block((1, wide), g2)
    state_block = block((1, NS, wide), m3)
    dec_block = block((1, blocks, wide), m3)
    bc_block = block((1, tokens, 2 * NS), m0)
    one_col = block((1, tokens, 1), m0)
    sums_block = block((1, tokens, 128), m0)
    tok_f32 = jax.ShapeDtypeStruct((1, tokens, chan), f32)
    tok_b16 = jax.ShapeDtypeStruct((1, tokens, chan), bf16)
    state_f32 = jax.ShapeDtypeStruct((1, NS, chan), f32)
    bc_f32 = jax.ShapeDtypeStruct((1, tokens, 2 * NS), f32)
    sums_f32 = jax.ShapeDtypeStruct((1, tokens, 128), f32)
    edge_f32 = jax.ShapeDtypeStruct((1, 8, chan), f32)
    edge_block = block((1, 8, wide), m3)
    act_bytes = tokens * chan * 4

    def cols(v):
        return jnp.transpose(v.reshape(tokens, groups, HG), (1, 0, 2))[None]

    def rows_of(v):
        return jnp.transpose(v.reshape(tokens, groups, HG), (1, 2, 0))[None]

    S = [dict() for _ in range(micros)]
    for m in range(micros):
        s = S[m]
        x = x_rows[m].astype(f32)
        s["inv"] = lax.rsqrt(jnp.mean(x * x, axis=-1, keepdims=True) + eps)
        low_own = (x * s["inv"] * norm_gain).astype(bf16)
        s["low"] = pair_cat(low_own, other(low_own), 0)
        cot = cot_rows[m]
        s["mask_own"] = (own_pos < lengths[m, 0]).astype(f32)[:, None]
        s["mask"] = (all_pos < lengths[m, 0]).astype(f32)[:, None]
        gb_own = cot * s["mask_own"].astype(bf16)
        s["gb"] = pair_cat(gb_own, other(gb_own), 0)
        k = adapter_ids[m, 0]
        s["pick"] = (k == jnp.arange(ADAPT)).astype(f32)
        s["a_in"] = lax.dynamic_index_in_dim(wide_down, k, 0, False)
        s["u_in"] = lax.dynamic_index_in_dim(up_in, k, 0, False)
        s["a_out"] = lax.dynamic_index_in_dim(down_out, k, 0, False)
        s["u_out"] = lax.dynamic_index_in_dim(wide_up, k, 0, False)

    for m in range(micros):
        s = S[m]
        low = s["low"]
        s["lr"] = split_low(dot32(low, s["a_in"], ((1,), (1,))))
        u2 = jnp.concatenate([s["u_in"], s["u_in"]], 0)
        s["z"] = (dot32(low, zx_weight[0]) + dot32(s["lr"], u2[:, :chan]))[None]
        s["xin"] = (dot32(low, zx_weight[1]) + dot32(s["lr"], u2[:, chan:])).astype(bf16)[None]
        s["bcin"] = dot32(low, bc_weight).astype(bf16)[None]
        s["rate_in"] = dot32(low, dt_weight) + bias
        tail = jnp.concatenate([s["xin"][:, tokens - HALO :], s["bcin"][:, tokens - HALO :]], axis=2)
        halo = lax.ppermute(tail, "mp", forward_edge)
        s["halo"], s["bchalo"] = halo[..., :chan], halo[..., chan:]
        step = jax.nn.softplus(s["rate_in"]) * s["mask"]
        log = (step * rate).reshape(blocks, Q, heads)
        cum = jnp.einsum("ts,bsh->bth", tri, log, precision=precise)
        total = cum[:, -1]
        before = jnp.concatenate([jnp.zeros((1, heads), f32), jnp.cumsum(total, axis=0)[:-1]], 0)
        s["step"] = cols(step)
        s["stept"] = rows_of(step)
        s["cum"] = cols(cum)
        s["cumt"] = rows_of(cum)
        rest = jnp.exp(total[:, None] - cum).reshape(tokens, heads)
        s["wt0"] = cols(rest)
        s["wt"] = cols(rest * step)
        s["ec"] = cols(jnp.exp(cum))
        s["el"] = cols(jnp.exp(cum + before[:, None]))
        s["dec"] = jnp.repeat(jnp.exp(total), P_SIZE, axis=1)[None]
        s["all"] = jnp.repeat(jnp.exp(jnp.sum(total, axis=0)), P_SIZE)[None, None]
        s["y"], s["sloc"], s["bc"] = call(
            local_kernel, "ssd_local", groups,
            [(s["xin"], chan_block), (s["halo"], halo_block), (taps, taps_block),
             (s["bcin"], bc_block), (s["bchalo"], block((1, HALO, 2 * NS), m0)), (conv_bc, block((KC, 2 * NS), z2)),
             (s["cum"], col), (s["cumt"], row), (s["stept"], row), (s["wt"], col), (s["ec"], col),
             (s["dec"], dec_block), (skip, line_block)],
            [(tok_f32, chan_block), (state_f32, state_block), (bc_f32, bc_block)],
            [pltpu.VMEM((blocks, Q, Q), f32), pltpu.VMEM((2, blocks, NS, Q), bf16)],
            6 * tokens * Q * chan * 2, act_bytes * 2,
        )
    for m in range(micros):
        s = S[m]
        state = jnp.zeros_like(s["sloc"])
        for hop in range(nz - 1):
            state = state + lax.ppermute(s["all"] * state + s["sloc"], "mp", [(hop, hop + 1)])
        s["state"] = state
        s["send"] = s["all"] * state + s["sloc"]
    for m in range(micros):
        s = S[m]
        s["mixed"], square = call(
            carry_kernel, "ssd_carry", groups,
            [(s["y"], chan_block), (s["state"], state_block), (s["bc"], bc_block), (s["el"], col), (s["z"], chan_block)],
            [(tok_f32, chan_block), (sums_f32, sums_block)], [], 6 * tokens * NS * chan, act_bytes * 3,
        )
        square = jnp.sum(square, axis=-1)
        s["inv_gate"] = lax.rsqrt((square + other(square)) / DI + eps)[..., None]
        zz = s["z"]
        s["gated"] = s["mixed"] * (zz * jax.nn.sigmoid(zz))
        scaled = (s["gated"] * s["inv_gate"] * gain).astype(bf16)[0]
        s["scaled"] = scaled
        gb = s["gb"]
        s["ro"] = split_low(dot32(scaled, s["a_out"], ((1,), (1,))))
        rank_grad = dot32(gb, s["u_out"], ((1,), (1,)))
        s["rg"] = split_low(rank_grad)
        a2 = jnp.concatenate([s["a_out"], s["a_out"]], 0)
        s["gs"] = (dot32(gb, out_weight, ((1,), (1,))) + dot32(s["rg"], a2))[None]
        dots = jnp.sum(s["gs"] * gain * s["gated"], axis=-1)
        inv = s["inv_gate"]
        s["coef"] = inv**3 * ((dots + other(dots)) / DI)[..., None]
        s["dy"], s["gz"], s["lloc"], s["q"] = call(
            gate_back_kernel, "gate_back", groups,
            [(s["gs"], chan_block), (s["mixed"], chan_block), (zz, chan_block), (inv, one_col), (s["coef"], one_col),
             (gain, line_block), (s["bc"], bc_block), (s["el"], col)],
            [(tok_f32, chan_block), (tok_b16, chan_block), (state_f32, state_block), (sums_f32, sums_block)],
            [pltpu.VMEM((2, NS, tokens), bf16)], 6 * tokens * NS * chan, act_bytes * 5,
        )
    for m in range(micros):
        s = S[m]
        lam = jnp.zeros_like(s["lloc"])
        for hop in range(nz - 1, 0, -1):
            lam = lam + lax.ppermute(s["all"] * lam + s["lloc"], "mp", [(hop, hop - 1)])
        s["lam"] = lam

    def reduce_rows(v):
        theirs = lax.dynamic_slice_in_dim(v, (1 - core) * own, own, 0)
        return lax.dynamic_slice_in_dim(v, core * own, own, 0) + other(theirs)

    outs = []
    for m in range(micros):
        s = S[m]
        u2 = jnp.concatenate([s["u_out"], s["u_out"]], 0)
        branch = reduce_rows(dot32(s["scaled"], out_weight) + dot32(s["ro"], u2))
        rows = (x_rows[m].astype(f32) + s["mask_own"] * branch).astype(bf16)
        outs.append(to_features(rows[None]))
        s["g_up_out"] = dot32(s["ro"], s["gb"], ((0,), (0,)))
        s["g_up_out"] = s["g_up_out"][:R] + s["g_up_out"][R:]
        g_out = dot32(s["rg"], s["scaled"], ((0,), (0,)))
        s["g_out"] = g_out[:R] + g_out[R:]

    grads = []
    for m in range(micros):
        s = S[m]
        gx, head, tail, gbc, xu, dx = call(
            scan_back_kernel, "ssd_back", groups,
            [(s["dy"], chan_block), (s["xin"], chan_block), (s["halo"], halo_block), (taps, taps_block), (s["bc"], bc_block),
             (s["cum"], col), (s["cumt"], row), (s["step"], col), (s["wt0"], col), (s["ec"], col), (s["dec"], dec_block),
             (skip, line_block), (s["state"], state_block), (s["lam"], state_block)],
            [(tok_b16, chan_block), (edge_f32, edge_block), (edge_f32, edge_block), (bc_f32, bc_block), (sums_f32, sums_block),
             (sums_f32, sums_block)],
            [pltpu.VMEM((blocks, Q, Q), f32), pltpu.VMEM((blocks, Q, Q), f32), pltpu.VMEM((2, blocks, NS, Q), bf16),
             pltpu.VMEM((2, blocks, NS, Q), bf16)],
            12 * tokens * Q * chan * 2, act_bytes * 3,
        )
        gbc = gbc + other(gbc)
        one = lambda m, g: (0, 0, 0)
        edge_bc = jax.ShapeDtypeStruct((1, 8, 2 * NS), f32)
        gbc, bhead, btail = call(
            bc_back_kernel, "bc_back", 1,
            [(gbc, bc_block), (s["bcin"], bc_block), (s["bchalo"], block((1, HALO, 2 * NS), one)),
             (conv_bc, block((KC, 2 * NS), z2))],
            [(bc_f32, bc_block), (edge_bc, block((1, 8, 2 * NS), one)), (edge_bc, block((1, 8, 2 * NS), one))],
            [], 0, tokens * 2 * NS * 8,
        )
        back = lax.ppermute(jnp.concatenate([head, bhead], 2), "mp", backward_edge)
        tail = tail.at[:, 8 - (KC - 1) :].add(back[:, 8 - (KC - 1) :, :chan])
        btail = btail.at[:, 8 - (KC - 1) :].add(back[:, 8 - (KC - 1) :, chan:])
        gx = lax.dynamic_update_slice_in_dim(gx, tail.astype(bf16), tokens - 8, 1)[0]
        gbc = lax.dynamic_update_slice_in_dim(gbc, btail, tokens - 8, 1)[0].astype(bf16)
        step = s["step"][0].transpose(1, 0, 2).reshape(tokens, heads)
        xu = xu[0, :, :heads]
        flow = s["q"][0, :, :heads] - dx[0, :, :heads] - step * xu
        ends = jnp.sum((s["lam"] * s["send"]).reshape(NS, heads, P_SIZE), axis=(0, 2))
        g_log = jnp.einsum("ts,sh->th", tri_all, flow, precision=precise) + ends
        g_rate = ((xu + g_log * rate) * s["mask"] * jax.nn.sigmoid(s["rate_in"])).astype(bf16)
        gz = s["gz"][0]
        low = s["low"]
        ri = dot32(gz, s["u_in"][:, :chan], ((1,), (1,))) + dot32(gx, s["u_in"][:, chan:], ((1,), (1,)))
        ri = split_low(ri)
        lr = s["lr"]
        s["g_up_z"] = dot32(lr, gz, ((0,), (0,)))
        s["g_up_x"] = dot32(lr, gx, ((0,), (0,)))
        s["g_up_z"] = s["g_up_z"][:R] + s["g_up_z"][R:]
        s["g_up_x"] = s["g_up_x"][:R] + s["g_up_x"][R:]
        g_down = dot32(ri, low, ((0,), (0,)))
        s["g_down"] = g_down[:R] + g_down[R:]
        a2 = jnp.concatenate([s["a_in"], s["a_in"]], 0)
        half = lax.dynamic_slice_in_dim(gbc, core * NS, NS, 1)
        bc_half = lax.dynamic_slice_in_dim(bc_weight, core * NS, NS, 1)
        g_low = (
            dot32(gz, zx_weight[0], ((1,), (1,)))
            + dot32(gx, zx_weight[1], ((1,), (1,)))
            + dot32(jnp.concatenate([half, g_rate], 1), jnp.concatenate([bc_half, dt_weight], 1), ((1,), (1,)))
            + dot32(ri, a2)
        )
        g_normed = reduce_rows(g_low)
        gn = g_normed * norm_gain
        x = x_rows[m].astype(f32)
        inv = s["inv"]
        x_grad = cot_rows[m].astype(f32) + inv * gn - x * (inv**3 * jnp.mean(gn * x, axis=-1, keepdims=True))
        grads.append(to_features(x_grad[None]))

    picks = jnp.stack([s["pick"] for s in S])
    near = []
    for s in S:
        near.append(
            jnp.concatenate(
                [s["g_up_z"].reshape(R, nz, part), s["g_up_x"].reshape(R, nz, part), s["g_out"].reshape(R, nz, part)], 2
            )
        )
    near = jnp.transpose(jnp.stack(near), (2, 0, 1, 3))
    near = lax.psum_scatter(near, "mp", scatter_dimension=0, tiled=False)
    near = jnp.einsum("ma,mrf->arf", picks, near, precision=precise)
    near = lax.psum_scatter(near, "dp", scatter_dimension=0, tiled=True)
    keep = lax.dynamic_index_in_dim(near, core, 0, False)
    give = lax.dynamic_index_in_dim(near, 1 - core, 0, False)
    near = pair_cat(keep[None], other(give)[None], 0)
    g_in_up = jnp.transpose(near[:, :, : 2 * part].reshape(2, R, 2, part), (1, 2, 0, 3)).reshape(R, 2, 2 * part)
    g_out_down = jnp.transpose(near[:, :, 2 * part :], (0, 2, 1)).reshape(2 * part, R)
    far = jnp.stack([jnp.stack([s["g_down"], s["g_up_out"]]) for s in S])
    each = D // (nd * 2 * nz)
    far = far.reshape(micros, 2, R, nd, 2, nz, each)
    far = jnp.transpose(far, (4, 5, 0, 1, 2, 3, 6)).reshape(2 * nz, micros, 2, R, nd, each)
    far = lax.psum_scatter(far, ("seq", "mp"), scatter_dimension=0, tiled=False)
    far = jnp.einsum("ma,mkrde->dakre", picks, far, precision=precise)
    far = lax.psum_scatter(far, "dp", scatter_dimension=0, tiled=False)
    g_in_down = jnp.transpose(far[:, 0], (0, 2, 1))
    g_out_up = far[:, 1].reshape(ADAPT * R, each)
    return (jnp.stack(outs), jnp.stack(grads), g_in_down, g_in_up, g_out_down, g_out_up)


def solution(mesh):
    in_specs = (
        P(None, "dp", "seq", "mp"),
        P(None, "dp", "seq", "mp"),
        P(None, "dp"),
        P(None, "dp"),
        P(),
        P(("dp", "seq"), None, "mp"),
        P(("dp", "seq"), None),
        P(("dp", "seq"), "mp"),
        P("mp"),
        P("mp"),
        P("mp"),
        P(None, "mp"),
        P(),
        P("mp"),
        P("mp", ("dp", "seq")),
        P(None, ("dp", "seq", "mp"), None),
        P(("dp", "seq"), None, "mp"),
        P("mp", ("dp", "seq")),
        P(None, ("dp", "seq", "mp")),
    )
    out_specs = (
        P(None, "dp", "seq", "mp"),
        P(None, "dp", "seq", "mp"),
        P(None, ("dp", "seq", "mp"), None),
        P(("dp", "seq"), None, "mp"),
        P("mp", ("dp", "seq")),
        P(None, ("dp", "seq", "mp")),
    )
    sizes = dict(mesh.shape)
    by_chip = (
        sizes["seq"] == 2
        and sizes["dp"] * 2 == ADAPT
        and sizes["mp"] % 2 == 0
        and sizes["mp"] & (sizes["mp"] - 1) == 0
        and (2048 // sizes["mp"]) % Q == 0
    )
    return jax.shard_map(fast_body if by_chip else body, mesh=mesh, in_specs=in_specs, out_specs=out_specs, check_vma=False)
```

```python
import functools

import jax
import jax.numpy as jnp
from jax import lax
from jax.experimental import pallas as pl
from jax.experimental.pallas import tpu as pltpu
from jax.sharding import PartitionSpec as P

D = 2048
P_SIZE = 64
NS = 128
KC = 4
Q = 256
R = 16
ADAPT = 8
DI = 4096
HG = 4
HALO = 16


eps = 1e-05
precise = lax.Precision.HIGHEST
VMEM_LIMIT = 56 * 1024 * 1024


def shifted(array, axis, by):
    size = lax.axis_size(axis)
    pairs = [(i, i + by) for i in range(size) if 0 <= i + by < size]
    return lax.ppermute(array, axis, pairs)


def entering(part, axis, combine, identity, reverse):
    count = lax.axis_size(axis)
    place = lax.axis_index(axis)
    ahead = count - 1 - place if reverse else place
    gathered = jax.tree.map(lambda a: lax.all_gather(a, axis), part)
    state = jax.tree.map(lambda a, e: jnp.zeros_like(a) + jnp.asarray(e, a.dtype), part, identity)

    def one(hop, state):
        source = count - 1 - hop if reverse else hop
        return combine(
            state, jax.tree.map(lambda a: lax.dynamic_index_in_dim(a, source, 0, False), gathered)
        )

    return lax.fori_loop(0, ahead, one, state)


def silu_grad(value):
    sigmoid_val = jax.nn.sigmoid(value)
    return sigmoid_val * (1.0 + value * (1.0 - sigmoid_val))


def block_step(carry_state, pieces):
    x_part, b_part, c_part, log_part, step_part = pieces
    length = log_part.shape[0]
    cumulative = jnp.cumsum(log_part, axis=0)
    causal = jnp.arange(length)[:, None] >= jnp.arange(length)[None, :]
    spread = cumulative[:, None, :] - cumulative[None, :, :]
    decay_mat = jnp.exp(jnp.where(causal[:, :, None], spread, -10000.0))
    scores = jnp.dot(c_part, b_part.T, precision=precise)
    mixing = scores[:, :, None] * decay_mat * step_part[None, :, :]
    inner_out = jnp.einsum("tsh,shp->thp", mixing, x_part, precision=precise)
    carried = jnp.exp(cumulative)[:, :, None] * jnp.einsum(
        "tn,hpn->thp", c_part, carry_state, precision=precise
    )
    weights = jnp.exp(cumulative[-1][None, :] - cumulative) * step_part
    update = jnp.einsum("sh,shp,sn->hpn", weights, x_part, b_part, precision=precise)
    new_state = jnp.exp(cumulative[-1])[:, None, None] * carry_state + update
    return (new_state, inner_out + carried)


def local_scan(x_heads, b_rows, c_rows, log_rows, step_rows):
    seg_rows = x_heads.shape[0]
    blocks = seg_rows // Q

    def blocked(tensor):
        return tensor.reshape((blocks, Q) + tensor.shape[1:])

    init_state = jnp.zeros((x_heads.shape[1], x_heads.shape[2], b_rows.shape[1]), jnp.float32)
    final_state, outputs = lax.scan(
        block_step,
        init_state,
        (blocked(x_heads), blocked(b_rows), blocked(c_rows), blocked(log_rows), blocked(step_rows)),
    )
    return (outputs.reshape(x_heads.shape), final_state, jnp.sum(log_rows, axis=0))


def incoming(c_rows, log_rows, state_in):
    cumulative = jnp.cumsum(log_rows, axis=0)
    return jnp.exp(cumulative)[:, :, None] * jnp.einsum(
        "tn,hpn->thp", c_rows, state_in, precision=precise
    )


def compose(earlier, later):
    return (later[0] * earlier[0], later[1] + later[0][..., None, None] * earlier[1])


def fetch_weights(w_zx, w_bc, w_dt, w_out, in_up, out_down):
    return (
        lax.all_gather(w_zx, ("dp", "seq"), axis=0, tiled=True),
        lax.all_gather(w_bc, ("dp", "seq"), axis=0, tiled=True),
        lax.all_gather(w_dt, ("dp", "seq"), axis=0, tiled=True),
        lax.all_gather(w_out, ("dp", "seq"), axis=1, tiled=True),
        lax.all_gather(in_up, ("dp", "seq"), axis=0, tiled=True),
        lax.all_gather(out_down, ("dp", "seq"), axis=1, tiled=True),
    )


def reduce_adapters(grads):
    near_sums = (
        lax.psum_scatter(grads[1], ("dp", "seq"), scatter_dimension=0, tiled=True),
        lax.psum_scatter(grads[2], ("dp", "seq"), scatter_dimension=1, tiled=True),
    )
    wide_sums = (
        lax.psum_scatter(grads[0], ("dp", "seq", "mp"), scatter_dimension=1, tiled=True),
        lax.psum_scatter(grads[3], ("dp", "seq", "mp"), scatter_dimension=1, tiled=True),
    )
    return (wide_sums[0], near_sums[0], near_sums[1], wide_sums[1])


def body(
    x_in,
    cotangent,
    lengths,
    adapter_ids,
    norm_gain,
    w_zx,
    w_bc,
    w_dt,
    dt_bias,
    a_log,
    d_skip,
    conv_x,
    conv_bc,
    gate_gain,
    w_out,
    in_down,
    in_up,
    out_down,
    out_up,
):
    micro_count, slot_count, seg_len, model_part = x_in.shape
    head_local = dt_bias.shape[0]
    inner_local = head_local * P_SIZE
    wide_down, wide_up = (
        lax.all_gather(in_down, ("dp", "seq", "mp"), axis=1, tiled=True),
        lax.all_gather(out_up, ("dp", "seq", "mp"), axis=1, tiled=True),
    )
    wide_down = wide_down.astype(jnp.float32)
    wide_up = wide_up.astype(jnp.float32)
    conv_taps = jnp.concatenate([conv_x, conv_bc], axis=1)
    decay_rate = -jnp.exp(a_log)
    positions = lax.axis_index("seq") * seg_len + jnp.arange(seg_len)
    feature_start = lax.axis_index("mp") * model_part
    scan_local = jax.vmap(local_scan)
    incoming_map = jax.vmap(incoming)
    gathered = None
    outputs = []
    x_grads = []
    running = None
    for batch_index in range(micro_count):
        gathered = fetch_weights(w_zx, w_bc, w_dt, w_out, in_up, out_down)
        zx_weight, bc_weight, dt_weight, out_weight, up_in, down_out = gathered
        rows_own = x_in[batch_index]
        cot_own = cotangent[batch_index]
        rows_full, cot_full = (
            lax.all_gather(rows_own, "mp", axis=2, tiled=True),
            lax.all_gather(cot_own, "mp", axis=2, tiled=True),
        )
        rows_value = rows_full.astype(jnp.float32)
        inv_rms = lax.rsqrt(jnp.mean(rows_value * rows_value, axis=-1, keepdims=True) + eps)
        normed = rows_value * inv_rms * norm_gain
        normed_low = normed.astype(jnp.bfloat16)
        normed_value = normed_low.astype(jnp.float32)
        select = jax.nn.one_hot(adapter_ids[batch_index], ADAPT, dtype=jnp.float32)
        down_sel = jnp.einsum("sa,adr->sdr", select, wide_down, precision=precise)
        up_sel = jnp.einsum(
            "sa,arcf->srcf",
            select,
            up_in.astype(jnp.float32).reshape(ADAPT, R, 2, inner_local),
            precision=precise,
        )
        low_rank = jnp.einsum("std,sdr->str", normed_value, down_sel, precision=precise)
        proj_zx = jnp.einsum(
            "std,dcf->stcf", normed_low, zx_weight, preferred_element_type=jnp.float32
        )
        proj_zx = proj_zx + jnp.einsum("str,srcf->stcf", low_rank, up_sel, precision=precise)
        proj_bc = jnp.einsum(
            "std,dn->stn", normed_low, bc_weight, preferred_element_type=jnp.float32
        )
        proj_dt = jnp.einsum(
            "std,dh->sth", normed_low, dt_weight, preferred_element_type=jnp.float32
        )
        gate_in = proj_zx[:, :, 0]
        conv_in = jnp.concatenate(
            [proj_zx[:, :, 1].astype(jnp.bfloat16), proj_bc.astype(jnp.bfloat16)], axis=-1
        )
        earlier_rows = shifted(conv_in[:, seg_len - (KC - 1) :], "seq", 1)
        extended = jnp.concatenate([earlier_rows, conv_in], axis=1).astype(jnp.float32)
        conv_pre = sum(
            (
                conv_taps[tap_index] * extended[:, tap_index : tap_index + seg_len]
                for tap_index in range(KC)
            )
        )
        conv_out = jax.nn.silu(conv_pre)
        x_heads = conv_out[..., :inner_local].reshape(slot_count, seg_len, head_local, P_SIZE)
        b_rows = conv_out[..., inner_local : inner_local + NS]
        c_rows = conv_out[..., inner_local + NS :]
        mask_rows = (positions[None, :] < lengths[batch_index][:, None]).astype(jnp.float32)
        rate_in = proj_dt + dt_bias
        step_rows = jax.nn.softplus(rate_in) * mask_rows[..., None]
        log_rows = step_rows * decay_rate
        (plain_out, state_local, log_total), scan_back = jax.vjp(
            scan_local, x_heads, b_rows, c_rows, log_rows, step_rows
        )
        factor = jnp.exp(log_total)
        identity = (jnp.ones_like(factor), jnp.zeros_like(state_local))
        state_in = entering((factor, state_local), "seq", compose, identity, False)[1]
        from_state, state_back = jax.vjp(incoming_map, c_rows, log_rows, state_in)
        mixed_heads = plain_out + from_state + d_skip[:, None] * x_heads
        mixed_flat = mixed_heads.reshape(slot_count, seg_len, inner_local)
        gate_act = jax.nn.silu(gate_in)
        gated_out = mixed_flat * gate_act
        square_sum = lax.psum(jnp.sum(gated_out * gated_out, axis=-1), "mp")
        inv_gate = lax.rsqrt(square_sum / DI + eps)
        scaled = gated_out * inv_gate[..., None] * gate_gain
        scaled_low = scaled.astype(jnp.bfloat16)
        scaled_value = scaled_low.astype(jnp.float32)
        out_sel = jnp.einsum(
            "sa,far->sfr",
            select,
            down_out.astype(jnp.float32).reshape(inner_local, ADAPT, R),
            precision=precise,
        )
        up_out = jnp.einsum("sa,ard->srd", select, wide_up.reshape(ADAPT, R, D), precision=precise)
        rank_out = jnp.einsum("stf,sfr->str", scaled_value, out_sel, precision=precise)
        partial_out = jnp.einsum(
            "stf,fd->std", scaled_low, out_weight, preferred_element_type=jnp.float32
        )
        partial_out = partial_out + jnp.einsum("str,srd->std", rank_out, up_out, precision=precise)
        branch = lax.psum_scatter(partial_out, "mp", scatter_dimension=2, tiled=True)
        outputs.append(
            (rows_own.astype(jnp.float32) + mask_rows[..., None] * branch).astype(jnp.bfloat16)
        )
        branch_grad = cot_full * mask_rows[..., None].astype(jnp.bfloat16)
        branch_value = branch_grad.astype(jnp.float32)
        rank_grad = jnp.einsum("std,srd->str", branch_value, up_out, precision=precise)
        grad_up_out = jnp.einsum("str,std->srd", rank_out, branch_value, precision=precise)
        grad_out_sel = jnp.einsum("stf,str->sfr", scaled_value, rank_grad, precision=precise)
        scaled_grad = jnp.einsum(
            "std,fd->stf", branch_grad, out_weight, preferred_element_type=jnp.float32
        )
        scaled_grad = scaled_grad + jnp.einsum(
            "str,sfr->stf", rank_grad, out_sel, precision=precise
        )
        weighted = scaled_grad * gate_gain
        dot_sum = lax.psum(jnp.sum(weighted * gated_out, axis=-1), "mp")
        gated_grad = (
            weighted * inv_gate[..., None] - gated_out * (inv_gate**3 * dot_sum / DI)[..., None]
        )
        mixed_grad = (gated_grad * gate_act).reshape(slot_count, seg_len, head_local, P_SIZE)
        gate_grad = gated_grad * mixed_flat * silu_grad(gate_in)
        c_grad_in, log_grad_in, state_in_grad = state_back(mixed_grad)
        later_grads = entering((factor, state_in_grad), "seq", compose, identity, True)[1]
        total_grad = jnp.sum(later_grads * state_in, axis=(2, 3)) * factor
        x_heads_grad, b_grad, c_grad, log_grad, step_grad = scan_back(
            (mixed_grad, later_grads, total_grad)
        )
        x_heads_grad = x_heads_grad + d_skip[:, None] * mixed_grad
        c_grad = c_grad + c_grad_in
        step_grad = step_grad + (log_grad + log_grad_in) * decay_rate
        rate_grad = step_grad * mask_rows[..., None] * jax.nn.sigmoid(rate_in)
        conv_out_grad = jnp.concatenate(
            [x_heads_grad.reshape(slot_count, seg_len, inner_local), b_grad, c_grad], axis=-1
        )
        pre_grad = conv_out_grad * silu_grad(conv_pre)
        padded_grad = jnp.pad(pre_grad, ((0, 0), (KC - 1, KC - 1), (0, 0)))
        ext_grad = sum(
            (
                conv_taps[tap_index]
                * padded_grad[:, KC - 1 - tap_index : KC - 1 - tap_index + seg_len + KC - 1]
                for tap_index in range(KC)
            )
        )
        returned = shifted(ext_grad[:, : KC - 1], "seq", -1)
        in_grad = ext_grad[:, KC - 1 :]
        in_grad = in_grad.at[:, seg_len - (KC - 1) :].add(returned)
        zx_grad = jnp.stack([gate_grad, in_grad[..., :inner_local]], axis=2).astype(jnp.bfloat16)
        dt_grad_low = rate_grad.astype(jnp.bfloat16)
        zx_grad_value = zx_grad.astype(jnp.float32)
        rank_in_grad = jnp.einsum("stcf,srcf->str", zx_grad_value, up_sel, precision=precise)
        grad_up_sel = jnp.einsum("str,stcf->srcf", low_rank, zx_grad_value, precision=precise)
        grad_down_sel = jnp.einsum("std,str->sdr", normed_value, rank_in_grad, precision=precise)
        normed_part = jnp.einsum(
            "stcf,dcf->std", zx_grad, zx_weight, preferred_element_type=jnp.float32
        )
        normed_part = normed_part + jnp.einsum(
            "sth,dh->std", dt_grad_low, dt_weight, preferred_element_type=jnp.float32
        )
        normed_part = normed_part + jnp.einsum(
            "str,sdr->std", rank_in_grad, down_sel, precision=precise
        )
        bc_partial = in_grad[..., inner_local:]
        normed_sum, bc_sum = lax.psum((normed_part, bc_partial), "mp")
        normed_grad = normed_sum + jnp.einsum(
            "stn,dn->std",
            bc_sum.astype(jnp.bfloat16),
            bc_weight,
            preferred_element_type=jnp.float32,
        )
        scaled_in = normed_grad * norm_gain
        row_grad = inv_rms * scaled_in - rows_value * inv_rms**3 * jnp.mean(
            scaled_in * rows_value, axis=-1, keepdims=True
        )
        own_slice = lax.dynamic_slice_in_dim(row_grad, feature_start, model_part, 2)
        x_grads.append(cot_own.astype(jnp.float32) + own_slice)
        local_grads = (
            jnp.einsum("sa,sdr->adr", select, grad_down_sel, precision=precise),
            jnp.einsum("sa,srcf->arcf", select, grad_up_sel, precision=precise).reshape(
                ADAPT * R, 2, inner_local
            ),
            jnp.einsum("sa,sfr->far", select, grad_out_sel, precision=precise).reshape(
                inner_local, ADAPT * R
            ),
            jnp.einsum("sa,srd->ard", select, grad_up_out, precision=precise).reshape(ADAPT * R, D),
        )
        running = local_grads if running is None else jax.tree.map(jnp.add, running, local_grads)
    running = reduce_adapters(running)
    return (jnp.stack(outputs), jnp.stack(x_grads), running[0], running[1], running[2], running[3])


MESH = pl.DeviceIdType.MESH


def flip(v, mask, count):
    total = 0
    bit = 1
    while bit < count:
        b = lax.rem(v // bit, 2)
        total = total + (1 - b if mask & bit else b) * bit
        bit *= 2
    return total


def gather_kernel(
    nd, nz, wt_ref, x_ref, w_ref, rows_ref, local_sem, pair_sem, up_sem, down_sem, zrecv_sem, xsend_sem, xrecv_sem, ysend_sem,
    yrecv_sem, hsend_sem, hrecv_sem, asend_sem, arecv_sem
):
    d, c, z = lax.axis_index("dp"), lax.axis_index("seq"), lax.axis_index("mp")
    xn, yn = flip(d, 1, nd), flip(d, 2, nd)
    rows, part = wt_ref.shape[1], wt_ref.shape[2] // 2
    own, feats = x_ref.shape[1] // nz, x_ref.shape[2]
    chunk = nz // 2
    mine = lax.rem(z, chunk) * 2 + c

    def remote(src, dst, send, recv, device):
        return pltpu.make_async_remote_copy(
            src_ref=src, dst_ref=dst, send_sem=send, recv_sem=recv, device_id=device, device_id_type=MESH
        )

    barrier = pltpu.get_barrier_semaphore()
    for cc in range(2):
        for r in range(nz):
            if cc or r:
                pl.semaphore_signal(barrier, 1, device_id=(d, flip(c, cc, 2), flip(z, r, nz)), device_id_type=MESH)
    for dd in (xn, yn):
        pl.semaphore_signal(barrier, 1, device_id=(dd, c, z), device_id_type=MESH)
    pl.semaphore_wait(barrier, 2 * nz - 1 + 2)

    def cols(s):
        return pl.ds(pl.multiple_of(s * part, 128), part)

    def area(dd, s):
        return w_ref.at[:, pl.ds(pl.multiple_of(dd * (2 * rows), 16), 2 * rows), cols(s)]

    def half_area(dd, s, h):
        return w_ref.at[:, pl.ds(pl.multiple_of(dd * (2 * rows) + h * rows, 16), rows), cols(s)]

    mine_area = w_ref.at[:, pl.ds(pl.multiple_of((2 * d + c) * rows, 16), rows), cols(z)]
    keep = pltpu.make_async_copy(wt_ref.at[:, :, cols(c)], mine_area, local_sem.at[0])
    pair = remote(wt_ref.at[:, :, cols(1 - c)], mine_area, pair_sem.at[0], pair_sem.at[1], (d, 1 - c, z))
    keep.start()
    pair.start()

    def piece(r):
        q = flip(z, r, nz)
        src = x_ref.at[:, pl.ds(pl.multiple_of(q * own, 16), own), :]
        dst = rows_ref.at[:, :, pl.ds(pl.multiple_of(z * feats, 128), feats)]
        to_c, to_z = lax.rem(q, 2), c * chunk + q // 2
        here = jnp.logical_and(to_c == c, to_z == z)
        far = remote(src, dst, asend_sem.at[r], arecv_sem.at[r], (d, to_c, to_z))
        near = pltpu.make_async_copy(src, dst, arecv_sem.at[r])
        return here, far, near

    for r in range(nz):
        here, far, near = piece(r)

        @pl.when(here)
        def _():
            near.start()

        @pl.when(jnp.logical_not(here))
        def _():
            far.start()

    keep.wait()
    pair.wait()

    def spread(s):
        remote(area(d, s), area(d, s), xsend_sem.at[s], xrecv_sem.at[s], (xn, c, z)).start()
        remote(area(d, s), area(d, s), ysend_sem.at[s], yrecv_sem.at[s], (yn, c, z)).start()

    def send_up(s):
        @pl.when(z < nz - 1)
        def _():
            remote(area(d, s), area(d, s), up_sem.at[s], zrecv_sem.at[s], (d, c, z + 1)).start()

    def send_down(s):
        @pl.when(z > 0)
        def _():
            remote(area(d, s), area(d, s), down_sem.at[s], zrecv_sem.at[s], (d, c, z - 1)).start()

    def relay(s):
        remote(area(xn, s), area(xn, s), xsend_sem.at[s], xrecv_sem.at[s], (xn, c, z)).wait_recv()
        remote(half_area(xn, s, 0), half_area(xn, s, 0), hsend_sem.at[0, s], hrecv_sem.at[0, s], (yn, c, z)).start()
        remote(area(yn, s), area(yn, s), ysend_sem.at[s], yrecv_sem.at[s], (yn, c, z)).wait_recv()
        remote(half_area(yn, s, 1), half_area(yn, s, 1), hsend_sem.at[1, s], hrecv_sem.at[1, s], (xn, c, z)).start()

    send_up(z)
    send_down(z)
    spread(z)
    for r in range(1, nz + 1):
        if r < nz:
            @pl.when(z - r >= 0)
            def _():
                s = z - r
                remote(area(d, s), area(d, s), up_sem.at[s], zrecv_sem.at[s], (d, c, z)).wait_recv()
                send_up(s)
                spread(s)

            @pl.when(z + r < nz)
            def _():
                s = z + r
                remote(area(d, s), area(d, s), up_sem.at[s], zrecv_sem.at[s], (d, c, z)).wait_recv()
                send_down(s)
                spread(s)

        if r == 1:
            relay(z)
        else:
            @pl.when(z - r + 1 >= 0)
            def _():
                relay(z - r + 1)

            @pl.when(z + r - 1 < nz)
            def _():
                relay(z + r - 1)

    for r in range(nz):
        here, far, near = piece(r)
        src_z = flip(mine, r, nz)
        dst = rows_ref.at[:, :, pl.ds(pl.multiple_of(src_z * feats, 128), feats)]
        pltpu.make_async_copy(dst, dst, arecv_sem.at[r]).wait()

        @pl.when(jnp.logical_not(here))
        def _():
            far.wait_send()

    for s in range(nz):
        remote(half_area(d, s, 0), half_area(d, s, 0), hsend_sem.at[0, s], hrecv_sem.at[0, s], (yn, c, z)).wait()
        remote(half_area(d, s, 1), half_area(d, s, 1), hsend_sem.at[1, s], hrecv_sem.at[1, s], (xn, c, z)).wait()
        remote(area(d, s), area(d, s), xsend_sem.at[s], xrecv_sem.at[s], (xn, c, z)).wait_send()
        remote(area(d, s), area(d, s), ysend_sem.at[s], yrecv_sem.at[s], (yn, c, z)).wait_send()

        @pl.when(jnp.logical_and(s <= z, z < nz - 1))
        def _():
            remote(area(d, s), area(d, s), up_sem.at[s], zrecv_sem.at[s], (d, c, z)).wait_send()

        @pl.when(jnp.logical_and(s >= z, z > 0))
        def _():
            remote(area(d, s), area(d, s), down_sem.at[s], zrecv_sem.at[s], (d, c, z)).wait_send()


def gather(wt, x, nd, nz):
    half = wt.shape[2] // 2
    dma = pltpu.SemaphoreType.DMA
    anywhere = pl.BlockSpec(memory_space=pl.ANY)
    return pl.pallas_call(
        functools.partial(gather_kernel, nd, nz),
        name="gather",
        out_shape=(
            jax.ShapeDtypeStruct((2, wt.shape[1] * 2 * nd, half * nz), wt.dtype),
            jax.ShapeDtypeStruct((x.shape[0], x.shape[1] // nz, x.shape[2] * nz), x.dtype),
        ),
        in_specs=[anywhere] * 2,
        out_specs=(anywhere,) * 2,
        scratch_shapes=[
            dma((1,)), dma((2,)), dma((nz,)), dma((nz,)), dma((nz,)), dma((nz,)), dma((nz,)), dma((nz,)), dma((nz,)),
            dma((2, nz)), dma((2, nz)), dma((nz,)), dma((nz,)),
        ],
        compiler_params=pltpu.CompilerParams(collective_id=1, has_side_effects=True),
    )(wt, x)


def split(v):
    hi = v.astype(jnp.bfloat16)
    return hi, (v - hi.astype(jnp.float32)).astype(jnp.bfloat16)


def mm(a, b):
    return lax.dot_general(a, b, (((1,), (0,)), ((), ())), preferred_element_type=jnp.float32)


def mm_t(a, b):
    return lax.dot_general(a, b, (((1,), (1,)), ((), ())), preferred_element_type=jnp.float32)


def mm3(a, b):
    return mm(a[0], b[0]) + mm(a[0], b[1]) + mm(a[1], b[0])


def mm3_t(a, b):
    return mm_t(a[0], b[0]) + mm_t(a[0], b[1]) + mm_t(a[1], b[0])


def ones_mm(ones, v):
    hi, lo = split(v)
    rest = v - hi.astype(jnp.float32) - lo.astype(jnp.float32)
    return mm(ones, hi) + mm(ones, lo) + mm(ones, rest.astype(jnp.bfloat16))


def conv_rows(rows, halo, taps):
    count = rows.shape[0]
    ext = jnp.concatenate([halo, rows], axis=0).astype(jnp.float32)
    first = HALO - (KC - 1)
    total = taps[0:1] * ext[first : first + count]
    for j in range(1, KC):
        total = total + taps[j : j + 1] * ext[first + j : first + j + count]
    return total


def conv_rows_back(grad, taps):
    count, width = grad.shape
    zero = jnp.zeros((8, width), jnp.float32)
    ext = jnp.concatenate([zero, grad, zero], axis=0)
    total = taps[0:1] * ext[3 : 3 + count + 8]
    for j in range(1, KC):
        total = total + taps[j : j + 1] * ext[3 - j : 3 - j + count + 8]
    return total


def widen(columns):
    rows = columns.shape[0]
    lane = lax.broadcasted_iota(jnp.int32, (rows, 2 * P_SIZE), 1)
    return jnp.concatenate(
        [jnp.where(lane < P_SIZE, columns[:, h : h + 1], columns[:, h + 1 : h + 2]) for h in range(0, HG, 2)], axis=1
    )


def of_group(value, group):
    return pltpu.roll(value, lax.rem(128 - group * HG, 128), 1)


def head_sums(prod, group):
    rows = prod.shape[1]
    row = lax.broadcasted_iota(jnp.int32, (rows, 128), 0) // P_SIZE + group * HG
    lane = lax.broadcasted_iota(jnp.int32, (rows, 128), 1)
    pick = (row == lane).astype(jnp.float32).astype(jnp.bfloat16)
    hi, lo = split(prod)
    return mm(hi, pick) + mm(lo, pick)


def lane_sum(v):
    part = v[:, :128]
    for k in range(1, v.shape[1] // 128):
        part = part + v[:, k * 128 : (k + 1) * 128]
    return part


def add_up(ref, value, group):
    @pl.when(group == 0)
    def _():
        ref[0] = value

    @pl.when(group > 0)
    def _():
        ref[0] += value


class Mover:
    def __init__(self, src_ref, dst_ref, send_sem, recv_sem, count, first, to_rows):
        self.refs = src_ref, dst_ref, send_sem, recv_sem
        self.count, self.first, self.to_rows = count, first, to_rows
        self.d, self.c, self.z = lax.axis_index("dp"), lax.axis_index("seq"), lax.axis_index("mp")
        self.chunk = count // 2
        self.mine = lax.rem(self.z, self.chunk) * 2 + self.c

    def keeper(self, q):
        return lax.rem(q, 2), self.c * self.chunk + q // 2

    def owner(self, p):
        return self.z // self.chunk, p

    def target(self, k):
        at = lax.rem(self.z + k, self.count)
        return at, *(self.keeper(at) if self.to_rows else self.owner(at))

    def here(self, device):
        return jnp.logical_and(device[0] == self.c, device[1] == self.z)

    def piece(self, k, near):
        src_ref, dst_ref, send_sem, recv_sem = self.refs
        at, to_c, to_z = self.target(k)
        if self.to_rows:
            rows, feats = dst_ref.shape[0], src_ref.shape[1]
            own = src_ref.shape[0] // self.count
            src = src_ref.at[pl.ds(pl.multiple_of(at * own + self.first, 16), rows), :]
            slot = self.z
        else:
            rows, feats = dst_ref.shape[0] // self.count, dst_ref.shape[1]
            src = src_ref.at[self.first : self.first + rows, pl.ds(pl.multiple_of(at * feats, 128), feats)]
            slot = self.mine
        if near:
            return pltpu.make_async_copy(src, self.landing(slot), recv_sem.at[slot])
        return pltpu.make_async_remote_copy(
            src_ref=src, dst_ref=self.landing(slot), send_sem=send_sem.at[k], recv_sem=recv_sem.at[slot],
            device_id=(self.d, to_c, to_z), device_id_type=MESH,
        )

    def landing(self, slot):
        dst_ref = self.refs[1]
        if self.to_rows:
            feats = dst_ref.shape[1] // self.count
            return dst_ref.at[:, pl.ds(pl.multiple_of(slot * feats, 128), feats)]
        rows = dst_ref.shape[0] // self.count
        return dst_ref.at[pl.ds(pl.multiple_of(slot * rows, 16), rows), :]

    def greet(self, barrier):
        for q in range(self.count):
            source = self.owner(q) if self.to_rows else self.keeper(q)

            @pl.when(jnp.logical_not(self.here(source)))
            def _():
                pl.semaphore_signal(barrier, 1, device_id=(self.d, *source), device_id_type=MESH)
        return self.count - jnp.where(self.z // self.chunk == self.c, 1, 0)

    def start(self, k):
        here = self.here(self.target(k)[1:])

        @pl.when(here)
        def _():
            self.piece(k, True).start()

        @pl.when(jnp.logical_not(here))
        def _():
            self.piece(k, False).start()

    def start_at(self, step, steps):
        for k in range(self.count):
            @pl.when(step == k * steps * 3 // (4 * self.count))
            def _():
                self.start(k)

    def finish(self):
        for slot in range(self.count):
            pltpu.make_async_copy(self.landing(slot), self.landing(slot), self.refs[3].at[slot]).wait()
        for k in range(self.count):
            @pl.when(jnp.logical_not(self.here(self.target(k)[1:])))
            def _():
                self.piece(k, False).wait_send()


class Line:
    def __init__(self, held_ref, sent_ref, send_sem, recv_sem, count, step):
        self.refs = held_ref, sent_ref, send_sem, recv_sem
        self.step = step
        self.d, self.c, self.z = lax.axis_index("dp"), lax.axis_index("seq"), lax.axis_index("mp")
        low, high = self.z > 0, self.z < count - 1
        self.has_source, self.has_target = (low, high) if step > 0 else (high, low)

    def greet(self, barrier):
        @pl.when(self.has_source)
        def _():
            pl.semaphore_signal(barrier, 1, device_id=(self.d, self.c, self.z - self.step), device_id_type=MESH)
        return jnp.where(self.has_target, 1, 0)

    def copy(self, group):
        held_ref, sent_ref, send_sem, recv_sem = self.refs
        return pltpu.make_async_remote_copy(
            src_ref=sent_ref.at[group], dst_ref=held_ref.at[group], send_sem=send_sem.at[group], recv_sem=recv_sem.at[group],
            device_id=(self.d, self.c, self.z + self.step), device_id_type=MESH,
        )

    def receive(self, group):
        held_ref = self.refs[0]

        @pl.when(self.has_source)
        def _():
            self.copy(group).wait_recv()

        @pl.when(jnp.logical_not(self.has_source))
        def _():
            held_ref[group] = jnp.zeros(held_ref.shape[1:], jnp.float32)

        return held_ref[group]

    def send(self, group, value):
        self.refs[1][group] = value

        @pl.when(self.has_target)
        def _():
            self.copy(group).start()

    def finish(self):
        @pl.when(self.has_target)
        def _():
            for g in range(self.refs[0].shape[0]):
                self.copy(g).wait_send()


def carried_by(kernel, count, first, to_rows, n_in, n_out, *refs):
    ins, src_ref, outs, dst_ref = refs[:n_in], refs[n_in], refs[n_in + 1 : n_in + 1 + n_out], refs[n_in + 1 + n_out]
    scratch, sems = refs[n_in + n_out + 2 : -2], refs[-2:]
    kernel(*ins, *outs, *scratch, mover=Mover(src_ref, dst_ref, *sems, count, first, to_rows))


def begin(step, *parties):
    if parties:
        @pl.when(step == 0)
        def _():
            barrier = pltpu.get_barrier_semaphore()
            waits = 0
            for party in parties:
                waits = waits + party.greet(barrier)
            pl.semaphore_wait(barrier, waits)


def end(step, steps, *parties):
    if parties:
        @pl.when(step == steps - 1)
        def _():
            for party in parties:
                party.finish()


def parties_of(*given):
    return [p for p in given if p is not None]


def twice_split(v):
    hi, lo = split(v)
    lane = lax.broadcasted_iota(jnp.int32, v.shape, 1)
    return jnp.where(lane < v.shape[1] // 2, hi.astype(jnp.float32), lo.astype(jnp.float32)).astype(jnp.bfloat16)


def fold(v):
    half = v.shape[0] // 2
    return v[:half] + v[half:]


def project_kernel(
    low_ref, w_ref, tailw_ref, down_ref, up_ref, xin_ref, z_ref, bcin_ref, rate_ref, lr_ref, mover=None
):
    step, steps = pl.program_id(1), pl.num_programs(1)
    parties = parties_of(mover)
    begin(step, *parties)
    if mover:
        mover.start_at(step, 16)
    low = low_ref[0]

    @pl.when(step == 0)
    def _():
        tail = mm(low, tailw_ref[...])
        bcin_ref[0] = tail[:, : 2 * NS].astype(jnp.bfloat16)
        rate_ref[0] = tail[:, 2 * NS :]
        lr_ref[0] = twice_split(mm_t(low, down_ref[...]))

    value = mm(low, w_ref[0]) + mm(lr_ref[0], up_ref[...])

    @pl.when(step < steps // 2)
    def _():
        xin_ref[0] = value.astype(jnp.bfloat16)

    @pl.when(step >= steps // 2)
    def _():
        z_ref[0] = value

    end(step, steps, *parties)


def prep_kernel(rate_ref, bias_ref, decay_ref, mask_ref, bcin_ref, bchalo_ref, taps_ref, step_ref, cum_ref, lanes_ref, bc_ref):
    rows = rate_ref.shape[1]
    value = rate_ref[0] + bias_ref[...]
    step = (jnp.maximum(value, 0.0) + jnp.log1p(jnp.exp(-jnp.abs(value)))) * mask_ref[0]
    log = step * decay_ref[...]
    tri = lax.broadcasted_iota(jnp.int32, (Q, Q), 0) >= lax.broadcasted_iota(jnp.int32, (Q, Q), 1)
    tri = tri.astype(jnp.float32).astype(jnp.bfloat16)
    step_ref[0] = step
    cum = jnp.concatenate([ones_mm(tri, log[b * Q : (b + 1) * Q]) for b in range(rows // Q)], axis=0)
    cum_ref[0] = cum
    cum_t, step_t = cum.T, step.T
    for g in range(lanes_ref.shape[1]):
        lanes_ref[0, g, :HG] = cum_t[g * HG : (g + 1) * HG]
        lanes_ref[0, g, HG:] = step_t[g * HG : (g + 1) * HG]
    pre = conv_rows(bcin_ref[0], bchalo_ref[0], taps_ref[...])
    bc_ref[0] = pre * jax.nn.sigmoid(pre)


def forward_kernel(
    xin_ref, halo_ref, taps_ref, bc_ref, cum_ref, step_ref, lanes_ref, skip_ref, z_ref, mixed_ref, square_ref, state_ref,
    end_ref, scores_ref, bt_ref, held_ref, sent_ref, send_sem, recv_sem, mover=None
):
    group = pl.program_id(1)
    rows = xin_ref.shape[1]
    blocks = rows // Q
    line = Line(held_ref, sent_ref, send_sem, recv_sem, lax.axis_size("mp"), 1)
    parties = parties_of(line, mover)
    begin(group, *parties)
    if mover:
        mover.start_at(group, 8)

    @pl.when(group == 0)
    def _():
        for b in range(blocks):
            part = bc_ref[0, b * Q : (b + 1) * Q]
            b_part = split(part[:, :NS])
            c_part = split(part[:, NS:])
            scores_ref[b] = mm3_t(c_part, b_part)
            hi, lo = split(part[:, :NS].T)
            bt_ref[0, b] = hi
            bt_ref[1, b] = lo

    pre = conv_rows(xin_ref[0], halo_ref[0], taps_ref[...])
    x = pre * jax.nn.sigmoid(pre)
    cums, decs, updates = [], [], []
    for b in range(blocks):
        at = slice(b * Q, (b + 1) * Q)
        cum = of_group(cum_ref[0, at], group)
        step = of_group(step_ref[0, at], group)
        total = cum[Q - 1 : Q]
        wx = x[at] * widen(jnp.exp(total - cum) * step)
        cums.append(cum)
        decs.append(widen(jnp.exp(total)))
        updates.append(mm3((bt_ref[0, b], bt_ref[1, b]), split(wx)))

    states = [line.receive(group)]
    for b in range(blocks):
        states.append(decs[b] * states[b] + updates[b])
    state_ref[0] = states[0]
    end_ref[0] = states[blocks]
    line.send(group, states[blocks])
    lane = lax.broadcasted_iota(jnp.int32, (Q, 2 * P_SIZE), 1)
    causal = lax.broadcasted_iota(jnp.int32, (Q, Q), 0) >= lax.broadcasted_iota(jnp.int32, (Q, Q), 1)
    square = []
    for b in range(blocks):
        at = slice(b * Q, (b + 1) * Q)
        scores = scores_ref[b]
        xb = x[at]
        carried = widen(jnp.exp(cums[b])) * mm3(split(bc_ref[0, at, NS:]), split(states[b]))
        parts = []
        for h in range(0, HG, 2):
            pair = xb[:, h * P_SIZE : (h + 2) * P_SIZE]
            x_hi, x_lo = split(pair)
            both = jnp.concatenate([x_hi, x_lo], axis=1)
            halves = []
            for k in (h, h + 1):
                spread = cums[b][:, k : k + 1] - lanes_ref[0, 0, k : k + 1, at]
                decay = jnp.exp(jnp.where(causal, spread, -10000.0))
                m_hi, m_lo = split(scores * decay * lanes_ref[0, 0, HG + k : HG + k + 1, at])
                first = mm(m_hi, both)
                halves.append(first[:, : 2 * P_SIZE] + first[:, 2 * P_SIZE :] + mm(m_lo, x_hi))
            parts.append(jnp.where(lane < P_SIZE, halves[0], halves[1]))
        mixed = jnp.concatenate(parts, axis=1) + skip_ref[0:1] * xb + carried
        mixed_ref[0, at] = mixed
        z = z_ref[0, at]
        gated = mixed * (z * jax.nn.sigmoid(z))
        square.append(lane_sum(gated * gated))
    add_up(square_ref, jnp.concatenate(square, axis=0), group)

    end(group, pl.num_programs(1), *parties)


def chunk_decay(cum_ref, group):
    rows = cum_ref.shape[1]
    before = jnp.zeros((1, 128), jnp.float32)
    parts = []
    for b in range(rows // Q):
        cum = of_group(cum_ref[0, b * Q : (b + 1) * Q], group)
        parts.append(jnp.exp(cum + before))
        before = before + cum[Q - 1 : Q]
    return widen(jnp.concatenate(parts, axis=0))


def gs_kernel(gb_ref, w_ref, up_ref, down_ref, mixed_ref, z_ref, gain_ref, gs_ref, dot_ref, rg_ref, mover=None):
    step = pl.program_id(1)
    parties = parties_of(mover)
    begin(step, *parties)
    if mover:
        mover.start_at(step, 8)
    gb = gb_ref[0]

    @pl.when(step == 0)
    def _():
        rg_ref[0] = twice_split(mm_t(gb, up_ref[...]))

    gs = mm(rg_ref[0], down_ref[...])
    width = w_ref.shape[3]
    for n in range(w_ref.shape[0]):
        gs = gs + mm_t(gb[:, n * width : (n + 1) * width], w_ref[n, 0])
    gs_ref[0] = gs
    z = z_ref[0]
    add_up(dot_ref, lane_sum(gs * gain_ref[...] * (mixed_ref[0] * (z * jax.nn.sigmoid(z)))), step)
    end(step, pl.num_programs(1), *parties)


def branch_kernel(
    scaled_ref, w_ref, down_ref, up_ref, rg_ref, gb_ref, branch_ref, g_up_ref, g_down_ref, ro_ref, rot_ref, rgt_ref, mover=None
):
    step = pl.program_id(1)
    parties = parties_of(mover)
    begin(step, *parties)
    if mover:
        mover.start_at(step, 4)

    @pl.when(step == 0)
    def _():
        ro = twice_split(mm_t(scaled_ref[0], down_ref[...]))
        ro_ref[...] = ro
        rot_ref[...] = ro.astype(jnp.float32).T.astype(jnp.bfloat16)
        rgt_ref[...] = rg_ref[0].astype(jnp.float32).T.astype(jnp.bfloat16)

    width = w_ref.shape[2]
    total = mm(ro_ref[...], up_ref[...])
    for n in range(w_ref.shape[1]):
        total = total + mm(scaled_ref[0, :, n * width : (n + 1) * width], w_ref[0, n])
    branch_ref[0] = total
    g_up_ref[0] = fold(mm(rot_ref[...], gb_ref[0]))
    cols = g_down_ref.shape[2]
    g_down_ref[0] = fold(mm(rgt_ref[...], scaled_ref[0, :, pl.ds(pl.multiple_of(step * cols, 128), cols)]))
    end(step, pl.num_programs(1), *parties)


def unproject_kernel(
    gz_ref, gx_ref, tail_ref, w_ref, tailw_ref, up_ref, down_ref, lr_ref, low_ref, g_ref, upz_ref, upx_ref, g_down_ref, ri_ref,
    rit_ref, lrt_ref, mover=None
):
    step = pl.program_id(1)
    parties = parties_of(mover)
    begin(step, *parties)
    if mover:
        mover.start_at(step, 8)
    gz, gx = gz_ref[0], gx_ref[0]
    chan = gz.shape[1]

    @pl.when(step == 0)
    def _():
        ri = twice_split(mm_t(gz, up_ref[:, :chan]) + mm_t(gx, up_ref[:, chan:]))
        ri_ref[...] = ri
        rit_ref[...] = ri.astype(jnp.float32).T.astype(jnp.bfloat16)
        lrt_ref[...] = lr_ref[0].astype(jnp.float32).T.astype(jnp.bfloat16)

    g_ref[0] = mm_t(gz, w_ref[0]) + mm_t(gx, w_ref[1]) + mm_t(tail_ref[0], tailw_ref[...]) + mm(ri_ref[...], down_ref[...])
    cols = upz_ref.shape[2]
    at = pl.ds(pl.multiple_of(step * cols, 128), cols)
    upz_ref[0] = fold(mm(lrt_ref[...], gz_ref[0, :, at]))
    upx_ref[0] = fold(mm(lrt_ref[...], gx_ref[0, :, at]))
    g_down_ref[0] = fold(mm(rit_ref[...], low_ref[0]))
    end(step, pl.num_programs(1), *parties)


def gate_back_kernel(
    gs_ref, mixed_ref, z_ref, inv_ref, coef_ref, gain_ref, bc_ref, cum_ref, dy_ref, gz_ref, scaled_ref, lam_ref, q_ref, ct_ref,
    mover=None
):
    group = pl.program_id(1)
    parties = parties_of(mover)
    begin(group, *parties)
    if mover:
        mover.start_at(group, 8)

    @pl.when(group == 0)
    def _():
        hi, lo = split(bc_ref[0, :, NS:].T)
        ct_ref[0] = hi
        ct_ref[1] = lo

    z = z_ref[0]
    mixed = mixed_ref[0]
    sig = jax.nn.sigmoid(z)
    act = z * sig
    gated = mixed * act
    inv = inv_ref[0]
    gain = gain_ref[...]
    scaled_ref[0] = (gated * inv * gain).astype(jnp.bfloat16)
    g_gated = gs_ref[0] * gain * inv - gated * coef_ref[0]
    dy = g_gated * act
    dy_ref[0] = dy
    gz_ref[0] = (g_gated * mixed * (sig * (1.0 + z * (1.0 - sig)))).astype(jnp.bfloat16)
    lam_ref[0] = mm3((ct_ref[0], ct_ref[1]), split(dy * chunk_decay(cum_ref, group)))
    add_up(q_ref, head_sums(dy * mixed, group), group)

    end(group, pl.num_programs(1), *parties)


def scan_back_kernel(
    dy_ref, xin_ref, halo_ref, taps_ref, bc_ref, cum_ref, step_ref, lanes_ref, skip_ref, state_ref, lam_ref, end_ref,
    gx_ref, head_ref, tail_ref, gbc_ref, xu_ref, dx_ref, scorest_ref, dscorest_ref, bt_ref, ct_ref, held_ref, sent_ref, send_sem,
    recv_sem, mover=None
):
    group = pl.program_id(1)
    rows = xin_ref.shape[1]
    blocks = rows // Q
    line = Line(held_ref, sent_ref, send_sem, recv_sem, lax.axis_size("mp"), -1)
    parties = parties_of(line, mover)
    begin(group, *parties)
    if mover:
        mover.start_at(group, 8)

    @pl.when(group == 0)
    def _():
        for b in range(blocks):
            part = bc_ref[0, b * Q : (b + 1) * Q]
            scorest_ref[b] = mm3_t(split(part[:, :NS]), split(part[:, NS:]))
            dscorest_ref[b] = jnp.zeros((Q, Q), jnp.float32)
            hi, lo = split(part[:, :NS].T)
            bt_ref[0, b] = hi
            bt_ref[1, b] = lo
            hi, lo = split(part[:, NS:].T)
            ct_ref[0, b] = hi
            ct_ref[1, b] = lo
        gbc_ref[0] = jnp.zeros((rows, 2 * NS), jnp.float32)
        xu_ref[0] = jnp.zeros((rows, 128), jnp.float32)
        dx_ref[0] = jnp.zeros((rows, 128), jnp.float32)

    pre = conv_rows(xin_ref[0], halo_ref[0], taps_ref[...])
    sig = jax.nn.sigmoid(pre)
    x = pre * sig
    lane = lax.broadcasted_iota(jnp.int32, (Q, 2 * P_SIZE), 1)
    causal = lax.broadcasted_iota(jnp.int32, (Q, Q), 0) <= lax.broadcasted_iota(jnp.int32, (Q, Q), 1)
    cums, steps, decs, rests, wide_steps = [], [], [], [], []
    for b in range(blocks):
        at = slice(b * Q, (b + 1) * Q)
        cum = of_group(cum_ref[0, at], group)
        step = of_group(step_ref[0, at], group)
        total = cum[Q - 1 : Q]
        cums.append(cum)
        steps.append(step)
        decs.append(widen(jnp.exp(total)))
        rests.append(widen(jnp.exp(total - cum)))
        wide_steps.append(widen(step))
    states = [state_ref[0]]
    for b in range(blocks - 1):
        wx = x[b * Q : (b + 1) * Q] * rests[b] * wide_steps[b]
        states.append(decs[b] * states[b] + mm3((bt_ref[0, b], bt_ref[1, b]), split(wx)))
    lam = line.receive(group)
    whole = decs[0]
    for dec in decs[1:]:
        whole = whole * dec
    line.send(group, whole * lam + lam_ref[0])
    ends = jnp.sum(lam * end_ref[0], axis=0, keepdims=True)
    g_parts = [None] * blocks
    for b in reversed(range(blocks)):
        at = slice(b * Q, (b + 1) * Q)
        xb = x[at]
        dy = dy_ref[0, at]
        scores = scorest_ref[b]
        dscores = dscorest_ref[b]
        u_parts = []
        for h in range(0, HG, 2):
            pair = slice(h * P_SIZE, (h + 2) * P_SIZE)
            x_hi, x_lo = split(xb[:, pair])
            d_hi, d_lo = split(dy[:, pair])
            both = jnp.concatenate([d_hi, d_lo], axis=1)
            halves = []
            for k in (h, h + 1):
                mine = (lane < P_SIZE) if k == h else (lane >= P_SIZE)
                spread = lanes_ref[0, 0, k : k + 1, at] - cums[b][:, k : k + 1]
                decay = jnp.exp(jnp.where(causal, spread, -10000.0))
                zero = jnp.zeros_like(x_hi)
                xm_hi = jnp.where(mine, x_hi, zero)
                xm_lo = jnp.where(mine, x_lo, zero)
                dm = mm_t(xm_hi, d_hi) + mm_t(xm_hi, d_lo) + mm_t(xm_lo, d_hi)
                dscores = dscores + dm * decay * steps[b][:, k : k + 1]
                m_hi, m_lo = split(scores * decay)
                first = mm(m_hi, both)
                halves.append(first[:, : 2 * P_SIZE] + first[:, 2 * P_SIZE :] + mm(m_lo, d_hi))
            u_parts.append(jnp.where(lane < P_SIZE, halves[0], halves[1]))
        dscorest_ref[b] = dscores
        lam_s = split(lam)
        part = bc_ref[0, at]
        step = wide_steps[b]
        u = jnp.concatenate(u_parts, axis=1) + rests[b] * mm3(split(part[:, :NS]), lam_s)
        ev = split(widen(jnp.exp(cums[b])) * dy)
        gbc_ref[0, at, :NS] += mm3_t(split(rests[b] * step * xb), lam_s)
        gbc_ref[0, at, NS:] += mm3_t(ev, split(states[b]))
        if b > 0:
            lam = decs[b] * lam + mm3((ct_ref[0, b], ct_ref[1, b]), ev)
        xu_ref[0, at] += head_sums(xb * u, group)
        direct = xb * dy * skip_ref[0:1]
        if b == blocks - 1:
            row = lax.broadcasted_iota(jnp.int32, (Q, HG * P_SIZE), 0)
            direct = jnp.where(row == Q - 1, direct - ends, direct)
        dx_ref[0, at] += head_sums(direct, group)
        g_parts[b] = step * u + skip_ref[0:1] * dy
    g_pre = jnp.concatenate(g_parts, axis=0) * (sig * (1.0 + pre * (1.0 - sig)))
    g_ext = conv_rows_back(g_pre, taps_ref[...])
    gx_ref[0] = g_ext[8:].astype(jnp.bfloat16)
    head_ref[0] = g_ext[:8]
    tail_ref[0] = g_ext[rows:]

    @pl.when(group == pl.num_programs(1) - 1)
    def _():
        for b in range(blocks):
            at = slice(b * Q, (b + 1) * Q)
            part = bc_ref[0, at]
            ds = dscorest_ref[b]
            gbc_ref[0, at, :NS] += mm3(split(ds), split(part[:, NS:]))
            gbc_ref[0, at, NS:] += mm3(split(ds.T), split(part[:, :NS]))

    end(group, pl.num_programs(1), *parties)


def bc_back_kernel(
    g_ref, in_ref, halo_ref, taps_ref, q_ref, dx_ref, xu_ref, step_ref, rate_ref, bias_ref, decay_ref, mask_ref,
    out_ref, head_ref, tail_ref, g_rate_ref
):
    rows = in_ref.shape[1]
    pre = conv_rows(in_ref[0], halo_ref[0], taps_ref[...])
    sig = jax.nn.sigmoid(pre)
    g_ext = conv_rows_back(g_ref[0] * (sig * (1.0 + pre * (1.0 - sig))), taps_ref[...])
    out_ref[0] = g_ext[8:].astype(jnp.bfloat16)
    head_ref[0] = g_ext[:8]
    tail_ref[0] = g_ext[rows:]
    xu = xu_ref[0]
    flow = q_ref[0] - dx_ref[0] - step_ref[0] * xu
    later = lax.broadcasted_iota(jnp.int32, (rows, rows), 0) <= lax.broadcasted_iota(jnp.int32, (rows, rows), 1)
    g_log = ones_mm(later.astype(jnp.float32).astype(jnp.bfloat16), flow)
    sig = jax.nn.sigmoid(rate_ref[0] + bias_ref[...])
    g_rate_ref[0] = ((xu + g_log * decay_ref[...]) * mask_ref[0] * sig).astype(jnp.bfloat16)


class Slot:
    pass


def block(shape, index):
    return pl.BlockSpec(shape, index)


def call(kernel, name, grid, ins, outs, scratch, flops, size, comm=None, load=None):
    params = dict(vmem_limit_bytes=VMEM_LIMIT)
    ins, outs, scratch = list(ins), list(outs), list(scratch)
    if load is not None:
        rows, result, first, to_rows = load
        count = lax.axis_size("mp")
        kernel = functools.partial(carried_by, kernel, count, first, to_rows, len(ins), len(outs))
        ins.append((rows, pl.BlockSpec(memory_space=pl.ANY)))
        outs.append((result, pl.BlockSpec(memory_space=pl.ANY)))
        scratch += [pltpu.SemaphoreType.DMA((count,)), pltpu.SemaphoreType.DMA((count,))]
    if comm is not None:
        params.update(collective_id=comm, has_side_effects=True)
    return pl.pallas_call(
        kernel,
        name=name,
        grid=(1, grid),
        in_specs=[s for _, s in ins],
        out_specs=[s for _, s in outs],
        out_shape=[s for s, _ in outs],
        scratch_shapes=scratch,
        compiler_params=pltpu.CompilerParams(**params),
        cost_estimate=pl.CostEstimate(flops=flops, bytes_accessed=size, transcendentals=0),
    )(*[a for a, _ in ins])


def after(value, *deps):
    return lax.optimization_barrier((value,) + deps)[0]


def move_kernel(count, rows_ref, moved_ref, send_sem, recv_sem):
    mover = Mover(rows_ref, moved_ref, send_sem, recv_sem, count, 0, False)
    barrier = pltpu.get_barrier_semaphore()
    pl.semaphore_wait(barrier, mover.greet(barrier))
    for k in range(count):
        mover.start(k)
    mover.finish()


def move_last(rows, moved, count, comm):
    dma = pltpu.SemaphoreType.DMA
    anywhere = pl.BlockSpec(memory_space=pl.ANY)
    return pl.pallas_call(
        functools.partial(move_kernel, count),
        name="move",
        in_specs=[anywhere],
        out_specs=anywhere,
        out_shape=moved,
        scratch_shapes=[dma((count,)), dma((count,))],
        compiler_params=pltpu.CompilerParams(collective_id=comm, has_side_effects=True),
    )(rows)


def scatter_sum(v, axis):
    count, me = v.shape[0], lax.axis_index(axis)
    total = lax.dynamic_index_in_dim(v, me, 0, False)
    for k in range(1, count):
        give = lax.dynamic_index_in_dim(v, me ^ k, 0, False)
        total = total + lax.ppermute(give, axis, [(i, i ^ k) for i in range(count)])
    return total


def fast_body(
    x_in, cotangent, lengths, adapter_ids, norm_gain, w_zx, w_bc, w_dt, dt_bias, a_log, d_skip, conv_x, conv_bc,
    gate_gain, w_out, in_down, in_up, out_down, out_up
):
    bf16, f32 = jnp.bfloat16, jnp.float32
    micros, _, seg, feats = x_in.shape
    nz, nd = lax.axis_size("mp"), lax.axis_size("dp")
    core, z = lax.axis_index("seq"), lax.axis_index("mp")
    own = seg // nz
    tokens = 2 * own
    heads = dt_bias.shape[0] * nz // 2
    chan = heads * P_SIZE
    part = chan // nz
    groups = heads // HG
    wide = HG * P_SIZE
    blocks = tokens // Q
    each = D // (nd * 2 * nz)

    def other(v):
        return lax.ppermute(v, "seq", [(0, 1), (1, 0)])

    def pair_cat(mine, theirs, axis):
        return jnp.where(
            core == 0, jnp.concatenate([mine, theirs], axis), jnp.concatenate([theirs, mine], axis)
        )

    def halves(v, axis):
        v = v.reshape(v.shape[:axis] + (2, v.shape[axis] // 2) + v.shape[axis + 1 :])
        return (
            lax.dynamic_index_in_dim(v, core, axis, False),
            lax.dynamic_index_in_dim(v, 1 - core, axis, False),
        )

    line = 2 * part
    bc_piece = lax.dynamic_slice_in_dim(w_bc, z * (w_bc.shape[0] // nz), w_bc.shape[0] // nz, 0)
    same = [bc_piece, jnp.transpose(in_down, (0, 2, 1)), out_up]
    sized = [halves(in_up, 2), halves(out_down.T, 1), halves(w_dt.T, 0)]
    packs = []
    for k in range(2):
        packs.append(jnp.concatenate([v.reshape(-1, line) for v in [s[k] for s in sized] + same], 0))
    bounds = [0]
    for v in [s[0] for s in sized] + same:
        bounds.append(bounds[-1] + v.size // line)
    pack = pair_cat(packs[0][None], other(packs[1])[None], 0)
    params = jnp.concatenate([dt_bias, a_log, d_skip, gate_gain, conv_x.reshape(-1)])
    params = lax.all_gather(params, "mp")
    pack = lax.all_gather(pack, ("dp", "mp")).reshape((nd, nz) + pack.shape)
    zx_weight, x_rows = gather(jnp.transpose(w_zx, (1, 0, 2)), x_in[:, 0], nd, nz)
    out_mine, out_theirs = halves(after(w_out, x_rows), 0)
    out_pair = pair_cat(out_mine, other(out_theirs), 1)
    out_all = lax.all_gather(out_pair, ("dp", "mp")).reshape((nd, nz) + out_pair.shape)
    dt_rows = pack[:, :, :, bounds[2] : bounds[3]].reshape(nd, nz, 2, heads // nz, -1)
    dt_weight = jnp.transpose(dt_rows, (1, 3, 0, 2, 4)).reshape(heads, D)
    dt_weight = jnp.pad(dt_weight, ((0, 128 - heads), (0, 0)))
    bc_rows = pack[:, :, :, bounds[3] : bounds[4]].reshape(nd, nz, 2, -1, 2 * NS)
    bc_weight = jnp.transpose(bc_rows, (0, 2, 1, 3, 4)).reshape(D, 2 * NS)
    bc_half = lax.dynamic_slice_in_dim(bc_weight, core * NS, NS, 1)
    dt_weight = dt_weight.T
    tail_weight = jnp.concatenate([bc_half, dt_weight], 1)
    first_weight = jnp.concatenate([bc_weight, dt_weight], 1)

    hl = dt_bias.shape[0]

    def own_part(v):
        v = v.reshape(v.shape[0], 2, v.shape[1] // 2)
        return lax.dynamic_index_in_dim(v, core, 1, False).reshape(-1)

    bias = jnp.pad(own_part(params[:, :hl]), (0, 128 - heads))[None]
    rate = jnp.pad(-jnp.exp(own_part(params[:, hl : 2 * hl])), (0, 128 - heads))[None]
    skip = jnp.repeat(own_part(params[:, 2 * hl : 3 * hl]), P_SIZE)[None]
    width = gate_gain.shape[0]
    gain = own_part(params[:, 3 * hl : 3 * hl + width])[None]
    taps = params[:, 3 * hl + width :].reshape(nz, KC, 2, part)
    taps = jnp.transpose(lax.dynamic_index_in_dim(taps, core, 2, False), (1, 0, 2)).reshape(KC, chan)

    chunk = nz // 2
    mine = (z % chunk) * 2 + core

    start = z * tokens
    own_pos = start + core * own + jnp.arange(own)
    all_pos = start + jnp.arange(tokens)
    forward_edge = [(i, i + 1) for i in range(nz - 1)]
    backward_edge = [(i + 1, i) for i in range(nz - 1)]

    m3 = lambda m, g: (0, 0, g)
    m0 = lambda m, g: (0, 0, 0)
    z2 = lambda m, g: (0, 0)
    chan_block = block((1, tokens, wide), m3)
    halo_block = block((1, HALO, wide), m3)
    taps_block = block((KC, wide), lambda m, g: (0, g))
    line_block = block((1, wide), lambda m, g: (0, g))
    state_block = block((1, NS, wide), m3)
    bc_block = block((1, tokens, 2 * NS), m0)
    bc_halo = block((1, HALO, 2 * NS), m0)
    bc_taps = block((KC, 2 * NS), z2)
    bc_edge = block((1, 8, 2 * NS), m0)
    one_col = block((1, tokens, 1), m0)
    sums = block((1, tokens, 128), m0)
    lanes_block = block((1, 1, 2 * HG, tokens), lambda m, g: (0, g, 0, 0))
    head_line = block((1, 128), z2)
    edge_block = block((1, 8, wide), m3)
    shape = jax.ShapeDtypeStruct
    tok_f32 = shape((1, tokens, chan), f32)
    tok_b16 = shape((1, tokens, chan), bf16)
    state_f32 = shape((1, NS, chan), f32)
    bc_f32 = shape((1, tokens, 2 * NS), f32)
    sums_f32 = shape((1, tokens, 128), f32)
    edge_f32 = shape((1, 8, chan), f32)
    act_bytes = tokens * chan * 4

    dma = pltpu.SemaphoreType.DMA
    line_scratch = [pltpu.VMEM((groups, NS, wide), f32)] * 2 + [dma((groups,))] * 2
    anywhere = pl.BlockSpec(memory_space=pl.ANY)
    moved_b16 = shape((seg, feats), bf16)
    halfway = own // 2
    moved_half = shape((seg // 2, feats), bf16)
    rows_half = shape((halfway, D), bf16)

    slots = [Slot() for _ in range(micros)]
    for m, s in enumerate(slots):
        x = x_rows[m].astype(f32)
        s.inv = lax.rsqrt(jnp.mean(x * x, axis=-1, keepdims=True) + eps)
        low_own = (x * s.inv * norm_gain).astype(bf16)
        s.low = pair_cat(low_own, other(low_own), 0)
        s.mask_own = (own_pos < lengths[m, 0]).astype(f32)[:, None]
        s.mask = (all_pos < lengths[m, 0]).astype(f32)[:, None]
        k = adapter_ids[m, 0]
        s.pick = (k == jnp.arange(ADAPT)).astype(f32)
        near = lax.dynamic_index_in_dim(lax.dynamic_index_in_dim(pack, k // 2, 0, False), k % 2, 1, False)
        up = near[:, bounds[0] : bounds[1]].reshape(nz, R, 2, part)
        s.u_in = jnp.transpose(up, (1, 2, 0, 3)).reshape(R, 2 * chan)
        down = near[:, bounds[1] : bounds[2]].reshape(nz, R, part)
        s.a_out = jnp.transpose(down, (1, 0, 2)).reshape(R, chan)
        wide_rows = []
        for first in (bounds[4], bounds[5]):
            got = lax.dynamic_index_in_dim(pack, first + k, 3, False).reshape(nd, nz, 2, R, each)
            wide_rows.append(jnp.transpose(got, (3, 0, 2, 1, 4)).reshape(R, D))
        s.a_in, s.u_out = wide_rows
        factors = [s.a_in, s.u_out, s.u_in, s.a_out]
        s.a_in, s.u_out, s.u_in, s.a_out = [jnp.concatenate([v, v], 0) for v in factors]

    full_low = block((1, tokens, D), m0)
    rank_block = block((1, tokens, 2 * R), m0)
    rank_b16 = shape((1, tokens, 2 * R), bf16)
    all_down = block((2 * R, D), z2)
    line_down = block((2 * R, wide), lambda m, g: (0, g))
    done = None
    for m, s in enumerate(slots):
        low = s.low if done is None else after(s.low, done)
        cot = cotangent[m, 0]
        s.xin, s.z, s.bcin, s.rate_in, s.lr, s.cot0 = call(
            project_kernel, "project", 2 * groups,
            [(low[None], full_low),
             (zx_weight, block((1, D, wide), lambda m, g: (1 - g // groups, 0, g % groups))),
             (first_weight, block((D, 2 * NS + 128), z2)), (s.a_in, all_down),
             (s.u_in, block((2 * R, wide), lambda m, g: (0, (g + groups) % (2 * groups))))],
            [(tok_b16, block((1, tokens, wide), lambda m, g: (0, 0, jnp.minimum(g, groups - 1)))),
             (tok_f32, block((1, tokens, wide), lambda m, g: (0, 0, jnp.maximum(g - groups, 0)))),
             (shape((1, tokens, 2 * NS), bf16), bc_block), (sums_f32, sums), (rank_b16, rank_block)],
            [], 4 * tokens * D * chan, act_bytes * 4, 2, (cot, rows_half, 0, True),
        )
        tail = jnp.concatenate([s.xin[:, tokens - HALO :], s.bcin[:, tokens - HALO :]], axis=2)
        halo = lax.ppermute(tail, "mp", forward_edge)
        s.halo, s.bchalo = halo[..., :chan], halo[..., chan:]
        s.step, s.cum, s.lanes, s.bc = call(
            prep_kernel, "prep", 1,
            [(s.rate_in, sums), (bias, head_line), (rate, head_line), (s.mask[None], one_col), (s.bcin, bc_block),
             (s.bchalo, bc_halo), (conv_bc, bc_taps)],
            [(sums_f32, sums), (sums_f32, sums),
             (shape((1, groups, 2 * HG, tokens), f32), block((1, groups, 2 * HG, tokens), lambda m, g: (0, 0, 0, 0))),
             (bc_f32, bc_block)],
            [], tokens * Q * 128 * 6, tokens * 128 * 24,
        )
        s.mixed, s.square, s.state, s.end, s.cot1 = call(
            forward_kernel, "ssd_forward", groups,
            [(s.xin, chan_block), (s.halo, halo_block), (taps, taps_block), (s.bc, bc_block), (s.cum, sums), (s.step, sums),
             (s.lanes, lanes_block), (skip, line_block), (s.z, chan_block)],
            [(tok_f32, chan_block), (sums_f32, sums), (state_f32, state_block), (state_f32, state_block)],
            [pltpu.VMEM((blocks, Q, Q), f32), pltpu.VMEM((2, blocks, NS, Q), bf16), *line_scratch],
            6 * tokens * Q * chan * 2, act_bytes * 3, 3, (cot, rows_half, halfway, True),
        )
        done = s.mixed

    def reduce_rows(v):
        theirs = lax.dynamic_slice_in_dim(v, (1 - core) * own, own, 0)
        return lax.dynamic_slice_in_dim(v, core * own, own, 0) + other(theirs)

    def fold(v):
        return v[:R] + v[R:]

    waiting = []
    moved = []

    def give(rows):
        waiting.extend([(rows, moved_half, first, False) for first in (0, halfway)])

    def carry(kernel, name, grid, ins, outs, scratch, flops, size, comm):
        load = waiting.pop(0) if waiting else None
        got = call(kernel, name, grid, ins, outs, scratch, flops, size, comm[load is not None] if not load or not load[2] else comm[1] + 10, load)
        if load is not None:
            moved.append(got[-1])
            got = got[:-1]
        return got

    per = part // wide
    cols = out_all.shape[3]
    gs_weight = block((nd, 1, wide, cols), lambda m, g: (0, g // per, g % per, 0))
    branch_weight = block((1,) + out_all.shape[1:], lambda m, g: (g, 0, 0, 0))
    step_cols = block((1, tokens, cols), m3)
    rank_rows = block((1, R, cols), m3)
    rank_chan = block((1, R, chan // nd), m3)
    full_chan = block((1, tokens, chan), m0)

    def gated_grad(s):
        cot = jnp.concatenate([s.cot0, s.cot1], 0)
        gb_own = cot * s.mask_own.astype(bf16)
        s.gb = pair_cat(gb_own, other(gb_own), 0)[None]
        s.gs, dots, s.rg = carry(
            gs_kernel, "gs", groups,
            [(s.gb, full_low), (out_all, gs_weight), (s.u_out, all_down), (s.a_out, line_down), (s.mixed, chan_block),
             (s.z, chan_block), (gain, line_block)],
            [(tok_f32, chan_block), (sums_f32, sums), (rank_b16, rank_block)], [], 2 * tokens * D * chan, act_bytes * 5, (None, 4),
        )
        both = jnp.stack([jnp.sum(s.square, axis=-1), jnp.sum(dots, axis=-1)])
        both = (both + other(both)) / DI
        s.inv_gate = lax.rsqrt(both[0] + eps)[..., None]
        s.coef = s.inv_gate**3 * both[1][..., None]

    def gate_back(s):
        s.dy, s.gz, s.scaled, s.lloc, s.q = carry(
            gate_back_kernel, "gate_back", groups,
            [(s.gs, chan_block), (s.mixed, chan_block), (s.z, chan_block), (s.inv_gate, one_col), (s.coef, one_col),
             (gain, line_block), (s.bc, bc_block), (s.cum, sums)],
            [(tok_f32, chan_block), (tok_b16, chan_block), (tok_b16, chan_block), (state_f32, state_block), (sums_f32, sums)],
            [pltpu.VMEM((2, NS, tokens), bf16)], 6 * tokens * NS * chan, act_bytes * 5, (None, 5),
        )

    def project_out(m, s):
        partial, s.g_up_out, s.g_out = carry(
            branch_kernel, "branch", nd,
            [(s.scaled, full_chan), (out_all, branch_weight), (s.a_out, block((2 * R, chan), z2)),
             (s.u_out, block((2 * R, cols), lambda m, g: (0, g))), (s.rg, rank_block), (s.gb, step_cols)],
            [(shape((1, tokens, D), f32), step_cols), (shape((1, R, D), f32), rank_rows), (shape((1, R, chan), f32), rank_chan)],
            [pltpu.VMEM((tokens, 2 * R), bf16), pltpu.VMEM((2 * R, tokens), bf16), pltpu.VMEM((2 * R, tokens), bf16)],
            2 * tokens * D * chan, act_bytes * 4, (None, 6),
        )
        branch = reduce_rows(partial[0])
        give((x_rows[m].astype(f32) + s.mask_own * branch).astype(bf16))

    def scan_back(s):
        gx, head, tail, gbc, xu, dx = carry(
            scan_back_kernel, "ssd_back", groups,
            [(s.dy, chan_block), (s.xin, chan_block), (s.halo, halo_block), (taps, taps_block), (s.bc, bc_block), (s.cum, sums),
             (s.step, sums), (s.lanes, lanes_block), (skip, line_block), (s.state, state_block), (s.lloc, state_block),
             (s.end, state_block)],
            [(tok_b16, chan_block), (edge_f32, edge_block), (edge_f32, edge_block), (bc_f32, bc_block), (sums_f32, sums),
             (sums_f32, sums)],
            [pltpu.VMEM((blocks, Q, Q), f32), pltpu.VMEM((blocks, Q, Q), f32), pltpu.VMEM((2, blocks, NS, Q), bf16),
             pltpu.VMEM((2, blocks, NS, Q), bf16), *line_scratch],
            12 * tokens * Q * chan * 2, act_bytes * 3, (7, 8),
        )
        gbc = gbc + other(gbc)
        edge_bc = shape((1, 8, 2 * NS), f32)
        gbc, bhead, btail, g_rate = call(
            bc_back_kernel, "bc_back", 1,
            [(gbc, bc_block), (s.bcin, bc_block), (s.bchalo, bc_halo), (conv_bc, bc_taps), (s.q, sums), (dx, sums), (xu, sums),
             (s.step, sums), (s.rate_in, sums), (bias, head_line), (rate, head_line), (s.mask[None], one_col)],
            [(shape((1, tokens, 2 * NS), bf16), bc_block), (edge_bc, bc_edge), (edge_bc, bc_edge),
             (shape((1, tokens, 128), bf16), sums)],
            [], tokens * tokens * 128 * 6, tokens * 2 * NS * 8,
        )
        back = lax.ppermute(jnp.concatenate([head, bhead], 2), "mp", backward_edge)
        tail = jnp.concatenate([tail, btail], 2).at[:, 8 - (KC - 1) :].add(back[:, 8 - (KC - 1) :]).astype(bf16)
        gx = lax.dynamic_update_slice_in_dim(gx, tail[..., :chan], tokens - 8, 1)
        gbc = lax.dynamic_update_slice_in_dim(gbc, tail[..., chan:], tokens - 8, 1)[0]
        half = lax.dynamic_slice_in_dim(gbc, core * NS, NS, 1)
        tail = jnp.concatenate([half[None], g_rate], 2)
        g_low, s.g_up_z, s.g_up_x, s.g_down = carry(
            unproject_kernel, "unproject", D // wide,
            [(s.gz, full_chan), (gx, full_chan), (tail, block((1, tokens, NS + 128), m0)),
             (zx_weight, block((2, wide, chan), lambda m, g: (0, g, 0))), (tail_weight, block((wide, NS + 128), lambda m, g: (g, 0))),
             (s.u_in, block((2 * R, 2 * chan), z2)), (s.a_in, line_down), (s.lr, rank_block), (s.low[None], chan_block)],
            [(shape((1, tokens, D), f32), chan_block), (shape((1, R, chan), f32), block((1, R, wide), m3)),
             (shape((1, R, chan), f32), block((1, R, wide), m3)), (shape((1, R, D), f32), block((1, R, wide), m3))],
            [pltpu.VMEM((tokens, 2 * R), bf16), pltpu.VMEM((2 * R, tokens), bf16), pltpu.VMEM((2 * R, tokens), bf16)],
            4 * tokens * D * chan, act_bytes * 3, (None, 9),
        )
        return g_low[0]

    def input_grad(m, s, g_low):
        gn = reduce_rows(g_low) * norm_gain
        x = x_rows[m].astype(f32)
        delta = s.inv * gn - x * (s.inv**3 * jnp.mean(gn * x, axis=-1, keepdims=True))
        return delta.astype(bf16)

    gated_grad(slots[0])
    for m, s in enumerate(slots):
        if m + 1 < micros:
            gated_grad(slots[m + 1])
        gate_back(s)
        project_out(m, s)
    for m, s in enumerate(slots):
        delta = input_grad(m, s, scan_back(s))
        if m + 1 < micros:
            give(delta)
    together = []
    for at in range(0, len(moved), 2):
        pair = jnp.stack([v.reshape(nz, halfway, feats) for v in moved[at : at + 2]], 1)
        together.append(pair.reshape(seg, feats))
    together.append(move_last(delta, moved_b16, nz, 30))
    out = jnp.stack(together[:micros])[:, None]
    grad = cotangent.astype(f32) + jnp.stack(together[micros:])[:, None].astype(f32)

    picks = jnp.stack([s.pick for s in slots])

    def near_sum(values):
        v = jnp.stack([jnp.stack([g.reshape(R, nz, part) for g in gs]) for gs in values])
        v = scatter_sum(jnp.transpose(v, (3, 0, 1, 2, 4)), "mp")
        v = jnp.sum(picks[:, :, None, None, None] * v[:, None], axis=0)
        v = scatter_sum(v.reshape((nd, 2) + v.shape[1:]), "dp")
        keep = lax.dynamic_index_in_dim(v, core, 0, False)
        give = lax.dynamic_index_in_dim(v, 1 - core, 0, False)
        return pair_cat(keep[None], other(give)[None], 0)

    def far_sum(values):
        v = jnp.stack(values).reshape(micros, R, nd, 2, nz, each)
        v = jnp.transpose(v, (3, 4, 0, 1, 2, 5))
        v = lax.dynamic_index_in_dim(v, core, 0, False) + other(lax.dynamic_index_in_dim(v, 1 - core, 0, False))
        v = scatter_sum(v, "mp")
        v = jnp.sum(picks[:, :, None, None, None] * v[:, None], axis=0)
        return scatter_sum(jnp.transpose(v, (2, 0, 1, 3)), "dp")

    g_out_down = near_sum([[s.g_out] for s in slots])
    g_out_down = jnp.transpose(g_out_down[:, 0], (0, 2, 1)).reshape(2 * part, R)
    g_out_up = far_sum([s.g_up_out for s in slots]).reshape(ADAPT * R, each)
    g_in_up = near_sum([[s.g_up_z, s.g_up_x] for s in slots])
    g_in_up = jnp.transpose(g_in_up, (2, 1, 0, 3)).reshape(R, 2, 2 * part)
    g_in_down = jnp.transpose(far_sum([s.g_down for s in slots]), (0, 2, 1))
    return (out, grad, g_in_down, g_in_up, g_out_down, g_out_up)


def solution(mesh):
    in_specs = (
        P(None, "dp", "seq", "mp"),
        P(None, "dp", "seq", "mp"),
        P(None, "dp"),
        P(None, "dp"),
        P(),
        P(("dp", "seq"), None, "mp"),
        P(("dp", "seq"), None),
        P(("dp", "seq"), "mp"),
        P("mp"),
        P("mp"),
        P("mp"),
        P(None, "mp"),
        P(),
        P("mp"),
        P("mp", ("dp", "seq")),
        P(None, ("dp", "seq", "mp"), None),
        P(("dp", "seq"), None, "mp"),
        P("mp", ("dp", "seq")),
        P(None, ("dp", "seq", "mp")),
    )
    out_specs = (
        P(None, "dp", "seq", "mp"),
        P(None, "dp", "seq", "mp"),
        P(None, ("dp", "seq", "mp"), None),
        P(("dp", "seq"), None, "mp"),
        P("mp", ("dp", "seq")),
        P(None, ("dp", "seq", "mp")),
    )
    sizes = dict(mesh.shape)
    by_chip = (
        sizes["seq"] == 2
        and sizes["dp"] * 2 == ADAPT
        and sizes["mp"] % 2 == 0
        and sizes["mp"] & (sizes["mp"] - 1) == 0
        and (2048 // sizes["mp"]) % Q == 0
    )
    return jax.shard_map(fast_body if by_chip else body, mesh=mesh, in_specs=in_specs, out_specs=out_specs, check_vma=False)
```

```python
import functools

import jax
import jax.numpy as jnp
from jax import lax
from jax.experimental import pallas as pl
from jax.experimental.pallas import tpu as pltpu
from jax.sharding import PartitionSpec as P

D = 2048
P_SIZE = 64
NS = 128
KC = 4
Q = 256
R = 16
ADAPT = 8
DI = 4096
HG = 4
HALO = 16
SLOTS = 3


eps = 1e-05
precise = lax.Precision.HIGHEST
VMEM_LIMIT = 56 * 1024 * 1024


def shifted(array, axis, by):
    size = lax.axis_size(axis)
    pairs = [(i, i + by) for i in range(size) if 0 <= i + by < size]
    return lax.ppermute(array, axis, pairs)


def entering(part, axis, combine, identity, reverse):
    count = lax.axis_size(axis)
    place = lax.axis_index(axis)
    ahead = count - 1 - place if reverse else place
    gathered = jax.tree.map(lambda a: lax.all_gather(a, axis), part)
    state = jax.tree.map(lambda a, e: jnp.zeros_like(a) + jnp.asarray(e, a.dtype), part, identity)

    def one(hop, state):
        source = count - 1 - hop if reverse else hop
        return combine(
            state, jax.tree.map(lambda a: lax.dynamic_index_in_dim(a, source, 0, False), gathered)
        )

    return lax.fori_loop(0, ahead, one, state)


def silu_grad(value):
    sigmoid_val = jax.nn.sigmoid(value)
    return sigmoid_val * (1.0 + value * (1.0 - sigmoid_val))


def block_step(carry_state, pieces):
    x_part, b_part, c_part, log_part, step_part = pieces
    length = log_part.shape[0]
    cumulative = jnp.cumsum(log_part, axis=0)
    causal = jnp.arange(length)[:, None] >= jnp.arange(length)[None, :]
    spread = cumulative[:, None, :] - cumulative[None, :, :]
    decay_mat = jnp.exp(jnp.where(causal[:, :, None], spread, -10000.0))
    scores = jnp.dot(c_part, b_part.T, precision=precise)
    mixing = scores[:, :, None] * decay_mat * step_part[None, :, :]
    inner_out = jnp.einsum("tsh,shp->thp", mixing, x_part, precision=precise)
    carried = jnp.exp(cumulative)[:, :, None] * jnp.einsum(
        "tn,hpn->thp", c_part, carry_state, precision=precise
    )
    weights = jnp.exp(cumulative[-1][None, :] - cumulative) * step_part
    update = jnp.einsum("sh,shp,sn->hpn", weights, x_part, b_part, precision=precise)
    new_state = jnp.exp(cumulative[-1])[:, None, None] * carry_state + update
    return (new_state, inner_out + carried)


def local_scan(x_heads, b_rows, c_rows, log_rows, step_rows):
    seg_rows = x_heads.shape[0]
    blocks = seg_rows // Q

    def blocked(tensor):
        return tensor.reshape((blocks, Q) + tensor.shape[1:])

    init_state = jnp.zeros((x_heads.shape[1], x_heads.shape[2], b_rows.shape[1]), jnp.float32)
    final_state, outputs = lax.scan(
        block_step,
        init_state,
        (blocked(x_heads), blocked(b_rows), blocked(c_rows), blocked(log_rows), blocked(step_rows)),
    )
    return (outputs.reshape(x_heads.shape), final_state, jnp.sum(log_rows, axis=0))


def incoming(c_rows, log_rows, state_in):
    cumulative = jnp.cumsum(log_rows, axis=0)
    return jnp.exp(cumulative)[:, :, None] * jnp.einsum(
        "tn,hpn->thp", c_rows, state_in, precision=precise
    )


def compose(earlier, later):
    return (later[0] * earlier[0], later[1] + later[0][..., None, None] * earlier[1])


def fetch_weights(w_zx, w_bc, w_dt, w_out, in_up, out_down):
    return (
        lax.all_gather(w_zx, ("dp", "seq"), axis=0, tiled=True),
        lax.all_gather(w_bc, ("dp", "seq"), axis=0, tiled=True),
        lax.all_gather(w_dt, ("dp", "seq"), axis=0, tiled=True),
        lax.all_gather(w_out, ("dp", "seq"), axis=1, tiled=True),
        lax.all_gather(in_up, ("dp", "seq"), axis=0, tiled=True),
        lax.all_gather(out_down, ("dp", "seq"), axis=1, tiled=True),
    )


def reduce_adapters(grads):
    near_sums = (
        lax.psum_scatter(grads[1], ("dp", "seq"), scatter_dimension=0, tiled=True),
        lax.psum_scatter(grads[2], ("dp", "seq"), scatter_dimension=1, tiled=True),
    )
    wide_sums = (
        lax.psum_scatter(grads[0], ("dp", "seq", "mp"), scatter_dimension=1, tiled=True),
        lax.psum_scatter(grads[3], ("dp", "seq", "mp"), scatter_dimension=1, tiled=True),
    )
    return (wide_sums[0], near_sums[0], near_sums[1], wide_sums[1])


def body(
    x_in,
    cotangent,
    lengths,
    adapter_ids,
    norm_gain,
    w_zx,
    w_bc,
    w_dt,
    dt_bias,
    a_log,
    d_skip,
    conv_x,
    conv_bc,
    gate_gain,
    w_out,
    in_down,
    in_up,
    out_down,
    out_up,
):
    micro_count, slot_count, seg_len, model_part = x_in.shape
    head_local = dt_bias.shape[0]
    inner_local = head_local * P_SIZE
    wide_down, wide_up = (
        lax.all_gather(in_down, ("dp", "seq", "mp"), axis=1, tiled=True),
        lax.all_gather(out_up, ("dp", "seq", "mp"), axis=1, tiled=True),
    )
    wide_down = wide_down.astype(jnp.float32)
    wide_up = wide_up.astype(jnp.float32)
    conv_taps = jnp.concatenate([conv_x, conv_bc], axis=1)
    decay_rate = -jnp.exp(a_log)
    positions = lax.axis_index("seq") * seg_len + jnp.arange(seg_len)
    feature_start = lax.axis_index("mp") * model_part
    scan_local = jax.vmap(local_scan)
    incoming_map = jax.vmap(incoming)
    gathered = None
    outputs = []
    x_grads = []
    running = None
    for batch_index in range(micro_count):
        gathered = fetch_weights(w_zx, w_bc, w_dt, w_out, in_up, out_down)
        zx_weight, bc_weight, dt_weight, out_weight, up_in, down_out = gathered
        rows_own = x_in[batch_index]
        cot_own = cotangent[batch_index]
        rows_full, cot_full = (
            lax.all_gather(rows_own, "mp", axis=2, tiled=True),
            lax.all_gather(cot_own, "mp", axis=2, tiled=True),
        )
        rows_value = rows_full.astype(jnp.float32)
        inv_rms = lax.rsqrt(jnp.mean(rows_value * rows_value, axis=-1, keepdims=True) + eps)
        normed = rows_value * inv_rms * norm_gain
        normed_low = normed.astype(jnp.bfloat16)
        normed_value = normed_low.astype(jnp.float32)
        select = jax.nn.one_hot(adapter_ids[batch_index], ADAPT, dtype=jnp.float32)
        down_sel = jnp.einsum("sa,adr->sdr", select, wide_down, precision=precise)
        up_sel = jnp.einsum(
            "sa,arcf->srcf",
            select,
            up_in.astype(jnp.float32).reshape(ADAPT, R, 2, inner_local),
            precision=precise,
        )
        low_rank = jnp.einsum("std,sdr->str", normed_value, down_sel, precision=precise)
        proj_zx = jnp.einsum(
            "std,dcf->stcf", normed_low, zx_weight, preferred_element_type=jnp.float32
        )
        proj_zx = proj_zx + jnp.einsum("str,srcf->stcf", low_rank, up_sel, precision=precise)
        proj_bc = jnp.einsum(
            "std,dn->stn", normed_low, bc_weight, preferred_element_type=jnp.float32
        )
        proj_dt = jnp.einsum(
            "std,dh->sth", normed_low, dt_weight, preferred_element_type=jnp.float32
        )
        gate_in = proj_zx[:, :, 0]
        conv_in = jnp.concatenate(
            [proj_zx[:, :, 1].astype(jnp.bfloat16), proj_bc.astype(jnp.bfloat16)], axis=-1
        )
        earlier_rows = shifted(conv_in[:, seg_len - (KC - 1) :], "seq", 1)
        extended = jnp.concatenate([earlier_rows, conv_in], axis=1).astype(jnp.float32)
        conv_pre = sum(
            (
                conv_taps[tap_index] * extended[:, tap_index : tap_index + seg_len]
                for tap_index in range(KC)
            )
        )
        conv_out = jax.nn.silu(conv_pre)
        x_heads = conv_out[..., :inner_local].reshape(slot_count, seg_len, head_local, P_SIZE)
        b_rows = conv_out[..., inner_local : inner_local + NS]
        c_rows = conv_out[..., inner_local + NS :]
        mask_rows = (positions[None, :] < lengths[batch_index][:, None]).astype(jnp.float32)
        rate_in = proj_dt + dt_bias
        step_rows = jax.nn.softplus(rate_in) * mask_rows[..., None]
        log_rows = step_rows * decay_rate
        (plain_out, state_local, log_total), scan_back = jax.vjp(
            scan_local, x_heads, b_rows, c_rows, log_rows, step_rows
        )
        factor = jnp.exp(log_total)
        identity = (jnp.ones_like(factor), jnp.zeros_like(state_local))
        state_in = entering((factor, state_local), "seq", compose, identity, False)[1]
        from_state, state_back = jax.vjp(incoming_map, c_rows, log_rows, state_in)
        mixed_heads = plain_out + from_state + d_skip[:, None] * x_heads
        mixed_flat = mixed_heads.reshape(slot_count, seg_len, inner_local)
        gate_act = jax.nn.silu(gate_in)
        gated_out = mixed_flat * gate_act
        square_sum = lax.psum(jnp.sum(gated_out * gated_out, axis=-1), "mp")
        inv_gate = lax.rsqrt(square_sum / DI + eps)
        scaled = gated_out * inv_gate[..., None] * gate_gain
        scaled_low = scaled.astype(jnp.bfloat16)
        scaled_value = scaled_low.astype(jnp.float32)
        out_sel = jnp.einsum(
            "sa,far->sfr",
            select,
            down_out.astype(jnp.float32).reshape(inner_local, ADAPT, R),
            precision=precise,
        )
        up_out = jnp.einsum("sa,ard->srd", select, wide_up.reshape(ADAPT, R, D), precision=precise)
        rank_out = jnp.einsum("stf,sfr->str", scaled_value, out_sel, precision=precise)
        partial_out = jnp.einsum(
            "stf,fd->std", scaled_low, out_weight, preferred_element_type=jnp.float32
        )
        partial_out = partial_out + jnp.einsum("str,srd->std", rank_out, up_out, precision=precise)
        branch = lax.psum_scatter(partial_out, "mp", scatter_dimension=2, tiled=True)
        outputs.append(
            (rows_own.astype(jnp.float32) + mask_rows[..., None] * branch).astype(jnp.bfloat16)
        )
        branch_grad = cot_full * mask_rows[..., None].astype(jnp.bfloat16)
        branch_value = branch_grad.astype(jnp.float32)
        rank_grad = jnp.einsum("std,srd->str", branch_value, up_out, precision=precise)
        grad_up_out = jnp.einsum("str,std->srd", rank_out, branch_value, precision=precise)
        grad_out_sel = jnp.einsum("stf,str->sfr", scaled_value, rank_grad, precision=precise)
        scaled_grad = jnp.einsum(
            "std,fd->stf", branch_grad, out_weight, preferred_element_type=jnp.float32
        )
        scaled_grad = scaled_grad + jnp.einsum(
            "str,sfr->stf", rank_grad, out_sel, precision=precise
        )
        weighted = scaled_grad * gate_gain
        dot_sum = lax.psum(jnp.sum(weighted * gated_out, axis=-1), "mp")
        gated_grad = (
            weighted * inv_gate[..., None] - gated_out * (inv_gate**3 * dot_sum / DI)[..., None]
        )
        mixed_grad = (gated_grad * gate_act).reshape(slot_count, seg_len, head_local, P_SIZE)
        gate_grad = gated_grad * mixed_flat * silu_grad(gate_in)
        c_grad_in, log_grad_in, state_in_grad = state_back(mixed_grad)
        later_grads = entering((factor, state_in_grad), "seq", compose, identity, True)[1]
        total_grad = jnp.sum(later_grads * state_in, axis=(2, 3)) * factor
        x_heads_grad, b_grad, c_grad, log_grad, step_grad = scan_back(
            (mixed_grad, later_grads, total_grad)
        )
        x_heads_grad = x_heads_grad + d_skip[:, None] * mixed_grad
        c_grad = c_grad + c_grad_in
        step_grad = step_grad + (log_grad + log_grad_in) * decay_rate
        rate_grad = step_grad * mask_rows[..., None] * jax.nn.sigmoid(rate_in)
        conv_out_grad = jnp.concatenate(
            [x_heads_grad.reshape(slot_count, seg_len, inner_local), b_grad, c_grad], axis=-1
        )
        pre_grad = conv_out_grad * silu_grad(conv_pre)
        padded_grad = jnp.pad(pre_grad, ((0, 0), (KC - 1, KC - 1), (0, 0)))
        ext_grad = sum(
            (
                conv_taps[tap_index]
                * padded_grad[:, KC - 1 - tap_index : KC - 1 - tap_index + seg_len + KC - 1]
                for tap_index in range(KC)
            )
        )
        returned = shifted(ext_grad[:, : KC - 1], "seq", -1)
        in_grad = ext_grad[:, KC - 1 :]
        in_grad = in_grad.at[:, seg_len - (KC - 1) :].add(returned)
        zx_grad = jnp.stack([gate_grad, in_grad[..., :inner_local]], axis=2).astype(jnp.bfloat16)
        dt_grad_low = rate_grad.astype(jnp.bfloat16)
        zx_grad_value = zx_grad.astype(jnp.float32)
        rank_in_grad = jnp.einsum("stcf,srcf->str", zx_grad_value, up_sel, precision=precise)
        grad_up_sel = jnp.einsum("str,stcf->srcf", low_rank, zx_grad_value, precision=precise)
        grad_down_sel = jnp.einsum("std,str->sdr", normed_value, rank_in_grad, precision=precise)
        normed_part = jnp.einsum(
            "stcf,dcf->std", zx_grad, zx_weight, preferred_element_type=jnp.float32
        )
        normed_part = normed_part + jnp.einsum(
            "sth,dh->std", dt_grad_low, dt_weight, preferred_element_type=jnp.float32
        )
        normed_part = normed_part + jnp.einsum(
            "str,sdr->std", rank_in_grad, down_sel, precision=precise
        )
        bc_partial = in_grad[..., inner_local:]
        normed_sum, bc_sum = lax.psum((normed_part, bc_partial), "mp")
        normed_grad = normed_sum + jnp.einsum(
            "stn,dn->std",
            bc_sum.astype(jnp.bfloat16),
            bc_weight,
            preferred_element_type=jnp.float32,
        )
        scaled_in = normed_grad * norm_gain
        row_grad = inv_rms * scaled_in - rows_value * inv_rms**3 * jnp.mean(
            scaled_in * rows_value, axis=-1, keepdims=True
        )
        own_slice = lax.dynamic_slice_in_dim(row_grad, feature_start, model_part, 2)
        x_grads.append(cot_own.astype(jnp.float32) + own_slice)
        local_grads = (
            jnp.einsum("sa,sdr->adr", select, grad_down_sel, precision=precise),
            jnp.einsum("sa,srcf->arcf", select, grad_up_sel, precision=precise).reshape(
                ADAPT * R, 2, inner_local
            ),
            jnp.einsum("sa,sfr->far", select, grad_out_sel, precision=precise).reshape(
                inner_local, ADAPT * R
            ),
            jnp.einsum("sa,srd->ard", select, grad_up_out, precision=precise).reshape(ADAPT * R, D),
        )
        running = local_grads if running is None else jax.tree.map(jnp.add, running, local_grads)
    running = reduce_adapters(running)
    return (jnp.stack(outputs), jnp.stack(x_grads), running[0], running[1], running[2], running[3])


MESH = pl.DeviceIdType.MESH


def split(v):
    hi = v.astype(jnp.bfloat16)
    return hi, (v - hi.astype(jnp.float32)).astype(jnp.bfloat16)


def mm(a, b):
    return lax.dot_general(a, b, (((1,), (0,)), ((), ())), preferred_element_type=jnp.float32)


def mm_t(a, b):
    return lax.dot_general(a, b, (((1,), (1,)), ((), ())), preferred_element_type=jnp.float32)


def mm3(a, b):
    return mm(a[0], b[0]) + mm(a[0], b[1]) + mm(a[1], b[0])


def mm3_t(a, b):
    return mm_t(a[0], b[0]) + mm_t(a[0], b[1]) + mm_t(a[1], b[0])


def ones_mm(ones, v):
    hi, lo = split(v)
    rest = v - hi.astype(jnp.float32) - lo.astype(jnp.float32)
    return mm(ones, hi) + mm(ones, lo) + mm(ones, rest.astype(jnp.bfloat16))


def conv_rows(rows, halo, taps):
    count = rows.shape[0]
    ext = jnp.concatenate([halo, rows], axis=0).astype(jnp.float32)
    first = HALO - (KC - 1)
    total = taps[0:1] * ext[first : first + count]
    for j in range(1, KC):
        total = total + taps[j : j + 1] * ext[first + j : first + j + count]
    return total


def conv_rows_back(grad, taps):
    count, width = grad.shape
    zero = jnp.zeros((8, width), jnp.float32)
    ext = jnp.concatenate([zero, grad, zero], axis=0)
    total = taps[0:1] * ext[3 : 3 + count + 8]
    for j in range(1, KC):
        total = total + taps[j : j + 1] * ext[3 - j : 3 - j + count + 8]
    return total


def widen(columns):
    rows = columns.shape[0]
    lane = lax.broadcasted_iota(jnp.int32, (rows, 2 * P_SIZE), 1)
    return jnp.concatenate(
        [jnp.where(lane < P_SIZE, columns[:, h : h + 1], columns[:, h + 1 : h + 2]) for h in range(0, HG, 2)], axis=1
    )


def of_group(value, group):
    return pltpu.roll(value, lax.rem(128 - group * HG, 128), 1)


def head_sums(prod, group):
    rows = prod.shape[1]
    row = lax.broadcasted_iota(jnp.int32, (rows, 128), 0) // P_SIZE + group * HG
    lane = lax.broadcasted_iota(jnp.int32, (rows, 128), 1)
    pick = (row == lane).astype(jnp.float32).astype(jnp.bfloat16)
    hi, lo = split(prod)
    return mm(hi, pick) + mm(lo, pick)


def lane_sum(v):
    part = v[:, :128]
    for k in range(1, v.shape[1] // 128):
        part = part + v[:, k * 128 : (k + 1) * 128]
    return part


def add_up(ref, value, group):
    @pl.when(group == 0)
    def _():
        ref[0] = value

    @pl.when(group > 0)
    def _():
        ref[0] += value


def run_of(slot, z):
    return SLOTS * z + lax.rem(slot + z, SLOTS)


def place_of(run):
    z = run // SLOTS
    return z, lax.rem(lax.rem(run, SLOTS) + SLOTS * SLOTS - z, SLOTS)


class Mover:
    def __init__(self, src_ref, dst_ref, send_sem, recv_sem, count, slots, to_rows):
        self.refs = src_ref, dst_ref, send_sem, recv_sem
        self.count, self.slots, self.to_rows = count, slots, to_rows
        self.d, self.c, self.z = lax.axis_index("dp"), lax.axis_index("seq"), lax.axis_index("mp")
        self.pieces = 4 * SLOTS if to_rows else count * len(slots)

    def piece(self, n):
        src_ref, dst_ref, send_sem, recv_sem = self.refs
        if self.to_rows:
            m, h, to_c = n // 4, n // 2 % 2, lax.rem(n + self.c, 2)
            to_z, slot = place_of(m * self.count + 2 * self.c + h)
            own = src_ref.shape[1] // 4
            src = src_ref.at[m, pl.ds(pl.multiple_of((2 * h + to_c) * own, 16), own), :]
            dst, sem = self.landing(slot - self.slots[0], self.z), (slot, self.z)
            due = jnp.logical_and(slot >= self.slots[0], slot <= self.slots[-1])
        else:
            slot = self.slots[n // self.count]
            to_z = lax.rem(self.z + n % self.count, self.count)
            run = run_of(slot, self.z)
            m, chunk = run // self.count, lax.rem(run, self.count)
            to_c, q = chunk // 2, lax.rem(chunk, 2) * 2 + self.c
            feats = dst_ref.shape[2]
            src = src_ref.at[slot - self.slots[0], :, pl.ds(pl.multiple_of(to_z * feats, 128), feats)]
            dst, sem = self.landing(m, q), (m, q)
            due = True
        here = jnp.logical_and(to_c == self.c, to_z == self.z)
        near = pltpu.make_async_copy(src, dst, recv_sem.at[sem])
        far = pltpu.make_async_remote_copy(
            src_ref=src, dst_ref=dst, send_sem=send_sem.at[n], recv_sem=recv_sem.at[sem],
            device_id=(self.d, to_c, to_z), device_id_type=MESH,
        )
        return jnp.logical_and(due, here), jnp.logical_and(due, jnp.logical_not(here)), near, far

    def landing(self, first, slot):
        dst_ref = self.refs[1]
        if self.to_rows:
            feats = dst_ref.shape[2] // self.count
            return dst_ref.at[first, :, pl.ds(pl.multiple_of(slot * feats, 128), feats)]
        rows = dst_ref.shape[1] // 4
        return dst_ref.at[first, pl.ds(pl.multiple_of(slot * rows, 16), rows), :]

    def greet(self, barrier):
        for cc in range(2):
            for r in range(self.count):
                if cc or r:
                    device = (self.d, lax.rem(self.c + cc, 2), lax.rem(self.z + r, self.count))
                    pl.semaphore_signal(barrier, 1, device_id=device, device_id_type=MESH)
        return 2 * self.count - 1

    def start(self, n):
        stays, goes, near, far = self.piece(n)

        @pl.when(stays)
        def _():
            near.start()

        @pl.when(goes)
        def _():
            far.start()

    def start_at(self, step, steps):
        for n in range(self.pieces):
            @pl.when(step == n * steps * 7 // (8 * self.pieces))
            def _():
                self.start(n)

    def finish(self):
        recv_sem = self.refs[3]
        if self.to_rows:
            for slot in self.slots:
                for s in range(self.count):
                    area = self.landing(slot - self.slots[0], s)
                    pltpu.make_async_copy(area, area, recv_sem.at[slot, s]).wait()
        else:
            for m in range(SLOTS):
                for q in range(4):
                    run = m * self.count + 2 * self.c + q // 2
                    slot = place_of(run)[1]

                    @pl.when(jnp.logical_and(slot >= self.slots[0], slot <= self.slots[-1]))
                    def _():
                        area = self.landing(m, q)
                        pltpu.make_async_copy(area, area, recv_sem.at[m, q]).wait()
        for n in range(self.pieces):
            _, goes, _, far = self.piece(n)

            @pl.when(goes)
            def _():
                far.wait_send()


class Line:
    def __init__(self, held_ref, sent_ref, send_sem, recv_sem, count, step):
        self.refs = held_ref, sent_ref, send_sem, recv_sem
        self.step, self.count = step, count
        self.d, self.c, self.z = lax.axis_index("dp"), lax.axis_index("seq"), lax.axis_index("mp")
        low, high = self.z > 0, self.z < count - 1
        self.has_source, self.has_target = (low, high) if step > 0 else (high, low)
        above, below = count - 1 - self.z, count - 2 - self.z
        self.from_slot, self.to_slot = (above, below) if step > 0 else (below, above)

    def greet(self, barrier):
        @pl.when(self.has_source)
        def _():
            pl.semaphore_signal(barrier, 1, device_id=(self.d, self.c, self.z - self.step), device_id_type=MESH)
        return jnp.where(self.has_target, 1, 0)

    def copy(self, group):
        held_ref, sent_ref, send_sem, recv_sem = self.refs
        return pltpu.make_async_remote_copy(
            src_ref=sent_ref.at[group], dst_ref=held_ref.at[group], send_sem=send_sem.at[group], recv_sem=recv_sem.at[group],
            device_id=(self.d, self.c, self.z + self.step), device_id_type=MESH,
        )

    def receive(self, slot, group):
        held_ref, sent_ref = self.refs[:2]
        remote = jnp.logical_and(self.has_source, slot == self.from_slot)
        fresh = slot == (0 if self.step > 0 else SLOTS - 1)
        local = jnp.logical_not(jnp.logical_or(remote, fresh))

        @pl.when(remote)
        def _():
            self.copy(group).wait_recv()
            sent_ref[held_ref.shape[0] + group] = held_ref[group]

        return jnp.where(jnp.logical_or(remote, local), sent_ref[held_ref.shape[0] + group], 0.0)

    def send(self, slot, group, value):
        held_ref, sent_ref = self.refs[:2]
        sent_ref[held_ref.shape[0] + group] = value

        @pl.when(jnp.logical_and(self.has_target, slot == self.to_slot))
        def _():
            sent_ref[group] = value
            self.copy(group).start()

    def finish(self):
        @pl.when(self.has_target)
        def _():
            for g in range(self.refs[0].shape[0]):
                self.copy(g).wait_send()


class PairFill:
    def __init__(self, own_ref, both_ref, buffer_ref, sems):
        self.d, self.c, self.z = lax.axis_index("dp"), lax.axis_index("seq"), lax.axis_index("mp")
        own = own_ref.shape[1]
        mine = buffer_ref.at[:, pl.ds(pl.multiple_of(self.c * own, 16), own), :]
        theirs = buffer_ref.at[:, pl.ds(pl.multiple_of((1 - self.c) * own, 16), own), :]
        self.near = pltpu.make_async_copy(own_ref, mine, sems.at[0])
        self.far = pltpu.make_async_remote_copy(
            src_ref=own_ref, dst_ref=mine, send_sem=sems.at[1], recv_sem=sems.at[2], device_id=(self.d, 1 - self.c, self.z),
            device_id_type=MESH,
        )
        self.arrival = pltpu.make_async_copy(theirs, theirs, sems.at[2])
        self.keep = pltpu.make_async_copy(buffer_ref, both_ref, sems.at[3])

    def greet(self, barrier):
        pl.semaphore_signal(barrier, 1, device_id=(self.d, 1 - self.c, self.z), device_id_type=MESH)
        return 1

    def fill(self):
        self.far.start()
        self.near.start()
        self.near.wait()
        self.arrival.wait()
        self.keep.start()

    def finish(self):
        self.far.wait_send()
        self.keep.wait()


def carried_by(kernel, count, first, to_rows, n_in, n_out, *refs):
    ins, src_ref, outs, dst_ref = refs[:n_in], refs[n_in], refs[n_in + 1 : n_in + 1 + n_out], refs[n_in + 1 + n_out]
    scratch, sems = refs[n_in + n_out + 2 : -2], refs[-2:]
    kernel(*ins, *outs, *scratch, mover=Mover(src_ref, dst_ref, *sems, count, first, to_rows))


def step_of(grid):
    return pl.program_id(0) * grid[1] + pl.program_id(1)


def begin(grid, *parties):
    parties = [p for p in parties if p is not None]
    if parties:
        @pl.when(step_of(grid) == 0)
        def _():
            barrier = pltpu.get_barrier_semaphore()
            waits = 0
            for party in parties:
                waits = waits + party.greet(barrier)
            pl.semaphore_wait(barrier, waits)
            for party in parties:
                if isinstance(party, PairFill):
                    party.fill()
    for party in parties:
        if isinstance(party, Mover):
            party.start_at(step_of(grid), grid[0] * grid[1])


def end(grid, *parties):
    parties = [p for p in parties if p is not None]
    if parties:
        @pl.when(step_of(grid) == grid[0] * grid[1] - 1)
        def _():
            for party in parties:
                party.finish()


def twice_split(v):
    hi, lo = split(v)
    lane = lax.broadcasted_iota(jnp.int32, v.shape, 1)
    return jnp.where(lane < v.shape[1] // 2, hi.astype(jnp.float32), lo.astype(jnp.float32)).astype(jnp.bfloat16)


def fold(v):
    half = v.shape[0] // 2
    return v[:half] + v[half:]


def merge(ref):
    return ref[...].reshape(ref.shape[0] * ref.shape[1], ref.shape[2])


def project_kernel(
    grid, own_ref, w_ref, tailw_ref, down_ref, up_ref, xin_ref, z_ref, bcin_ref, rate_ref, lr_ref, both_ref, low_ref, sems,
    mover=None
):
    step = pl.program_id(1)
    pair = PairFill(own_ref, both_ref, low_ref, sems)
    begin(grid, pair, mover)
    slots, tokens = low_ref.shape[:2]

    @pl.when(step == 0)
    def _():
        for m in range(slots):
            tail = mm(low_ref[m], tailw_ref[...])
            bcin_ref[m] = tail[:, : 2 * NS].astype(jnp.bfloat16)
            rate_ref[m] = tail[:, 2 * NS :]
            lr_ref[m] = twice_split(mm_t(low_ref[m], down_ref[m]))

    value = mm(merge(low_ref), w_ref[0])
    for m in range(slots):
        part = value[m * tokens : (m + 1) * tokens] + mm(lr_ref[m], up_ref[m])

        @pl.when(step < grid[1] // 2)
        def _():
            xin_ref[m] = part.astype(jnp.bfloat16)

        @pl.when(step >= grid[1] // 2)
        def _():
            z_ref[m] = part

    end(grid, pair, mover)


def prep_kernel(rate_ref, bias_ref, decay_ref, mask_ref, bcin_ref, bchalo_ref, taps_ref, step_ref, cum_ref, lanes_ref, bc_ref):
    rows = rate_ref.shape[1]
    value = rate_ref[0] + bias_ref[...]
    step = (jnp.maximum(value, 0.0) + jnp.log1p(jnp.exp(-jnp.abs(value)))) * mask_ref[0]
    log = step * decay_ref[...]
    tri = lax.broadcasted_iota(jnp.int32, (Q, Q), 0) >= lax.broadcasted_iota(jnp.int32, (Q, Q), 1)
    tri = tri.astype(jnp.float32).astype(jnp.bfloat16)
    step_ref[0] = step
    cum = jnp.concatenate([ones_mm(tri, log[b * Q : (b + 1) * Q]) for b in range(rows // Q)], axis=0)
    cum_ref[0] = cum
    cum_t, step_t = cum.T, step.T
    for g in range(lanes_ref.shape[1]):
        lanes_ref[0, g, :HG] = cum_t[g * HG : (g + 1) * HG]
        lanes_ref[0, g, HG:] = step_t[g * HG : (g + 1) * HG]
    pre = conv_rows(bcin_ref[0], bchalo_ref[0], taps_ref[...])
    bc_ref[0] = pre * jax.nn.sigmoid(pre)


def forward_kernel(
    grid, xin_ref, halo_ref, taps_ref, bc_ref, cum_ref, step_ref, lanes_ref, skip_ref, z_ref, mixed_ref, square_ref, state_ref,
    end_ref, scores_ref, bt_ref, held_ref, sent_ref, send_sem, recv_sem, mover=None
):
    group = pl.program_id(1)
    rows = xin_ref.shape[1]
    blocks = rows // Q
    line = Line(held_ref, sent_ref, send_sem, recv_sem, lax.axis_size("mp"), 1)
    begin(grid, line, mover)

    @pl.when(step_of(grid) == 0)
    def _():
        sent_ref[...] = jnp.zeros(sent_ref.shape, jnp.float32)

    @pl.when(group == 0)
    def _():
        for b in range(blocks):
            part = bc_ref[0, b * Q : (b + 1) * Q]
            b_part = split(part[:, :NS])
            c_part = split(part[:, NS:])
            scores_ref[b] = mm3_t(c_part, b_part)
            hi, lo = split(part[:, :NS].T)
            bt_ref[0, b] = hi
            bt_ref[1, b] = lo

    pre = conv_rows(xin_ref[0], halo_ref[0], taps_ref[...])
    x = pre * jax.nn.sigmoid(pre)
    cums, decs, updates = [], [], []
    for b in range(blocks):
        at = slice(b * Q, (b + 1) * Q)
        cum = of_group(cum_ref[0, at], group)
        step = of_group(step_ref[0, at], group)
        total = cum[Q - 1 : Q]
        wx = x[at] * widen(jnp.exp(total - cum) * step)
        cums.append(cum)
        decs.append(widen(jnp.exp(total)))
        updates.append(mm3((bt_ref[0, b], bt_ref[1, b]), split(wx)))

    slot = pl.program_id(0)
    states = [line.receive(slot, group)]
    for b in range(blocks):
        states.append(decs[b] * states[b] + updates[b])
    state_ref[0] = states[0]
    end_ref[0] = states[blocks]
    line.send(slot, group, states[blocks])
    lane = lax.broadcasted_iota(jnp.int32, (Q, 2 * P_SIZE), 1)
    causal = lax.broadcasted_iota(jnp.int32, (Q, Q), 0) >= lax.broadcasted_iota(jnp.int32, (Q, Q), 1)
    square = []
    for b in range(blocks):
        at = slice(b * Q, (b + 1) * Q)
        scores = scores_ref[b]
        xb = x[at]
        carried = widen(jnp.exp(cums[b])) * mm3(split(bc_ref[0, at, NS:]), split(states[b]))
        parts = []
        for h in range(0, HG, 2):
            pair = xb[:, h * P_SIZE : (h + 2) * P_SIZE]
            x_hi, x_lo = split(pair)
            both = jnp.concatenate([x_hi, x_lo], axis=1)
            halves = []
            for k in (h, h + 1):
                spread = cums[b][:, k : k + 1] - lanes_ref[0, 0, k : k + 1, at]
                decay = jnp.exp(jnp.where(causal, spread, -10000.0))
                m_hi, m_lo = split(scores * decay * lanes_ref[0, 0, HG + k : HG + k + 1, at])
                first = mm(m_hi, both)
                halves.append(first[:, : 2 * P_SIZE] + first[:, 2 * P_SIZE :] + mm(m_lo, x_hi))
            parts.append(jnp.where(lane < P_SIZE, halves[0], halves[1]))
        mixed = jnp.concatenate(parts, axis=1) + skip_ref[0:1] * xb + carried
        mixed_ref[0, at] = mixed
        z = z_ref[0, at]
        gated = mixed * (z * jax.nn.sigmoid(z))
        square.append(lane_sum(gated * gated))
    add_up(square_ref, jnp.concatenate(square, axis=0), group)

    end(grid, line, mover)


def chunk_decay(cum_ref, group):
    rows = cum_ref.shape[1]
    before = jnp.zeros((1, 128), jnp.float32)
    parts = []
    for b in range(rows // Q):
        cum = of_group(cum_ref[0, b * Q : (b + 1) * Q], group)
        parts.append(jnp.exp(cum + before))
        before = before + cum[Q - 1 : Q]
    return widen(jnp.concatenate(parts, axis=0))


def gs_kernel(
    grid, own_ref, w_ref, up_ref, down_ref, mixed_ref, z_ref, gain_ref, gs_ref, dot_ref, rg_ref, both_ref, gb_ref, sems
):
    step = pl.program_id(1)
    pair = PairFill(own_ref, both_ref, gb_ref, sems)
    begin(grid, pair)
    slots, tokens = gb_ref.shape[:2]

    @pl.when(step == 0)
    def _():
        for m in range(slots):
            rg_ref[m] = twice_split(mm_t(gb_ref[m], up_ref[m]))

    gb = merge(gb_ref)
    width = w_ref.shape[3]
    total = mm_t(gb[:, :width], w_ref[0, 0])
    for n in range(1, w_ref.shape[0]):
        total = total + mm_t(gb[:, n * width : (n + 1) * width], w_ref[n, 0])
    for m in range(slots):
        gs = total[m * tokens : (m + 1) * tokens] + mm(rg_ref[m], down_ref[m])
        gs_ref[m] = gs
        z = z_ref[m]
        dots = lane_sum(gs * gain_ref[...] * (mixed_ref[m] * (z * jax.nn.sigmoid(z))))

        @pl.when(step == 0)
        def _():
            dot_ref[m] = dots

        @pl.when(step > 0)
        def _():
            dot_ref[m] += dots

    end(grid, pair)


def turned(v):
    return v.astype(jnp.float32).T.astype(jnp.bfloat16)


def branch_kernel(
    grid, scaled_ref, w_ref, down_ref, up_ref, rg_ref, gb_ref, branch_ref, g_up_ref, g_down_ref, ro_ref, rot_ref, rgt_ref, mover=None
):
    step = pl.program_id(1)
    begin(grid, mover)
    slots, tokens = scaled_ref.shape[:2]

    @pl.when(step == 0)
    def _():
        for m in range(slots):
            ro = twice_split(mm_t(scaled_ref[m], down_ref[m]))
            ro_ref[m] = ro
            rot_ref[m] = turned(ro)
            rgt_ref[m] = turned(rg_ref[m])

    scaled = merge(scaled_ref)
    width = w_ref.shape[2]
    total = mm(scaled[:, :width], w_ref[0, 0])
    for n in range(1, w_ref.shape[1]):
        total = total + mm(scaled[:, n * width : (n + 1) * width], w_ref[0, n])
    cols = g_down_ref.shape[2]
    for m in range(slots):
        branch_ref[m] = total[m * tokens : (m + 1) * tokens] + mm(ro_ref[m], up_ref[m])
        g_up_ref[m] = fold(mm(rot_ref[m], gb_ref[m]))
        g_down_ref[m] = fold(mm(rgt_ref[m], scaled_ref[m, :, pl.ds(pl.multiple_of(step * cols, 128), cols)]))
    end(grid, mover)


def unproject_kernel(
    grid, gz_ref, gx_ref, tail_ref, w_ref, tailw_ref, up_ref, down_ref, lr_ref, low_ref, g_ref, upz_ref, upx_ref, g_down_ref,
    ri_ref, rit_ref, lrt_ref, mover=None
):
    step = pl.program_id(1)
    begin(grid, mover)
    slots, tokens, chan = gz_ref.shape

    @pl.when(step == 0)
    def _():
        for m in range(slots):
            ri = twice_split(mm_t(gz_ref[m], up_ref[m, :, :chan]) + mm_t(gx_ref[m], up_ref[m, :, chan:]))
            ri_ref[m] = ri
            rit_ref[m] = turned(ri)
            lrt_ref[m] = turned(lr_ref[m])

    total = mm_t(merge(gz_ref), w_ref[0]) + mm_t(merge(gx_ref), w_ref[1]) + mm_t(merge(tail_ref), tailw_ref[...])
    cols = upz_ref.shape[2]
    at = pl.ds(pl.multiple_of(step * cols, 128), cols)
    for m in range(slots):
        g_ref[m] = total[m * tokens : (m + 1) * tokens] + mm(ri_ref[m], down_ref[m])
        upz_ref[m] = fold(mm(lrt_ref[m], gz_ref[m, :, at]))
        upx_ref[m] = fold(mm(lrt_ref[m], gx_ref[m, :, at]))
        g_down_ref[m] = fold(mm(rit_ref[m], low_ref[m]))
    end(grid, mover)


def gate_back_kernel(
    grid, gs_ref, mixed_ref, z_ref, inv_ref, coef_ref, gain_ref, bc_ref, cum_ref, dy_ref, gz_ref, scaled_ref, lam_ref, q_ref, ct_ref,
    mover=None
):
    group = pl.program_id(1)
    begin(grid, mover)

    @pl.when(group == 0)
    def _():
        hi, lo = split(bc_ref[0, :, NS:].T)
        ct_ref[0] = hi
        ct_ref[1] = lo

    z = z_ref[0]
    mixed = mixed_ref[0]
    sig = jax.nn.sigmoid(z)
    act = z * sig
    gated = mixed * act
    inv = inv_ref[0]
    gain = gain_ref[...]
    scaled_ref[0] = (gated * inv * gain).astype(jnp.bfloat16)
    g_gated = gs_ref[0] * gain * inv - gated * coef_ref[0]
    dy = g_gated * act
    dy_ref[0] = dy
    gz_ref[0] = (g_gated * mixed * (sig * (1.0 + z * (1.0 - sig)))).astype(jnp.bfloat16)
    lam_ref[0] = mm3((ct_ref[0], ct_ref[1]), split(dy * chunk_decay(cum_ref, group)))
    add_up(q_ref, head_sums(dy * mixed, group), group)

    end(grid, mover)


def scan_back_kernel(
    grid, dy_ref, xin_ref, halo_ref, taps_ref, bc_ref, cum_ref, step_ref, lanes_ref, skip_ref, state_ref, lam_ref, end_ref,
    gx_ref, head_ref, tail_ref, gbc_ref, xu_ref, dx_ref, scorest_ref, dscorest_ref, bt_ref, ct_ref, held_ref, sent_ref, send_sem,
    recv_sem, mover=None
):
    group = pl.program_id(1)
    rows = xin_ref.shape[1]
    blocks = rows // Q
    line = Line(held_ref, sent_ref, send_sem, recv_sem, lax.axis_size("mp"), -1)
    begin(grid, line, mover)

    @pl.when(step_of(grid) == 0)
    def _():
        sent_ref[...] = jnp.zeros(sent_ref.shape, jnp.float32)

    @pl.when(group == 0)
    def _():
        for b in range(blocks):
            part = bc_ref[0, b * Q : (b + 1) * Q]
            scorest_ref[b] = mm3_t(split(part[:, :NS]), split(part[:, NS:]))
            dscorest_ref[b] = jnp.zeros((Q, Q), jnp.float32)
            hi, lo = split(part[:, :NS].T)
            bt_ref[0, b] = hi
            bt_ref[1, b] = lo
            hi, lo = split(part[:, NS:].T)
            ct_ref[0, b] = hi
            ct_ref[1, b] = lo
        gbc_ref[0] = jnp.zeros((rows, 2 * NS), jnp.float32)
        xu_ref[0] = jnp.zeros((rows, 128), jnp.float32)
        dx_ref[0] = jnp.zeros((rows, 128), jnp.float32)

    pre = conv_rows(xin_ref[0], halo_ref[0], taps_ref[...])
    sig = jax.nn.sigmoid(pre)
    x = pre * sig
    lane = lax.broadcasted_iota(jnp.int32, (Q, 2 * P_SIZE), 1)
    causal = lax.broadcasted_iota(jnp.int32, (Q, Q), 0) <= lax.broadcasted_iota(jnp.int32, (Q, Q), 1)
    cums, step_cols, decs, rests, wide_steps = [], [], [], [], []
    for b in range(blocks):
        at = slice(b * Q, (b + 1) * Q)
        cum = of_group(cum_ref[0, at], group)
        step = of_group(step_ref[0, at], group)
        total = cum[Q - 1 : Q]
        cums.append(cum)
        step_cols.append(step)
        decs.append(widen(jnp.exp(total)))
        rests.append(widen(jnp.exp(total - cum)))
        wide_steps.append(widen(step))
    states = [state_ref[0]]
    for b in range(blocks - 1):
        wx = x[b * Q : (b + 1) * Q] * rests[b] * wide_steps[b]
        states.append(decs[b] * states[b] + mm3((bt_ref[0, b], bt_ref[1, b]), split(wx)))
    slot = SLOTS - 1 - pl.program_id(0)
    lam = line.receive(slot, group)
    whole = decs[0]
    for dec in decs[1:]:
        whole = whole * dec
    line.send(slot, group, whole * lam + lam_ref[0])
    ends = jnp.sum(lam * end_ref[0], axis=0, keepdims=True)
    g_parts = [None] * blocks
    for b in reversed(range(blocks)):
        at = slice(b * Q, (b + 1) * Q)
        xb = x[at]
        dy = dy_ref[0, at]
        scores = scorest_ref[b]
        dscores = dscorest_ref[b]
        u_parts = []
        for h in range(0, HG, 2):
            pair = slice(h * P_SIZE, (h + 2) * P_SIZE)
            x_hi, x_lo = split(xb[:, pair])
            d_hi, d_lo = split(dy[:, pair])
            both = jnp.concatenate([d_hi, d_lo], axis=1)
            halves = []
            for k in (h, h + 1):
                mine = (lane < P_SIZE) if k == h else (lane >= P_SIZE)
                spread = lanes_ref[0, 0, k : k + 1, at] - cums[b][:, k : k + 1]
                decay = jnp.exp(jnp.where(causal, spread, -10000.0))
                zero = jnp.zeros_like(x_hi)
                xm_hi = jnp.where(mine, x_hi, zero)
                xm_lo = jnp.where(mine, x_lo, zero)
                dm = mm_t(xm_hi, d_hi) + mm_t(xm_hi, d_lo) + mm_t(xm_lo, d_hi)
                dscores = dscores + dm * decay * step_cols[b][:, k : k + 1]
                m_hi, m_lo = split(scores * decay)
                first = mm(m_hi, both)
                halves.append(first[:, : 2 * P_SIZE] + first[:, 2 * P_SIZE :] + mm(m_lo, d_hi))
            u_parts.append(jnp.where(lane < P_SIZE, halves[0], halves[1]))
        dscorest_ref[b] = dscores
        lam_s = split(lam)
        part = bc_ref[0, at]
        step = wide_steps[b]
        u = jnp.concatenate(u_parts, axis=1) + rests[b] * mm3(split(part[:, :NS]), lam_s)
        ev = split(widen(jnp.exp(cums[b])) * dy)
        gbc_ref[0, at, :NS] += mm3_t(split(rests[b] * step * xb), lam_s)
        gbc_ref[0, at, NS:] += mm3_t(ev, split(states[b]))
        if b > 0:
            lam = decs[b] * lam + mm3((ct_ref[0, b], ct_ref[1, b]), ev)
        xu_ref[0, at] += head_sums(xb * u, group)
        direct = xb * dy * skip_ref[0:1]
        if b == blocks - 1:
            row = lax.broadcasted_iota(jnp.int32, (Q, HG * P_SIZE), 0)
            direct = jnp.where(row == Q - 1, direct - ends, direct)
        dx_ref[0, at] += head_sums(direct, group)
        g_parts[b] = step * u + skip_ref[0:1] * dy
    g_pre = jnp.concatenate(g_parts, axis=0) * (sig * (1.0 + pre * (1.0 - sig)))
    g_ext = conv_rows_back(g_pre, taps_ref[...])
    gx_ref[0] = g_ext[8:].astype(jnp.bfloat16)
    head_ref[0] = g_ext[:8]
    tail_ref[0] = g_ext[rows:]

    @pl.when(group == pl.num_programs(1) - 1)
    def _():
        for b in range(blocks):
            at = slice(b * Q, (b + 1) * Q)
            part = bc_ref[0, at]
            ds = dscorest_ref[b]
            gbc_ref[0, at, :NS] += mm3(split(ds), split(part[:, NS:]))
            gbc_ref[0, at, NS:] += mm3(split(ds.T), split(part[:, :NS]))

    end(grid, line, mover)


def finish_kernel(
    count, near_ref, far_ref, picks_ref, rows_ref, moved_ref, near_out_ref, far_out_ref, near1_ref, far1_ref, near2_ref,
    near2_in_ref, far2_ref, far2_in_ref, n1s, n1r, f1s, f1r, n2s, n2r, f2s, f2r, send_sem, recv_sem
):
    d, c, z = lax.axis_index("dp"), lax.axis_index("seq"), lax.axis_index("mp")
    mover = Mover(rows_ref, moved_ref, send_sem, recv_sem, count, tuple(range(SLOTS)), False)
    blocks = far2_ref.shape[0]
    barrier = pltpu.get_barrier_semaphore()
    waits = mover.greet(barrier)
    others = [(i, j) for i in range(blocks) for j in range(2) if i or j]
    for i, j in others:
        device = (lax.rem(d + i, blocks), lax.rem(c + j, 2), z)
        pl.semaphore_signal(barrier, 1, device_id=device, device_id_type=MESH)
    pl.semaphore_wait(barrier, waits + len(others))

    def remote(src, dst, send, recv, *device):
        return pltpu.make_async_remote_copy(
            src_ref=src, dst_ref=dst, send_sem=send, recv_sem=recv, device_id=device, device_id_type=MESH
        )

    def arrival(ref, at, sem):
        pltpu.make_async_copy(ref.at[at], ref.at[at], sem.at[at]).wait()

    me = c * count + z
    copies = []
    for i in range(1, count):
        to = lax.rem(z + i, count)
        copies.append(remote(near_ref.at[to], near1_ref.at[z], n1s.at[i], n1r.at[z], d, c, to))
    column = [(j, i) for j in range(2) for i in range(count) if i or j]
    for j, i in column:
        to_c, to = lax.rem(c + j, 2), lax.rem(z + i, count)
        copies.append(remote(far_ref.at[to_c * count + to], far1_ref.at[me], f1s.at[j * count + i], f1r.at[me], d, to_c, to))
    for copy in copies:
        copy.start()
    for n in range(mover.pieces):
        mover.start(n)

    near = near_ref[z].astype(jnp.float32)
    for i in range(1, count):
        at = lax.rem(z + i, count)
        arrival(near1_ref, at, n1r)
        near = near + near1_ref[at].astype(jnp.float32)
    far = far_ref[me].astype(jnp.float32)
    for j, i in column:
        at = lax.rem(c + j, 2) * count + lax.rem(z + i, count)
        arrival(far1_ref, at, f1r)
        far = far + far1_ref[at].astype(jnp.float32)
    for a in range(ADAPT):
        near2_ref[a] = sum(picks_ref[m, a] * near[m] for m in range(SLOTS))
        for b in range(blocks):
            far2_ref[b, a] = sum(picks_ref[m, a] * far[m, :, b] for m in range(SLOTS))

    here = d * 2 + c
    copies2 = []
    for i, j in others:
        to_d, to_c = lax.rem(d + i, blocks), lax.rem(c + j, 2)
        copies2.append(
            remote(near2_ref.at[to_d * 2 + to_c], near2_in_ref.at[here], n2s.at[i * 2 + j], n2r.at[here], to_d, to_c, z)
        )
    for i in range(1, blocks):
        to = lax.rem(d + i, blocks)
        copies2.append(remote(far2_ref.at[to], far2_in_ref.at[d], f2s.at[i], f2r.at[d], to, c, z))
    for copy in copies2:
        copy.start()
    near2_in_ref[here] = near2_ref[here]
    far_sum = far2_ref[d]
    for i in range(1, blocks):
        at = lax.rem(d + i, blocks)
        arrival(far2_in_ref, at, f2r)
        far_sum = far_sum + far2_in_ref[at]
    far_out_ref[...] = far_sum
    for i, j in others:
        arrival(near2_in_ref, lax.rem(d + i, blocks) * 2 + lax.rem(c + j, 2), n2r)
    for half in range(2):
        near_out_ref[half] = sum(near2_in_ref[b * 2 + half] for b in range(blocks))
    for copy in copies + copies2:
        copy.wait_send()
    mover.finish()


def bc_back_kernel(
    g_ref, in_ref, halo_ref, taps_ref, q_ref, dx_ref, xu_ref, step_ref, rate_ref, bias_ref, decay_ref, mask_ref,
    out_ref, head_ref, tail_ref, g_rate_ref
):
    rows = in_ref.shape[1]
    pre = conv_rows(in_ref[0], halo_ref[0], taps_ref[...])
    sig = jax.nn.sigmoid(pre)
    g_ext = conv_rows_back(g_ref[0] * (sig * (1.0 + pre * (1.0 - sig))), taps_ref[...])
    out_ref[0] = g_ext[8:].astype(jnp.bfloat16)
    head_ref[0] = g_ext[:8]
    tail_ref[0] = g_ext[rows:]
    xu = xu_ref[0]
    flow = q_ref[0] - dx_ref[0] - step_ref[0] * xu
    later = lax.broadcasted_iota(jnp.int32, (rows, rows), 0) <= lax.broadcasted_iota(jnp.int32, (rows, rows), 1)
    g_log = ones_mm(later.astype(jnp.float32).astype(jnp.bfloat16), flow)
    sig = jax.nn.sigmoid(rate_ref[0] + bias_ref[...])
    g_rate_ref[0] = ((xu + g_log * decay_ref[...]) * mask_ref[0] * sig).astype(jnp.bfloat16)


def flip(v, mask, count):
    total = 0
    bit = 1
    while bit < count:
        b = lax.rem(v // bit, 2)
        total = total + (1 - b if mask & bit else b) * bit
        bit *= 2
    return total


def gather_kernel(
    nd, nz, wt_ref, x_ref, w_ref, rows_ref, local_sem, pair_sem, up_sem, down_sem, zrecv_sem, xsend_sem, xrecv_sem, ysend_sem,
    yrecv_sem, hsend_sem, hrecv_sem, asend_sem, arecv_sem
):
    d, c, z = lax.axis_index("dp"), lax.axis_index("seq"), lax.axis_index("mp")
    xn, yn = flip(d, 1, nd), flip(d, 2, nd)
    rows, part = wt_ref.shape[1], wt_ref.shape[2] // 2

    def remote(src, dst, send, recv, device):
        return pltpu.make_async_remote_copy(
            src_ref=src, dst_ref=dst, send_sem=send, recv_sem=recv, device_id=device, device_id_type=MESH
        )

    barrier = pltpu.get_barrier_semaphore()
    for cc in range(2):
        for r in range(nz):
            if cc or r:
                pl.semaphore_signal(barrier, 1, device_id=(d, flip(c, cc, 2), flip(z, r, nz)), device_id_type=MESH)
    for dd in (xn, yn):
        pl.semaphore_signal(barrier, 1, device_id=(dd, c, z), device_id_type=MESH)
    pl.semaphore_wait(barrier, 2 * nz - 1 + 2)

    def cols(s):
        return pl.ds(pl.multiple_of(s * part, 128), part)

    def area(dd, s):
        return w_ref.at[:, pl.ds(pl.multiple_of(dd * (2 * rows), 16), 2 * rows), cols(s)]

    def half_area(dd, s, h):
        return w_ref.at[:, pl.ds(pl.multiple_of(dd * (2 * rows) + h * rows, 16), rows), cols(s)]

    mine_area = w_ref.at[:, pl.ds(pl.multiple_of((2 * d + c) * rows, 16), rows), cols(z)]
    keep = pltpu.make_async_copy(wt_ref.at[:, :, cols(c)], mine_area, local_sem.at[0])
    pair = remote(wt_ref.at[:, :, cols(1 - c)], mine_area, pair_sem.at[0], pair_sem.at[1], (d, 1 - c, z))
    keep.start()
    pair.start()

    mover = Mover(x_ref, rows_ref, asend_sem, arecv_sem, nz, tuple(range(SLOTS)), True)
    for n in range(mover.pieces):
        mover.start(n)

    keep.wait()
    pair.wait()

    def spread(s):
        remote(area(d, s), area(d, s), xsend_sem.at[s], xrecv_sem.at[s], (xn, c, z)).start()
        remote(area(d, s), area(d, s), ysend_sem.at[s], yrecv_sem.at[s], (yn, c, z)).start()

    def send_up(s):
        @pl.when(z < nz - 1)
        def _():
            remote(area(d, s), area(d, s), up_sem.at[s], zrecv_sem.at[s], (d, c, z + 1)).start()

    def send_down(s):
        @pl.when(z > 0)
        def _():
            remote(area(d, s), area(d, s), down_sem.at[s], zrecv_sem.at[s], (d, c, z - 1)).start()

    def relay(s):
        remote(area(xn, s), area(xn, s), xsend_sem.at[s], xrecv_sem.at[s], (xn, c, z)).wait_recv()
        remote(half_area(xn, s, 0), half_area(xn, s, 0), hsend_sem.at[0, s], hrecv_sem.at[0, s], (yn, c, z)).start()
        remote(area(yn, s), area(yn, s), ysend_sem.at[s], yrecv_sem.at[s], (yn, c, z)).wait_recv()
        remote(half_area(yn, s, 1), half_area(yn, s, 1), hsend_sem.at[1, s], hrecv_sem.at[1, s], (xn, c, z)).start()

    send_up(z)
    send_down(z)
    spread(z)
    for r in range(1, nz + 1):
        if r < nz:
            @pl.when(z - r >= 0)
            def _():
                s = z - r
                remote(area(d, s), area(d, s), up_sem.at[s], zrecv_sem.at[s], (d, c, z)).wait_recv()
                send_up(s)
                spread(s)

            @pl.when(z + r < nz)
            def _():
                s = z + r
                remote(area(d, s), area(d, s), up_sem.at[s], zrecv_sem.at[s], (d, c, z)).wait_recv()
                send_down(s)
                spread(s)

        if r == 1:
            relay(z)
        else:
            @pl.when(z - r + 1 >= 0)
            def _():
                relay(z - r + 1)

            @pl.when(z + r - 1 < nz)
            def _():
                relay(z + r - 1)

    mover.finish()
    for s in range(nz):
        remote(half_area(d, s, 0), half_area(d, s, 0), hsend_sem.at[0, s], hrecv_sem.at[0, s], (yn, c, z)).wait()
        remote(half_area(d, s, 1), half_area(d, s, 1), hsend_sem.at[1, s], hrecv_sem.at[1, s], (xn, c, z)).wait()
        remote(area(d, s), area(d, s), xsend_sem.at[s], xrecv_sem.at[s], (xn, c, z)).wait_send()
        remote(area(d, s), area(d, s), ysend_sem.at[s], yrecv_sem.at[s], (yn, c, z)).wait_send()

        @pl.when(jnp.logical_and(s <= z, z < nz - 1))
        def _():
            remote(area(d, s), area(d, s), up_sem.at[s], zrecv_sem.at[s], (d, c, z)).wait_send()

        @pl.when(jnp.logical_and(s >= z, z > 0))
        def _():
            remote(area(d, s), area(d, s), down_sem.at[s], zrecv_sem.at[s], (d, c, z)).wait_send()


def gather(wt, x, nd, nz):
    half = wt.shape[2] // 2
    dma = pltpu.SemaphoreType.DMA
    anywhere = pl.BlockSpec(memory_space=pl.ANY)
    return pl.pallas_call(
        functools.partial(gather_kernel, nd, nz),
        name="gather",
        out_shape=(
            jax.ShapeDtypeStruct((2, wt.shape[1] * 2 * nd, half * nz), wt.dtype),
            jax.ShapeDtypeStruct((SLOTS, x.shape[1] // 4, x.shape[2] * nz), x.dtype),
        ),
        in_specs=[anywhere] * 2,
        out_specs=(anywhere,) * 2,
        scratch_shapes=[
            dma((1,)), dma((2,)), dma((nz,)), dma((nz,)), dma((nz,)), dma((nz,)), dma((nz,)), dma((nz,)), dma((nz,)),
            dma((2, nz)), dma((2, nz)), dma((4 * SLOTS,)), dma((SLOTS, nz)),
        ],
        compiler_params=pltpu.CompilerParams(collective_id=1, has_side_effects=True),
    )(wt, x)


def block(shape, index):
    return pl.BlockSpec(shape, index)


def call(kernel, name, grid, ins, outs, scratch, flops, size, comm=None, load=None):
    params = dict(vmem_limit_bytes=VMEM_LIMIT)
    kernel = functools.partial(kernel, grid)
    ins, outs, scratch = list(ins), list(outs), list(scratch)
    if load is not None:
        rows, result, first, to_rows = load
        count = lax.axis_size("mp")
        kernel = functools.partial(carried_by, kernel, count, first, to_rows, len(ins), len(outs))
        ins.append((rows, pl.BlockSpec(memory_space=pl.ANY)))
        outs.append((result, pl.BlockSpec(memory_space=pl.ANY)))
        sends = 4 * SLOTS if to_rows else count * len(first)
        scratch += [pltpu.SemaphoreType.DMA((sends,)), pltpu.SemaphoreType.DMA((SLOTS, 4))]
    if comm is not None:
        params.update(collective_id=comm, has_side_effects=True)
    return pl.pallas_call(
        kernel,
        name=name,
        grid=grid,
        in_specs=[s for _, s in ins],
        out_specs=[s for _, s in outs],
        out_shape=[s for s, _ in outs],
        scratch_shapes=scratch,
        compiler_params=pltpu.CompilerParams(**params),
        cost_estimate=pl.CostEstimate(flops=flops, bytes_accessed=size, transcendentals=0),
    )(*[a for a, _ in ins])


def skip_grid(kernel):
    return lambda grid, *refs: kernel(*refs)


def after(value, *deps):
    return lax.optimization_barrier((value,) + deps)[0]


def finish(near, far, picks, rows, moved, count):
    dma, f32 = pltpu.SemaphoreType.DMA, jnp.float32
    anywhere, vmem = pl.BlockSpec(memory_space=pl.ANY), pl.BlockSpec(memory_space=pltpu.VMEM)
    blocks = far.shape[3]
    near_shape, far_shape = near.shape[2:], far.shape[2:3] + far.shape[4:]
    return pl.pallas_call(
        functools.partial(finish_kernel, count),
        name="finish",
        in_specs=[vmem, vmem, pl.BlockSpec(memory_space=pltpu.SMEM), anywhere],
        out_specs=[anywhere, vmem, vmem],
        out_shape=[moved, jax.ShapeDtypeStruct((2,) + near_shape, f32), jax.ShapeDtypeStruct((ADAPT,) + far_shape, f32)],
        scratch_shapes=[
            pltpu.VMEM(near.shape, near.dtype), pltpu.VMEM(far.shape, far.dtype), pltpu.VMEM((ADAPT,) + near_shape, f32),
            pltpu.VMEM((2 * blocks,) + near_shape, f32), pltpu.VMEM((blocks, ADAPT) + far_shape, f32),
            pltpu.VMEM((blocks, ADAPT) + far_shape, f32), dma((count,)), dma((count,)), dma((2 * count,)), dma((2 * count,)),
            dma((2 * blocks,)), dma((2 * blocks,)), dma((blocks,)), dma((blocks,)), dma((count * SLOTS,)), dma((SLOTS, 4)),
        ],
        compiler_params=pltpu.CompilerParams(vmem_limit_bytes=VMEM_LIMIT, collective_id=5, has_side_effects=True),
    )(near, far, picks, rows)


def fast_body(
    x_in, cotangent, lengths, adapter_ids, norm_gain, w_zx, w_bc, w_dt, dt_bias, a_log, d_skip, conv_x, conv_bc,
    gate_gain, w_out, in_down, in_up, out_down, out_up
):
    bf16, f32 = jnp.bfloat16, jnp.float32
    micros, _, seg, feats = x_in.shape
    nz, nd = lax.axis_size("mp"), lax.axis_size("dp")
    core, z = lax.axis_index("seq"), lax.axis_index("mp")
    own = seg // nz
    tokens = 2 * own
    heads = dt_bias.shape[0] * nz // 2
    chan = heads * P_SIZE
    part = chan // nz
    groups = heads // HG
    wide = HG * P_SIZE
    blocks = tokens // Q
    each = D // (nd * 2 * nz)

    def other(v):
        return lax.ppermute(v, "seq", [(0, 1), (1, 0)])

    def pair_cat(mine, theirs, axis):
        return jnp.where(
            core == 0, jnp.concatenate([mine, theirs], axis), jnp.concatenate([theirs, mine], axis)
        )

    def halves(v, axis):
        v = v.reshape(v.shape[:axis] + (2, v.shape[axis] // 2) + v.shape[axis + 1 :])
        return (
            lax.dynamic_index_in_dim(v, core, axis, False),
            lax.dynamic_index_in_dim(v, 1 - core, axis, False),
        )

    line = 2 * part
    bc_piece = lax.dynamic_slice_in_dim(w_bc, z * (w_bc.shape[0] // nz), w_bc.shape[0] // nz, 0)
    pairs = jnp.stack([jnp.transpose(in_down, (0, 2, 1)), out_up.reshape(ADAPT, R, -1)], 1)
    same = [bc_piece, pairs]
    sized = [halves(in_up, 2), halves(out_down.T, 1), halves(w_dt.T, 0)]
    packs = []
    for k in range(2):
        packs.append(jnp.concatenate([v.reshape(-1, line) for v in [s[k] for s in sized] + same], 0))
    bounds = [0]
    for v in [s[0] for s in sized] + same:
        bounds.append(bounds[-1] + v.size // line)
    pack = pair_cat(packs[0][None], other(packs[1])[None], 0)
    params = jnp.concatenate([dt_bias, a_log, d_skip, gate_gain, conv_x.reshape(-1)])
    params = lax.all_gather(params, "mp")
    pack = lax.all_gather(pack, ("dp", "mp")).reshape((nd, nz) + pack.shape)
    zx_weight, x_rows = gather(jnp.transpose(w_zx, (1, 0, 2)), x_in[:, 0], nd, nz)
    out_mine, out_theirs = halves(after(w_out, x_rows), 0)
    out_pair = pair_cat(out_mine, other(out_theirs), 1)
    out_all = lax.all_gather(out_pair, ("dp", "mp")).reshape((nd, nz) + out_pair.shape)
    dt_rows = pack[:, :, :, bounds[2] : bounds[3]].reshape(nd, nz, 2, heads // nz, -1)
    dt_weight = jnp.transpose(dt_rows, (1, 3, 0, 2, 4)).reshape(heads, D)
    dt_weight = jnp.pad(dt_weight, ((0, 128 - heads), (0, 0)))
    bc_rows = pack[:, :, :, bounds[3] : bounds[4]].reshape(nd, nz, 2, -1, 2 * NS)
    bc_weight = jnp.transpose(bc_rows, (0, 2, 1, 3, 4)).reshape(D, 2 * NS)
    bc_half = lax.dynamic_slice_in_dim(bc_weight, core * NS, NS, 1)
    dt_weight = dt_weight.T
    tail_weight = jnp.concatenate([bc_half, dt_weight], 1)
    first_weight = jnp.concatenate([bc_weight, dt_weight], 1)

    hl = dt_bias.shape[0]

    def own_part(v):
        v = v.reshape(v.shape[0], 2, v.shape[1] // 2)
        return lax.dynamic_index_in_dim(v, core, 1, False).reshape(-1)

    bias = jnp.pad(own_part(params[:, :hl]), (0, 128 - heads))[None]
    rate = jnp.pad(-jnp.exp(own_part(params[:, hl : 2 * hl])), (0, 128 - heads))[None]
    skip = jnp.repeat(own_part(params[:, 2 * hl : 3 * hl]), P_SIZE)[None]
    width = gate_gain.shape[0]
    gain = own_part(params[:, 3 * hl : 3 * hl + width])[None]
    taps = params[:, 3 * hl + width :].reshape(nz, KC, 2, part)
    taps = jnp.transpose(lax.dynamic_index_in_dim(taps, core, 2, False), (1, 0, 2)).reshape(KC, chan)

    order = jnp.arange(micros)
    runs = run_of(order, z)
    sequence, chunk = runs // nz, lax.rem(runs, nz)
    lengths = jnp.take(lengths[:, 0], sequence)[:, None]
    ids = jnp.take(adapter_ids[:, 0], sequence)
    all_pos = (chunk * tokens)[:, None] + jnp.arange(tokens)
    own_pos = (chunk * tokens)[:, None] + core * own + jnp.arange(own)
    enters = (order == nz - 1 - z)[:, None, None]
    leaves = (order == nz - 2 - z)[:, None, None]
    forward_edge = [(i, i + 1) for i in range(nz - 1)]
    backward_edge = [(i + 1, i) for i in range(nz - 1)]

    m3 = lambda m, g: (m, 0, g)
    m0 = lambda m, g: (m, 0, 0)
    z2 = lambda m, g: (0, 0)
    shape = jax.ShapeDtypeStruct

    def per_token(width, index=m3):
        return block((1, tokens, width), index)

    chan_block = per_token(wide)
    halo_block = block((1, HALO, wide), m3)
    taps_block = block((KC, wide), lambda m, g: (0, g))
    line_block = block((1, wide), lambda m, g: (0, g))
    state_block = block((1, NS, wide), m3)
    bc_block = per_token(2 * NS, m0)
    bc_halo = block((1, HALO, 2 * NS), m0)
    bc_taps = block((KC, 2 * NS), z2)
    bc_edge = block((1, 8, 2 * NS), m0)
    one_col = per_token(1, m0)
    sums = per_token(128, m0)
    lanes_block = block((1, 1, 2 * HG, tokens), lambda m, g: (m, g, 0, 0))
    head_line = block((1, 128), z2)
    edge_block = block((1, 8, wide), m3)
    tok_f32 = shape((micros, tokens, chan), f32)
    tok_b16 = shape((micros, tokens, chan), bf16)
    state_f32 = shape((micros, NS, chan), f32)
    bc_f32 = shape((micros, tokens, 2 * NS), f32)
    sums_f32 = shape((micros, tokens, 128), f32)
    edge_f32 = shape((micros, 8, chan), f32)
    act_bytes = tokens * chan * 4
    dma = pltpu.SemaphoreType.DMA
    line_scratch = [pltpu.VMEM((groups, NS, wide), f32), pltpu.VMEM((2 * groups, NS, wide), f32)] + [dma((groups,))] * 2
    scan_grid = (micros, groups)

    x_rows = x_rows.astype(f32)
    inv_rms = lax.rsqrt(jnp.mean(x_rows * x_rows, axis=-1, keepdims=True) + eps)
    low_own = (x_rows * inv_rms * norm_gain).astype(bf16)
    mask_own = (own_pos < lengths).astype(f32)[..., None]
    mask = (all_pos < lengths).astype(f32)[..., None]
    picks = (adapter_ids == jnp.arange(ADAPT)).astype(f32)
    near, wide_rows = [], []
    for m in range(micros):
        got = lax.dynamic_index_in_dim(pack, ids[m] // 2, 0, False)[:, :, : bounds[2]]
        near.append(lax.dynamic_index_in_dim(got, ids[m] % 2, 1, False))
        wide_rows.append(lax.dynamic_slice_in_dim(pack, bounds[4] + 2 * ids[m], 2, 3))
    near = jnp.stack(near)
    u_in = near[:, :, : bounds[1]].reshape(micros, nz, R, 2, part)
    u_in = jnp.transpose(u_in, (0, 2, 3, 1, 4)).reshape(micros, R, 2 * chan)
    a_out = near[:, :, bounds[1] :].reshape(micros, nz, R, part)
    a_out = jnp.transpose(a_out, (0, 2, 1, 3)).reshape(micros, R, chan)
    wide_rows = jnp.stack(wide_rows).reshape(micros, nd, nz, 2, 2, R, each)
    wide_rows = jnp.transpose(wide_rows, (4, 0, 5, 1, 3, 2, 6)).reshape(2, micros, R, D)
    u_in, a_out = [jnp.concatenate([v, v], 1) for v in (u_in, a_out)]
    a_in, u_out = jnp.concatenate([wide_rows, wide_rows], 2)

    def every(width, index=None):
        if index is None:
            return pl.BlockSpec((micros, tokens, width), lambda m, g: (0, 0, 0), pipeline_mode=pl.Buffered(1))
        return block((micros, tokens, width), index)

    by_step = lambda m, g: (0, 0, g)
    rank_b16 = shape((micros, tokens, 2 * R), bf16)
    all_down = block((micros, 2 * R, D), lambda m, g: (0, 0, 0))
    half_steps = chan // part
    steps = 2 * half_steps
    cot = cotangent[:, 0]
    early = 1
    hbm = pl.BlockSpec(memory_space=pl.ANY)
    pair_scratch = [pltpu.VMEM((micros, tokens, D), bf16), dma((4,))]
    xin, z_in, bcin, rate_in, lr, low, cot_early = call(
        project_kernel, "project", (1, steps),
        [(low_own, hbm), (zx_weight, block((1, D, part), lambda m, g: (1 - g // half_steps, 0, g % half_steps))),
         (first_weight, block((D, 2 * NS + 128), z2)), (a_in, all_down),
         (u_in, block((micros, 2 * R, part), lambda m, g: (0, 0, (g + half_steps) % steps)))],
        [(tok_b16, every(part, lambda m, g: (0, 0, jnp.minimum(g, half_steps - 1)))),
         (tok_f32, every(part, lambda m, g: (0, 0, jnp.maximum(g - half_steps, 0)))),
         (shape((micros, tokens, 2 * NS), bf16), every(2 * NS)), (sums_f32, every(128)), (rank_b16, every(2 * R)), (shape((micros, tokens, D), bf16), hbm)],
        pair_scratch, 4 * tokens * D * chan, act_bytes * 4, 2, (cot, shape((early, own, D), bf16), tuple(range(early)), True),
    )
    tail = jnp.concatenate([xin[:, tokens - HALO :], bcin[:, tokens - HALO :]], axis=2)
    goes = jnp.sum(jnp.where(leaves, tail, 0), axis=0, dtype=bf16)
    halo = jnp.where(enters, lax.ppermute(goes, "mp", forward_edge)[None], jnp.pad(tail[:-1], ((1, 0), (0, 0), (0, 0))))
    halo, bchalo = halo[..., :chan], halo[..., chan:]
    step, cum, lanes, bc = call(
        skip_grid(prep_kernel), "prep", (micros, 1),
        [(rate_in, sums), (bias, head_line), (rate, head_line), (mask, one_col), (bcin, bc_block), (bchalo, bc_halo),
         (conv_bc, bc_taps)],
        [(sums_f32, sums), (sums_f32, sums),
         (shape((micros, groups, 2 * HG, tokens), f32), block((1, groups, 2 * HG, tokens), lambda m, g: (m, 0, 0, 0))),
         (bc_f32, bc_block)],
        [], tokens * Q * 128 * 6, tokens * 128 * 24,
    )
    mixed, square, state, end_state, cot_late = call(
        forward_kernel, "ssd_forward", scan_grid,
        [(xin, chan_block), (halo, halo_block), (taps, taps_block), (bc, bc_block), (cum, sums), (step, sums),
         (lanes, lanes_block), (skip, line_block), (z_in, chan_block)],
        [(tok_f32, chan_block), (sums_f32, sums), (state_f32, state_block), (state_f32, state_block)],
        [pltpu.VMEM((blocks, Q, Q), f32), pltpu.VMEM((2, blocks, NS, Q), bf16), *line_scratch],
        6 * tokens * Q * chan * 2, act_bytes * 3, 3, (cot, shape((micros - early, own, D), bf16), tuple(range(early, micros)), True),
    )

    def reduce_rows(v):
        theirs = lax.dynamic_slice_in_dim(v, (1 - core) * own, own, 1)
        return lax.dynamic_slice_in_dim(v, core * own, own, 1) + other(theirs)

    cols = out_all.shape[3]
    gb_own = jnp.concatenate([cot_early, cot_late], 0) * mask_own.astype(bf16)
    part_block = every(part, by_step)
    gs, dots, rg, gb = call(
        gs_kernel, "gs", (1, nz),
        [(gb_own, hbm), (out_all, block((nd, 1, part, cols), lambda m, g: (0, g, 0, 0))), (u_out, all_down),
         (a_out, block((micros, 2 * R, part), by_step)), (mixed, part_block), (z_in, part_block),
         (gain, block((1, part), lambda m, g: (0, g)))],
        [(tok_f32, part_block), (sums_f32, every(128)), (rank_b16, every(2 * R)), (shape((micros, tokens, D), bf16), hbm)],
        pair_scratch, 6 * tokens * D * chan, act_bytes * 15, 7,
    )
    both = jnp.stack([jnp.sum(square, axis=-1), jnp.sum(dots, axis=-1)])
    both = (both + other(both)) / DI
    inv_gate = lax.rsqrt(both[0] + eps)[..., None]
    coef = inv_gate**3 * both[1][..., None]
    dy, gz, scaled, lloc, q = call(
        gate_back_kernel, "gate_back", scan_grid,
        [(gs, chan_block), (mixed, chan_block), (z_in, chan_block), (inv_gate, one_col), (coef, one_col), (gain, line_block),
         (bc, bc_block), (cum, sums)],
        [(tok_f32, chan_block), (tok_b16, chan_block), (tok_b16, chan_block), (state_f32, state_block), (sums_f32, sums)],
        [pltpu.VMEM((2, NS, tokens), bf16)], 6 * tokens * NS * chan, act_bytes * 5,
    )
    step_cols = every(cols, by_step)
    rank_scratch = [pltpu.VMEM((micros, tokens, 2 * R), bf16)] + [pltpu.VMEM((micros, 2 * R, tokens), bf16)] * 2
    rank_cols = block((micros, R, cols), by_step)
    partial, g_up_out, g_out = call(
        branch_kernel, "branch", (1, nd),
        [(scaled, every(chan)), (out_all, block((1,) + out_all.shape[1:], lambda m, g: (g, 0, 0, 0))),
         (a_out, block((micros, 2 * R, chan), lambda m, g: (0, 0, 0))), (u_out, block((micros, 2 * R, cols), by_step)),
         (rg, every(2 * R)), (gb, step_cols)],
        [(shape((micros, tokens, D), f32), step_cols), (shape((micros, R, D), f32), rank_cols),
         (shape((micros, R, chan), f32), block((micros, R, chan // nd), by_step))],
        rank_scratch, 6 * tokens * D * chan, act_bytes * 12,
    )
    out_rows = (x_rows + mask_own * reduce_rows(partial)).astype(bf16)

    first_slots, last_slots = tuple(range(micros - 1)), (micros - 1,)

    def last_first(spec):
        index = spec.index_map
        return block(spec.block_shape, lambda m, g: index(micros - 1 - m, g))

    ins = [(dy, chan_block), (xin, chan_block), (halo, halo_block), (taps, taps_block), (bc, bc_block), (cum, sums), (step, sums),
           (lanes, lanes_block), (skip, line_block), (state, state_block), (lloc, state_block), (end_state, state_block)]
    outs = [(tok_b16, chan_block), (edge_f32, edge_block), (edge_f32, edge_block), (bc_f32, bc_block), (sums_f32, sums),
            (sums_f32, sums)]
    gx, head, tail, gbc, xu, dx, out_first = call(
        scan_back_kernel, "ssd_back", scan_grid,
        [(a, last_first(s)) for a, s in ins], [(a, last_first(s)) for a, s in outs],
        [pltpu.VMEM((blocks, Q, Q), f32), pltpu.VMEM((blocks, Q, Q), f32), pltpu.VMEM((2, blocks, NS, Q), bf16),
         pltpu.VMEM((2, blocks, NS, Q), bf16), *line_scratch],
        12 * tokens * Q * chan * 2, act_bytes * 3, 4, (out_rows, shape((micros, seg, feats), bf16), first_slots, False),
    )
    gbc = gbc + other(gbc)
    edge_bc = shape((micros, 8, 2 * NS), f32)
    gbc, bhead, btail, g_rate = call(
        skip_grid(bc_back_kernel), "bc_back", (micros, 1),
        [(gbc, bc_block), (bcin, bc_block), (bchalo, bc_halo), (conv_bc, bc_taps), (q, sums), (dx, sums), (xu, sums),
         (step, sums), (rate_in, sums), (bias, head_line), (rate, head_line), (mask, one_col)],
        [(shape((micros, tokens, 2 * NS), bf16), bc_block), (edge_bc, bc_edge), (edge_bc, bc_edge),
         (shape((micros, tokens, 128), bf16), sums)],
        [], tokens * tokens * 128 * 6, tokens * 2 * NS * 8,
    )
    head = jnp.concatenate([head, bhead], 2)
    goes = lax.ppermute(jnp.sum(jnp.where(enters, head, 0), axis=0), "mp", backward_edge)
    back = jnp.pad(jnp.where(enters, 0, head)[1:], ((0, 1), (0, 0), (0, 0))) + jnp.where(leaves, goes[None], 0)
    tail = jnp.concatenate([tail, btail], 2).at[:, 8 - (KC - 1) :].add(back[:, 8 - (KC - 1) :]).astype(bf16)
    gx = lax.dynamic_update_slice_in_dim(gx, tail[..., :chan], tokens - 8, 1)
    gbc = lax.dynamic_update_slice_in_dim(gbc, tail[..., chan:], tokens - 8, 1)
    tail = jnp.concatenate([lax.dynamic_slice_in_dim(gbc, core * NS, NS, 2), g_rate], 2)
    wide_cols = D // nz
    g_low, g_up_z, g_up_x, g_down, out_last = call(
        unproject_kernel, "unproject", (1, nz),
        [(gz, every(chan)), (gx, every(chan)), (tail, every(NS + 128)),
         (zx_weight, block((2, wide_cols, chan), lambda m, g: (0, g, 0))), (tail_weight, block((wide_cols, NS + 128), lambda m, g: (g, 0))),
         (u_in, block((micros, 2 * R, 2 * chan), lambda m, g: (0, 0, 0))), (a_in, block((micros, 2 * R, wide_cols), by_step)),
         (lr, every(2 * R)), (low, every(wide_cols, by_step))],
        [(shape((micros, tokens, D), f32), every(wide_cols, by_step)), (shape((micros, R, chan), f32), block((micros, R, part), by_step)),
         (shape((micros, R, chan), f32), block((micros, R, part), by_step)),
         (shape((micros, R, D), f32), block((micros, R, wide_cols), by_step))],
        rank_scratch, 12 * tokens * D * chan, act_bytes * 9, 6, (out_rows[-1:], shape((micros, seg, feats), bf16), last_slots, False),
    )
    gn = reduce_rows(g_low) * norm_gain
    delta = inv_rms * gn - x_rows * (inv_rms**3 * jnp.mean(gn * x_rows, axis=-1, keepdims=True))
    held_runs = jnp.arange(micros)[:, None] * nz + 2 * core + jnp.arange(2)
    in_last = place_of(held_runs)[1] == micros - 1
    in_last = jnp.repeat(in_last, tokens, axis=1)[..., None]
    out = jnp.where(in_last, out_last, out_first)[:, None]
    mine = (sequence == jnp.arange(micros)[:, None]).astype(f32)

    def by_sequence(v):
        return jnp.sum(mine.reshape(mine.shape + (1,) * (v.ndim - 1)) * v[None], axis=1)

    near = jnp.stack([by_sequence(g).reshape(micros, R, nz, part) for g in (g_out, g_up_z, g_up_x)])
    near = jnp.transpose(near, (3, 1, 0, 2, 4)).astype(bf16)
    far = jnp.stack([by_sequence(g).reshape(micros, R, nd, 2, nz, each) for g in (g_up_out, g_down)])
    far = jnp.transpose(far, (4, 5, 1, 0, 3, 2, 6)).astype(bf16).reshape(2 * nz, micros, 2, nd, R, each)
    delta, near, far = finish(near, far, picks, delta.astype(bf16), shape((micros, seg, feats), bf16), nz)
    grad = cotangent.astype(f32) + delta[:, None].astype(f32)
    g_out_down = jnp.transpose(near[:, 0], (0, 2, 1)).reshape(2 * part, R)
    g_in_up = jnp.transpose(near[:, 1:], (2, 1, 0, 3)).reshape(R, 2, 2 * part)
    g_out_up = far[:, 0].reshape(ADAPT * R, each)
    g_in_down = jnp.transpose(far[:, 1], (0, 2, 1))
    return (out, grad, g_in_down, g_in_up, g_out_down, g_out_up)


def solution(mesh):
    in_specs = (
        P(None, "dp", "seq", "mp"),
        P(None, "dp", "seq", "mp"),
        P(None, "dp"),
        P(None, "dp"),
        P(),
        P(("dp", "seq"), None, "mp"),
        P(("dp", "seq"), None),
        P(("dp", "seq"), "mp"),
        P("mp"),
        P("mp"),
        P("mp"),
        P(None, "mp"),
        P(),
        P("mp"),
        P("mp", ("dp", "seq")),
        P(None, ("dp", "seq", "mp"), None),
        P(("dp", "seq"), None, "mp"),
        P("mp", ("dp", "seq")),
        P(None, ("dp", "seq", "mp")),
    )
    out_specs = (
        P(None, "dp", "seq", "mp"),
        P(None, "dp", "seq", "mp"),
        P(None, ("dp", "seq", "mp"), None),
        P(("dp", "seq"), None, "mp"),
        P("mp", ("dp", "seq")),
        P(None, ("dp", "seq", "mp")),
    )
    sizes = dict(mesh.shape)
    by_chip = (
        sizes["seq"] == 2
        and sizes["dp"] * 2 == ADAPT
        and sizes["mp"] == SLOTS + 1
    )
    return jax.shard_map(fast_body if by_chip else body, mesh=mesh, in_specs=in_specs, out_specs=out_specs, check_vma=False)
```

```python
import functools

import jax
import jax.numpy as jnp
from jax import lax
from jax.experimental import pallas as pl
from jax.experimental.pallas import tpu as pltpu
from jax.sharding import PartitionSpec as P

D = 2048
P_SIZE = 64
NS = 128
KC = 4
Q = 256
R = 16
ADAPT = 8
DI = 4096
HG = 4
HALO = 16
SLOTS = 3


eps = 1e-05
precise = lax.Precision.HIGHEST
VMEM_LIMIT = 56 * 1024 * 1024


def shifted(array, axis, by):
    size = lax.axis_size(axis)
    pairs = [(i, i + by) for i in range(size) if 0 <= i + by < size]
    return lax.ppermute(array, axis, pairs)


def entering(part, axis, combine, identity, reverse):
    count = lax.axis_size(axis)
    place = lax.axis_index(axis)
    ahead = count - 1 - place if reverse else place
    gathered = jax.tree.map(lambda a: lax.all_gather(a, axis), part)
    state = jax.tree.map(lambda a, e: jnp.zeros_like(a) + jnp.asarray(e, a.dtype), part, identity)

    def one(hop, state):
        source = count - 1 - hop if reverse else hop
        return combine(
            state, jax.tree.map(lambda a: lax.dynamic_index_in_dim(a, source, 0, False), gathered)
        )

    return lax.fori_loop(0, ahead, one, state)


def silu_grad(value):
    sigmoid_val = jax.nn.sigmoid(value)
    return sigmoid_val * (1.0 + value * (1.0 - sigmoid_val))


def block_step(carry_state, pieces):
    x_part, b_part, c_part, log_part, step_part = pieces
    length = log_part.shape[0]
    cumulative = jnp.cumsum(log_part, axis=0)
    causal = jnp.arange(length)[:, None] >= jnp.arange(length)[None, :]
    spread = cumulative[:, None, :] - cumulative[None, :, :]
    decay_mat = jnp.exp(jnp.where(causal[:, :, None], spread, -10000.0))
    scores = jnp.dot(c_part, b_part.T, precision=precise)
    mixing = scores[:, :, None] * decay_mat * step_part[None, :, :]
    inner_out = jnp.einsum("tsh,shp->thp", mixing, x_part, precision=precise)
    carried = jnp.exp(cumulative)[:, :, None] * jnp.einsum(
        "tn,hpn->thp", c_part, carry_state, precision=precise
    )
    weights = jnp.exp(cumulative[-1][None, :] - cumulative) * step_part
    update = jnp.einsum("sh,shp,sn->hpn", weights, x_part, b_part, precision=precise)
    new_state = jnp.exp(cumulative[-1])[:, None, None] * carry_state + update
    return (new_state, inner_out + carried)


def local_scan(x_heads, b_rows, c_rows, log_rows, step_rows):
    seg_rows = x_heads.shape[0]
    blocks = seg_rows // Q

    def blocked(tensor):
        return tensor.reshape((blocks, Q) + tensor.shape[1:])

    init_state = jnp.zeros((x_heads.shape[1], x_heads.shape[2], b_rows.shape[1]), jnp.float32)
    final_state, outputs = lax.scan(
        block_step,
        init_state,
        (blocked(x_heads), blocked(b_rows), blocked(c_rows), blocked(log_rows), blocked(step_rows)),
    )
    return (outputs.reshape(x_heads.shape), final_state, jnp.sum(log_rows, axis=0))


def incoming(c_rows, log_rows, state_in):
    cumulative = jnp.cumsum(log_rows, axis=0)
    return jnp.exp(cumulative)[:, :, None] * jnp.einsum(
        "tn,hpn->thp", c_rows, state_in, precision=precise
    )


def compose(earlier, later):
    return (later[0] * earlier[0], later[1] + later[0][..., None, None] * earlier[1])


def fetch_weights(w_zx, w_bc, w_dt, w_out, in_up, out_down):
    return (
        lax.all_gather(w_zx, ("dp", "seq"), axis=0, tiled=True),
        lax.all_gather(w_bc, ("dp", "seq"), axis=0, tiled=True),
        lax.all_gather(w_dt, ("dp", "seq"), axis=0, tiled=True),
        lax.all_gather(w_out, ("dp", "seq"), axis=1, tiled=True),
        lax.all_gather(in_up, ("dp", "seq"), axis=0, tiled=True),
        lax.all_gather(out_down, ("dp", "seq"), axis=1, tiled=True),
    )


def reduce_adapters(grads):
    near_sums = (
        lax.psum_scatter(grads[1], ("dp", "seq"), scatter_dimension=0, tiled=True),
        lax.psum_scatter(grads[2], ("dp", "seq"), scatter_dimension=1, tiled=True),
    )
    wide_sums = (
        lax.psum_scatter(grads[0], ("dp", "seq", "mp"), scatter_dimension=1, tiled=True),
        lax.psum_scatter(grads[3], ("dp", "seq", "mp"), scatter_dimension=1, tiled=True),
    )
    return (wide_sums[0], near_sums[0], near_sums[1], wide_sums[1])


def body(
    x_in,
    cotangent,
    lengths,
    adapter_ids,
    norm_gain,
    w_zx,
    w_bc,
    w_dt,
    dt_bias,
    a_log,
    d_skip,
    conv_x,
    conv_bc,
    gate_gain,
    w_out,
    in_down,
    in_up,
    out_down,
    out_up,
):
    micro_count, slot_count, seg_len, model_part = x_in.shape
    head_local = dt_bias.shape[0]
    inner_local = head_local * P_SIZE
    wide_down, wide_up = (
        lax.all_gather(in_down, ("dp", "seq", "mp"), axis=1, tiled=True),
        lax.all_gather(out_up, ("dp", "seq", "mp"), axis=1, tiled=True),
    )
    wide_down = wide_down.astype(jnp.float32)
    wide_up = wide_up.astype(jnp.float32)
    conv_taps = jnp.concatenate([conv_x, conv_bc], axis=1)
    decay_rate = -jnp.exp(a_log)
    positions = lax.axis_index("seq") * seg_len + jnp.arange(seg_len)
    feature_start = lax.axis_index("mp") * model_part
    scan_local = jax.vmap(local_scan)
    incoming_map = jax.vmap(incoming)
    gathered = None
    outputs = []
    x_grads = []
    running = None
    for batch_index in range(micro_count):
        gathered = fetch_weights(w_zx, w_bc, w_dt, w_out, in_up, out_down)
        zx_weight, bc_weight, dt_weight, out_weight, up_in, down_out = gathered
        rows_own = x_in[batch_index]
        cot_own = cotangent[batch_index]
        rows_full, cot_full = (
            lax.all_gather(rows_own, "mp", axis=2, tiled=True),
            lax.all_gather(cot_own, "mp", axis=2, tiled=True),
        )
        rows_value = rows_full.astype(jnp.float32)
        inv_rms = lax.rsqrt(jnp.mean(rows_value * rows_value, axis=-1, keepdims=True) + eps)
        normed = rows_value * inv_rms * norm_gain
        normed_low = normed.astype(jnp.bfloat16)
        normed_value = normed_low.astype(jnp.float32)
        select = jax.nn.one_hot(adapter_ids[batch_index], ADAPT, dtype=jnp.float32)
        down_sel = jnp.einsum("sa,adr->sdr", select, wide_down, precision=precise)
        up_sel = jnp.einsum(
            "sa,arcf->srcf",
            select,
            up_in.astype(jnp.float32).reshape(ADAPT, R, 2, inner_local),
            precision=precise,
        )
        low_rank = jnp.einsum("std,sdr->str", normed_value, down_sel, precision=precise)
        proj_zx = jnp.einsum(
            "std,dcf->stcf", normed_low, zx_weight, preferred_element_type=jnp.float32
        )
        proj_zx = proj_zx + jnp.einsum("str,srcf->stcf", low_rank, up_sel, precision=precise)
        proj_bc = jnp.einsum(
            "std,dn->stn", normed_low, bc_weight, preferred_element_type=jnp.float32
        )
        proj_dt = jnp.einsum(
            "std,dh->sth", normed_low, dt_weight, preferred_element_type=jnp.float32
        )
        gate_in = proj_zx[:, :, 0]
        conv_in = jnp.concatenate(
            [proj_zx[:, :, 1].astype(jnp.bfloat16), proj_bc.astype(jnp.bfloat16)], axis=-1
        )
        earlier_rows = shifted(conv_in[:, seg_len - (KC - 1) :], "seq", 1)
        extended = jnp.concatenate([earlier_rows, conv_in], axis=1).astype(jnp.float32)
        conv_pre = sum(
            (
                conv_taps[tap_index] * extended[:, tap_index : tap_index + seg_len]
                for tap_index in range(KC)
            )
        )
        conv_out = jax.nn.silu(conv_pre)
        x_heads = conv_out[..., :inner_local].reshape(slot_count, seg_len, head_local, P_SIZE)
        b_rows = conv_out[..., inner_local : inner_local + NS]
        c_rows = conv_out[..., inner_local + NS :]
        mask_rows = (positions[None, :] < lengths[batch_index][:, None]).astype(jnp.float32)
        rate_in = proj_dt + dt_bias
        step_rows = jax.nn.softplus(rate_in) * mask_rows[..., None]
        log_rows = step_rows * decay_rate
        (plain_out, state_local, log_total), scan_back = jax.vjp(
            scan_local, x_heads, b_rows, c_rows, log_rows, step_rows
        )
        factor = jnp.exp(log_total)
        identity = (jnp.ones_like(factor), jnp.zeros_like(state_local))
        state_in = entering((factor, state_local), "seq", compose, identity, False)[1]
        from_state, state_back = jax.vjp(incoming_map, c_rows, log_rows, state_in)
        mixed_heads = plain_out + from_state + d_skip[:, None] * x_heads
        mixed_flat = mixed_heads.reshape(slot_count, seg_len, inner_local)
        gate_act = jax.nn.silu(gate_in)
        gated_out = mixed_flat * gate_act
        square_sum = lax.psum(jnp.sum(gated_out * gated_out, axis=-1), "mp")
        inv_gate = lax.rsqrt(square_sum / DI + eps)
        scaled = gated_out * inv_gate[..., None] * gate_gain
        scaled_low = scaled.astype(jnp.bfloat16)
        scaled_value = scaled_low.astype(jnp.float32)
        out_sel = jnp.einsum(
            "sa,far->sfr",
            select,
            down_out.astype(jnp.float32).reshape(inner_local, ADAPT, R),
            precision=precise,
        )
        up_out = jnp.einsum("sa,ard->srd", select, wide_up.reshape(ADAPT, R, D), precision=precise)
        rank_out = jnp.einsum("stf,sfr->str", scaled_value, out_sel, precision=precise)
        partial_out = jnp.einsum(
            "stf,fd->std", scaled_low, out_weight, preferred_element_type=jnp.float32
        )
        partial_out = partial_out + jnp.einsum("str,srd->std", rank_out, up_out, precision=precise)
        branch = lax.psum_scatter(partial_out, "mp", scatter_dimension=2, tiled=True)
        outputs.append(
            (rows_own.astype(jnp.float32) + mask_rows[..., None] * branch).astype(jnp.bfloat16)
        )
        branch_grad = cot_full * mask_rows[..., None].astype(jnp.bfloat16)
        branch_value = branch_grad.astype(jnp.float32)
        rank_grad = jnp.einsum("std,srd->str", branch_value, up_out, precision=precise)
        grad_up_out = jnp.einsum("str,std->srd", rank_out, branch_value, precision=precise)
        grad_out_sel = jnp.einsum("stf,str->sfr", scaled_value, rank_grad, precision=precise)
        scaled_grad = jnp.einsum(
            "std,fd->stf", branch_grad, out_weight, preferred_element_type=jnp.float32
        )
        scaled_grad = scaled_grad + jnp.einsum(
            "str,sfr->stf", rank_grad, out_sel, precision=precise
        )
        weighted = scaled_grad * gate_gain
        dot_sum = lax.psum(jnp.sum(weighted * gated_out, axis=-1), "mp")
        gated_grad = (
            weighted * inv_gate[..., None] - gated_out * (inv_gate**3 * dot_sum / DI)[..., None]
        )
        mixed_grad = (gated_grad * gate_act).reshape(slot_count, seg_len, head_local, P_SIZE)
        gate_grad = gated_grad * mixed_flat * silu_grad(gate_in)
        c_grad_in, log_grad_in, state_in_grad = state_back(mixed_grad)
        later_grads = entering((factor, state_in_grad), "seq", compose, identity, True)[1]
        total_grad = jnp.sum(later_grads * state_in, axis=(2, 3)) * factor
        x_heads_grad, b_grad, c_grad, log_grad, step_grad = scan_back(
            (mixed_grad, later_grads, total_grad)
        )
        x_heads_grad = x_heads_grad + d_skip[:, None] * mixed_grad
        c_grad = c_grad + c_grad_in
        step_grad = step_grad + (log_grad + log_grad_in) * decay_rate
        rate_grad = step_grad * mask_rows[..., None] * jax.nn.sigmoid(rate_in)
        conv_out_grad = jnp.concatenate(
            [x_heads_grad.reshape(slot_count, seg_len, inner_local), b_grad, c_grad], axis=-1
        )
        pre_grad = conv_out_grad * silu_grad(conv_pre)
        padded_grad = jnp.pad(pre_grad, ((0, 0), (KC - 1, KC - 1), (0, 0)))
        ext_grad = sum(
            (
                conv_taps[tap_index]
                * padded_grad[:, KC - 1 - tap_index : KC - 1 - tap_index + seg_len + KC - 1]
                for tap_index in range(KC)
            )
        )
        returned = shifted(ext_grad[:, : KC - 1], "seq", -1)
        in_grad = ext_grad[:, KC - 1 :]
        in_grad = in_grad.at[:, seg_len - (KC - 1) :].add(returned)
        zx_grad = jnp.stack([gate_grad, in_grad[..., :inner_local]], axis=2).astype(jnp.bfloat16)
        dt_grad_low = rate_grad.astype(jnp.bfloat16)
        zx_grad_value = zx_grad.astype(jnp.float32)
        rank_in_grad = jnp.einsum("stcf,srcf->str", zx_grad_value, up_sel, precision=precise)
        grad_up_sel = jnp.einsum("str,stcf->srcf", low_rank, zx_grad_value, precision=precise)
        grad_down_sel = jnp.einsum("std,str->sdr", normed_value, rank_in_grad, precision=precise)
        normed_part = jnp.einsum(
            "stcf,dcf->std", zx_grad, zx_weight, preferred_element_type=jnp.float32
        )
        normed_part = normed_part + jnp.einsum(
            "sth,dh->std", dt_grad_low, dt_weight, preferred_element_type=jnp.float32
        )
        normed_part = normed_part + jnp.einsum(
            "str,sdr->std", rank_in_grad, down_sel, precision=precise
        )
        bc_partial = in_grad[..., inner_local:]
        normed_sum, bc_sum = lax.psum((normed_part, bc_partial), "mp")
        normed_grad = normed_sum + jnp.einsum(
            "stn,dn->std",
            bc_sum.astype(jnp.bfloat16),
            bc_weight,
            preferred_element_type=jnp.float32,
        )
        scaled_in = normed_grad * norm_gain
        row_grad = inv_rms * scaled_in - rows_value * inv_rms**3 * jnp.mean(
            scaled_in * rows_value, axis=-1, keepdims=True
        )
        own_slice = lax.dynamic_slice_in_dim(row_grad, feature_start, model_part, 2)
        x_grads.append(cot_own.astype(jnp.float32) + own_slice)
        local_grads = (
            jnp.einsum("sa,sdr->adr", select, grad_down_sel, precision=precise),
            jnp.einsum("sa,srcf->arcf", select, grad_up_sel, precision=precise).reshape(
                ADAPT * R, 2, inner_local
            ),
            jnp.einsum("sa,sfr->far", select, grad_out_sel, precision=precise).reshape(
                inner_local, ADAPT * R
            ),
            jnp.einsum("sa,srd->ard", select, grad_up_out, precision=precise).reshape(ADAPT * R, D),
        )
        running = local_grads if running is None else jax.tree.map(jnp.add, running, local_grads)
    running = reduce_adapters(running)
    return (jnp.stack(outputs), jnp.stack(x_grads), running[0], running[1], running[2], running[3])


MESH = pl.DeviceIdType.MESH


def split(v):
    hi = v.astype(jnp.bfloat16)
    return hi, (v - hi.astype(jnp.float32)).astype(jnp.bfloat16)


def mm(a, b):
    return lax.dot_general(a, b, (((1,), (0,)), ((), ())), preferred_element_type=jnp.float32)


def mm_t(a, b):
    return lax.dot_general(a, b, (((1,), (1,)), ((), ())), preferred_element_type=jnp.float32)


def mm3(a, b):
    return mm(a[0], b[0]) + mm(a[0], b[1]) + mm(a[1], b[0])


def mm3_t(a, b):
    return mm_t(a[0], b[0]) + mm_t(a[0], b[1]) + mm_t(a[1], b[0])


def ones_mm(ones, v):
    hi, lo = split(v)
    rest = v - hi.astype(jnp.float32) - lo.astype(jnp.float32)
    return mm(ones, hi) + mm(ones, lo) + mm(ones, rest.astype(jnp.bfloat16))


def conv_rows(rows, halo, taps):
    count = rows.shape[0]
    ext = jnp.concatenate([halo, rows], axis=0).astype(jnp.float32)
    first = HALO - (KC - 1)
    total = taps[0:1] * ext[first : first + count]
    for j in range(1, KC):
        total = total + taps[j : j + 1] * ext[first + j : first + j + count]
    return total


def conv_rows_back(grad, taps):
    count, width = grad.shape
    zero = jnp.zeros((8, width), jnp.float32)
    ext = jnp.concatenate([zero, grad, zero], axis=0)
    total = taps[0:1] * ext[3 : 3 + count + 8]
    for j in range(1, KC):
        total = total + taps[j : j + 1] * ext[3 - j : 3 - j + count + 8]
    return total


def widen(columns):
    rows = columns.shape[0]
    lane = lax.broadcasted_iota(jnp.int32, (rows, 2 * P_SIZE), 1)
    return jnp.concatenate(
        [jnp.where(lane < P_SIZE, columns[:, h : h + 1], columns[:, h + 1 : h + 2]) for h in range(0, HG, 2)], axis=1
    )


def of_group(value, group):
    return pltpu.roll(value, lax.rem(128 - group * HG, 128), 1)


def head_sums(prod, group):
    rows = prod.shape[1]
    row = lax.broadcasted_iota(jnp.int32, (rows, 128), 0) // P_SIZE + group * HG
    lane = lax.broadcasted_iota(jnp.int32, (rows, 128), 1)
    pick = (row == lane).astype(jnp.float32).astype(jnp.bfloat16)
    hi, lo = split(prod)
    return mm(hi, pick) + mm(lo, pick)


def lane_sum(v):
    part = v[:, :128]
    for k in range(1, v.shape[1] // 128):
        part = part + v[:, k * 128 : (k + 1) * 128]
    return part


def add_up(ref, value, group):
    @pl.when(group == 0)
    def _():
        ref[0] = value

    @pl.when(group > 0)
    def _():
        ref[0] += value


def run_of(slot, z):
    return SLOTS * z + lax.rem(slot + z, SLOTS)


def place_of(run):
    z = run // SLOTS
    return z, lax.rem(lax.rem(run, SLOTS) + SLOTS * SLOTS - z, SLOTS)


class Mover:
    def __init__(self, src_ref, dst_ref, send_sem, recv_sem, count, slots, to_rows):
        self.refs = src_ref, dst_ref, send_sem, recv_sem
        self.count, self.slots, self.to_rows = count, slots, to_rows
        self.d, self.c, self.z = lax.axis_index("dp"), lax.axis_index("seq"), lax.axis_index("mp")
        self.pieces = 4 * SLOTS if to_rows else count * len(slots)

    def piece(self, n):
        src_ref, dst_ref, send_sem, recv_sem = self.refs
        if self.to_rows:
            m, h, to_c = lax.rem(n // 4 + self.z, SLOTS), n // 2 % 2, lax.rem(n + self.c, 2)
            to_z, slot = place_of(m * self.count + 2 * self.c + h)
            own = src_ref.shape[1] // 4
            src = src_ref.at[m, pl.ds(pl.multiple_of((2 * h + to_c) * own, 16), own), :]
            dst, sem = self.landing(slot - self.slots[0], self.z), (slot, self.z)
            due = jnp.logical_and(slot >= self.slots[0], slot <= self.slots[-1])
        else:
            slot = self.slots[n // self.count]
            to_z = lax.rem(self.z + n % self.count, self.count)
            run = run_of(slot, self.z)
            m, chunk = run // self.count, lax.rem(run, self.count)
            to_c, q = chunk // 2, lax.rem(chunk, 2) * 2 + self.c
            feats = dst_ref.shape[2]
            src = src_ref.at[slot - self.slots[0], :, pl.ds(pl.multiple_of(to_z * feats, 128), feats)]
            dst, sem = self.landing(m, q), (m, q)
            due = True
        here = jnp.logical_and(to_c == self.c, to_z == self.z)
        near = pltpu.make_async_copy(src, dst, recv_sem.at[sem])
        far = pltpu.make_async_remote_copy(
            src_ref=src, dst_ref=dst, send_sem=send_sem.at[n], recv_sem=recv_sem.at[sem],
            device_id=(self.d, to_c, to_z), device_id_type=MESH,
        )
        return jnp.logical_and(due, here), jnp.logical_and(due, jnp.logical_not(here)), near, far

    def landing(self, first, slot):
        dst_ref = self.refs[1]
        if self.to_rows:
            feats = dst_ref.shape[2] // self.count
            return dst_ref.at[first, :, pl.ds(pl.multiple_of(slot * feats, 128), feats)]
        rows = dst_ref.shape[1] // 4
        return dst_ref.at[first, pl.ds(pl.multiple_of(slot * rows, 16), rows), :]

    def greet(self, barrier):
        for cc in range(2):
            for r in range(self.count):
                if cc or r:
                    device = (self.d, lax.rem(self.c + cc, 2), lax.rem(self.z + r, self.count))
                    pl.semaphore_signal(barrier, 1, device_id=device, device_id_type=MESH)
        return 2 * self.count - 1

    def start(self, n):
        stays, goes, near, far = self.piece(n)

        @pl.when(stays)
        def _():
            near.start()

        @pl.when(goes)
        def _():
            far.start()

    def start_at(self, step, steps):
        for n in range(self.pieces):
            @pl.when(step == n * steps // (2 * self.pieces))
            def _():
                self.start(n)

    def finish(self):
        recv_sem = self.refs[3]
        if self.to_rows:
            for slot in self.slots:
                for s in range(self.count):
                    area = self.landing(slot - self.slots[0], s)
                    pltpu.make_async_copy(area, area, recv_sem.at[slot, s]).wait()
        else:
            for m in range(SLOTS):
                for q in range(4):
                    run = m * self.count + 2 * self.c + q // 2
                    slot = place_of(run)[1]

                    @pl.when(jnp.logical_and(slot >= self.slots[0], slot <= self.slots[-1]))
                    def _():
                        area = self.landing(m, q)
                        pltpu.make_async_copy(area, area, recv_sem.at[m, q]).wait()
        for n in range(self.pieces):
            _, goes, _, far = self.piece(n)

            @pl.when(goes)
            def _():
                far.wait_send()


class Line:
    def __init__(self, held_ref, sent_ref, send_sem, recv_sem, count, step):
        self.refs = held_ref, sent_ref, send_sem, recv_sem
        self.step, self.count = step, count
        self.d, self.c, self.z = lax.axis_index("dp"), lax.axis_index("seq"), lax.axis_index("mp")
        low, high = self.z > 0, self.z < count - 1
        self.has_source, self.has_target = (low, high) if step > 0 else (high, low)
        above, below = count - 1 - self.z, count - 2 - self.z
        self.from_slot, self.to_slot = (above, below) if step > 0 else (below, above)

    def greet(self, barrier):
        @pl.when(self.has_source)
        def _():
            pl.semaphore_signal(barrier, 1, device_id=(self.d, self.c, self.z - self.step), device_id_type=MESH)
        return jnp.where(self.has_target, 1, 0)

    def copy(self, group):
        held_ref, sent_ref, send_sem, recv_sem = self.refs
        return pltpu.make_async_remote_copy(
            src_ref=sent_ref.at[group], dst_ref=held_ref.at[group], send_sem=send_sem.at[group], recv_sem=recv_sem.at[group],
            device_id=(self.d, self.c, self.z + self.step), device_id_type=MESH,
        )

    def receive(self, slot, group):
        held_ref, sent_ref = self.refs[:2]
        remote = jnp.logical_and(self.has_source, slot == self.from_slot)
        fresh = slot == (0 if self.step > 0 else SLOTS - 1)
        local = jnp.logical_not(jnp.logical_or(remote, fresh))

        @pl.when(remote)
        def _():
            self.copy(group).wait_recv()
            sent_ref[held_ref.shape[0] + group] = held_ref[group]

        return jnp.where(jnp.logical_or(remote, local), sent_ref[held_ref.shape[0] + group], 0.0)

    def send(self, slot, group, value):
        held_ref, sent_ref = self.refs[:2]
        sent_ref[held_ref.shape[0] + group] = value

        @pl.when(jnp.logical_and(self.has_target, slot == self.to_slot))
        def _():
            sent_ref[group] = value
            self.copy(group).start()

    def finish(self):
        @pl.when(self.has_target)
        def _():
            for g in range(self.refs[0].shape[0]):
                self.copy(g).wait_send()


class PairFill:
    def __init__(self, own_ref, both_ref, buffer_ref, sems):
        self.d, self.c, self.z = lax.axis_index("dp"), lax.axis_index("seq"), lax.axis_index("mp")
        own = own_ref.shape[1]
        mine = buffer_ref.at[:, pl.ds(pl.multiple_of(self.c * own, 16), own), :]
        theirs = buffer_ref.at[:, pl.ds(pl.multiple_of((1 - self.c) * own, 16), own), :]
        self.near = pltpu.make_async_copy(own_ref, mine, sems.at[0])
        self.far = pltpu.make_async_remote_copy(
            src_ref=own_ref, dst_ref=mine, send_sem=sems.at[1], recv_sem=sems.at[2], device_id=(self.d, 1 - self.c, self.z),
            device_id_type=MESH,
        )
        self.arrival = pltpu.make_async_copy(theirs, theirs, sems.at[2])
        self.keep = pltpu.make_async_copy(buffer_ref, both_ref, sems.at[3])

    def greet(self, barrier):
        pl.semaphore_signal(barrier, 1, device_id=(self.d, 1 - self.c, self.z), device_id_type=MESH)
        return 1

    def fill(self):
        self.far.start()
        self.near.start()
        self.near.wait()
        self.arrival.wait()
        self.keep.start()

    def finish(self):
        self.far.wait_send()
        self.keep.wait()


def carried_by(kernel, count, first, to_rows, n_in, n_out, *refs):
    ins, src_ref, outs, dst_ref = refs[:n_in], refs[n_in], refs[n_in + 1 : n_in + 1 + n_out], refs[n_in + 1 + n_out]
    scratch, sems = refs[n_in + n_out + 2 : -2], refs[-2:]
    kernel(*ins, *outs, *scratch, mover=Mover(src_ref, dst_ref, *sems, count, first, to_rows))


def step_of(grid):
    return pl.program_id(0) * grid[1] + pl.program_id(1)


def begin(grid, *parties):
    parties = [p for p in parties if p is not None]
    if parties:
        @pl.when(step_of(grid) == 0)
        def _():
            barrier = pltpu.get_barrier_semaphore()
            waits = 0
            for party in parties:
                waits = waits + party.greet(barrier)
            pl.semaphore_wait(barrier, waits)
            for party in parties:
                if isinstance(party, PairFill):
                    party.fill()
    for party in parties:
        if isinstance(party, Mover):
            party.start_at(step_of(grid), grid[0] * grid[1])


def end(grid, *parties):
    parties = [p for p in parties if p is not None]
    if parties:
        @pl.when(step_of(grid) == grid[0] * grid[1] - 1)
        def _():
            for party in parties:
                party.finish()


def twice_split(v):
    hi, lo = split(v)
    lane = lax.broadcasted_iota(jnp.int32, v.shape, 1)
    return jnp.where(lane < v.shape[1] // 2, hi.astype(jnp.float32), lo.astype(jnp.float32)).astype(jnp.bfloat16)


def fold(v):
    half = v.shape[0] // 2
    return v[:half] + v[half:]


def twice(v):
    return jnp.concatenate([v, v], axis=0)


def pick_kernel(ids_ref, pack_ref, out_ref):
    out_ref[0, 0] = pack_ref[0, 0, 0]


def merge(ref):
    return ref[...].reshape(ref.shape[0] * ref.shape[1], ref.shape[2])


def project_kernel(
    grid, own_ref, w_ref, tailw_ref, down_ref, up_ref, xin_ref, z_ref, bcin_ref, rate_ref, lr_ref, both_ref, low_ref, sems,
    mover=None
):
    step = pl.program_id(1)
    pair = PairFill(own_ref, both_ref, low_ref, sems)
    begin(grid, pair, mover)
    slots, tokens = low_ref.shape[:2]

    @pl.when(step == 0)
    def _():
        for m in range(slots):
            tail = mm(low_ref[m], tailw_ref[...])
            bcin_ref[m] = tail[:, : 2 * NS].astype(jnp.bfloat16)
            rate_ref[m] = tail[:, 2 * NS :]
            lr_ref[m] = twice_split(mm_t(low_ref[m], twice(down_ref[0, m])))

    value = mm(merge(low_ref), w_ref[0])
    for m in range(slots):
        part = value[m * tokens : (m + 1) * tokens] + mm(lr_ref[m], twice(up_ref[m, 0]))

        @pl.when(step < grid[1] // 2)
        def _():
            xin_ref[m] = part.astype(jnp.bfloat16)

        @pl.when(step >= grid[1] // 2)
        def _():
            z_ref[m] = part

    end(grid, pair, mover)


def prep_kernel(rate_ref, bias_ref, decay_ref, mask_ref, bcin_ref, bchalo_ref, taps_ref, step_ref, cum_ref, lanes_ref, bc_ref):
    rows = rate_ref.shape[1]
    value = rate_ref[0] + bias_ref[...]
    step = (jnp.maximum(value, 0.0) + jnp.log1p(jnp.exp(-jnp.abs(value)))) * mask_ref[0]
    log = step * decay_ref[...]
    tri = lax.broadcasted_iota(jnp.int32, (Q, Q), 0) >= lax.broadcasted_iota(jnp.int32, (Q, Q), 1)
    tri = tri.astype(jnp.float32).astype(jnp.bfloat16)
    step_ref[0] = step
    cum = jnp.concatenate([ones_mm(tri, log[b * Q : (b + 1) * Q]) for b in range(rows // Q)], axis=0)
    cum_ref[0] = cum
    cum_t, step_t = cum.T, step.T
    for g in range(lanes_ref.shape[1]):
        lanes_ref[0, g, :HG] = cum_t[g * HG : (g + 1) * HG]
        lanes_ref[0, g, HG:] = step_t[g * HG : (g + 1) * HG]
    pre = conv_rows(bcin_ref[0], bchalo_ref[0], taps_ref[...])
    bc_ref[0] = pre * jax.nn.sigmoid(pre)


def forward_kernel(
    grid, xin_ref, halo_ref, taps_ref, bc_ref, cum_ref, step_ref, lanes_ref, skip_ref, z_ref, mixed_ref, square_ref, state_ref,
    end_ref, scores_ref, bt_ref, held_ref, sent_ref, send_sem, recv_sem, mover=None
):
    group = pl.program_id(1)
    rows = xin_ref.shape[1]
    blocks = rows // Q
    line = Line(held_ref, sent_ref, send_sem, recv_sem, lax.axis_size("mp"), 1)
    begin(grid, line, mover)

    @pl.when(step_of(grid) == 0)
    def _():
        sent_ref[...] = jnp.zeros(sent_ref.shape, jnp.float32)

    @pl.when(group == 0)
    def _():
        for b in range(blocks):
            part = bc_ref[0, b * Q : (b + 1) * Q]
            b_part = split(part[:, :NS])
            c_part = split(part[:, NS:])
            scores_ref[b] = mm3_t(c_part, b_part)
            hi, lo = split(part[:, :NS].T)
            bt_ref[0, b] = hi
            bt_ref[1, b] = lo

    pre = conv_rows(xin_ref[0], halo_ref[0], taps_ref[...])
    x = pre * jax.nn.sigmoid(pre)
    cums, decs, updates = [], [], []
    for b in range(blocks):
        at = slice(b * Q, (b + 1) * Q)
        cum = of_group(cum_ref[0, at], group)
        step = of_group(step_ref[0, at], group)
        total = cum[Q - 1 : Q]
        wx = x[at] * widen(jnp.exp(total - cum) * step)
        cums.append(cum)
        decs.append(widen(jnp.exp(total)))
        updates.append(mm3((bt_ref[0, b], bt_ref[1, b]), split(wx)))

    slot = pl.program_id(0)
    states = [line.receive(slot, group)]
    for b in range(blocks):
        states.append(decs[b] * states[b] + updates[b])
    state_ref[0] = states[0]
    end_ref[0] = states[blocks]
    line.send(slot, group, states[blocks])
    lane = lax.broadcasted_iota(jnp.int32, (Q, 2 * P_SIZE), 1)
    causal = lax.broadcasted_iota(jnp.int32, (Q, Q), 0) >= lax.broadcasted_iota(jnp.int32, (Q, Q), 1)
    square = []
    for b in range(blocks):
        at = slice(b * Q, (b + 1) * Q)
        scores = scores_ref[b]
        xb = x[at]
        carried = widen(jnp.exp(cums[b])) * mm3(split(bc_ref[0, at, NS:]), split(states[b]))
        parts = []
        for h in range(0, HG, 2):
            pair = xb[:, h * P_SIZE : (h + 2) * P_SIZE]
            x_hi, x_lo = split(pair)
            both = jnp.concatenate([x_hi, x_lo], axis=1)
            halves = []
            for k in (h, h + 1):
                spread = cums[b][:, k : k + 1] - lanes_ref[0, 0, k : k + 1, at]
                decay = jnp.exp(jnp.where(causal, spread, -10000.0))
                m_hi, m_lo = split(scores * decay * lanes_ref[0, 0, HG + k : HG + k + 1, at])
                first = mm(m_hi, both)
                halves.append(first[:, : 2 * P_SIZE] + first[:, 2 * P_SIZE :] + mm(m_lo, x_hi))
            parts.append(jnp.where(lane < P_SIZE, halves[0], halves[1]))
        mixed = jnp.concatenate(parts, axis=1) + skip_ref[0:1] * xb + carried
        mixed_ref[0, at] = mixed
        z = z_ref[0, at]
        gated = mixed * (z * jax.nn.sigmoid(z))
        square.append(lane_sum(gated * gated))
    add_up(square_ref, jnp.concatenate(square, axis=0), group)

    end(grid, line, mover)


def chunk_decay(cum_ref, group):
    rows = cum_ref.shape[1]
    before = jnp.zeros((1, 128), jnp.float32)
    parts = []
    for b in range(rows // Q):
        cum = of_group(cum_ref[0, b * Q : (b + 1) * Q], group)
        parts.append(jnp.exp(cum + before))
        before = before + cum[Q - 1 : Q]
    return widen(jnp.concatenate(parts, axis=0))


def gs_kernel(
    grid, own_ref, w_ref, up_ref, down_ref, mixed_ref, z_ref, gain_ref, gs_ref, dot_ref, rg_ref, both_ref, gb_ref, sems
):
    step = pl.program_id(1)
    pair = PairFill(own_ref, both_ref, gb_ref, sems)
    begin(grid, pair)
    slots, tokens = gb_ref.shape[:2]

    @pl.when(step == 0)
    def _():
        for m in range(slots):
            rg_ref[m] = twice_split(mm_t(gb_ref[m], twice(up_ref[0, m])))

    gb = merge(gb_ref)
    width = w_ref.shape[3]
    total = mm_t(gb[:, :width], w_ref[0, 0])
    for n in range(1, w_ref.shape[0]):
        total = total + mm_t(gb[:, n * width : (n + 1) * width], w_ref[n, 0])
    for m in range(slots):
        gs = total[m * tokens : (m + 1) * tokens] + mm(rg_ref[m], twice(down_ref[m, 0]))
        gs_ref[m] = gs
        z = z_ref[m]
        dots = lane_sum(gs * gain_ref[...] * (mixed_ref[m] * (z * jax.nn.sigmoid(z))))

        @pl.when(step == 0)
        def _():
            dot_ref[m] = dots

        @pl.when(step > 0)
        def _():
            dot_ref[m] += dots

    end(grid, pair)


def turned(v):
    return v.astype(jnp.float32).T.astype(jnp.bfloat16)


def rank_sum(rows_ref, m, factor_ref, first):
    width = factor_ref.shape[3]
    total = 0.0
    for n in range(factor_ref.shape[1]):
        factor = twice(factor_ref[m, n, first : first + R])
        total = total + mm_t(rows_ref[m, :, n * width : (n + 1) * width], factor)
    return total


def branch_kernel(
    grid, scaled_ref, w_ref, down_ref, up_ref, rg_ref, gb_ref, branch_ref, g_up_ref, g_down_ref, ro_ref, rot_ref, rgt_ref, mover=None
):
    step = pl.program_id(1)
    begin(grid, mover)
    slots, tokens = scaled_ref.shape[:2]

    @pl.when(step == 0)
    def _():
        for m in range(slots):
            ro = twice_split(rank_sum(scaled_ref, m, down_ref, 0))
            ro_ref[m] = ro
            rot_ref[m] = turned(ro)
            rgt_ref[m] = turned(rg_ref[m])

    scaled = merge(scaled_ref)
    width = w_ref.shape[2]
    total = mm(scaled[:, :width], w_ref[0, 0])
    for n in range(1, w_ref.shape[1]):
        total = total + mm(scaled[:, n * width : (n + 1) * width], w_ref[0, n])
    cols = g_down_ref.shape[2]
    for m in range(slots):
        branch_ref[m] = total[m * tokens : (m + 1) * tokens] + mm(ro_ref[m], twice(up_ref[0, m]))
        g_up_ref[m] = fold(mm(rot_ref[m], gb_ref[m]))
        g_down_ref[m] = fold(mm(rgt_ref[m], scaled_ref[m, :, pl.ds(pl.multiple_of(step * cols, 128), cols)]))
    end(grid, mover)


def unproject_kernel(
    grid, gz_ref, gx_ref, tail_ref, w_ref, tailw_ref, up_ref, down_ref, lr_ref, low_ref, g_ref, upz_ref, upx_ref, g_down_ref,
    ri_ref, rit_ref, lrt_ref, mover=None
):
    step = pl.program_id(1)
    begin(grid, mover)
    slots, tokens = gz_ref.shape[:2]

    @pl.when(step == 0)
    def _():
        for m in range(slots):
            ri = twice_split(rank_sum(gz_ref, m, up_ref, 0) + rank_sum(gx_ref, m, up_ref, R))
            ri_ref[m] = ri
            rit_ref[m] = turned(ri)
            lrt_ref[m] = turned(lr_ref[m])

    total = mm_t(merge(gz_ref), w_ref[0]) + mm_t(merge(gx_ref), w_ref[1]) + mm_t(merge(tail_ref), tailw_ref[...])
    cols = upz_ref.shape[2]
    at = pl.ds(pl.multiple_of(step * cols, 128), cols)
    for m in range(slots):
        g_ref[m] = total[m * tokens : (m + 1) * tokens] + mm(ri_ref[m], twice(down_ref[0, m]))
        upz_ref[m] = fold(mm(lrt_ref[m], gz_ref[m, :, at]))
        upx_ref[m] = fold(mm(lrt_ref[m], gx_ref[m, :, at]))
        g_down_ref[m] = fold(mm(rit_ref[m], low_ref[m]))
    end(grid, mover)


def gate_back_kernel(
    grid, gs_ref, mixed_ref, z_ref, inv_ref, coef_ref, gain_ref, bc_ref, cum_ref, dy_ref, gz_ref, scaled_ref, lam_ref, q_ref, ct_ref,
    mover=None
):
    group = pl.program_id(1)
    begin(grid, mover)

    @pl.when(group == 0)
    def _():
        hi, lo = split(bc_ref[0, :, NS:].T)
        ct_ref[0] = hi
        ct_ref[1] = lo

    z = z_ref[0]
    mixed = mixed_ref[0]
    sig = jax.nn.sigmoid(z)
    act = z * sig
    gated = mixed * act
    inv = inv_ref[0]
    gain = gain_ref[...]
    scaled_ref[0] = (gated * inv * gain).astype(jnp.bfloat16)
    g_gated = gs_ref[0] * gain * inv - gated * coef_ref[0]
    dy = g_gated * act
    dy_ref[0] = dy
    gz_ref[0] = (g_gated * mixed * (sig * (1.0 + z * (1.0 - sig)))).astype(jnp.bfloat16)
    lam_ref[0] = mm3((ct_ref[0], ct_ref[1]), split(dy * chunk_decay(cum_ref, group)))
    add_up(q_ref, head_sums(dy * mixed, group), group)

    end(grid, mover)


def scan_back_kernel(
    grid, dy_ref, xin_ref, halo_ref, taps_ref, bc_ref, cum_ref, step_ref, lanes_ref, skip_ref, state_ref, lam_ref, end_ref,
    gx_ref, head_ref, tail_ref, gbc_ref, xu_ref, dx_ref, scorest_ref, dscorest_ref, bt_ref, ct_ref, held_ref, sent_ref, send_sem,
    recv_sem, mover=None
):
    group = pl.program_id(1)
    rows = xin_ref.shape[1]
    blocks = rows // Q
    line = Line(held_ref, sent_ref, send_sem, recv_sem, lax.axis_size("mp"), -1)
    begin(grid, line, mover)

    @pl.when(step_of(grid) == 0)
    def _():
        sent_ref[...] = jnp.zeros(sent_ref.shape, jnp.float32)

    @pl.when(group == 0)
    def _():
        for b in range(blocks):
            part = bc_ref[0, b * Q : (b + 1) * Q]
            scorest_ref[b] = mm3_t(split(part[:, :NS]), split(part[:, NS:]))
            dscorest_ref[b] = jnp.zeros((Q, Q), jnp.float32)
            hi, lo = split(part[:, :NS].T)
            bt_ref[0, b] = hi
            bt_ref[1, b] = lo
            hi, lo = split(part[:, NS:].T)
            ct_ref[0, b] = hi
            ct_ref[1, b] = lo
        gbc_ref[0] = jnp.zeros((rows, 2 * NS), jnp.float32)
        xu_ref[0] = jnp.zeros((rows, 128), jnp.float32)
        dx_ref[0] = jnp.zeros((rows, 128), jnp.float32)

    pre = conv_rows(xin_ref[0], halo_ref[0], taps_ref[...])
    sig = jax.nn.sigmoid(pre)
    x = pre * sig
    lane = lax.broadcasted_iota(jnp.int32, (Q, 2 * P_SIZE), 1)
    causal = lax.broadcasted_iota(jnp.int32, (Q, Q), 0) <= lax.broadcasted_iota(jnp.int32, (Q, Q), 1)
    cums, step_cols, decs, rests, wide_steps = [], [], [], [], []
    for b in range(blocks):
        at = slice(b * Q, (b + 1) * Q)
        cum = of_group(cum_ref[0, at], group)
        step = of_group(step_ref[0, at], group)
        total = cum[Q - 1 : Q]
        cums.append(cum)
        step_cols.append(step)
        decs.append(widen(jnp.exp(total)))
        rests.append(widen(jnp.exp(total - cum)))
        wide_steps.append(widen(step))
    states = [state_ref[0]]
    for b in range(blocks - 1):
        wx = x[b * Q : (b + 1) * Q] * rests[b] * wide_steps[b]
        states.append(decs[b] * states[b] + mm3((bt_ref[0, b], bt_ref[1, b]), split(wx)))
    slot = SLOTS - 1 - pl.program_id(0)
    lam = line.receive(slot, group)
    whole = decs[0]
    for dec in decs[1:]:
        whole = whole * dec
    line.send(slot, group, whole * lam + lam_ref[0])
    ends = jnp.sum(lam * end_ref[0], axis=0, keepdims=True)
    g_parts = [None] * blocks
    for b in reversed(range(blocks)):
        at = slice(b * Q, (b + 1) * Q)
        xb = x[at]
        dy = dy_ref[0, at]
        scores = scorest_ref[b]
        dscores = dscorest_ref[b]
        u_parts = []
        for h in range(0, HG, 2):
            pair = slice(h * P_SIZE, (h + 2) * P_SIZE)
            x_hi, x_lo = split(xb[:, pair])
            d_hi, d_lo = split(dy[:, pair])
            both = jnp.concatenate([d_hi, d_lo], axis=1)
            halves = []
            for k in (h, h + 1):
                mine = (lane < P_SIZE) if k == h else (lane >= P_SIZE)
                spread = lanes_ref[0, 0, k : k + 1, at] - cums[b][:, k : k + 1]
                decay = jnp.exp(jnp.where(causal, spread, -10000.0))
                zero = jnp.zeros_like(x_hi)
                xm_hi = jnp.where(mine, x_hi, zero)
                xm_lo = jnp.where(mine, x_lo, zero)
                dm = mm_t(xm_hi, d_hi) + mm_t(xm_hi, d_lo) + mm_t(xm_lo, d_hi)
                dscores = dscores + dm * decay * step_cols[b][:, k : k + 1]
                m_hi, m_lo = split(scores * decay)
                first = mm(m_hi, both)
                halves.append(first[:, : 2 * P_SIZE] + first[:, 2 * P_SIZE :] + mm(m_lo, d_hi))
            u_parts.append(jnp.where(lane < P_SIZE, halves[0], halves[1]))
        dscorest_ref[b] = dscores
        lam_s = split(lam)
        part = bc_ref[0, at]
        step = wide_steps[b]
        u = jnp.concatenate(u_parts, axis=1) + rests[b] * mm3(split(part[:, :NS]), lam_s)
        ev = split(widen(jnp.exp(cums[b])) * dy)
        gbc_ref[0, at, :NS] += mm3_t(split(rests[b] * step * xb), lam_s)
        gbc_ref[0, at, NS:] += mm3_t(ev, split(states[b]))
        if b > 0:
            lam = decs[b] * lam + mm3((ct_ref[0, b], ct_ref[1, b]), ev)
        xu_ref[0, at] += head_sums(xb * u, group)
        direct = xb * dy * skip_ref[0:1]
        if b == blocks - 1:
            row = lax.broadcasted_iota(jnp.int32, (Q, HG * P_SIZE), 0)
            direct = jnp.where(row == Q - 1, direct - ends, direct)
        dx_ref[0, at] += head_sums(direct, group)
        g_parts[b] = step * u + skip_ref[0:1] * dy
    g_pre = jnp.concatenate(g_parts, axis=0) * (sig * (1.0 + pre * (1.0 - sig)))
    g_ext = conv_rows_back(g_pre, taps_ref[...])
    gx_ref[0] = g_ext[8:].astype(jnp.bfloat16)
    head_ref[0] = g_ext[:8]
    tail_ref[0] = g_ext[rows:]

    @pl.when(group == pl.num_programs(1) - 1)
    def _():
        for b in range(blocks):
            at = slice(b * Q, (b + 1) * Q)
            part = bc_ref[0, at]
            ds = dscorest_ref[b]
            gbc_ref[0, at, :NS] += mm3(split(ds), split(part[:, NS:]))
            gbc_ref[0, at, NS:] += mm3(split(ds.T), split(part[:, :NS]))

    end(grid, line, mover)


def finish_kernel(
    count, out_ref, up_z_ref, up_x_ref, up_out_ref, down_ref, mine_ref, picks_ref, rows_ref, moved_ref, near_out_ref, far_out_ref,
    near_ref, far_ref, near1_ref, far1_ref, near2_ref,
    near2_in_ref, far2_ref, far2_in_ref, n1s, n1r, f1s, f1r, n2s, n2r, f2s, f2r, send_sem, recv_sem
):
    d, c, z = lax.axis_index("dp"), lax.axis_index("seq"), lax.axis_index("mp")
    mover = Mover(rows_ref, moved_ref, send_sem, recv_sem, count, tuple(range(SLOTS)), False)
    blocks = far2_ref.shape[0]
    barrier = pltpu.get_barrier_semaphore()
    waits = mover.greet(barrier)
    others = [(i, j) for i in range(blocks) for j in range(2) if i or j]
    for i, j in others:
        device = (lax.rem(d + i, blocks), lax.rem(c + j, 2), z)
        pl.semaphore_signal(barrier, 1, device_id=device, device_id_type=MESH)

    def by_sequence(ref, m):
        return sum(mine_ref[m, i] * ref[i] for i in range(SLOTS))

    part, each = near_ref.shape[4], far_ref.shape[5]
    for m in range(SLOTS):
        for kind, ref in enumerate((out_ref, up_z_ref, up_x_ref)):
            total = by_sequence(ref, m).astype(jnp.bfloat16)
            for n in range(count):
                near_ref[n, m, kind] = total[:, n * part : (n + 1) * part]
        for kind, ref in enumerate((up_out_ref, down_ref)):
            total = by_sequence(ref, m)
            for b in range(blocks):
                for n in range(2 * count):
                    at = (b * 2 * count + n) * each
                    far_ref[n, m, kind, b] = total[:, at : at + each].astype(jnp.bfloat16)
    pl.semaphore_wait(barrier, waits + len(others))

    def remote(src, dst, send, recv, *device):
        return pltpu.make_async_remote_copy(
            src_ref=src, dst_ref=dst, send_sem=send, recv_sem=recv, device_id=device, device_id_type=MESH
        )

    def arrival(ref, at, sem):
        pltpu.make_async_copy(ref.at[at], ref.at[at], sem.at[at]).wait()

    me = c * count + z
    copies = []
    for i in range(1, count):
        to = lax.rem(z + i, count)
        copies.append(remote(near_ref.at[to], near1_ref.at[z], n1s.at[i], n1r.at[z], d, c, to))
    column = [(j, i) for j in range(2) for i in range(count) if i or j]
    for j, i in column:
        to_c, to = lax.rem(c + j, 2), lax.rem(z + i, count)
        copies.append(remote(far_ref.at[to_c * count + to], far1_ref.at[me], f1s.at[j * count + i], f1r.at[me], d, to_c, to))
    for copy in copies:
        copy.start()
    for n in range(mover.pieces):
        mover.start(n)

    near = near_ref[z].astype(jnp.float32)
    for i in range(1, count):
        at = lax.rem(z + i, count)
        arrival(near1_ref, at, n1r)
        near = near + near1_ref[at].astype(jnp.float32)
    far = far_ref[me].astype(jnp.float32)
    for j, i in column:
        at = lax.rem(c + j, 2) * count + lax.rem(z + i, count)
        arrival(far1_ref, at, f1r)
        far = far + far1_ref[at].astype(jnp.float32)
    for a in range(ADAPT):
        near2_ref[a] = sum(picks_ref[m, a] * near[m] for m in range(SLOTS))
        for b in range(blocks):
            far2_ref[b, a] = sum(picks_ref[m, a] * far[m, :, b] for m in range(SLOTS))

    here = d * 2 + c
    copies2 = []
    for i, j in others:
        to_d, to_c = lax.rem(d + i, blocks), lax.rem(c + j, 2)
        copies2.append(
            remote(near2_ref.at[to_d * 2 + to_c], near2_in_ref.at[here], n2s.at[i * 2 + j], n2r.at[here], to_d, to_c, z)
        )
    for i in range(1, blocks):
        to = lax.rem(d + i, blocks)
        copies2.append(remote(far2_ref.at[to], far2_in_ref.at[d], f2s.at[i], f2r.at[d], to, c, z))
    for copy in copies2:
        copy.start()
    near2_in_ref[here] = near2_ref[here]
    far_sum = far2_ref[d]
    for i in range(1, blocks):
        at = lax.rem(d + i, blocks)
        arrival(far2_in_ref, at, f2r)
        far_sum = far_sum + far2_in_ref[at]
    far_out_ref[...] = far_sum
    for i, j in others:
        arrival(near2_in_ref, lax.rem(d + i, blocks) * 2 + lax.rem(c + j, 2), n2r)
    for half in range(2):
        near_out_ref[half] = sum(near2_in_ref[b * 2 + half] for b in range(blocks))
    for copy in copies + copies2:
        copy.wait_send()
    mover.finish()


def bc_back_kernel(
    g_ref, in_ref, halo_ref, taps_ref, q_ref, dx_ref, xu_ref, step_ref, rate_ref, bias_ref, decay_ref, mask_ref,
    out_ref, head_ref, tail_ref, g_rate_ref
):
    rows = in_ref.shape[1]
    pre = conv_rows(in_ref[0], halo_ref[0], taps_ref[...])
    sig = jax.nn.sigmoid(pre)
    g_ext = conv_rows_back(g_ref[0] * (sig * (1.0 + pre * (1.0 - sig))), taps_ref[...])
    out_ref[0] = g_ext[8:].astype(jnp.bfloat16)
    head_ref[0] = g_ext[:8]
    tail_ref[0] = g_ext[rows:]
    xu = xu_ref[0]
    flow = q_ref[0] - dx_ref[0] - step_ref[0] * xu
    later = lax.broadcasted_iota(jnp.int32, (rows, rows), 0) <= lax.broadcasted_iota(jnp.int32, (rows, rows), 1)
    g_log = ones_mm(later.astype(jnp.float32).astype(jnp.bfloat16), flow)
    sig = jax.nn.sigmoid(rate_ref[0] + bias_ref[...])
    g_rate_ref[0] = ((xu + g_log * decay_ref[...]) * mask_ref[0] * sig).astype(jnp.bfloat16)


def flip(v, mask, count):
    total = 0
    bit = 1
    while bit < count:
        b = lax.rem(v // bit, 2)
        total = total + (1 - b if mask & bit else b) * bit
        bit *= 2
    return total


def gather_kernel(
    nd, nz, wt_ref, x_ref, w_ref, rows_ref, local_sem, pair_sem, up_sem, down_sem, zrecv_sem, xsend_sem, xrecv_sem, ysend_sem,
    yrecv_sem, hsend_sem, hrecv_sem, asend_sem, arecv_sem
):
    d, c, z = lax.axis_index("dp"), lax.axis_index("seq"), lax.axis_index("mp")
    xn, yn = flip(d, 1, nd), flip(d, 2, nd)
    rows, part = wt_ref.shape[1], wt_ref.shape[2] // 2

    def remote(src, dst, send, recv, device):
        return pltpu.make_async_remote_copy(
            src_ref=src, dst_ref=dst, send_sem=send, recv_sem=recv, device_id=device, device_id_type=MESH
        )

    barrier = pltpu.get_barrier_semaphore()
    for cc in range(2):
        for r in range(nz):
            if cc or r:
                pl.semaphore_signal(barrier, 1, device_id=(d, flip(c, cc, 2), flip(z, r, nz)), device_id_type=MESH)
    for dd in (xn, yn):
        pl.semaphore_signal(barrier, 1, device_id=(dd, c, z), device_id_type=MESH)
    pl.semaphore_wait(barrier, 2 * nz - 1 + 2)

    def cols(s):
        return pl.ds(pl.multiple_of(s * part, 128), part)

    def area(dd, s):
        return w_ref.at[:, pl.ds(pl.multiple_of(dd * (2 * rows), 16), 2 * rows), cols(s)]

    def half_area(dd, s, h):
        return w_ref.at[:, pl.ds(pl.multiple_of(dd * (2 * rows) + h * rows, 16), rows), cols(s)]

    mine_area = w_ref.at[:, pl.ds(pl.multiple_of((2 * d + c) * rows, 16), rows), cols(z)]
    keep = pltpu.make_async_copy(wt_ref.at[:, :, cols(c)], mine_area, local_sem.at[0])
    pair = remote(wt_ref.at[:, :, cols(1 - c)], mine_area, pair_sem.at[0], pair_sem.at[1], (d, 1 - c, z))
    keep.start()
    pair.start()

    mover = Mover(x_ref, rows_ref, asend_sem, arecv_sem, nz, tuple(range(SLOTS)), True)
    for n in range(mover.pieces):
        mover.start(n)

    keep.wait()
    pair.wait()

    def spread(s):
        remote(area(d, s), area(d, s), xsend_sem.at[s], xrecv_sem.at[s], (xn, c, z)).start()
        remote(area(d, s), area(d, s), ysend_sem.at[s], yrecv_sem.at[s], (yn, c, z)).start()

    def send_up(s):
        @pl.when(z < nz - 1)
        def _():
            remote(area(d, s), area(d, s), up_sem.at[s], zrecv_sem.at[s], (d, c, z + 1)).start()

    def send_down(s):
        @pl.when(z > 0)
        def _():
            remote(area(d, s), area(d, s), down_sem.at[s], zrecv_sem.at[s], (d, c, z - 1)).start()

    def relay(s):
        remote(area(xn, s), area(xn, s), xsend_sem.at[s], xrecv_sem.at[s], (xn, c, z)).wait_recv()
        remote(half_area(xn, s, 0), half_area(xn, s, 0), hsend_sem.at[0, s], hrecv_sem.at[0, s], (yn, c, z)).start()
        remote(area(yn, s), area(yn, s), ysend_sem.at[s], yrecv_sem.at[s], (yn, c, z)).wait_recv()
        remote(half_area(yn, s, 1), half_area(yn, s, 1), hsend_sem.at[1, s], hrecv_sem.at[1, s], (xn, c, z)).start()

    send_up(z)
    send_down(z)
    spread(z)
    for r in range(1, nz + 1):
        if r < nz:
            @pl.when(z - r >= 0)
            def _():
                s = z - r
                remote(area(d, s), area(d, s), up_sem.at[s], zrecv_sem.at[s], (d, c, z)).wait_recv()
                send_up(s)
                spread(s)

            @pl.when(z + r < nz)
            def _():
                s = z + r
                remote(area(d, s), area(d, s), up_sem.at[s], zrecv_sem.at[s], (d, c, z)).wait_recv()
                send_down(s)
                spread(s)

        if r == 1:
            relay(z)
        else:
            @pl.when(z - r + 1 >= 0)
            def _():
                relay(z - r + 1)

            @pl.when(z + r - 1 < nz)
            def _():
                relay(z + r - 1)

    mover.finish()
    for s in range(nz):
        remote(half_area(d, s, 0), half_area(d, s, 0), hsend_sem.at[0, s], hrecv_sem.at[0, s], (yn, c, z)).wait()
        remote(half_area(d, s, 1), half_area(d, s, 1), hsend_sem.at[1, s], hrecv_sem.at[1, s], (xn, c, z)).wait()
        remote(area(d, s), area(d, s), xsend_sem.at[s], xrecv_sem.at[s], (xn, c, z)).wait_send()
        remote(area(d, s), area(d, s), ysend_sem.at[s], yrecv_sem.at[s], (yn, c, z)).wait_send()

        @pl.when(jnp.logical_and(s <= z, z < nz - 1))
        def _():
            remote(area(d, s), area(d, s), up_sem.at[s], zrecv_sem.at[s], (d, c, z)).wait_send()

        @pl.when(jnp.logical_and(s >= z, z > 0))
        def _():
            remote(area(d, s), area(d, s), down_sem.at[s], zrecv_sem.at[s], (d, c, z)).wait_send()


def gather(wt, x, nd, nz):
    half = wt.shape[2] // 2
    dma = pltpu.SemaphoreType.DMA
    anywhere = pl.BlockSpec(memory_space=pl.ANY)
    return pl.pallas_call(
        functools.partial(gather_kernel, nd, nz),
        name="gather",
        out_shape=(
            jax.ShapeDtypeStruct((2, wt.shape[1] * 2 * nd, half * nz), wt.dtype),
            jax.ShapeDtypeStruct((SLOTS, x.shape[1] // 4, x.shape[2] * nz), x.dtype),
        ),
        in_specs=[anywhere] * 2,
        out_specs=(anywhere,) * 2,
        scratch_shapes=[
            dma((1,)), dma((2,)), dma((nz,)), dma((nz,)), dma((nz,)), dma((nz,)), dma((nz,)), dma((nz,)), dma((nz,)),
            dma((2, nz)), dma((2, nz)), dma((4 * SLOTS,)), dma((SLOTS, nz)),
        ],
        compiler_params=pltpu.CompilerParams(collective_id=1, has_side_effects=True),
    )(wt, x)


def block(shape, index):
    return pl.BlockSpec(shape, index)


def call(kernel, name, grid, ins, outs, scratch, flops, size, comm=None, load=None):
    params = dict(vmem_limit_bytes=VMEM_LIMIT)
    kernel = functools.partial(kernel, grid)
    ins, outs, scratch = list(ins), list(outs), list(scratch)
    if load is not None:
        rows, result, first, to_rows = load
        count = lax.axis_size("mp")
        kernel = functools.partial(carried_by, kernel, count, first, to_rows, len(ins), len(outs))
        ins.append((rows, pl.BlockSpec(memory_space=pl.ANY)))
        outs.append((result, pl.BlockSpec(memory_space=pl.ANY)))
        sends = 4 * SLOTS if to_rows else count * len(first)
        scratch += [pltpu.SemaphoreType.DMA((sends,)), pltpu.SemaphoreType.DMA((SLOTS, 4))]
    if comm is not None:
        params.update(collective_id=comm, has_side_effects=True)
    return pl.pallas_call(
        kernel,
        name=name,
        grid=grid,
        in_specs=[s for _, s in ins],
        out_specs=[s for _, s in outs],
        out_shape=[s for s, _ in outs],
        scratch_shapes=scratch,
        compiler_params=pltpu.CompilerParams(**params),
        cost_estimate=pl.CostEstimate(flops=flops, bytes_accessed=size, transcendentals=0),
    )(*[a for a, _ in ins])


def skip_grid(kernel):
    return lambda grid, *refs: kernel(*refs)


def after(value, *deps):
    return lax.optimization_barrier((value,) + deps)[0]


def finish(grads, mine, picks, rows, moved, count, blocks):
    dma, f32, bf16 = pltpu.SemaphoreType.DMA, jnp.float32, jnp.bfloat16
    anywhere, vmem = pl.BlockSpec(memory_space=pl.ANY), pl.BlockSpec(memory_space=pltpu.VMEM)
    smem = pl.BlockSpec(memory_space=pltpu.SMEM)
    near_shape = (3, R, grads[0].shape[2] // count)
    far_shape = (2, R, D // (2 * blocks * count))
    near_all = (count, SLOTS) + near_shape
    far_all = (2 * count, SLOTS, 2, blocks) + far_shape[1:]
    return pl.pallas_call(
        functools.partial(finish_kernel, count),
        name="finish",
        in_specs=[vmem] * 5 + [smem, smem, anywhere],
        out_specs=[anywhere, vmem, vmem],
        out_shape=[moved, jax.ShapeDtypeStruct((2,) + near_shape, f32), jax.ShapeDtypeStruct((ADAPT,) + far_shape, f32)],
        scratch_shapes=[
            pltpu.VMEM(near_all, bf16), pltpu.VMEM(far_all, bf16), pltpu.VMEM(near_all, bf16), pltpu.VMEM(far_all, bf16),
            pltpu.VMEM((ADAPT,) + near_shape, f32), pltpu.VMEM((2 * blocks,) + near_shape, f32),
            pltpu.VMEM((blocks, ADAPT) + far_shape, f32), pltpu.VMEM((blocks, ADAPT) + far_shape, f32), dma((count,)), dma((count,)),
            dma((2 * count,)), dma((2 * count,)), dma((2 * blocks,)), dma((2 * blocks,)), dma((blocks,)), dma((blocks,)),
            dma((count * SLOTS,)), dma((SLOTS, 4)),
        ],
        compiler_params=pltpu.CompilerParams(vmem_limit_bytes=VMEM_LIMIT, collective_id=5, has_side_effects=True),
    )(*grads, mine, picks, rows)


def fast_body(
    x_in, cotangent, lengths, adapter_ids, norm_gain, w_zx, w_bc, w_dt, dt_bias, a_log, d_skip, conv_x, conv_bc,
    gate_gain, w_out, in_down, in_up, out_down, out_up
):
    bf16, f32 = jnp.bfloat16, jnp.float32
    micros, _, seg, feats = x_in.shape
    nz, nd = lax.axis_size("mp"), lax.axis_size("dp")
    core, z = lax.axis_index("seq"), lax.axis_index("mp")
    own = seg // nz
    tokens = 2 * own
    heads = dt_bias.shape[0] * nz // 2
    chan = heads * P_SIZE
    part = chan // nz
    groups = heads // HG
    wide = HG * P_SIZE
    blocks = tokens // Q
    each = D // (nd * 2 * nz)

    def other(v):
        return lax.ppermute(v, "seq", [(0, 1), (1, 0)])

    def pair_cat(mine, theirs, axis):
        return jnp.where(
            core == 0, jnp.concatenate([mine, theirs], axis), jnp.concatenate([theirs, mine], axis)
        )

    def halves(v, axis):
        v = v.reshape(v.shape[:axis] + (2, v.shape[axis] // 2) + v.shape[axis + 1 :])
        return (
            lax.dynamic_index_in_dim(v, core, axis, False),
            lax.dynamic_index_in_dim(v, 1 - core, axis, False),
        )

    line = part
    bc_piece = lax.dynamic_slice_in_dim(w_bc, z * (w_bc.shape[0] // nz), w_bc.shape[0] // nz, 0)
    pairs = jnp.stack([jnp.transpose(in_down, (0, 2, 1)), out_up.reshape(ADAPT, R, -1)], 1)
    same = [bc_piece, pairs]
    sized = [halves(jnp.transpose(in_up, (1, 0, 2)), 2), halves(out_down.T, 1), halves(w_dt.T, 0)]
    packs = []
    for k in range(2):
        packs.append(jnp.concatenate([v.reshape(-1, line) for v in [s[k] for s in sized] + same], 0))
    bounds = [0]
    for v in [s[0] for s in sized] + same:
        bounds.append(bounds[-1] + v.size // line)
    pack = pair_cat(packs[0][None], other(packs[1])[None], 0)
    params = jnp.concatenate([dt_bias, a_log, d_skip, gate_gain, conv_x.reshape(-1)])
    params = lax.all_gather(params, "mp")
    pack = lax.all_gather(pack, ("dp", "mp")).reshape((nd, nz) + pack.shape)
    zx_weight, x_rows = gather(jnp.transpose(w_zx, (1, 0, 2)), x_in[:, 0], nd, nz)
    out_mine, out_theirs = halves(after(w_out, x_rows), 0)
    out_pair = pair_cat(out_mine, other(out_theirs), 1)
    out_all = lax.all_gather(out_pair, ("dp", "mp")).reshape((nd, nz) + out_pair.shape)
    dt_rows = pack[:, :, :, bounds[2] : bounds[3]].reshape(nd, nz, 2, heads // nz, -1)
    dt_weight = jnp.transpose(dt_rows, (1, 3, 0, 2, 4)).reshape(heads, D)
    dt_weight = jnp.pad(dt_weight, ((0, 128 - heads), (0, 0)))
    bc_rows = pack[:, :, :, bounds[3] : bounds[4]].reshape(nd, nz, 2, -1, 2 * NS)
    bc_weight = jnp.transpose(bc_rows, (0, 2, 1, 3, 4)).reshape(D, 2 * NS)
    bc_half = lax.dynamic_slice_in_dim(bc_weight, core * NS, NS, 1)
    dt_weight = dt_weight.T
    tail_weight = jnp.concatenate([bc_half, dt_weight], 1)
    first_weight = jnp.concatenate([bc_weight, dt_weight], 1)

    hl = dt_bias.shape[0]

    def own_part(v):
        v = v.reshape(v.shape[0], 2, v.shape[1] // 2)
        return lax.dynamic_index_in_dim(v, core, 1, False).reshape(-1)

    bias = jnp.pad(own_part(params[:, :hl]), (0, 128 - heads))[None]
    rate = jnp.pad(-jnp.exp(own_part(params[:, hl : 2 * hl])), (0, 128 - heads))[None]
    skip = jnp.repeat(own_part(params[:, 2 * hl : 3 * hl]), P_SIZE)[None]
    width = gate_gain.shape[0]
    gain = own_part(params[:, 3 * hl : 3 * hl + width])[None]
    taps = params[:, 3 * hl + width :].reshape(nz, KC, 2, part)
    taps = jnp.transpose(lax.dynamic_index_in_dim(taps, core, 2, False), (1, 0, 2)).reshape(KC, chan)

    order = jnp.arange(micros)
    runs = run_of(order, z)
    sequence, chunk = runs // nz, lax.rem(runs, nz)
    lengths = jnp.take(lengths[:, 0], sequence)[:, None]
    ids = jnp.take(adapter_ids[:, 0], sequence)
    all_pos = (chunk * tokens)[:, None] + jnp.arange(tokens)
    own_pos = (chunk * tokens)[:, None] + core * own + jnp.arange(own)
    enters = (order == nz - 1 - z)[:, None, None]
    leaves = (order == nz - 2 - z)[:, None, None]
    forward_edge = [(i, i + 1) for i in range(nz - 1)]
    backward_edge = [(i + 1, i) for i in range(nz - 1)]

    m3 = lambda m, g: (m, 0, g)
    m0 = lambda m, g: (m, 0, 0)
    z2 = lambda m, g: (0, 0)
    shape = jax.ShapeDtypeStruct

    def per_token(width, index=m3):
        return block((1, tokens, width), index)

    chan_block = per_token(wide)
    halo_block = block((1, HALO, wide), m3)
    taps_block = block((KC, wide), lambda m, g: (0, g))
    line_block = block((1, wide), lambda m, g: (0, g))
    state_block = block((1, NS, wide), m3)
    bc_block = per_token(2 * NS, m0)
    bc_halo = block((1, HALO, 2 * NS), m0)
    bc_taps = block((KC, 2 * NS), z2)
    bc_edge = block((1, 8, 2 * NS), m0)
    one_col = per_token(1, m0)
    sums = per_token(128, m0)
    lanes_block = block((1, 1, 2 * HG, tokens), lambda m, g: (m, g, 0, 0))
    head_line = block((1, 128), z2)
    edge_block = block((1, 8, wide), m3)
    tok_f32 = shape((micros, tokens, chan), f32)
    tok_b16 = shape((micros, tokens, chan), bf16)
    state_f32 = shape((micros, NS, chan), f32)
    bc_f32 = shape((micros, tokens, 2 * NS), f32)
    sums_f32 = shape((micros, tokens, 128), f32)
    edge_f32 = shape((micros, 8, chan), f32)
    act_bytes = tokens * chan * 4
    dma = pltpu.SemaphoreType.DMA
    line_scratch = [pltpu.VMEM((groups, NS, wide), f32), pltpu.VMEM((2 * groups, NS, wide), f32)] + [dma((groups,))] * 2
    scan_grid = (micros, groups)

    x_rows = x_rows.astype(f32)
    inv_rms = lax.rsqrt(jnp.mean(x_rows * x_rows, axis=-1, keepdims=True) + eps)
    low_own = (x_rows * inv_rms * norm_gain).astype(bf16)
    mask_own = (own_pos < lengths).astype(f32)[..., None]
    mask = (all_pos < lengths).astype(f32)[..., None]
    picks = (adapter_ids == jnp.arange(ADAPT)).astype(f32)
    tall = bounds[2]
    factors = pl.pallas_call(
        pick_kernel,
        name="pick",
        grid_spec=pltpu.PrefetchScalarGridSpec(
            num_scalar_prefetch=1,
            grid=(micros, nz),
            in_specs=[block((1, 1, 1, tall, part), lambda m, n, k: (k[m] // 2, n, lax.rem(k[m], 2), 0, 0))],
            out_specs=block((1, 1, tall, part), lambda m, n, k: (m, n, 0, 0)),
        ),
        out_shape=shape((micros, nz, tall, part), bf16),
    )(ids, pack)
    per = 2 * R * each // line
    wide_rows = [lax.dynamic_slice_in_dim(pack, bounds[4] + per * ids[m], per, 3) for m in range(micros)]
    wide_rows = jnp.stack(wide_rows).reshape(micros, nd, nz, 2, 2, R, each)
    wide_rows = jnp.transpose(wide_rows, (4, 0, 5, 1, 3, 2, 6)).reshape(2, micros, R, D)

    def wide_block(kind, width, index):
        return block((1, micros, R, width), lambda m, g: (kind, 0, 0, index(g)))

    def every(width, index=None):
        if index is None:
            return pl.BlockSpec((micros, tokens, width), lambda m, g: (0, 0, 0), pipeline_mode=pl.Buffered(1))
        return block((micros, tokens, width), index)

    by_step = lambda m, g: (0, 0, g)
    rank_b16 = shape((micros, tokens, 2 * R), bf16)
    half_steps = chan // part
    steps = 2 * half_steps
    cot = cotangent[:, 0]
    early = 1
    hbm = pl.BlockSpec(memory_space=pl.ANY)
    pair_scratch = [pltpu.VMEM((micros, tokens, D), bf16), dma((4,))]
    xin, z_in, bcin, rate_in, lr, low, cot_early = call(
        project_kernel, "project", (1, steps),
        [(low_own, hbm), (zx_weight, block((1, D, part), lambda m, g: (1 - g // half_steps, 0, g % half_steps))),
         (first_weight, block((D, 2 * NS + 128), z2)), (wide_rows, wide_block(0, D, lambda g: 0)),
         (factors, block((micros, 1, R, part), lambda m, g: (0, g % half_steps, 1 - g // half_steps, 0)))],
        [(tok_b16, every(part, lambda m, g: (0, 0, jnp.minimum(g, half_steps - 1)))),
         (tok_f32, every(part, lambda m, g: (0, 0, jnp.maximum(g - half_steps, 0)))),
         (shape((micros, tokens, 2 * NS), bf16), every(2 * NS)), (sums_f32, every(128)), (rank_b16, every(2 * R)), (shape((micros, tokens, D), bf16), hbm)],
        pair_scratch, 4 * tokens * D * chan, act_bytes * 4, 2, (cot, shape((early, own, D), bf16), tuple(range(early)), True),
    )
    tail = jnp.concatenate([xin[:, tokens - HALO :], bcin[:, tokens - HALO :]], axis=2)
    goes = jnp.sum(jnp.where(leaves, tail, 0), axis=0, dtype=bf16)
    halo = jnp.where(enters, lax.ppermute(goes, "mp", forward_edge)[None], jnp.pad(tail[:-1], ((1, 0), (0, 0), (0, 0))))
    halo, bchalo = halo[..., :chan], halo[..., chan:]
    step, cum, lanes, bc = call(
        skip_grid(prep_kernel), "prep", (micros, 1),
        [(rate_in, sums), (bias, head_line), (rate, head_line), (mask, one_col), (bcin, bc_block), (bchalo, bc_halo),
         (conv_bc, bc_taps)],
        [(sums_f32, sums), (sums_f32, sums),
         (shape((micros, groups, 2 * HG, tokens), f32), block((1, groups, 2 * HG, tokens), lambda m, g: (m, 0, 0, 0))),
         (bc_f32, bc_block)],
        [], tokens * Q * 128 * 6, tokens * 128 * 24,
    )
    mixed, square, state, end_state, cot_late = call(
        forward_kernel, "ssd_forward", scan_grid,
        [(xin, chan_block), (halo, halo_block), (taps, taps_block), (bc, bc_block), (cum, sums), (step, sums),
         (lanes, lanes_block), (skip, line_block), (z_in, chan_block)],
        [(tok_f32, chan_block), (sums_f32, sums), (state_f32, state_block), (state_f32, state_block)],
        [pltpu.VMEM((blocks, Q, Q), f32), pltpu.VMEM((2, blocks, NS, Q), bf16), *line_scratch],
        6 * tokens * Q * chan * 2, act_bytes * 3, 3, (cot, shape((micros - early, own, D), bf16), tuple(range(early, micros)), True),
    )

    def reduce_rows(v):
        theirs = lax.dynamic_slice_in_dim(v, (1 - core) * own, own, 1)
        return lax.dynamic_slice_in_dim(v, core * own, own, 1) + other(theirs)

    cols = out_all.shape[3]
    gb_own = jnp.concatenate([cot_early, cot_late], 0) * mask_own.astype(bf16)
    part_block = every(part, by_step)
    gs, dots, rg, gb = call(
        gs_kernel, "gs", (1, nz),
        [(gb_own, hbm), (out_all, block((nd, 1, part, cols), lambda m, g: (0, g, 0, 0))), (wide_rows, wide_block(1, D, lambda g: 0)),
         (factors, block((micros, 1, R, part), lambda m, g: (0, g, 2, 0))), (mixed, part_block), (z_in, part_block),
         (gain, block((1, part), lambda m, g: (0, g)))],
        [(tok_f32, part_block), (sums_f32, every(128)), (rank_b16, every(2 * R)), (shape((micros, tokens, D), bf16), hbm)],
        pair_scratch, 6 * tokens * D * chan, act_bytes * 15, 7,
    )
    both = jnp.stack([jnp.sum(square, axis=-1), jnp.sum(dots, axis=-1)])
    both = (both + other(both)) / DI
    inv_gate = lax.rsqrt(both[0] + eps)[..., None]
    coef = inv_gate**3 * both[1][..., None]
    dy, gz, scaled, lloc, q = call(
        gate_back_kernel, "gate_back", scan_grid,
        [(gs, chan_block), (mixed, chan_block), (z_in, chan_block), (inv_gate, one_col), (coef, one_col), (gain, line_block),
         (bc, bc_block), (cum, sums)],
        [(tok_f32, chan_block), (tok_b16, chan_block), (tok_b16, chan_block), (state_f32, state_block), (sums_f32, sums)],
        [pltpu.VMEM((2, NS, tokens), bf16)], 6 * tokens * NS * chan, act_bytes * 5,
    )
    step_cols = every(cols, by_step)
    rank_scratch = [pltpu.VMEM((micros, tokens, 2 * R), bf16)] + [pltpu.VMEM((micros, 2 * R, tokens), bf16)] * 2
    rank_cols = block((micros, R, cols), by_step)
    partial, g_up_out, g_out = call(
        branch_kernel, "branch", (1, nd),
        [(scaled, every(chan)), (out_all, block((1,) + out_all.shape[1:], lambda m, g: (g, 0, 0, 0))),
         (factors, block((micros, nz, R, part), lambda m, g: (0, 0, 2, 0))), (wide_rows, wide_block(1, cols, lambda g: g)),
         (rg, every(2 * R)), (gb, step_cols)],
        [(shape((micros, tokens, D), f32), step_cols), (shape((micros, R, D), f32), rank_cols),
         (shape((micros, R, chan), f32), block((micros, R, chan // nd), by_step))],
        rank_scratch, 6 * tokens * D * chan, act_bytes * 12,
    )
    out_rows = (x_rows + mask_own * reduce_rows(partial)).astype(bf16)

    first_slots, last_slots = tuple(range(micros - 1)), (micros - 1,)

    def last_first(spec):
        index = spec.index_map
        return block(spec.block_shape, lambda m, g: index(micros - 1 - m, g))

    ins = [(dy, chan_block), (xin, chan_block), (halo, halo_block), (taps, taps_block), (bc, bc_block), (cum, sums), (step, sums),
           (lanes, lanes_block), (skip, line_block), (state, state_block), (lloc, state_block), (end_state, state_block)]
    outs = [(tok_b16, chan_block), (edge_f32, edge_block), (edge_f32, edge_block), (bc_f32, bc_block), (sums_f32, sums),
            (sums_f32, sums)]
    gx, head, tail, gbc, xu, dx, out_first = call(
        scan_back_kernel, "ssd_back", scan_grid,
        [(a, last_first(s)) for a, s in ins], [(a, last_first(s)) for a, s in outs],
        [pltpu.VMEM((blocks, Q, Q), f32), pltpu.VMEM((blocks, Q, Q), f32), pltpu.VMEM((2, blocks, NS, Q), bf16),
         pltpu.VMEM((2, blocks, NS, Q), bf16), *line_scratch],
        12 * tokens * Q * chan * 2, act_bytes * 3, 4, (out_rows, shape((micros, seg, feats), bf16), first_slots, False),
    )
    gbc = gbc + other(gbc)
    edge_bc = shape((micros, 8, 2 * NS), f32)
    gbc, bhead, btail, g_rate = call(
        skip_grid(bc_back_kernel), "bc_back", (micros, 1),
        [(gbc, bc_block), (bcin, bc_block), (bchalo, bc_halo), (conv_bc, bc_taps), (q, sums), (dx, sums), (xu, sums),
         (step, sums), (rate_in, sums), (bias, head_line), (rate, head_line), (mask, one_col)],
        [(shape((micros, tokens, 2 * NS), bf16), bc_block), (edge_bc, bc_edge), (edge_bc, bc_edge),
         (shape((micros, tokens, 128), bf16), sums)],
        [], tokens * tokens * 128 * 6, tokens * 2 * NS * 8,
    )
    head = jnp.concatenate([head, bhead], 2)
    goes = lax.ppermute(jnp.sum(jnp.where(enters, head, 0), axis=0), "mp", backward_edge)
    back = jnp.pad(jnp.where(enters, 0, head)[1:], ((0, 1), (0, 0), (0, 0))) + jnp.where(leaves, goes[None], 0)
    tail = jnp.concatenate([tail, btail], 2).at[:, 8 - (KC - 1) :].add(back[:, 8 - (KC - 1) :]).astype(bf16)
    gx = lax.dynamic_update_slice_in_dim(gx, tail[..., :chan], tokens - 8, 1)
    gbc = lax.dynamic_update_slice_in_dim(gbc, tail[..., chan:], tokens - 8, 1)
    tail = jnp.concatenate([lax.dynamic_slice_in_dim(gbc, core * NS, NS, 2), g_rate], 2)
    wide_cols = D // nz
    g_low, g_up_z, g_up_x, g_down, out_last = call(
        unproject_kernel, "unproject", (1, nz),
        [(gz, every(chan)), (gx, every(chan)), (tail, every(NS + 128)),
         (zx_weight, block((2, wide_cols, chan), lambda m, g: (0, g, 0))), (tail_weight, block((wide_cols, NS + 128), lambda m, g: (g, 0))),
         (factors, block((micros, nz, 2 * R, part), lambda m, g: (0, 0, 0, 0))), (wide_rows, wide_block(0, wide_cols, lambda g: g)),
         (lr, every(2 * R)), (low, every(wide_cols, by_step))],
        [(shape((micros, tokens, D), f32), every(wide_cols, by_step)), (shape((micros, R, chan), f32), block((micros, R, part), by_step)),
         (shape((micros, R, chan), f32), block((micros, R, part), by_step)),
         (shape((micros, R, D), f32), block((micros, R, wide_cols), by_step))],
        rank_scratch, 12 * tokens * D * chan, act_bytes * 9, 6, (out_rows[-1:], shape((micros, seg, feats), bf16), last_slots, False),
    )
    gn = reduce_rows(g_low) * norm_gain
    delta = inv_rms * gn - x_rows * (inv_rms**3 * jnp.mean(gn * x_rows, axis=-1, keepdims=True))
    held_runs = jnp.arange(micros)[:, None] * nz + 2 * core + jnp.arange(2)
    in_last = place_of(held_runs)[1] == micros - 1
    in_last = jnp.repeat(in_last, tokens, axis=1)[..., None]
    out = jnp.where(in_last, out_last, out_first)[:, None]
    mine = (sequence == jnp.arange(micros)[:, None]).astype(f32)

    delta, near, far = finish(
        [g_out, g_up_z, g_up_x, g_up_out, g_down], mine, picks, delta.astype(bf16), shape((micros, seg, feats), bf16), nz, nd
    )
    grad = cotangent.astype(f32) + delta[:, None].astype(f32)
    g_out_down = jnp.transpose(near[:, 0], (0, 2, 1)).reshape(2 * part, R)
    g_in_up = jnp.transpose(near[:, 1:], (2, 1, 0, 3)).reshape(R, 2, 2 * part)
    g_out_up = far[:, 0].reshape(ADAPT * R, each)
    g_in_down = jnp.transpose(far[:, 1], (0, 2, 1))
    return (out, grad, g_in_down, g_in_up, g_out_down, g_out_up)


def solution(mesh):
    in_specs = (
        P(None, "dp", "seq", "mp"),
        P(None, "dp", "seq", "mp"),
        P(None, "dp"),
        P(None, "dp"),
        P(),
        P(("dp", "seq"), None, "mp"),
        P(("dp", "seq"), None),
        P(("dp", "seq"), "mp"),
        P("mp"),
        P("mp"),
        P("mp"),
        P(None, "mp"),
        P(),
        P("mp"),
        P("mp", ("dp", "seq")),
        P(None, ("dp", "seq", "mp"), None),
        P(("dp", "seq"), None, "mp"),
        P("mp", ("dp", "seq")),
        P(None, ("dp", "seq", "mp")),
    )
    out_specs = (
        P(None, "dp", "seq", "mp"),
        P(None, "dp", "seq", "mp"),
        P(None, ("dp", "seq", "mp"), None),
        P(("dp", "seq"), None, "mp"),
        P("mp", ("dp", "seq")),
        P(None, ("dp", "seq", "mp")),
    )
    sizes = dict(mesh.shape)
    by_chip = (
        sizes["seq"] == 2
        and sizes["dp"] * 2 == ADAPT
        and sizes["mp"] == SLOTS + 1
    )
    return jax.shard_map(fast_body if by_chip else body, mesh=mesh, in_specs=in_specs, out_specs=out_specs, check_vma=False)
```

```python
import functools

import jax
import jax.numpy as jnp
from jax import lax
from jax.experimental import pallas as pl
from jax.experimental.pallas import tpu as pltpu
from jax.sharding import PartitionSpec as P

D = 2048
P_SIZE = 64
NS = 128
KC = 4
Q = 256
R = 16
ADAPT = 8
DI = 4096
HG = 4
HALO = 16
SLOTS = 3


eps = 1e-05
precise = lax.Precision.HIGHEST
VMEM_LIMIT = 56 * 1024 * 1024


def shifted(array, axis, by):
    size = lax.axis_size(axis)
    pairs = [(i, i + by) for i in range(size) if 0 <= i + by < size]
    return lax.ppermute(array, axis, pairs)


def entering(part, axis, combine, identity, reverse):
    count = lax.axis_size(axis)
    place = lax.axis_index(axis)
    ahead = count - 1 - place if reverse else place
    gathered = jax.tree.map(lambda a: lax.all_gather(a, axis), part)
    state = jax.tree.map(lambda a, e: jnp.zeros_like(a) + jnp.asarray(e, a.dtype), part, identity)

    def one(hop, state):
        source = count - 1 - hop if reverse else hop
        return combine(
            state, jax.tree.map(lambda a: lax.dynamic_index_in_dim(a, source, 0, False), gathered)
        )

    return lax.fori_loop(0, ahead, one, state)


def silu_grad(value):
    sigmoid_val = jax.nn.sigmoid(value)
    return sigmoid_val * (1.0 + value * (1.0 - sigmoid_val))


def block_step(carry_state, pieces):
    x_part, b_part, c_part, log_part, step_part = pieces
    length = log_part.shape[0]
    cumulative = jnp.cumsum(log_part, axis=0)
    causal = jnp.arange(length)[:, None] >= jnp.arange(length)[None, :]
    spread = cumulative[:, None, :] - cumulative[None, :, :]
    decay_mat = jnp.exp(jnp.where(causal[:, :, None], spread, -10000.0))
    scores = jnp.dot(c_part, b_part.T, precision=precise)
    mixing = scores[:, :, None] * decay_mat * step_part[None, :, :]
    inner_out = jnp.einsum("tsh,shp->thp", mixing, x_part, precision=precise)
    carried = jnp.exp(cumulative)[:, :, None] * jnp.einsum(
        "tn,hpn->thp", c_part, carry_state, precision=precise
    )
    weights = jnp.exp(cumulative[-1][None, :] - cumulative) * step_part
    update = jnp.einsum("sh,shp,sn->hpn", weights, x_part, b_part, precision=precise)
    new_state = jnp.exp(cumulative[-1])[:, None, None] * carry_state + update
    return (new_state, inner_out + carried)


def local_scan(x_heads, b_rows, c_rows, log_rows, step_rows):
    seg_rows = x_heads.shape[0]
    blocks = seg_rows // Q

    def blocked(tensor):
        return tensor.reshape((blocks, Q) + tensor.shape[1:])

    init_state = jnp.zeros((x_heads.shape[1], x_heads.shape[2], b_rows.shape[1]), jnp.float32)
    final_state, outputs = lax.scan(
        block_step,
        init_state,
        (blocked(x_heads), blocked(b_rows), blocked(c_rows), blocked(log_rows), blocked(step_rows)),
    )
    return (outputs.reshape(x_heads.shape), final_state, jnp.sum(log_rows, axis=0))


def incoming(c_rows, log_rows, state_in):
    cumulative = jnp.cumsum(log_rows, axis=0)
    return jnp.exp(cumulative)[:, :, None] * jnp.einsum(
        "tn,hpn->thp", c_rows, state_in, precision=precise
    )


def compose(earlier, later):
    return (later[0] * earlier[0], later[1] + later[0][..., None, None] * earlier[1])


def fetch_weights(w_zx, w_bc, w_dt, w_out, in_up, out_down):
    return (
        lax.all_gather(w_zx, ("dp", "seq"), axis=0, tiled=True),
        lax.all_gather(w_bc, ("dp", "seq"), axis=0, tiled=True),
        lax.all_gather(w_dt, ("dp", "seq"), axis=0, tiled=True),
        lax.all_gather(w_out, ("dp", "seq"), axis=1, tiled=True),
        lax.all_gather(in_up, ("dp", "seq"), axis=0, tiled=True),
        lax.all_gather(out_down, ("dp", "seq"), axis=1, tiled=True),
    )


def reduce_adapters(grads):
    near_sums = (
        lax.psum_scatter(grads[1], ("dp", "seq"), scatter_dimension=0, tiled=True),
        lax.psum_scatter(grads[2], ("dp", "seq"), scatter_dimension=1, tiled=True),
    )
    wide_sums = (
        lax.psum_scatter(grads[0], ("dp", "seq", "mp"), scatter_dimension=1, tiled=True),
        lax.psum_scatter(grads[3], ("dp", "seq", "mp"), scatter_dimension=1, tiled=True),
    )
    return (wide_sums[0], near_sums[0], near_sums[1], wide_sums[1])


def body(
    x_in,
    cotangent,
    lengths,
    adapter_ids,
    norm_gain,
    w_zx,
    w_bc,
    w_dt,
    dt_bias,
    a_log,
    d_skip,
    conv_x,
    conv_bc,
    gate_gain,
    w_out,
    in_down,
    in_up,
    out_down,
    out_up,
):
    micro_count, slot_count, seg_len, model_part = x_in.shape
    head_local = dt_bias.shape[0]
    inner_local = head_local * P_SIZE
    wide_down, wide_up = (
        lax.all_gather(in_down, ("dp", "seq", "mp"), axis=1, tiled=True),
        lax.all_gather(out_up, ("dp", "seq", "mp"), axis=1, tiled=True),
    )
    wide_down = wide_down.astype(jnp.float32)
    wide_up = wide_up.astype(jnp.float32)
    conv_taps = jnp.concatenate([conv_x, conv_bc], axis=1)
    decay_rate = -jnp.exp(a_log)
    positions = lax.axis_index("seq") * seg_len + jnp.arange(seg_len)
    feature_start = lax.axis_index("mp") * model_part
    scan_local = jax.vmap(local_scan)
    incoming_map = jax.vmap(incoming)
    gathered = None
    outputs = []
    x_grads = []
    running = None
    for batch_index in range(micro_count):
        gathered = fetch_weights(w_zx, w_bc, w_dt, w_out, in_up, out_down)
        zx_weight, bc_weight, dt_weight, out_weight, up_in, down_out = gathered
        rows_own = x_in[batch_index]
        cot_own = cotangent[batch_index]
        rows_full, cot_full = (
            lax.all_gather(rows_own, "mp", axis=2, tiled=True),
            lax.all_gather(cot_own, "mp", axis=2, tiled=True),
        )
        rows_value = rows_full.astype(jnp.float32)
        inv_rms = lax.rsqrt(jnp.mean(rows_value * rows_value, axis=-1, keepdims=True) + eps)
        normed = rows_value * inv_rms * norm_gain
        normed_low = normed.astype(jnp.bfloat16)
        normed_value = normed_low.astype(jnp.float32)
        select = jax.nn.one_hot(adapter_ids[batch_index], ADAPT, dtype=jnp.float32)
        down_sel = jnp.einsum("sa,adr->sdr", select, wide_down, precision=precise)
        up_sel = jnp.einsum(
            "sa,arcf->srcf",
            select,
            up_in.astype(jnp.float32).reshape(ADAPT, R, 2, inner_local),
            precision=precise,
        )
        low_rank = jnp.einsum("std,sdr->str", normed_value, down_sel, precision=precise)
        proj_zx = jnp.einsum(
            "std,dcf->stcf", normed_low, zx_weight, preferred_element_type=jnp.float32
        )
        proj_zx = proj_zx + jnp.einsum("str,srcf->stcf", low_rank, up_sel, precision=precise)
        proj_bc = jnp.einsum(
            "std,dn->stn", normed_low, bc_weight, preferred_element_type=jnp.float32
        )
        proj_dt = jnp.einsum(
            "std,dh->sth", normed_low, dt_weight, preferred_element_type=jnp.float32
        )
        gate_in = proj_zx[:, :, 0]
        conv_in = jnp.concatenate(
            [proj_zx[:, :, 1].astype(jnp.bfloat16), proj_bc.astype(jnp.bfloat16)], axis=-1
        )
        earlier_rows = shifted(conv_in[:, seg_len - (KC - 1) :], "seq", 1)
        extended = jnp.concatenate([earlier_rows, conv_in], axis=1).astype(jnp.float32)
        conv_pre = sum(
            (
                conv_taps[tap_index] * extended[:, tap_index : tap_index + seg_len]
                for tap_index in range(KC)
            )
        )
        conv_out = jax.nn.silu(conv_pre)
        x_heads = conv_out[..., :inner_local].reshape(slot_count, seg_len, head_local, P_SIZE)
        b_rows = conv_out[..., inner_local : inner_local + NS]
        c_rows = conv_out[..., inner_local + NS :]
        mask_rows = (positions[None, :] < lengths[batch_index][:, None]).astype(jnp.float32)
        rate_in = proj_dt + dt_bias
        step_rows = jax.nn.softplus(rate_in) * mask_rows[..., None]
        log_rows = step_rows * decay_rate
        (plain_out, state_local, log_total), scan_back = jax.vjp(
            scan_local, x_heads, b_rows, c_rows, log_rows, step_rows
        )
        factor = jnp.exp(log_total)
        identity = (jnp.ones_like(factor), jnp.zeros_like(state_local))
        state_in = entering((factor, state_local), "seq", compose, identity, False)[1]
        from_state, state_back = jax.vjp(incoming_map, c_rows, log_rows, state_in)
        mixed_heads = plain_out + from_state + d_skip[:, None] * x_heads
        mixed_flat = mixed_heads.reshape(slot_count, seg_len, inner_local)
        gate_act = jax.nn.silu(gate_in)
        gated_out = mixed_flat * gate_act
        square_sum = lax.psum(jnp.sum(gated_out * gated_out, axis=-1), "mp")
        inv_gate = lax.rsqrt(square_sum / DI + eps)
        scaled = gated_out * inv_gate[..., None] * gate_gain
        scaled_low = scaled.astype(jnp.bfloat16)
        scaled_value = scaled_low.astype(jnp.float32)
        out_sel = jnp.einsum(
            "sa,far->sfr",
            select,
            down_out.astype(jnp.float32).reshape(inner_local, ADAPT, R),
            precision=precise,
        )
        up_out = jnp.einsum("sa,ard->srd", select, wide_up.reshape(ADAPT, R, D), precision=precise)
        rank_out = jnp.einsum("stf,sfr->str", scaled_value, out_sel, precision=precise)
        partial_out = jnp.einsum(
            "stf,fd->std", scaled_low, out_weight, preferred_element_type=jnp.float32
        )
        partial_out = partial_out + jnp.einsum("str,srd->std", rank_out, up_out, precision=precise)
        branch = lax.psum_scatter(partial_out, "mp", scatter_dimension=2, tiled=True)
        outputs.append(
            (rows_own.astype(jnp.float32) + mask_rows[..., None] * branch).astype(jnp.bfloat16)
        )
        branch_grad = cot_full * mask_rows[..., None].astype(jnp.bfloat16)
        branch_value = branch_grad.astype(jnp.float32)
        rank_grad = jnp.einsum("std,srd->str", branch_value, up_out, precision=precise)
        grad_up_out = jnp.einsum("str,std->srd", rank_out, branch_value, precision=precise)
        grad_out_sel = jnp.einsum("stf,str->sfr", scaled_value, rank_grad, precision=precise)
        scaled_grad = jnp.einsum(
            "std,fd->stf", branch_grad, out_weight, preferred_element_type=jnp.float32
        )
        scaled_grad = scaled_grad + jnp.einsum(
            "str,sfr->stf", rank_grad, out_sel, precision=precise
        )
        weighted = scaled_grad * gate_gain
        dot_sum = lax.psum(jnp.sum(weighted * gated_out, axis=-1), "mp")
        gated_grad = (
            weighted * inv_gate[..., None] - gated_out * (inv_gate**3 * dot_sum / DI)[..., None]
        )
        mixed_grad = (gated_grad * gate_act).reshape(slot_count, seg_len, head_local, P_SIZE)
        gate_grad = gated_grad * mixed_flat * silu_grad(gate_in)
        c_grad_in, log_grad_in, state_in_grad = state_back(mixed_grad)
        later_grads = entering((factor, state_in_grad), "seq", compose, identity, True)[1]
        total_grad = jnp.sum(later_grads * state_in, axis=(2, 3)) * factor
        x_heads_grad, b_grad, c_grad, log_grad, step_grad = scan_back(
            (mixed_grad, later_grads, total_grad)
        )
        x_heads_grad = x_heads_grad + d_skip[:, None] * mixed_grad
        c_grad = c_grad + c_grad_in
        step_grad = step_grad + (log_grad + log_grad_in) * decay_rate
        rate_grad = step_grad * mask_rows[..., None] * jax.nn.sigmoid(rate_in)
        conv_out_grad = jnp.concatenate(
            [x_heads_grad.reshape(slot_count, seg_len, inner_local), b_grad, c_grad], axis=-1
        )
        pre_grad = conv_out_grad * silu_grad(conv_pre)
        padded_grad = jnp.pad(pre_grad, ((0, 0), (KC - 1, KC - 1), (0, 0)))
        ext_grad = sum(
            (
                conv_taps[tap_index]
                * padded_grad[:, KC - 1 - tap_index : KC - 1 - tap_index + seg_len + KC - 1]
                for tap_index in range(KC)
            )
        )
        returned = shifted(ext_grad[:, : KC - 1], "seq", -1)
        in_grad = ext_grad[:, KC - 1 :]
        in_grad = in_grad.at[:, seg_len - (KC - 1) :].add(returned)
        zx_grad = jnp.stack([gate_grad, in_grad[..., :inner_local]], axis=2).astype(jnp.bfloat16)
        dt_grad_low = rate_grad.astype(jnp.bfloat16)
        zx_grad_value = zx_grad.astype(jnp.float32)
        rank_in_grad = jnp.einsum("stcf,srcf->str", zx_grad_value, up_sel, precision=precise)
        grad_up_sel = jnp.einsum("str,stcf->srcf", low_rank, zx_grad_value, precision=precise)
        grad_down_sel = jnp.einsum("std,str->sdr", normed_value, rank_in_grad, precision=precise)
        normed_part = jnp.einsum(
            "stcf,dcf->std", zx_grad, zx_weight, preferred_element_type=jnp.float32
        )
        normed_part = normed_part + jnp.einsum(
            "sth,dh->std", dt_grad_low, dt_weight, preferred_element_type=jnp.float32
        )
        normed_part = normed_part + jnp.einsum(
            "str,sdr->std", rank_in_grad, down_sel, precision=precise
        )
        bc_partial = in_grad[..., inner_local:]
        normed_sum, bc_sum = lax.psum((normed_part, bc_partial), "mp")
        normed_grad = normed_sum + jnp.einsum(
            "stn,dn->std",
            bc_sum.astype(jnp.bfloat16),
            bc_weight,
            preferred_element_type=jnp.float32,
        )
        scaled_in = normed_grad * norm_gain
        row_grad = inv_rms * scaled_in - rows_value * inv_rms**3 * jnp.mean(
            scaled_in * rows_value, axis=-1, keepdims=True
        )
        own_slice = lax.dynamic_slice_in_dim(row_grad, feature_start, model_part, 2)
        x_grads.append(cot_own.astype(jnp.float32) + own_slice)
        local_grads = (
            jnp.einsum("sa,sdr->adr", select, grad_down_sel, precision=precise),
            jnp.einsum("sa,srcf->arcf", select, grad_up_sel, precision=precise).reshape(
                ADAPT * R, 2, inner_local
            ),
            jnp.einsum("sa,sfr->far", select, grad_out_sel, precision=precise).reshape(
                inner_local, ADAPT * R
            ),
            jnp.einsum("sa,srd->ard", select, grad_up_out, precision=precise).reshape(ADAPT * R, D),
        )
        running = local_grads if running is None else jax.tree.map(jnp.add, running, local_grads)
    running = reduce_adapters(running)
    return (jnp.stack(outputs), jnp.stack(x_grads), running[0], running[1], running[2], running[3])


MESH = pl.DeviceIdType.MESH


def split(v):
    hi = v.astype(jnp.bfloat16)
    return hi, (v - hi.astype(jnp.float32)).astype(jnp.bfloat16)


def mm(a, b):
    return lax.dot_general(a, b, (((1,), (0,)), ((), ())), preferred_element_type=jnp.float32)


def mm_t(a, b):
    return lax.dot_general(a, b, (((1,), (1,)), ((), ())), preferred_element_type=jnp.float32)


def mm3(a, b):
    return mm(a[0], b[0]) + mm(a[0], b[1]) + mm(a[1], b[0])


def mm3_t(a, b):
    return mm_t(a[0], b[0]) + mm_t(a[0], b[1]) + mm_t(a[1], b[0])


def ones_mm(ones, v):
    hi, lo = split(v)
    rest = v - hi.astype(jnp.float32) - lo.astype(jnp.float32)
    return mm(ones, hi) + mm(ones, lo) + mm(ones, rest.astype(jnp.bfloat16))


def conv_rows(rows, halo, taps):
    count = rows.shape[0]
    ext = jnp.concatenate([halo, rows], axis=0).astype(jnp.float32)
    first = HALO - (KC - 1)
    total = taps[0:1] * ext[first : first + count]
    for j in range(1, KC):
        total = total + taps[j : j + 1] * ext[first + j : first + j + count]
    return total


def conv_rows_back(grad, taps):
    count, width = grad.shape
    zero = jnp.zeros((8, width), jnp.float32)
    ext = jnp.concatenate([zero, grad, zero], axis=0)
    total = taps[0:1] * ext[3 : 3 + count + 8]
    for j in range(1, KC):
        total = total + taps[j : j + 1] * ext[3 - j : 3 - j + count + 8]
    return total


def widen(columns):
    rows = columns.shape[0]
    lane = lax.broadcasted_iota(jnp.int32, (rows, 2 * P_SIZE), 1)
    return jnp.concatenate(
        [jnp.where(lane < P_SIZE, columns[:, h : h + 1], columns[:, h + 1 : h + 2]) for h in range(0, HG, 2)], axis=1
    )


def of_group(value, group):
    return pltpu.roll(value, lax.rem(128 - group * HG, 128), 1)


def head_sums(prod, group):
    rows = prod.shape[1]
    row = lax.broadcasted_iota(jnp.int32, (rows, 128), 0) // P_SIZE + group * HG
    lane = lax.broadcasted_iota(jnp.int32, (rows, 128), 1)
    pick = (row == lane).astype(jnp.float32).astype(jnp.bfloat16)
    hi, lo = split(prod)
    return mm(hi, pick) + mm(lo, pick)


def lane_sum(v):
    part = v[:, :128]
    for k in range(1, v.shape[1] // 128):
        part = part + v[:, k * 128 : (k + 1) * 128]
    return part


def add_up(ref, value, group):
    @pl.when(group == 0)
    def _():
        ref[0] = value

    @pl.when(group > 0)
    def _():
        ref[0] += value


def run_of(slot, z):
    return SLOTS * z + lax.rem(slot + z, SLOTS)


def place_of(run):
    z = run // SLOTS
    return z, lax.rem(lax.rem(run, SLOTS) + SLOTS * SLOTS - z, SLOTS)


class Mover:
    def __init__(self, src_ref, dst_ref, send_sem, recv_sem, count, slots, to_rows):
        self.refs = src_ref, dst_ref, send_sem, recv_sem
        self.count, self.slots, self.to_rows = count, slots, to_rows
        self.d, self.c, self.z = lax.axis_index("dp"), lax.axis_index("seq"), lax.axis_index("mp")
        self.pieces = 4 * SLOTS if to_rows else count * len(slots)

    def piece(self, n):
        src_ref, dst_ref, send_sem, recv_sem = self.refs
        if self.to_rows:
            m, h, to_c = lax.rem(n // 4 + self.z, SLOTS), n // 2 % 2, lax.rem(n + self.c, 2)
            to_z, slot = place_of(m * self.count + 2 * self.c + h)
            own = src_ref.shape[1] // 4
            src = src_ref.at[m, pl.ds(pl.multiple_of((2 * h + to_c) * own, 16), own), :]
            dst, sem = self.landing(slot - self.slots[0], self.z), (slot, self.z)
            due = jnp.logical_and(slot >= self.slots[0], slot <= self.slots[-1])
        else:
            slot = self.slots[n // self.count]
            to_z = lax.rem(self.z + n % self.count, self.count)
            run = run_of(slot, self.z)
            m, chunk = run // self.count, lax.rem(run, self.count)
            to_c, q = chunk // 2, lax.rem(chunk, 2) * 2 + self.c
            feats = dst_ref.shape[2]
            src = src_ref.at[slot - self.slots[0], :, pl.ds(pl.multiple_of(to_z * feats, 128), feats)]
            dst, sem = self.landing(m, q), (m, q)
            due = True
        here = jnp.logical_and(to_c == self.c, to_z == self.z)
        near = pltpu.make_async_copy(src, dst, recv_sem.at[sem])
        far = pltpu.make_async_remote_copy(
            src_ref=src, dst_ref=dst, send_sem=send_sem.at[n], recv_sem=recv_sem.at[sem],
            device_id=(self.d, to_c, to_z), device_id_type=MESH,
        )
        return jnp.logical_and(due, here), jnp.logical_and(due, jnp.logical_not(here)), near, far

    def landing(self, first, slot):
        dst_ref = self.refs[1]
        if self.to_rows:
            feats = dst_ref.shape[2] // self.count
            return dst_ref.at[first, :, pl.ds(pl.multiple_of(slot * feats, 128), feats)]
        rows = dst_ref.shape[1] // 4
        return dst_ref.at[first, pl.ds(pl.multiple_of(slot * rows, 16), rows), :]

    def greet(self, barrier):
        for cc in range(2):
            for r in range(self.count):
                if cc or r:
                    device = (self.d, lax.rem(self.c + cc, 2), lax.rem(self.z + r, self.count))
                    pl.semaphore_signal(barrier, 1, device_id=device, device_id_type=MESH)
        return 2 * self.count - 1

    def start(self, n):
        stays, goes, near, far = self.piece(n)

        @pl.when(stays)
        def _():
            near.start()

        @pl.when(goes)
        def _():
            far.start()

    def start_at(self, step, steps):
        for n in range(self.pieces):
            @pl.when(step == n * steps // (2 * self.pieces))
            def _():
                self.start(n)

    def finish(self):
        recv_sem = self.refs[3]
        if self.to_rows:
            for slot in self.slots:
                for s in range(self.count):
                    area = self.landing(slot - self.slots[0], s)
                    pltpu.make_async_copy(area, area, recv_sem.at[slot, s]).wait()
        else:
            for m in range(SLOTS):
                for q in range(4):
                    run = m * self.count + 2 * self.c + q // 2
                    slot = place_of(run)[1]

                    @pl.when(jnp.logical_and(slot >= self.slots[0], slot <= self.slots[-1]))
                    def _():
                        area = self.landing(m, q)
                        pltpu.make_async_copy(area, area, recv_sem.at[m, q]).wait()
        for n in range(self.pieces):
            _, goes, _, far = self.piece(n)

            @pl.when(goes)
            def _():
                far.wait_send()


class Line:
    def __init__(self, held_ref, sent_ref, send_sem, recv_sem, count, step):
        self.refs = held_ref, sent_ref, send_sem, recv_sem
        self.step, self.count = step, count
        self.d, self.c, self.z = lax.axis_index("dp"), lax.axis_index("seq"), lax.axis_index("mp")
        low, high = self.z > 0, self.z < count - 1
        self.has_source, self.has_target = (low, high) if step > 0 else (high, low)
        above, below = count - 1 - self.z, count - 2 - self.z
        self.from_slot, self.to_slot = (above, below) if step > 0 else (below, above)

    def greet(self, barrier):
        @pl.when(self.has_source)
        def _():
            pl.semaphore_signal(barrier, 1, device_id=(self.d, self.c, self.z - self.step), device_id_type=MESH)
        return jnp.where(self.has_target, 1, 0)

    def copy(self, group):
        held_ref, sent_ref, send_sem, recv_sem = self.refs
        return pltpu.make_async_remote_copy(
            src_ref=sent_ref.at[group], dst_ref=held_ref.at[group], send_sem=send_sem.at[group], recv_sem=recv_sem.at[group],
            device_id=(self.d, self.c, self.z + self.step), device_id_type=MESH,
        )

    def receive(self, slot, group):
        held_ref, sent_ref = self.refs[:2]
        remote = jnp.logical_and(self.has_source, slot == self.from_slot)
        fresh = slot == (0 if self.step > 0 else SLOTS - 1)
        local = jnp.logical_not(jnp.logical_or(remote, fresh))

        @pl.when(remote)
        def _():
            self.copy(group).wait_recv()
            sent_ref[held_ref.shape[0] + group] = held_ref[group]

        return jnp.where(jnp.logical_or(remote, local), sent_ref[held_ref.shape[0] + group], 0.0)

    def send(self, slot, group, value):
        held_ref, sent_ref = self.refs[:2]
        sent_ref[held_ref.shape[0] + group] = value

        @pl.when(jnp.logical_and(self.has_target, slot == self.to_slot))
        def _():
            sent_ref[group] = value
            self.copy(group).start()

    def finish(self):
        @pl.when(self.has_target)
        def _():
            for g in range(self.refs[0].shape[0]):
                self.copy(g).wait_send()


class PairFill:
    def __init__(self, own_ref, both_ref, buffer_ref, sems):
        self.d, self.c, self.z = lax.axis_index("dp"), lax.axis_index("seq"), lax.axis_index("mp")
        own = own_ref.shape[1]
        mine = buffer_ref.at[:, pl.ds(pl.multiple_of(self.c * own, 16), own), :]
        theirs = buffer_ref.at[:, pl.ds(pl.multiple_of((1 - self.c) * own, 16), own), :]
        self.near = pltpu.make_async_copy(own_ref, mine, sems.at[0])
        self.far = pltpu.make_async_remote_copy(
            src_ref=own_ref, dst_ref=mine, send_sem=sems.at[1], recv_sem=sems.at[2], device_id=(self.d, 1 - self.c, self.z),
            device_id_type=MESH,
        )
        self.arrival = pltpu.make_async_copy(theirs, theirs, sems.at[2])
        self.keep = pltpu.make_async_copy(buffer_ref, both_ref, sems.at[3])

    def greet(self, barrier):
        pl.semaphore_signal(barrier, 1, device_id=(self.d, 1 - self.c, self.z), device_id_type=MESH)
        return 1

    def fill(self):
        self.far.start()
        self.near.start()
        self.near.wait()
        self.arrival.wait()
        self.keep.start()

    def finish(self):
        self.far.wait_send()
        self.keep.wait()


class PairSum:
    def __init__(self, part_ref, sum_ref, send_sem, recv_sem):
        self.refs = part_ref, sum_ref, send_sem, recv_sem
        self.d, self.c, self.z = lax.axis_index("dp"), lax.axis_index("seq"), lax.axis_index("mp")

    def greet(self, barrier):
        pl.semaphore_signal(barrier, 1, device_id=(self.d, 1 - self.c, self.z), device_id_type=MESH)
        return 1

    def rows(self, c):
        own = self.refs[1].shape[2]
        return pl.ds(pl.multiple_of(c * own, 16), own)

    def copy(self, step):
        part_ref, sum_ref, send_sem, recv_sem = self.refs
        return pltpu.make_async_remote_copy(
            src_ref=part_ref.at[lax.rem(step, 2), :, self.rows(1 - self.c), :], dst_ref=sum_ref.at[step],
            send_sem=send_sem.at[step], recv_sem=recv_sem.at[step], device_id=(self.d, 1 - self.c, self.z), device_id_type=MESH,
        )

    def free(self, step):
        @pl.when(step >= 2)
        def _():
            self.copy(step - 2).wait_send()

    def send(self, step):
        self.copy(step).start()

    def take(self, step):
        part_ref, sum_ref = self.refs[:2]
        self.copy(step).wait_recv()
        for m in range(sum_ref.shape[1]):
            sum_ref[step, m] += part_ref[lax.rem(step, 2), m, self.rows(self.c), :]

    def finish(self):
        steps = self.refs[1].shape[0]
        for step in (steps - 2, steps - 1):
            self.copy(step).wait_send()


def carried_by(kernel, count, first, to_rows, n_in, n_out, *refs):
    ins, src_ref, outs, dst_ref = refs[:n_in], refs[n_in], refs[n_in + 1 : n_in + 1 + n_out], refs[n_in + 1 + n_out]
    scratch, sems = refs[n_in + n_out + 2 : -2], refs[-2:]
    kernel(*ins, *outs, *scratch, mover=Mover(src_ref, dst_ref, *sems, count, first, to_rows))


def step_of(grid):
    return pl.program_id(0) * grid[1] + pl.program_id(1)


def begin(grid, *parties):
    parties = [p for p in parties if p is not None]
    if parties:
        @pl.when(step_of(grid) == 0)
        def _():
            barrier = pltpu.get_barrier_semaphore()
            waits = 0
            for party in parties:
                waits = waits + party.greet(barrier)
            pl.semaphore_wait(barrier, waits)
            for party in parties:
                if isinstance(party, PairFill):
                    party.fill()
    for party in parties:
        if isinstance(party, Mover):
            party.start_at(step_of(grid), grid[0] * grid[1])


def end(grid, *parties):
    parties = [p for p in parties if p is not None]
    if parties:
        @pl.when(step_of(grid) == grid[0] * grid[1] - 1)
        def _():
            for party in parties:
                party.finish()


def twice_split(v):
    hi, lo = split(v)
    lane = lax.broadcasted_iota(jnp.int32, v.shape, 1)
    return jnp.where(lane < v.shape[1] // 2, hi.astype(jnp.float32), lo.astype(jnp.float32)).astype(jnp.bfloat16)


def fold(v):
    half = v.shape[0] // 2
    return v[:half] + v[half:]


def twice(v):
    return jnp.concatenate([v, v], axis=0)


def pick_kernel(ids_ref, pack_ref, out_ref):
    out_ref[0, 0] = pack_ref[0, 0, 0]


def merge(ref):
    return ref[...].reshape(ref.shape[0] * ref.shape[1], ref.shape[2])


def project_kernel(
    grid, own_ref, w_ref, tailw_ref, down_ref, up_ref, xin_ref, z_ref, bcin_ref, rate_ref, lr_ref, both_ref, low_ref, sems,
    mover=None
):
    step = pl.program_id(1)
    pair = PairFill(own_ref, both_ref, low_ref, sems)
    begin(grid, pair, mover)
    slots, tokens = low_ref.shape[:2]

    @pl.when(step == 0)
    def _():
        for m in range(slots):
            tail = mm(low_ref[m], tailw_ref[...])
            bcin_ref[m] = tail[:, : 2 * NS].astype(jnp.bfloat16)
            rate_ref[m] = tail[:, 2 * NS :]
            lr_ref[m] = twice_split(mm_t(low_ref[m], twice(down_ref[0, m])))

    value = mm(merge(low_ref), w_ref[0])
    for m in range(slots):
        part = value[m * tokens : (m + 1) * tokens] + mm(lr_ref[m], twice(up_ref[m, 0]))

        @pl.when(step < grid[1] // 2)
        def _():
            xin_ref[m] = part.astype(jnp.bfloat16)

        @pl.when(step >= grid[1] // 2)
        def _():
            z_ref[m] = part

    end(grid, pair, mover)


def prep_kernel(rate_ref, bias_ref, decay_ref, mask_ref, bcin_ref, bchalo_ref, taps_ref, step_ref, cum_ref, lanes_ref, bc_ref):
    rows = rate_ref.shape[1]
    value = rate_ref[0] + bias_ref[...]
    step = (jnp.maximum(value, 0.0) + jnp.log1p(jnp.exp(-jnp.abs(value)))) * mask_ref[0]
    log = step * decay_ref[...]
    tri = lax.broadcasted_iota(jnp.int32, (Q, Q), 0) >= lax.broadcasted_iota(jnp.int32, (Q, Q), 1)
    tri = tri.astype(jnp.float32).astype(jnp.bfloat16)
    step_ref[0] = step
    cum = jnp.concatenate([ones_mm(tri, log[b * Q : (b + 1) * Q]) for b in range(rows // Q)], axis=0)
    cum_ref[0] = cum
    cum_t, step_t = cum.T, step.T
    for g in range(lanes_ref.shape[1]):
        lanes_ref[0, g, :HG] = cum_t[g * HG : (g + 1) * HG]
        lanes_ref[0, g, HG:] = step_t[g * HG : (g + 1) * HG]
    pre = conv_rows(bcin_ref[0], bchalo_ref[0], taps_ref[...])
    bc_ref[0] = pre * jax.nn.sigmoid(pre)


def forward_kernel(
    grid, xin_ref, halo_ref, taps_ref, bc_ref, cum_ref, step_ref, lanes_ref, skip_ref, z_ref, mixed_ref, square_ref, state_ref,
    end_ref, scores_ref, bt_ref, held_ref, sent_ref, send_sem, recv_sem, mover=None
):
    group = pl.program_id(1)
    rows = xin_ref.shape[1]
    blocks = rows // Q
    line = Line(held_ref, sent_ref, send_sem, recv_sem, lax.axis_size("mp"), 1)
    begin(grid, line, mover)

    @pl.when(step_of(grid) == 0)
    def _():
        sent_ref[...] = jnp.zeros(sent_ref.shape, jnp.float32)

    @pl.when(group == 0)
    def _():
        for b in range(blocks):
            part = bc_ref[0, b * Q : (b + 1) * Q]
            b_part = split(part[:, :NS])
            c_part = split(part[:, NS:])
            scores_ref[b] = mm3_t(c_part, b_part)
            hi, lo = split(part[:, :NS].T)
            bt_ref[0, b] = hi
            bt_ref[1, b] = lo

    pre = conv_rows(xin_ref[0], halo_ref[0], taps_ref[...])
    x = pre * jax.nn.sigmoid(pre)
    cums, decs, updates = [], [], []
    for b in range(blocks):
        at = slice(b * Q, (b + 1) * Q)
        cum = of_group(cum_ref[0, at], group)
        step = of_group(step_ref[0, at], group)
        total = cum[Q - 1 : Q]
        wx = x[at] * widen(jnp.exp(total - cum) * step)
        cums.append(cum)
        decs.append(widen(jnp.exp(total)))
        updates.append(mm3((bt_ref[0, b], bt_ref[1, b]), split(wx)))

    slot = pl.program_id(0)
    states = [line.receive(slot, group)]
    for b in range(blocks):
        states.append(decs[b] * states[b] + updates[b])
    state_ref[0] = states[0]
    end_ref[0] = states[blocks]
    line.send(slot, group, states[blocks])
    lane = lax.broadcasted_iota(jnp.int32, (Q, 2 * P_SIZE), 1)
    causal = lax.broadcasted_iota(jnp.int32, (Q, Q), 0) >= lax.broadcasted_iota(jnp.int32, (Q, Q), 1)
    square = []
    for b in range(blocks):
        at = slice(b * Q, (b + 1) * Q)
        scores = scores_ref[b]
        xb = x[at]
        carried = widen(jnp.exp(cums[b])) * mm3(split(bc_ref[0, at, NS:]), split(states[b]))
        parts = []
        for h in range(0, HG, 2):
            pair = xb[:, h * P_SIZE : (h + 2) * P_SIZE]
            x_hi, x_lo = split(pair)
            both = jnp.concatenate([x_hi, x_lo], axis=1)
            halves = []
            for k in (h, h + 1):
                spread = cums[b][:, k : k + 1] - lanes_ref[0, 0, k : k + 1, at]
                decay = jnp.exp(jnp.where(causal, spread, -10000.0))
                m_hi, m_lo = split(scores * decay * lanes_ref[0, 0, HG + k : HG + k + 1, at])
                first = mm(m_hi, both)
                halves.append(first[:, : 2 * P_SIZE] + first[:, 2 * P_SIZE :] + mm(m_lo, x_hi))
            parts.append(jnp.where(lane < P_SIZE, halves[0], halves[1]))
        mixed = jnp.concatenate(parts, axis=1) + skip_ref[0:1] * xb + carried
        mixed_ref[0, at] = mixed
        z = z_ref[0, at]
        gated = mixed * (z * jax.nn.sigmoid(z))
        square.append(lane_sum(gated * gated))
    add_up(square_ref, jnp.concatenate(square, axis=0), group)

    end(grid, line, mover)


def chunk_decay(cum_ref, group):
    rows = cum_ref.shape[1]
    before = jnp.zeros((1, 128), jnp.float32)
    parts = []
    for b in range(rows // Q):
        cum = of_group(cum_ref[0, b * Q : (b + 1) * Q], group)
        parts.append(jnp.exp(cum + before))
        before = before + cum[Q - 1 : Q]
    return widen(jnp.concatenate(parts, axis=0))


def gs_kernel(
    grid, own_ref, w_ref, up_ref, down_ref, mixed_ref, z_ref, gain_ref, gs_ref, dot_ref, rg_ref, both_ref, gb_ref, sems
):
    step = pl.program_id(1)
    pair = PairFill(own_ref, both_ref, gb_ref, sems)
    begin(grid, pair)
    slots, tokens = gb_ref.shape[:2]

    @pl.when(step == 0)
    def _():
        for m in range(slots):
            rg_ref[m] = twice_split(mm_t(gb_ref[m], twice(up_ref[0, m])))

    gb = merge(gb_ref)
    width = w_ref.shape[3]
    total = mm_t(gb[:, :width], w_ref[0, 0])
    for n in range(1, w_ref.shape[0]):
        total = total + mm_t(gb[:, n * width : (n + 1) * width], w_ref[n, 0])
    for m in range(slots):
        gs = total[m * tokens : (m + 1) * tokens] + mm(rg_ref[m], twice(down_ref[m, 0]))
        gs_ref[m] = gs
        z = z_ref[m]
        dots = lane_sum(gs * gain_ref[...] * (mixed_ref[m] * (z * jax.nn.sigmoid(z))))

        @pl.when(step == 0)
        def _():
            dot_ref[m] = dots

        @pl.when(step > 0)
        def _():
            dot_ref[m] += dots

    end(grid, pair)


def turned(v):
    return v.astype(jnp.float32).T.astype(jnp.bfloat16)


def rank_sum(rows_ref, m, factor_ref, first):
    width = factor_ref.shape[3]
    total = 0.0
    for n in range(factor_ref.shape[1]):
        factor = twice(factor_ref[m, n, first : first + R])
        total = total + mm_t(rows_ref[m, :, n * width : (n + 1) * width], factor)
    return total


def branch_kernel(
    grid, scaled_ref, w_ref, down_ref, up_ref, rg_ref, gb_ref, x_ref, mask_ref, out_ref, g_up_ref, g_down_ref, ro_ref, rot_ref,
    rgt_ref, part_ref, sum_ref, send_sem, recv_sem
):
    step = pl.program_id(1)
    pair = PairSum(part_ref, sum_ref, send_sem, recv_sem)
    begin(grid, pair)
    slots, tokens = scaled_ref.shape[:2]

    @pl.when(step == 0)
    def _():
        for m in range(slots):
            ro = twice_split(rank_sum(scaled_ref, m, down_ref, 0))
            ro_ref[m] = ro
            rot_ref[m] = turned(ro)
            rgt_ref[m] = turned(rg_ref[m])

    scaled = merge(scaled_ref)
    width = w_ref.shape[2]
    total = mm(scaled[:, :width], w_ref[0, 0])
    for n in range(1, w_ref.shape[1]):
        total = total + mm(scaled[:, n * width : (n + 1) * width], w_ref[0, n])
    cols = g_down_ref.shape[2]
    width = up_ref.shape[3]
    pair.free(step)
    for m in range(slots):
        part_ref[lax.rem(step, 2), m] = total[m * tokens : (m + 1) * tokens] + mm(ro_ref[m], twice(up_ref[0, m]))
    pair.send(step)
    for m in range(slots):
        g_up_ref[m] = fold(mm(rot_ref[m], gb_ref[m]))
        g_down_ref[m] = fold(mm(rgt_ref[m], scaled_ref[m, :, pl.ds(pl.multiple_of(step * cols, 128), cols)]))

    def put(n):
        pair.take(n)
        at = pl.ds(pl.multiple_of(n * width, 128), width)
        for m in range(slots):
            out_ref[m, :, at] = (x_ref[m, :, at].astype(jnp.float32) + mask_ref[m] * sum_ref[n, m]).astype(jnp.bfloat16)

    @pl.when(step > 0)
    def _():
        put(step - 1)

    @pl.when(step == grid[1] - 1)
    def _():
        put(step)

    end(grid, pair)


def unproject_kernel(
    grid, gz_ref, gx_ref, tail_ref, w_ref, tailw_ref, up_ref, down_ref, lr_ref, low_ref, x_ref, inv_ref, gain_ref, delta_ref,
    upz_ref, upx_ref, g_down_ref, ri_ref, rit_ref, lrt_ref, part_ref, sum_ref, send_sem, recv_sem, mover=None
):
    step = pl.program_id(1)
    pair = PairSum(part_ref, sum_ref, send_sem, recv_sem)
    begin(grid, pair, mover)
    slots, tokens = gz_ref.shape[:2]

    @pl.when(step == 0)
    def _():
        for m in range(slots):
            ri = twice_split(rank_sum(gz_ref, m, up_ref, 0) + rank_sum(gx_ref, m, up_ref, R))
            ri_ref[m] = ri
            rit_ref[m] = turned(ri)
            lrt_ref[m] = turned(lr_ref[m])

    total = mm_t(merge(gz_ref), w_ref[0]) + mm_t(merge(gx_ref), w_ref[1]) + mm_t(merge(tail_ref), tailw_ref[...])
    cols = upz_ref.shape[2]
    at = pl.ds(pl.multiple_of(step * cols, 128), cols)
    pair.free(step)
    for m in range(slots):
        part_ref[lax.rem(step, 2), m] = total[m * tokens : (m + 1) * tokens] + mm(ri_ref[m], twice(down_ref[0, m]))
    pair.send(step)
    for m in range(slots):
        upz_ref[m] = fold(mm(lrt_ref[m], gz_ref[m, :, at]))
        upx_ref[m] = fold(mm(lrt_ref[m], gx_ref[m, :, at]))
        g_down_ref[m] = fold(mm(rit_ref[m], low_ref[m]))

    @pl.when(step > 0)
    def _():
        pair.take(step - 1)

    @pl.when(step == grid[1] - 1)
    def _():
        pair.take(step)
        width = sum_ref.shape[3]
        for m in range(slots):
            spread = 0.0
            for n in range(sum_ref.shape[0]):
                at = slice(n * width, (n + 1) * width)
                gn = sum_ref[n, m] * gain_ref[:, at]
                sum_ref[n, m] = gn
                spread = spread + jnp.sum(gn * x_ref[m, :, at].astype(jnp.float32), axis=1, keepdims=True)
            inv = inv_ref[m]
            spread = spread * (inv * inv * inv / x_ref.shape[2])
            for n in range(sum_ref.shape[0]):
                at = slice(n * width, (n + 1) * width)
                delta_ref[m, :, at] = (inv * sum_ref[n, m] - x_ref[m, :, at].astype(jnp.float32) * spread).astype(jnp.bfloat16)

    end(grid, pair, mover)


def gate_back_kernel(
    grid, gs_ref, mixed_ref, z_ref, inv_ref, coef_ref, gain_ref, bc_ref, cum_ref, dy_ref, gz_ref, scaled_ref, lam_ref, q_ref, ct_ref,
    mover=None
):
    group = pl.program_id(1)
    begin(grid, mover)

    @pl.when(group == 0)
    def _():
        hi, lo = split(bc_ref[0, :, NS:].T)
        ct_ref[0] = hi
        ct_ref[1] = lo

    z = z_ref[0]
    mixed = mixed_ref[0]
    sig = jax.nn.sigmoid(z)
    act = z * sig
    gated = mixed * act
    inv = inv_ref[0]
    gain = gain_ref[...]
    scaled_ref[0] = (gated * inv * gain).astype(jnp.bfloat16)
    g_gated = gs_ref[0] * gain * inv - gated * coef_ref[0]
    dy = g_gated * act
    dy_ref[0] = dy
    gz_ref[0] = (g_gated * mixed * (sig * (1.0 + z * (1.0 - sig)))).astype(jnp.bfloat16)
    lam_ref[0] = mm3((ct_ref[0], ct_ref[1]), split(dy * chunk_decay(cum_ref, group)))
    add_up(q_ref, head_sums(dy * mixed, group), group)

    end(grid, mover)


def scan_back_kernel(
    grid, dy_ref, xin_ref, halo_ref, taps_ref, bc_ref, cum_ref, step_ref, lanes_ref, skip_ref, state_ref, lam_ref, end_ref,
    gx_ref, head_ref, tail_ref, gbc_ref, xu_ref, dx_ref, scorest_ref, dscorest_ref, bt_ref, ct_ref, held_ref, sent_ref, send_sem,
    recv_sem, mover=None
):
    group = pl.program_id(1)
    rows = xin_ref.shape[1]
    blocks = rows // Q
    line = Line(held_ref, sent_ref, send_sem, recv_sem, lax.axis_size("mp"), -1)
    begin(grid, line, mover)

    @pl.when(step_of(grid) == 0)
    def _():
        sent_ref[...] = jnp.zeros(sent_ref.shape, jnp.float32)

    @pl.when(group == 0)
    def _():
        for b in range(blocks):
            part = bc_ref[0, b * Q : (b + 1) * Q]
            scorest_ref[b] = mm3_t(split(part[:, :NS]), split(part[:, NS:]))
            dscorest_ref[b] = jnp.zeros((Q, Q), jnp.float32)
            hi, lo = split(part[:, :NS].T)
            bt_ref[0, b] = hi
            bt_ref[1, b] = lo
            hi, lo = split(part[:, NS:].T)
            ct_ref[0, b] = hi
            ct_ref[1, b] = lo
        gbc_ref[0] = jnp.zeros((rows, 2 * NS), jnp.float32)
        xu_ref[0] = jnp.zeros((rows, 128), jnp.float32)
        dx_ref[0] = jnp.zeros((rows, 128), jnp.float32)

    pre = conv_rows(xin_ref[0], halo_ref[0], taps_ref[...])
    sig = jax.nn.sigmoid(pre)
    x = pre * sig
    lane = lax.broadcasted_iota(jnp.int32, (Q, 2 * P_SIZE), 1)
    causal = lax.broadcasted_iota(jnp.int32, (Q, Q), 0) <= lax.broadcasted_iota(jnp.int32, (Q, Q), 1)
    cums, step_cols, decs, rests, wide_steps = [], [], [], [], []
    for b in range(blocks):
        at = slice(b * Q, (b + 1) * Q)
        cum = of_group(cum_ref[0, at], group)
        step = of_group(step_ref[0, at], group)
        total = cum[Q - 1 : Q]
        cums.append(cum)
        step_cols.append(step)
        decs.append(widen(jnp.exp(total)))
        rests.append(widen(jnp.exp(total - cum)))
        wide_steps.append(widen(step))
    states = [state_ref[0]]
    for b in range(blocks - 1):
        wx = x[b * Q : (b + 1) * Q] * rests[b] * wide_steps[b]
        states.append(decs[b] * states[b] + mm3((bt_ref[0, b], bt_ref[1, b]), split(wx)))
    slot = SLOTS - 1 - pl.program_id(0)
    lam = line.receive(slot, group)
    whole = decs[0]
    for dec in decs[1:]:
        whole = whole * dec
    line.send(slot, group, whole * lam + lam_ref[0])
    ends = jnp.sum(lam * end_ref[0], axis=0, keepdims=True)
    g_parts = [None] * blocks
    for b in reversed(range(blocks)):
        at = slice(b * Q, (b + 1) * Q)
        xb = x[at]
        dy = dy_ref[0, at]
        scores = scorest_ref[b]
        dscores = dscorest_ref[b]
        u_parts = []
        for h in range(0, HG, 2):
            pair = slice(h * P_SIZE, (h + 2) * P_SIZE)
            x_hi, x_lo = split(xb[:, pair])
            d_hi, d_lo = split(dy[:, pair])
            both = jnp.concatenate([d_hi, d_lo], axis=1)
            halves = []
            for k in (h, h + 1):
                mine = (lane < P_SIZE) if k == h else (lane >= P_SIZE)
                spread = lanes_ref[0, 0, k : k + 1, at] - cums[b][:, k : k + 1]
                decay = jnp.exp(jnp.where(causal, spread, -10000.0))
                zero = jnp.zeros_like(x_hi)
                xm_hi = jnp.where(mine, x_hi, zero)
                xm_lo = jnp.where(mine, x_lo, zero)
                dm = mm_t(xm_hi, d_hi) + mm_t(xm_hi, d_lo) + mm_t(xm_lo, d_hi)
                dscores = dscores + dm * decay * step_cols[b][:, k : k + 1]
                m_hi, m_lo = split(scores * decay)
                first = mm(m_hi, both)
                halves.append(first[:, : 2 * P_SIZE] + first[:, 2 * P_SIZE :] + mm(m_lo, d_hi))
            u_parts.append(jnp.where(lane < P_SIZE, halves[0], halves[1]))
        dscorest_ref[b] = dscores
        lam_s = split(lam)
        part = bc_ref[0, at]
        step = wide_steps[b]
        u = jnp.concatenate(u_parts, axis=1) + rests[b] * mm3(split(part[:, :NS]), lam_s)
        ev = split(widen(jnp.exp(cums[b])) * dy)
        gbc_ref[0, at, :NS] += mm3_t(split(rests[b] * step * xb), lam_s)
        gbc_ref[0, at, NS:] += mm3_t(ev, split(states[b]))
        if b > 0:
            lam = decs[b] * lam + mm3((ct_ref[0, b], ct_ref[1, b]), ev)
        xu_ref[0, at] += head_sums(xb * u, group)
        direct = xb * dy * skip_ref[0:1]
        if b == blocks - 1:
            row = lax.broadcasted_iota(jnp.int32, (Q, HG * P_SIZE), 0)
            direct = jnp.where(row == Q - 1, direct - ends, direct)
        dx_ref[0, at] += head_sums(direct, group)
        g_parts[b] = step * u + skip_ref[0:1] * dy
    g_pre = jnp.concatenate(g_parts, axis=0) * (sig * (1.0 + pre * (1.0 - sig)))
    g_ext = conv_rows_back(g_pre, taps_ref[...])
    gx_ref[0] = g_ext[8:].astype(jnp.bfloat16)
    head_ref[0] = g_ext[:8]
    tail_ref[0] = g_ext[rows:]

    @pl.when(group == pl.num_programs(1) - 1)
    def _():
        for b in range(blocks):
            at = slice(b * Q, (b + 1) * Q)
            part = bc_ref[0, at]
            ds = dscorest_ref[b]
            gbc_ref[0, at, :NS] += mm3(split(ds), split(part[:, NS:]))
            gbc_ref[0, at, NS:] += mm3(split(ds.T), split(part[:, :NS]))

    end(grid, line, mover)


def finish_kernel(
    count, out_ref, up_z_ref, up_x_ref, up_out_ref, down_ref, mine_ref, picks_ref, rows_ref, moved_ref, near_out_ref, far_out_ref,
    near_ref, far_ref, near1_ref, far1_ref, near2_ref,
    near2_in_ref, far2_ref, far2_in_ref, n1s, n1r, f1s, f1r, n2s, n2r, f2s, f2r, send_sem, recv_sem
):
    d, c, z = lax.axis_index("dp"), lax.axis_index("seq"), lax.axis_index("mp")
    mover = Mover(rows_ref, moved_ref, send_sem, recv_sem, count, tuple(range(SLOTS)), False)
    blocks = far2_ref.shape[0]
    barrier = pltpu.get_barrier_semaphore()
    waits = mover.greet(barrier)
    others = [(i, j) for i in range(blocks) for j in range(2) if i or j]
    for i, j in others:
        device = (lax.rem(d + i, blocks), lax.rem(c + j, 2), z)
        pl.semaphore_signal(barrier, 1, device_id=device, device_id_type=MESH)

    def by_sequence(ref, m):
        return sum(mine_ref[m, i] * ref[i] for i in range(SLOTS))

    part, each = near_ref.shape[4], far_ref.shape[5]
    for m in range(SLOTS):
        for kind, ref in enumerate((out_ref, up_z_ref, up_x_ref)):
            total = by_sequence(ref, m).astype(jnp.bfloat16)
            for n in range(count):
                near_ref[n, m, kind] = total[:, n * part : (n + 1) * part]
        for kind, ref in enumerate((up_out_ref, down_ref)):
            total = by_sequence(ref, m)
            for b in range(blocks):
                for n in range(2 * count):
                    at = (b * 2 * count + n) * each
                    far_ref[n, m, kind, b] = total[:, at : at + each].astype(jnp.bfloat16)
    pl.semaphore_wait(barrier, waits + len(others))

    def remote(src, dst, send, recv, *device):
        return pltpu.make_async_remote_copy(
            src_ref=src, dst_ref=dst, send_sem=send, recv_sem=recv, device_id=device, device_id_type=MESH
        )

    def arrival(ref, at, sem):
        pltpu.make_async_copy(ref.at[at], ref.at[at], sem.at[at]).wait()

    me = c * count + z
    copies = []
    for i in range(1, count):
        to = lax.rem(z + i, count)
        copies.append(remote(near_ref.at[to], near1_ref.at[z], n1s.at[i], n1r.at[z], d, c, to))
    column = [(j, i) for j in range(2) for i in range(count) if i or j]
    for j, i in column:
        to_c, to = lax.rem(c + j, 2), lax.rem(z + i, count)
        copies.append(remote(far_ref.at[to_c * count + to], far1_ref.at[me], f1s.at[j * count + i], f1r.at[me], d, to_c, to))
    for copy in copies:
        copy.start()
    for n in range(mover.pieces):
        mover.start(n)

    near = near_ref[z].astype(jnp.float32)
    for i in range(1, count):
        at = lax.rem(z + i, count)
        arrival(near1_ref, at, n1r)
        near = near + near1_ref[at].astype(jnp.float32)
    far = far_ref[me].astype(jnp.float32)
    for j, i in column:
        at = lax.rem(c + j, 2) * count + lax.rem(z + i, count)
        arrival(far1_ref, at, f1r)
        far = far + far1_ref[at].astype(jnp.float32)
    for a in range(ADAPT):
        near2_ref[a] = sum(picks_ref[m, a] * near[m] for m in range(SLOTS))
        for b in range(blocks):
            far2_ref[b, a] = sum(picks_ref[m, a] * far[m, :, b] for m in range(SLOTS))

    here = d * 2 + c
    copies2 = []
    for i, j in others:
        to_d, to_c = lax.rem(d + i, blocks), lax.rem(c + j, 2)
        copies2.append(
            remote(near2_ref.at[to_d * 2 + to_c], near2_in_ref.at[here], n2s.at[i * 2 + j], n2r.at[here], to_d, to_c, z)
        )
    for i in range(1, blocks):
        to = lax.rem(d + i, blocks)
        copies2.append(remote(far2_ref.at[to], far2_in_ref.at[d], f2s.at[i], f2r.at[d], to, c, z))
    for copy in copies2:
        copy.start()
    near2_in_ref[here] = near2_ref[here]
    far_sum = far2_ref[d]
    for i in range(1, blocks):
        at = lax.rem(d + i, blocks)
        arrival(far2_in_ref, at, f2r)
        far_sum = far_sum + far2_in_ref[at]
    far_out_ref[...] = far_sum
    for i, j in others:
        arrival(near2_in_ref, lax.rem(d + i, blocks) * 2 + lax.rem(c + j, 2), n2r)
    for half in range(2):
        near_out_ref[half] = sum(near2_in_ref[b * 2 + half] for b in range(blocks))
    for copy in copies + copies2:
        copy.wait_send()
    mover.finish()


def bc_back_kernel(
    g_ref, in_ref, halo_ref, taps_ref, q_ref, dx_ref, xu_ref, step_ref, rate_ref, bias_ref, decay_ref, mask_ref,
    out_ref, head_ref, tail_ref, g_rate_ref
):
    rows = in_ref.shape[1]
    pre = conv_rows(in_ref[0], halo_ref[0], taps_ref[...])
    sig = jax.nn.sigmoid(pre)
    g_ext = conv_rows_back(g_ref[0] * (sig * (1.0 + pre * (1.0 - sig))), taps_ref[...])
    out_ref[0] = g_ext[8:].astype(jnp.bfloat16)
    head_ref[0] = g_ext[:8]
    tail_ref[0] = g_ext[rows:]
    xu = xu_ref[0]
    flow = q_ref[0] - dx_ref[0] - step_ref[0] * xu
    later = lax.broadcasted_iota(jnp.int32, (rows, rows), 0) <= lax.broadcasted_iota(jnp.int32, (rows, rows), 1)
    g_log = ones_mm(later.astype(jnp.float32).astype(jnp.bfloat16), flow)
    sig = jax.nn.sigmoid(rate_ref[0] + bias_ref[...])
    g_rate_ref[0] = ((xu + g_log * decay_ref[...]) * mask_ref[0] * sig).astype(jnp.bfloat16)


def flip(v, mask, count):
    total = 0
    bit = 1
    while bit < count:
        b = lax.rem(v // bit, 2)
        total = total + (1 - b if mask & bit else b) * bit
        bit *= 2
    return total


def gather_kernel(
    nd, nz, wt_ref, x_ref, w_ref, rows_ref, local_sem, pair_sem, up_sem, down_sem, zrecv_sem, xsend_sem, xrecv_sem, ysend_sem,
    yrecv_sem, hsend_sem, hrecv_sem, asend_sem, arecv_sem
):
    d, c, z = lax.axis_index("dp"), lax.axis_index("seq"), lax.axis_index("mp")
    xn, yn = flip(d, 1, nd), flip(d, 2, nd)
    rows, part = wt_ref.shape[1], wt_ref.shape[2] // 2

    def remote(src, dst, send, recv, device):
        return pltpu.make_async_remote_copy(
            src_ref=src, dst_ref=dst, send_sem=send, recv_sem=recv, device_id=device, device_id_type=MESH
        )

    barrier = pltpu.get_barrier_semaphore()
    for cc in range(2):
        for r in range(nz):
            if cc or r:
                pl.semaphore_signal(barrier, 1, device_id=(d, flip(c, cc, 2), flip(z, r, nz)), device_id_type=MESH)
    for dd in (xn, yn):
        pl.semaphore_signal(barrier, 1, device_id=(dd, c, z), device_id_type=MESH)
    pl.semaphore_wait(barrier, 2 * nz - 1 + 2)

    def cols(s):
        return pl.ds(pl.multiple_of(s * part, 128), part)

    def area(dd, s):
        return w_ref.at[:, pl.ds(pl.multiple_of(dd * (2 * rows), 16), 2 * rows), cols(s)]

    def half_area(dd, s, h):
        return w_ref.at[:, pl.ds(pl.multiple_of(dd * (2 * rows) + h * rows, 16), rows), cols(s)]

    mine_area = w_ref.at[:, pl.ds(pl.multiple_of((2 * d + c) * rows, 16), rows), cols(z)]
    keep = pltpu.make_async_copy(wt_ref.at[:, :, cols(c)], mine_area, local_sem.at[0])
    pair = remote(wt_ref.at[:, :, cols(1 - c)], mine_area, pair_sem.at[0], pair_sem.at[1], (d, 1 - c, z))
    keep.start()
    pair.start()

    mover = Mover(x_ref, rows_ref, asend_sem, arecv_sem, nz, tuple(range(SLOTS)), True)
    for n in range(mover.pieces):
        mover.start(n)

    keep.wait()
    pair.wait()

    def spread(s):
        remote(area(d, s), area(d, s), xsend_sem.at[s], xrecv_sem.at[s], (xn, c, z)).start()
        remote(area(d, s), area(d, s), ysend_sem.at[s], yrecv_sem.at[s], (yn, c, z)).start()

    def send_up(s):
        @pl.when(z < nz - 1)
        def _():
            remote(area(d, s), area(d, s), up_sem.at[s], zrecv_sem.at[s], (d, c, z + 1)).start()

    def send_down(s):
        @pl.when(z > 0)
        def _():
            remote(area(d, s), area(d, s), down_sem.at[s], zrecv_sem.at[s], (d, c, z - 1)).start()

    def relay(s):
        remote(area(xn, s), area(xn, s), xsend_sem.at[s], xrecv_sem.at[s], (xn, c, z)).wait_recv()
        remote(half_area(xn, s, 0), half_area(xn, s, 0), hsend_sem.at[0, s], hrecv_sem.at[0, s], (yn, c, z)).start()
        remote(area(yn, s), area(yn, s), ysend_sem.at[s], yrecv_sem.at[s], (yn, c, z)).wait_recv()
        remote(half_area(yn, s, 1), half_area(yn, s, 1), hsend_sem.at[1, s], hrecv_sem.at[1, s], (xn, c, z)).start()

    send_up(z)
    send_down(z)
    spread(z)
    for r in range(1, nz + 1):
        if r < nz:
            @pl.when(z - r >= 0)
            def _():
                s = z - r
                remote(area(d, s), area(d, s), up_sem.at[s], zrecv_sem.at[s], (d, c, z)).wait_recv()
                send_up(s)
                spread(s)

            @pl.when(z + r < nz)
            def _():
                s = z + r
                remote(area(d, s), area(d, s), up_sem.at[s], zrecv_sem.at[s], (d, c, z)).wait_recv()
                send_down(s)
                spread(s)

        if r == 1:
            relay(z)
        else:
            @pl.when(z - r + 1 >= 0)
            def _():
                relay(z - r + 1)

            @pl.when(z + r - 1 < nz)
            def _():
                relay(z + r - 1)

    mover.finish()
    for s in range(nz):
        remote(half_area(d, s, 0), half_area(d, s, 0), hsend_sem.at[0, s], hrecv_sem.at[0, s], (yn, c, z)).wait()
        remote(half_area(d, s, 1), half_area(d, s, 1), hsend_sem.at[1, s], hrecv_sem.at[1, s], (xn, c, z)).wait()
        remote(area(d, s), area(d, s), xsend_sem.at[s], xrecv_sem.at[s], (xn, c, z)).wait_send()
        remote(area(d, s), area(d, s), ysend_sem.at[s], yrecv_sem.at[s], (yn, c, z)).wait_send()

        @pl.when(jnp.logical_and(s <= z, z < nz - 1))
        def _():
            remote(area(d, s), area(d, s), up_sem.at[s], zrecv_sem.at[s], (d, c, z)).wait_send()

        @pl.when(jnp.logical_and(s >= z, z > 0))
        def _():
            remote(area(d, s), area(d, s), down_sem.at[s], zrecv_sem.at[s], (d, c, z)).wait_send()


def gather(wt, x, nd, nz):
    half = wt.shape[2] // 2
    dma = pltpu.SemaphoreType.DMA
    anywhere = pl.BlockSpec(memory_space=pl.ANY)
    return pl.pallas_call(
        functools.partial(gather_kernel, nd, nz),
        name="gather",
        out_shape=(
            jax.ShapeDtypeStruct((2, wt.shape[1] * 2 * nd, half * nz), wt.dtype),
            jax.ShapeDtypeStruct((SLOTS, x.shape[1] // 4, x.shape[2] * nz), x.dtype),
        ),
        in_specs=[anywhere] * 2,
        out_specs=(anywhere,) * 2,
        scratch_shapes=[
            dma((1,)), dma((2,)), dma((nz,)), dma((nz,)), dma((nz,)), dma((nz,)), dma((nz,)), dma((nz,)), dma((nz,)),
            dma((2, nz)), dma((2, nz)), dma((4 * SLOTS,)), dma((SLOTS, nz)),
        ],
        compiler_params=pltpu.CompilerParams(collective_id=1, has_side_effects=True),
    )(wt, x)


def block(shape, index):
    return pl.BlockSpec(shape, index)


def call(kernel, name, grid, ins, outs, scratch, flops, size, comm=None, load=None):
    params = dict(vmem_limit_bytes=VMEM_LIMIT)
    kernel = functools.partial(kernel, grid)
    ins, outs, scratch = list(ins), list(outs), list(scratch)
    if load is not None:
        rows, result, first, to_rows = load
        count = lax.axis_size("mp")
        kernel = functools.partial(carried_by, kernel, count, first, to_rows, len(ins), len(outs))
        ins.append((rows, pl.BlockSpec(memory_space=pl.ANY)))
        outs.append((result, pl.BlockSpec(memory_space=pl.ANY)))
        sends = 4 * SLOTS if to_rows else count * len(first)
        scratch += [pltpu.SemaphoreType.DMA((sends,)), pltpu.SemaphoreType.DMA((SLOTS, 4))]
    if comm is not None:
        params.update(collective_id=comm, has_side_effects=True)
    return pl.pallas_call(
        kernel,
        name=name,
        grid=grid,
        in_specs=[s for _, s in ins],
        out_specs=[s for _, s in outs],
        out_shape=[s for s, _ in outs],
        scratch_shapes=scratch,
        compiler_params=pltpu.CompilerParams(**params),
        cost_estimate=pl.CostEstimate(flops=flops, bytes_accessed=size, transcendentals=0),
    )(*[a for a, _ in ins])


def skip_grid(kernel):
    return lambda grid, *refs: kernel(*refs)


def after(value, *deps):
    return lax.optimization_barrier((value,) + deps)[0]


def finish(grads, mine, picks, rows, moved, count, blocks):
    dma, f32, bf16 = pltpu.SemaphoreType.DMA, jnp.float32, jnp.bfloat16
    anywhere, vmem = pl.BlockSpec(memory_space=pl.ANY), pl.BlockSpec(memory_space=pltpu.VMEM)
    smem = pl.BlockSpec(memory_space=pltpu.SMEM)
    near_shape = (3, R, grads[0].shape[2] // count)
    far_shape = (2, R, D // (2 * blocks * count))
    near_all = (count, SLOTS) + near_shape
    far_all = (2 * count, SLOTS, 2, blocks) + far_shape[1:]
    return pl.pallas_call(
        functools.partial(finish_kernel, count),
        name="finish",
        in_specs=[vmem] * 5 + [smem, smem, anywhere],
        out_specs=[anywhere, vmem, vmem],
        out_shape=[moved, jax.ShapeDtypeStruct((2,) + near_shape, f32), jax.ShapeDtypeStruct((ADAPT,) + far_shape, f32)],
        scratch_shapes=[
            pltpu.VMEM(near_all, bf16), pltpu.VMEM(far_all, bf16), pltpu.VMEM(near_all, bf16), pltpu.VMEM(far_all, bf16),
            pltpu.VMEM((ADAPT,) + near_shape, f32), pltpu.VMEM((2 * blocks,) + near_shape, f32),
            pltpu.VMEM((blocks, ADAPT) + far_shape, f32), pltpu.VMEM((blocks, ADAPT) + far_shape, f32), dma((count,)), dma((count,)),
            dma((2 * count,)), dma((2 * count,)), dma((2 * blocks,)), dma((2 * blocks,)), dma((blocks,)), dma((blocks,)),
            dma((count * SLOTS,)), dma((SLOTS, 4)),
        ],
        compiler_params=pltpu.CompilerParams(vmem_limit_bytes=VMEM_LIMIT, collective_id=5, has_side_effects=True),
    )(*grads, mine, picks, rows)


def fast_body(
    x_in, cotangent, lengths, adapter_ids, norm_gain, w_zx, w_bc, w_dt, dt_bias, a_log, d_skip, conv_x, conv_bc,
    gate_gain, w_out, in_down, in_up, out_down, out_up
):
    bf16, f32 = jnp.bfloat16, jnp.float32
    micros, _, seg, feats = x_in.shape
    nz, nd = lax.axis_size("mp"), lax.axis_size("dp")
    core, z = lax.axis_index("seq"), lax.axis_index("mp")
    own = seg // nz
    tokens = 2 * own
    heads = dt_bias.shape[0] * nz // 2
    chan = heads * P_SIZE
    part = chan // nz
    groups = heads // HG
    wide = HG * P_SIZE
    blocks = tokens // Q
    each = D // (nd * 2 * nz)

    def other(v):
        return lax.ppermute(v, "seq", [(0, 1), (1, 0)])

    def pair_cat(mine, theirs, axis):
        return jnp.where(
            core == 0, jnp.concatenate([mine, theirs], axis), jnp.concatenate([theirs, mine], axis)
        )

    def halves(v, axis):
        v = v.reshape(v.shape[:axis] + (2, v.shape[axis] // 2) + v.shape[axis + 1 :])
        return (
            lax.dynamic_index_in_dim(v, core, axis, False),
            lax.dynamic_index_in_dim(v, 1 - core, axis, False),
        )

    line = part
    bc_piece = lax.dynamic_slice_in_dim(w_bc, z * (w_bc.shape[0] // nz), w_bc.shape[0] // nz, 0)
    pairs = jnp.stack([jnp.transpose(in_down, (0, 2, 1)), out_up.reshape(ADAPT, R, -1)], 1)
    same = [bc_piece, pairs]
    sized = [halves(jnp.transpose(in_up, (1, 0, 2)), 2), halves(out_down.T, 1), halves(w_dt.T, 0)]
    packs = []
    for k in range(2):
        packs.append(jnp.concatenate([v.reshape(-1, line) for v in [s[k] for s in sized] + same], 0))
    bounds = [0]
    for v in [s[0] for s in sized] + same:
        bounds.append(bounds[-1] + v.size // line)
    pack = pair_cat(packs[0][None], other(packs[1])[None], 0)
    params = jnp.concatenate([dt_bias, a_log, d_skip, gate_gain, conv_x.reshape(-1)])
    params = lax.all_gather(params, "mp")
    pack = lax.all_gather(pack, ("dp", "mp")).reshape((nd, nz) + pack.shape)
    zx_weight, x_rows = gather(jnp.transpose(w_zx, (1, 0, 2)), x_in[:, 0], nd, nz)
    out_mine, out_theirs = halves(after(w_out, x_rows), 0)
    out_pair = pair_cat(out_mine, other(out_theirs), 1)
    out_all = lax.all_gather(out_pair, ("dp", "mp")).reshape((nd, nz) + out_pair.shape)
    dt_rows = pack[:, :, :, bounds[2] : bounds[3]].reshape(nd, nz, 2, heads // nz, -1)
    dt_weight = jnp.transpose(dt_rows, (1, 3, 0, 2, 4)).reshape(heads, D)
    dt_weight = jnp.pad(dt_weight, ((0, 128 - heads), (0, 0)))
    bc_rows = pack[:, :, :, bounds[3] : bounds[4]].reshape(nd, nz, 2, -1, 2 * NS)
    bc_weight = jnp.transpose(bc_rows, (0, 2, 1, 3, 4)).reshape(D, 2 * NS)
    bc_half = lax.dynamic_slice_in_dim(bc_weight, core * NS, NS, 1)
    dt_weight = dt_weight.T
    tail_weight = jnp.concatenate([bc_half, dt_weight], 1)
    first_weight = jnp.concatenate([bc_weight, dt_weight], 1)

    hl = dt_bias.shape[0]

    def own_part(v):
        v = v.reshape(v.shape[0], 2, v.shape[1] // 2)
        return lax.dynamic_index_in_dim(v, core, 1, False).reshape(-1)

    bias = jnp.pad(own_part(params[:, :hl]), (0, 128 - heads))[None]
    rate = jnp.pad(-jnp.exp(own_part(params[:, hl : 2 * hl])), (0, 128 - heads))[None]
    skip = jnp.repeat(own_part(params[:, 2 * hl : 3 * hl]), P_SIZE)[None]
    width = gate_gain.shape[0]
    gain = own_part(params[:, 3 * hl : 3 * hl + width])[None]
    taps = params[:, 3 * hl + width :].reshape(nz, KC, 2, part)
    taps = jnp.transpose(lax.dynamic_index_in_dim(taps, core, 2, False), (1, 0, 2)).reshape(KC, chan)

    order = jnp.arange(micros)
    runs = run_of(order, z)
    sequence, chunk = runs // nz, lax.rem(runs, nz)
    lengths = jnp.take(lengths[:, 0], sequence)[:, None]
    ids = jnp.take(adapter_ids[:, 0], sequence)
    all_pos = (chunk * tokens)[:, None] + jnp.arange(tokens)
    own_pos = (chunk * tokens)[:, None] + core * own + jnp.arange(own)
    enters = (order == nz - 1 - z)[:, None, None]
    leaves = (order == nz - 2 - z)[:, None, None]
    forward_edge = [(i, i + 1) for i in range(nz - 1)]
    backward_edge = [(i + 1, i) for i in range(nz - 1)]

    m3 = lambda m, g: (m, 0, g)
    m0 = lambda m, g: (m, 0, 0)
    z2 = lambda m, g: (0, 0)
    shape = jax.ShapeDtypeStruct

    def per_token(width, index=m3):
        return block((1, tokens, width), index)

    chan_block = per_token(wide)
    halo_block = block((1, HALO, wide), m3)
    taps_block = block((KC, wide), lambda m, g: (0, g))
    line_block = block((1, wide), lambda m, g: (0, g))
    state_block = block((1, NS, wide), m3)
    bc_block = per_token(2 * NS, m0)
    bc_halo = block((1, HALO, 2 * NS), m0)
    bc_taps = block((KC, 2 * NS), z2)
    bc_edge = block((1, 8, 2 * NS), m0)
    one_col = per_token(1, m0)
    sums = per_token(128, m0)
    lanes_block = block((1, 1, 2 * HG, tokens), lambda m, g: (m, g, 0, 0))
    head_line = block((1, 128), z2)
    edge_block = block((1, 8, wide), m3)
    tok_f32 = shape((micros, tokens, chan), f32)
    tok_b16 = shape((micros, tokens, chan), bf16)
    state_f32 = shape((micros, NS, chan), f32)
    bc_f32 = shape((micros, tokens, 2 * NS), f32)
    sums_f32 = shape((micros, tokens, 128), f32)
    edge_f32 = shape((micros, 8, chan), f32)
    act_bytes = tokens * chan * 4
    dma = pltpu.SemaphoreType.DMA
    line_scratch = [pltpu.VMEM((groups, NS, wide), f32), pltpu.VMEM((2 * groups, NS, wide), f32)] + [dma((groups,))] * 2
    scan_grid = (micros, groups)

    x_low = x_rows
    x_rows = x_rows.astype(f32)
    inv_rms = lax.rsqrt(jnp.mean(x_rows * x_rows, axis=-1, keepdims=True) + eps)
    low_own = (x_rows * inv_rms * norm_gain).astype(bf16)
    mask_own = (own_pos < lengths).astype(f32)[..., None]
    mask = (all_pos < lengths).astype(f32)[..., None]
    picks = (adapter_ids == jnp.arange(ADAPT)).astype(f32)
    tall = bounds[2]
    factors = pl.pallas_call(
        pick_kernel,
        name="pick",
        grid_spec=pltpu.PrefetchScalarGridSpec(
            num_scalar_prefetch=1,
            grid=(micros, nz),
            in_specs=[block((1, 1, 1, tall, part), lambda m, n, k: (k[m] // 2, n, lax.rem(k[m], 2), 0, 0))],
            out_specs=block((1, 1, tall, part), lambda m, n, k: (m, n, 0, 0)),
        ),
        out_shape=shape((micros, nz, tall, part), bf16),
    )(ids, pack)
    per = 2 * R * each // line
    wide_rows = [lax.dynamic_slice_in_dim(pack, bounds[4] + per * ids[m], per, 3) for m in range(micros)]
    wide_rows = jnp.stack(wide_rows).reshape(micros, nd, nz, 2, 2, R, each)
    wide_rows = jnp.transpose(wide_rows, (4, 0, 5, 1, 3, 2, 6)).reshape(2, micros, R, D)

    def wide_block(kind, width, index):
        return block((1, micros, R, width), lambda m, g: (kind, 0, 0, index(g)))

    def every(width, index=None):
        if index is None:
            return pl.BlockSpec((micros, tokens, width), lambda m, g: (0, 0, 0), pipeline_mode=pl.Buffered(1))
        return block((micros, tokens, width), index)

    by_step = lambda m, g: (0, 0, g)
    rank_b16 = shape((micros, tokens, 2 * R), bf16)
    half_steps = chan // part
    steps = 2 * half_steps
    cot = cotangent[:, 0]
    early = 1
    hbm = pl.BlockSpec(memory_space=pl.ANY)
    pair_scratch = [pltpu.VMEM((micros, tokens, D), bf16), dma((4,))]
    xin, z_in, bcin, rate_in, lr, low, cot_early = call(
        project_kernel, "project", (1, steps),
        [(low_own, hbm), (zx_weight, block((1, D, part), lambda m, g: (1 - g // half_steps, 0, g % half_steps))),
         (first_weight, block((D, 2 * NS + 128), z2)), (wide_rows, wide_block(0, D, lambda g: 0)),
         (factors, block((micros, 1, R, part), lambda m, g: (0, g % half_steps, 1 - g // half_steps, 0)))],
        [(tok_b16, every(part, lambda m, g: (0, 0, jnp.minimum(g, half_steps - 1)))),
         (tok_f32, every(part, lambda m, g: (0, 0, jnp.maximum(g - half_steps, 0)))),
         (shape((micros, tokens, 2 * NS), bf16), every(2 * NS)), (sums_f32, every(128)), (rank_b16, every(2 * R)), (shape((micros, tokens, D), bf16), hbm)],
        pair_scratch, 4 * tokens * D * chan, act_bytes * 4, 2, (cot, shape((early, own, D), bf16), tuple(range(early)), True),
    )
    tail = jnp.concatenate([xin[:, tokens - HALO :], bcin[:, tokens - HALO :]], axis=2)
    goes = jnp.sum(jnp.where(leaves, tail, 0), axis=0, dtype=bf16)
    halo = jnp.where(enters, lax.ppermute(goes, "mp", forward_edge)[None], jnp.pad(tail[:-1], ((1, 0), (0, 0), (0, 0))))
    halo, bchalo = halo[..., :chan], halo[..., chan:]
    step, cum, lanes, bc = call(
        skip_grid(prep_kernel), "prep", (micros, 1),
        [(rate_in, sums), (bias, head_line), (rate, head_line), (mask, one_col), (bcin, bc_block), (bchalo, bc_halo),
         (conv_bc, bc_taps)],
        [(sums_f32, sums), (sums_f32, sums),
         (shape((micros, groups, 2 * HG, tokens), f32), block((1, groups, 2 * HG, tokens), lambda m, g: (m, 0, 0, 0))),
         (bc_f32, bc_block)],
        [], tokens * Q * 128 * 6, tokens * 128 * 24,
    )
    mixed, square, state, end_state, cot_late = call(
        forward_kernel, "ssd_forward", scan_grid,
        [(xin, chan_block), (halo, halo_block), (taps, taps_block), (bc, bc_block), (cum, sums), (step, sums),
         (lanes, lanes_block), (skip, line_block), (z_in, chan_block)],
        [(tok_f32, chan_block), (sums_f32, sums), (state_f32, state_block), (state_f32, state_block)],
        [pltpu.VMEM((blocks, Q, Q), f32), pltpu.VMEM((2, blocks, NS, Q), bf16), *line_scratch],
        6 * tokens * Q * chan * 2, act_bytes * 3, 3, (cot, shape((micros - early, own, D), bf16), tuple(range(early, micros)), True),
    )

    cols = out_all.shape[3]
    gb_own = jnp.concatenate([cot_early, cot_late], 0) * mask_own.astype(bf16)
    part_block = every(part, by_step)
    gs, dots, rg, gb = call(
        gs_kernel, "gs", (1, nz),
        [(gb_own, hbm), (out_all, block((nd, 1, part, cols), lambda m, g: (0, g, 0, 0))), (wide_rows, wide_block(1, D, lambda g: 0)),
         (factors, block((micros, 1, R, part), lambda m, g: (0, g, 2, 0))), (mixed, part_block), (z_in, part_block),
         (gain, block((1, part), lambda m, g: (0, g)))],
        [(tok_f32, part_block), (sums_f32, every(128)), (rank_b16, every(2 * R)), (shape((micros, tokens, D), bf16), hbm)],
        pair_scratch, 6 * tokens * D * chan, act_bytes * 15, 7,
    )
    both = jnp.stack([jnp.sum(square, axis=-1), jnp.sum(dots, axis=-1)])
    both = (both + other(both)) / DI
    inv_gate = lax.rsqrt(both[0] + eps)[..., None]
    coef = inv_gate**3 * both[1][..., None]
    dy, gz, scaled, lloc, q = call(
        gate_back_kernel, "gate_back", scan_grid,
        [(gs, chan_block), (mixed, chan_block), (z_in, chan_block), (inv_gate, one_col), (coef, one_col), (gain, line_block),
         (bc, bc_block), (cum, sums)],
        [(tok_f32, chan_block), (tok_b16, chan_block), (tok_b16, chan_block), (state_f32, state_block), (sums_f32, sums)],
        [pltpu.VMEM((2, NS, tokens), bf16)], 6 * tokens * NS * chan, act_bytes * 5,
    )
    step_cols = every(cols, by_step)
    rank_scratch = [pltpu.VMEM((micros, tokens, 2 * R), bf16)] + [pltpu.VMEM((micros, 2 * R, tokens), bf16)] * 2
    rank_cols = block((micros, R, cols), by_step)
    own_rows = pl.BlockSpec((micros, own, D), lambda m, g: (0, 0, 0), pipeline_mode=pl.Buffered(1))
    own_col = block((micros, own, 1), lambda m, g: (0, 0, 0))

    def pair_sum(steps):
        width = D // steps
        return [pltpu.VMEM((2, micros, tokens, width), f32), pltpu.VMEM((steps, micros, own, width), f32), dma((steps,)), dma((steps,))]

    out_rows, g_up_out, g_out = call(
        branch_kernel, "branch", (1, nd),
        [(scaled, every(chan)), (out_all, block((1,) + out_all.shape[1:], lambda m, g: (g, 0, 0, 0))),
         (factors, block((micros, nz, R, part), lambda m, g: (0, 0, 2, 0))), (wide_rows, wide_block(1, cols, lambda g: g)),
         (rg, every(2 * R)), (gb, step_cols), (x_low, own_rows), (mask_own, own_col)],
        [(shape((micros, own, D), bf16), own_rows), (shape((micros, R, D), f32), rank_cols),
         (shape((micros, R, chan), f32), block((micros, R, chan // nd), by_step))],
        rank_scratch + pair_sum(nd), 6 * tokens * D * chan, act_bytes * 12, 8,
    )

    first_slots, last_slots = tuple(range(micros - 1)), (micros - 1,)

    def last_first(spec):
        index = spec.index_map
        return block(spec.block_shape, lambda m, g: index(micros - 1 - m, g))

    ins = [(dy, chan_block), (xin, chan_block), (halo, halo_block), (taps, taps_block), (bc, bc_block), (cum, sums), (step, sums),
           (lanes, lanes_block), (skip, line_block), (state, state_block), (lloc, state_block), (end_state, state_block)]
    outs = [(tok_b16, chan_block), (edge_f32, edge_block), (edge_f32, edge_block), (bc_f32, bc_block), (sums_f32, sums),
            (sums_f32, sums)]
    gx, head, tail, gbc, xu, dx, out_first = call(
        scan_back_kernel, "ssd_back", scan_grid,
        [(a, last_first(s)) for a, s in ins], [(a, last_first(s)) for a, s in outs],
        [pltpu.VMEM((blocks, Q, Q), f32), pltpu.VMEM((blocks, Q, Q), f32), pltpu.VMEM((2, blocks, NS, Q), bf16),
         pltpu.VMEM((2, blocks, NS, Q), bf16), *line_scratch],
        12 * tokens * Q * chan * 2, act_bytes * 3, 4, (out_rows, shape((micros, seg, feats), bf16), first_slots, False),
    )
    gbc = gbc + other(gbc)
    edge_bc = shape((micros, 8, 2 * NS), f32)
    gbc, bhead, btail, g_rate = call(
        skip_grid(bc_back_kernel), "bc_back", (micros, 1),
        [(gbc, bc_block), (bcin, bc_block), (bchalo, bc_halo), (conv_bc, bc_taps), (q, sums), (dx, sums), (xu, sums),
         (step, sums), (rate_in, sums), (bias, head_line), (rate, head_line), (mask, one_col)],
        [(shape((micros, tokens, 2 * NS), bf16), bc_block), (edge_bc, bc_edge), (edge_bc, bc_edge),
         (shape((micros, tokens, 128), bf16), sums)],
        [], tokens * tokens * 128 * 6, tokens * 2 * NS * 8,
    )
    head = jnp.concatenate([head, bhead], 2)
    goes = lax.ppermute(jnp.sum(jnp.where(enters, head, 0), axis=0), "mp", backward_edge)
    back = jnp.pad(jnp.where(enters, 0, head)[1:], ((0, 1), (0, 0), (0, 0))) + jnp.where(leaves, goes[None], 0)
    tail = jnp.concatenate([tail, btail], 2).at[:, 8 - (KC - 1) :].add(back[:, 8 - (KC - 1) :]).astype(bf16)
    gx = lax.dynamic_update_slice_in_dim(gx, tail[..., :chan], tokens - 8, 1)
    gbc = lax.dynamic_update_slice_in_dim(gbc, tail[..., chan:], tokens - 8, 1)
    tail = jnp.concatenate([lax.dynamic_slice_in_dim(gbc, core * NS, NS, 2), g_rate], 2)
    back_steps = 2 * nz
    wide_cols, back_chan = D // back_steps, chan // back_steps
    delta, g_up_z, g_up_x, g_down, out_last = call(
        unproject_kernel, "unproject", (1, back_steps),
        [(gz, every(chan)), (gx, every(chan)), (tail, every(NS + 128)),
         (zx_weight, block((2, wide_cols, chan), lambda m, g: (0, g, 0))), (tail_weight, block((wide_cols, NS + 128), lambda m, g: (g, 0))),
         (factors, block((micros, nz, 2 * R, part), lambda m, g: (0, 0, 0, 0))), (wide_rows, wide_block(0, wide_cols, lambda g: g)),
         (lr, every(2 * R)), (low, every(wide_cols, by_step)), (x_low, own_rows), (inv_rms, own_col),
         (norm_gain[None], block((1, D), z2))],
        [(shape((micros, own, D), bf16), own_rows), (shape((micros, R, chan), f32), block((micros, R, back_chan), by_step)),
         (shape((micros, R, chan), f32), block((micros, R, back_chan), by_step)),
         (shape((micros, R, D), f32), block((micros, R, wide_cols), by_step))],
        rank_scratch + pair_sum(back_steps), 12 * tokens * D * chan, act_bytes * 9, 6, (out_rows[-1:], shape((micros, seg, feats), bf16), last_slots, False),
    )
    held_runs = jnp.arange(micros)[:, None] * nz + 2 * core + jnp.arange(2)
    in_last = place_of(held_runs)[1] == micros - 1
    in_last = jnp.repeat(in_last, tokens, axis=1)[..., None]
    out = jnp.where(in_last, out_last, out_first)[:, None]
    mine = (sequence == jnp.arange(micros)[:, None]).astype(f32)

    delta, near, far = finish(
        [g_out, g_up_z, g_up_x, g_up_out, g_down], mine, picks, delta, shape((micros, seg, feats), bf16), nz, nd
    )
    grad = cotangent.astype(f32) + delta[:, None].astype(f32)
    g_out_down = jnp.transpose(near[:, 0], (0, 2, 1)).reshape(2 * part, R)
    g_in_up = jnp.transpose(near[:, 1:], (2, 1, 0, 3)).reshape(R, 2, 2 * part)
    g_out_up = far[:, 0].reshape(ADAPT * R, each)
    g_in_down = jnp.transpose(far[:, 1], (0, 2, 1))
    return (out, grad, g_in_down, g_in_up, g_out_down, g_out_up)


def solution(mesh):
    in_specs = (
        P(None, "dp", "seq", "mp"),
        P(None, "dp", "seq", "mp"),
        P(None, "dp"),
        P(None, "dp"),
        P(),
        P(("dp", "seq"), None, "mp"),
        P(("dp", "seq"), None),
        P(("dp", "seq"), "mp"),
        P("mp"),
        P("mp"),
        P("mp"),
        P(None, "mp"),
        P(),
        P("mp"),
        P("mp", ("dp", "seq")),
        P(None, ("dp", "seq", "mp"), None),
        P(("dp", "seq"), None, "mp"),
        P("mp", ("dp", "seq")),
        P(None, ("dp", "seq", "mp")),
    )
    out_specs = (
        P(None, "dp", "seq", "mp"),
        P(None, "dp", "seq", "mp"),
        P(None, ("dp", "seq", "mp"), None),
        P(("dp", "seq"), None, "mp"),
        P("mp", ("dp", "seq")),
        P(None, ("dp", "seq", "mp")),
    )
    sizes = dict(mesh.shape)
    by_chip = (
        sizes["seq"] == 2
        and sizes["dp"] * 2 == ADAPT
        and sizes["mp"] == SLOTS + 1
    )
    return jax.shard_map(fast_body if by_chip else body, mesh=mesh, in_specs=in_specs, out_specs=out_specs, check_vma=False)
```

```python
import functools

import jax
import jax.numpy as jnp
from jax import lax
from jax.experimental import pallas as pl
from jax.experimental.pallas import tpu as pltpu
from jax.sharding import PartitionSpec as P

D = 2048
P_SIZE = 64
NS = 128
KC = 4
Q = 256
R = 16
ADAPT = 8
DI = 4096
HG = 4
HALO = 16
SLOTS = 3


eps = 1e-05
precise = lax.Precision.HIGHEST
VMEM_LIMIT = 56 * 1024 * 1024


def shifted(array, axis, by):
    size = lax.axis_size(axis)
    pairs = [(i, i + by) for i in range(size) if 0 <= i + by < size]
    return lax.ppermute(array, axis, pairs)


def entering(part, axis, combine, identity, reverse):
    count = lax.axis_size(axis)
    place = lax.axis_index(axis)
    ahead = count - 1 - place if reverse else place
    gathered = jax.tree.map(lambda a: lax.all_gather(a, axis), part)
    state = jax.tree.map(lambda a, e: jnp.zeros_like(a) + jnp.asarray(e, a.dtype), part, identity)

    def one(hop, state):
        source = count - 1 - hop if reverse else hop
        return combine(
            state, jax.tree.map(lambda a: lax.dynamic_index_in_dim(a, source, 0, False), gathered)
        )

    return lax.fori_loop(0, ahead, one, state)


def silu_grad(value):
    sigmoid_val = jax.nn.sigmoid(value)
    return sigmoid_val * (1.0 + value * (1.0 - sigmoid_val))


def block_step(carry_state, pieces):
    x_part, b_part, c_part, log_part, step_part = pieces
    length = log_part.shape[0]
    cumulative = jnp.cumsum(log_part, axis=0)
    causal = jnp.arange(length)[:, None] >= jnp.arange(length)[None, :]
    spread = cumulative[:, None, :] - cumulative[None, :, :]
    decay_mat = jnp.exp(jnp.where(causal[:, :, None], spread, -10000.0))
    scores = jnp.dot(c_part, b_part.T, precision=precise)
    mixing = scores[:, :, None] * decay_mat * step_part[None, :, :]
    inner_out = jnp.einsum("tsh,shp->thp", mixing, x_part, precision=precise)
    carried = jnp.exp(cumulative)[:, :, None] * jnp.einsum(
        "tn,hpn->thp", c_part, carry_state, precision=precise
    )
    weights = jnp.exp(cumulative[-1][None, :] - cumulative) * step_part
    update = jnp.einsum("sh,shp,sn->hpn", weights, x_part, b_part, precision=precise)
    new_state = jnp.exp(cumulative[-1])[:, None, None] * carry_state + update
    return (new_state, inner_out + carried)


def local_scan(x_heads, b_rows, c_rows, log_rows, step_rows):
    seg_rows = x_heads.shape[0]
    blocks = seg_rows // Q

    def blocked(tensor):
        return tensor.reshape((blocks, Q) + tensor.shape[1:])

    init_state = jnp.zeros((x_heads.shape[1], x_heads.shape[2], b_rows.shape[1]), jnp.float32)
    final_state, outputs = lax.scan(
        block_step,
        init_state,
        (blocked(x_heads), blocked(b_rows), blocked(c_rows), blocked(log_rows), blocked(step_rows)),
    )
    return (outputs.reshape(x_heads.shape), final_state, jnp.sum(log_rows, axis=0))


def incoming(c_rows, log_rows, state_in):
    cumulative = jnp.cumsum(log_rows, axis=0)
    return jnp.exp(cumulative)[:, :, None] * jnp.einsum(
        "tn,hpn->thp", c_rows, state_in, precision=precise
    )


def compose(earlier, later):
    return (later[0] * earlier[0], later[1] + later[0][..., None, None] * earlier[1])


def fetch_weights(w_zx, w_bc, w_dt, w_out, in_up, out_down):
    return (
        lax.all_gather(w_zx, ("dp", "seq"), axis=0, tiled=True),
        lax.all_gather(w_bc, ("dp", "seq"), axis=0, tiled=True),
        lax.all_gather(w_dt, ("dp", "seq"), axis=0, tiled=True),
        lax.all_gather(w_out, ("dp", "seq"), axis=1, tiled=True),
        lax.all_gather(in_up, ("dp", "seq"), axis=0, tiled=True),
        lax.all_gather(out_down, ("dp", "seq"), axis=1, tiled=True),
    )


def reduce_adapters(grads):
    near_sums = (
        lax.psum_scatter(grads[1], ("dp", "seq"), scatter_dimension=0, tiled=True),
        lax.psum_scatter(grads[2], ("dp", "seq"), scatter_dimension=1, tiled=True),
    )
    wide_sums = (
        lax.psum_scatter(grads[0], ("dp", "seq", "mp"), scatter_dimension=1, tiled=True),
        lax.psum_scatter(grads[3], ("dp", "seq", "mp"), scatter_dimension=1, tiled=True),
    )
    return (wide_sums[0], near_sums[0], near_sums[1], wide_sums[1])


def body(
    x_in,
    cotangent,
    lengths,
    adapter_ids,
    norm_gain,
    w_zx,
    w_bc,
    w_dt,
    dt_bias,
    a_log,
    d_skip,
    conv_x,
    conv_bc,
    gate_gain,
    w_out,
    in_down,
    in_up,
    out_down,
    out_up,
):
    micro_count, slot_count, seg_len, model_part = x_in.shape
    head_local = dt_bias.shape[0]
    inner_local = head_local * P_SIZE
    wide_down, wide_up = (
        lax.all_gather(in_down, ("dp", "seq", "mp"), axis=1, tiled=True),
        lax.all_gather(out_up, ("dp", "seq", "mp"), axis=1, tiled=True),
    )
    wide_down = wide_down.astype(jnp.float32)
    wide_up = wide_up.astype(jnp.float32)
    conv_taps = jnp.concatenate([conv_x, conv_bc], axis=1)
    decay_rate = -jnp.exp(a_log)
    positions = lax.axis_index("seq") * seg_len + jnp.arange(seg_len)
    feature_start = lax.axis_index("mp") * model_part
    scan_local = jax.vmap(local_scan)
    incoming_map = jax.vmap(incoming)
    gathered = None
    outputs = []
    x_grads = []
    running = None
    for batch_index in range(micro_count):
        gathered = fetch_weights(w_zx, w_bc, w_dt, w_out, in_up, out_down)
        zx_weight, bc_weight, dt_weight, out_weight, up_in, down_out = gathered
        rows_own = x_in[batch_index]
        cot_own = cotangent[batch_index]
        rows_full, cot_full = (
            lax.all_gather(rows_own, "mp", axis=2, tiled=True),
            lax.all_gather(cot_own, "mp", axis=2, tiled=True),
        )
        rows_value = rows_full.astype(jnp.float32)
        inv_rms = lax.rsqrt(jnp.mean(rows_value * rows_value, axis=-1, keepdims=True) + eps)
        normed = rows_value * inv_rms * norm_gain
        normed_low = normed.astype(jnp.bfloat16)
        normed_value = normed_low.astype(jnp.float32)
        select = jax.nn.one_hot(adapter_ids[batch_index], ADAPT, dtype=jnp.float32)
        down_sel = jnp.einsum("sa,adr->sdr", select, wide_down, precision=precise)
        up_sel = jnp.einsum(
            "sa,arcf->srcf",
            select,
            up_in.astype(jnp.float32).reshape(ADAPT, R, 2, inner_local),
            precision=precise,
        )
        low_rank = jnp.einsum("std,sdr->str", normed_value, down_sel, precision=precise)
        proj_zx = jnp.einsum(
            "std,dcf->stcf", normed_low, zx_weight, preferred_element_type=jnp.float32
        )
        proj_zx = proj_zx + jnp.einsum("str,srcf->stcf", low_rank, up_sel, precision=precise)
        proj_bc = jnp.einsum(
            "std,dn->stn", normed_low, bc_weight, preferred_element_type=jnp.float32
        )
        proj_dt = jnp.einsum(
            "std,dh->sth", normed_low, dt_weight, preferred_element_type=jnp.float32
        )
        gate_in = proj_zx[:, :, 0]
        conv_in = jnp.concatenate(
            [proj_zx[:, :, 1].astype(jnp.bfloat16), proj_bc.astype(jnp.bfloat16)], axis=-1
        )
        earlier_rows = shifted(conv_in[:, seg_len - (KC - 1) :], "seq", 1)
        extended = jnp.concatenate([earlier_rows, conv_in], axis=1).astype(jnp.float32)
        conv_pre = sum(
            (
                conv_taps[tap_index] * extended[:, tap_index : tap_index + seg_len]
                for tap_index in range(KC)
            )
        )
        conv_out = jax.nn.silu(conv_pre)
        x_heads = conv_out[..., :inner_local].reshape(slot_count, seg_len, head_local, P_SIZE)
        b_rows = conv_out[..., inner_local : inner_local + NS]
        c_rows = conv_out[..., inner_local + NS :]
        mask_rows = (positions[None, :] < lengths[batch_index][:, None]).astype(jnp.float32)
        rate_in = proj_dt + dt_bias
        step_rows = jax.nn.softplus(rate_in) * mask_rows[..., None]
        log_rows = step_rows * decay_rate
        (plain_out, state_local, log_total), scan_back = jax.vjp(
            scan_local, x_heads, b_rows, c_rows, log_rows, step_rows
        )
        factor = jnp.exp(log_total)
        identity = (jnp.ones_like(factor), jnp.zeros_like(state_local))
        state_in = entering((factor, state_local), "seq", compose, identity, False)[1]
        from_state, state_back = jax.vjp(incoming_map, c_rows, log_rows, state_in)
        mixed_heads = plain_out + from_state + d_skip[:, None] * x_heads
        mixed_flat = mixed_heads.reshape(slot_count, seg_len, inner_local)
        gate_act = jax.nn.silu(gate_in)
        gated_out = mixed_flat * gate_act
        square_sum = lax.psum(jnp.sum(gated_out * gated_out, axis=-1), "mp")
        inv_gate = lax.rsqrt(square_sum / DI + eps)
        scaled = gated_out * inv_gate[..., None] * gate_gain
        scaled_low = scaled.astype(jnp.bfloat16)
        scaled_value = scaled_low.astype(jnp.float32)
        out_sel = jnp.einsum(
            "sa,far->sfr",
            select,
            down_out.astype(jnp.float32).reshape(inner_local, ADAPT, R),
            precision=precise,
        )
        up_out = jnp.einsum("sa,ard->srd", select, wide_up.reshape(ADAPT, R, D), precision=precise)
        rank_out = jnp.einsum("stf,sfr->str", scaled_value, out_sel, precision=precise)
        partial_out = jnp.einsum(
            "stf,fd->std", scaled_low, out_weight, preferred_element_type=jnp.float32
        )
        partial_out = partial_out + jnp.einsum("str,srd->std", rank_out, up_out, precision=precise)
        branch = lax.psum_scatter(partial_out, "mp", scatter_dimension=2, tiled=True)
        outputs.append(
            (rows_own.astype(jnp.float32) + mask_rows[..., None] * branch).astype(jnp.bfloat16)
        )
        branch_grad = cot_full * mask_rows[..., None].astype(jnp.bfloat16)
        branch_value = branch_grad.astype(jnp.float32)
        rank_grad = jnp.einsum("std,srd->str", branch_value, up_out, precision=precise)
        grad_up_out = jnp.einsum("str,std->srd", rank_out, branch_value, precision=precise)
        grad_out_sel = jnp.einsum("stf,str->sfr", scaled_value, rank_grad, precision=precise)
        scaled_grad = jnp.einsum(
            "std,fd->stf", branch_grad, out_weight, preferred_element_type=jnp.float32
        )
        scaled_grad = scaled_grad + jnp.einsum(
            "str,sfr->stf", rank_grad, out_sel, precision=precise
        )
        weighted = scaled_grad * gate_gain
        dot_sum = lax.psum(jnp.sum(weighted * gated_out, axis=-1), "mp")
        gated_grad = (
            weighted * inv_gate[..., None] - gated_out * (inv_gate**3 * dot_sum / DI)[..., None]
        )
        mixed_grad = (gated_grad * gate_act).reshape(slot_count, seg_len, head_local, P_SIZE)
        gate_grad = gated_grad * mixed_flat * silu_grad(gate_in)
        c_grad_in, log_grad_in, state_in_grad = state_back(mixed_grad)
        later_grads = entering((factor, state_in_grad), "seq", compose, identity, True)[1]
        total_grad = jnp.sum(later_grads * state_in, axis=(2, 3)) * factor
        x_heads_grad, b_grad, c_grad, log_grad, step_grad = scan_back(
            (mixed_grad, later_grads, total_grad)
        )
        x_heads_grad = x_heads_grad + d_skip[:, None] * mixed_grad
        c_grad = c_grad + c_grad_in
        step_grad = step_grad + (log_grad + log_grad_in) * decay_rate
        rate_grad = step_grad * mask_rows[..., None] * jax.nn.sigmoid(rate_in)
        conv_out_grad = jnp.concatenate(
            [x_heads_grad.reshape(slot_count, seg_len, inner_local), b_grad, c_grad], axis=-1
        )
        pre_grad = conv_out_grad * silu_grad(conv_pre)
        padded_grad = jnp.pad(pre_grad, ((0, 0), (KC - 1, KC - 1), (0, 0)))
        ext_grad = sum(
            (
                conv_taps[tap_index]
                * padded_grad[:, KC - 1 - tap_index : KC - 1 - tap_index + seg_len + KC - 1]
                for tap_index in range(KC)
            )
        )
        returned = shifted(ext_grad[:, : KC - 1], "seq", -1)
        in_grad = ext_grad[:, KC - 1 :]
        in_grad = in_grad.at[:, seg_len - (KC - 1) :].add(returned)
        zx_grad = jnp.stack([gate_grad, in_grad[..., :inner_local]], axis=2).astype(jnp.bfloat16)
        dt_grad_low = rate_grad.astype(jnp.bfloat16)
        zx_grad_value = zx_grad.astype(jnp.float32)
        rank_in_grad = jnp.einsum("stcf,srcf->str", zx_grad_value, up_sel, precision=precise)
        grad_up_sel = jnp.einsum("str,stcf->srcf", low_rank, zx_grad_value, precision=precise)
        grad_down_sel = jnp.einsum("std,str->sdr", normed_value, rank_in_grad, precision=precise)
        normed_part = jnp.einsum(
            "stcf,dcf->std", zx_grad, zx_weight, preferred_element_type=jnp.float32
        )
        normed_part = normed_part + jnp.einsum(
            "sth,dh->std", dt_grad_low, dt_weight, preferred_element_type=jnp.float32
        )
        normed_part = normed_part + jnp.einsum(
            "str,sdr->std", rank_in_grad, down_sel, precision=precise
        )
        bc_partial = in_grad[..., inner_local:]
        normed_sum, bc_sum = lax.psum((normed_part, bc_partial), "mp")
        normed_grad = normed_sum + jnp.einsum(
            "stn,dn->std",
            bc_sum.astype(jnp.bfloat16),
            bc_weight,
            preferred_element_type=jnp.float32,
        )
        scaled_in = normed_grad * norm_gain
        row_grad = inv_rms * scaled_in - rows_value * inv_rms**3 * jnp.mean(
            scaled_in * rows_value, axis=-1, keepdims=True
        )
        own_slice = lax.dynamic_slice_in_dim(row_grad, feature_start, model_part, 2)
        x_grads.append(cot_own.astype(jnp.float32) + own_slice)
        local_grads = (
            jnp.einsum("sa,sdr->adr", select, grad_down_sel, precision=precise),
            jnp.einsum("sa,srcf->arcf", select, grad_up_sel, precision=precise).reshape(
                ADAPT * R, 2, inner_local
            ),
            jnp.einsum("sa,sfr->far", select, grad_out_sel, precision=precise).reshape(
                inner_local, ADAPT * R
            ),
            jnp.einsum("sa,srd->ard", select, grad_up_out, precision=precise).reshape(ADAPT * R, D),
        )
        running = local_grads if running is None else jax.tree.map(jnp.add, running, local_grads)
    running = reduce_adapters(running)
    return (jnp.stack(outputs), jnp.stack(x_grads), running[0], running[1], running[2], running[3])


MESH = pl.DeviceIdType.MESH


def split(v):
    hi = v.astype(jnp.bfloat16)
    return hi, (v - hi.astype(jnp.float32)).astype(jnp.bfloat16)


def mm(a, b):
    return lax.dot_general(a, b, (((1,), (0,)), ((), ())), preferred_element_type=jnp.float32)


def mm_t(a, b):
    return lax.dot_general(a, b, (((1,), (1,)), ((), ())), preferred_element_type=jnp.float32)


def mm3(a, b):
    return mm(a[0], b[0]) + mm(a[0], b[1]) + mm(a[1], b[0])


def mm3_t(a, b):
    return mm_t(a[0], b[0]) + mm_t(a[0], b[1]) + mm_t(a[1], b[0])


def ones_mm(ones, v):
    hi, lo = split(v)
    rest = v - hi.astype(jnp.float32) - lo.astype(jnp.float32)
    return mm(ones, hi) + mm(ones, lo) + mm(ones, rest.astype(jnp.bfloat16))


def conv_rows(rows, halo, taps):
    count = rows.shape[0]
    ext = jnp.concatenate([halo, rows], axis=0).astype(jnp.float32)
    first = HALO - (KC - 1)
    total = taps[0:1] * ext[first : first + count]
    for j in range(1, KC):
        total = total + taps[j : j + 1] * ext[first + j : first + j + count]
    return total


def conv_rows_back(grad, taps):
    count, width = grad.shape
    zero = jnp.zeros((8, width), jnp.float32)
    ext = jnp.concatenate([zero, grad, zero], axis=0)
    total = taps[0:1] * ext[3 : 3 + count + 8]
    for j in range(1, KC):
        total = total + taps[j : j + 1] * ext[3 - j : 3 - j + count + 8]
    return total


def widen(columns):
    rows = columns.shape[0]
    lane = lax.broadcasted_iota(jnp.int32, (rows, 2 * P_SIZE), 1)
    return jnp.concatenate(
        [jnp.where(lane < P_SIZE, columns[:, h : h + 1], columns[:, h + 1 : h + 2]) for h in range(0, HG, 2)], axis=1
    )


def of_group(value, group):
    return pltpu.roll(value, lax.rem(128 - group * HG, 128), 1)


def head_sums(prod, group):
    rows = prod.shape[1]
    row = lax.broadcasted_iota(jnp.int32, (rows, 128), 0) // P_SIZE + group * HG
    lane = lax.broadcasted_iota(jnp.int32, (rows, 128), 1)
    pick = (row == lane).astype(jnp.float32).astype(jnp.bfloat16)
    hi, lo = split(prod)
    return mm(hi, pick) + mm(lo, pick)


def lane_sum(v):
    part = v[:, :128]
    for k in range(1, v.shape[1] // 128):
        part = part + v[:, k * 128 : (k + 1) * 128]
    return part


def add_up(ref, value, group):
    @pl.when(group == 0)
    def _():
        ref[0] = value

    @pl.when(group > 0)
    def _():
        ref[0] += value


def run_of(slot, z):
    return SLOTS * z + lax.rem(slot + z, SLOTS)


def place_of(run):
    z = run // SLOTS
    return z, lax.rem(lax.rem(run, SLOTS) + SLOTS * SLOTS - z, SLOTS)


class Mover:
    def __init__(self, src_ref, dst_ref, send_sem, recv_sem, count, slots, to_rows):
        self.refs = src_ref, dst_ref, send_sem, recv_sem
        self.count, self.slots, self.to_rows = count, slots, to_rows
        self.d, self.c, self.z = lax.axis_index("dp"), lax.axis_index("seq"), lax.axis_index("mp")
        self.pieces = 4 * SLOTS if to_rows else count * len(slots)

    def piece(self, n):
        src_ref, dst_ref, send_sem, recv_sem = self.refs
        if self.to_rows:
            m, h, to_c = lax.rem(n // 4 + self.z, SLOTS), n // 2 % 2, lax.rem(n + self.c, 2)
            to_z, slot = place_of(m * self.count + 2 * self.c + h)
            own = src_ref.shape[1] // 4
            src = src_ref.at[m, pl.ds(pl.multiple_of((2 * h + to_c) * own, 16), own), :]
            dst, sem = self.landing(slot - self.slots[0], self.z), (slot, self.z)
            due = jnp.logical_and(slot >= self.slots[0], slot <= self.slots[-1])
        else:
            slot = self.slots[n // self.count]
            to_z = lax.rem(self.z + n % self.count, self.count)
            run = run_of(slot, self.z)
            m, chunk = run // self.count, lax.rem(run, self.count)
            to_c, q = chunk // 2, lax.rem(chunk, 2) * 2 + self.c
            feats = dst_ref.shape[2]
            src = src_ref.at[slot - self.slots[0], :, pl.ds(pl.multiple_of(to_z * feats, 128), feats)]
            dst, sem = self.landing(m, q), (m, q)
            due = True
        here = jnp.logical_and(to_c == self.c, to_z == self.z)
        near = pltpu.make_async_copy(src, dst, recv_sem.at[sem])
        far = pltpu.make_async_remote_copy(
            src_ref=src, dst_ref=dst, send_sem=send_sem.at[n], recv_sem=recv_sem.at[sem],
            device_id=(self.d, to_c, to_z), device_id_type=MESH,
        )
        return jnp.logical_and(due, here), jnp.logical_and(due, jnp.logical_not(here)), near, far

    def landing(self, first, slot):
        dst_ref = self.refs[1]
        if self.to_rows:
            feats = dst_ref.shape[2] // self.count
            return dst_ref.at[first, :, pl.ds(pl.multiple_of(slot * feats, 128), feats)]
        rows = dst_ref.shape[1] // 4
        return dst_ref.at[first, pl.ds(pl.multiple_of(slot * rows, 16), rows), :]

    def greet(self, barrier):
        for cc in range(2):
            for r in range(self.count):
                if cc or r:
                    device = (self.d, lax.rem(self.c + cc, 2), lax.rem(self.z + r, self.count))
                    pl.semaphore_signal(barrier, 1, device_id=device, device_id_type=MESH)
        return 2 * self.count - 1

    def start(self, n):
        stays, goes, near, far = self.piece(n)

        @pl.when(stays)
        def _():
            near.start()

        @pl.when(goes)
        def _():
            far.start()

    def start_at(self, step, steps):
        for n in range(self.pieces):
            @pl.when(step == n * steps // (2 * self.pieces))
            def _():
                self.start(n)

    def finish(self):
        recv_sem = self.refs[3]
        if self.to_rows:
            for slot in self.slots:
                for s in range(self.count):
                    area = self.landing(slot - self.slots[0], s)
                    pltpu.make_async_copy(area, area, recv_sem.at[slot, s]).wait()
        else:
            for m in range(SLOTS):
                for q in range(4):
                    run = m * self.count + 2 * self.c + q // 2
                    slot = place_of(run)[1]

                    @pl.when(jnp.logical_and(slot >= self.slots[0], slot <= self.slots[-1]))
                    def _():
                        area = self.landing(m, q)
                        pltpu.make_async_copy(area, area, recv_sem.at[m, q]).wait()
        for n in range(self.pieces):
            _, goes, _, far = self.piece(n)

            @pl.when(goes)
            def _():
                far.wait_send()


class Line:
    def __init__(self, held_ref, sent_ref, send_sem, recv_sem, count, step):
        self.refs = held_ref, sent_ref, send_sem, recv_sem
        self.step, self.count = step, count
        self.d, self.c, self.z = lax.axis_index("dp"), lax.axis_index("seq"), lax.axis_index("mp")
        low, high = self.z > 0, self.z < count - 1
        self.has_source, self.has_target = (low, high) if step > 0 else (high, low)
        above, below = count - 1 - self.z, count - 2 - self.z
        self.from_slot, self.to_slot = (above, below) if step > 0 else (below, above)

    def greet(self, barrier):
        @pl.when(self.has_source)
        def _():
            pl.semaphore_signal(barrier, 1, device_id=(self.d, self.c, self.z - self.step), device_id_type=MESH)
        return jnp.where(self.has_target, 1, 0)

    def copy(self, group):
        held_ref, sent_ref, send_sem, recv_sem = self.refs
        return pltpu.make_async_remote_copy(
            src_ref=sent_ref.at[group], dst_ref=held_ref.at[group], send_sem=send_sem.at[group], recv_sem=recv_sem.at[group],
            device_id=(self.d, self.c, self.z + self.step), device_id_type=MESH,
        )

    def receive(self, slot, group):
        held_ref, sent_ref = self.refs[:2]
        remote = jnp.logical_and(self.has_source, slot == self.from_slot)
        fresh = slot == (0 if self.step > 0 else SLOTS - 1)
        local = jnp.logical_not(jnp.logical_or(remote, fresh))

        @pl.when(remote)
        def _():
            self.copy(group).wait_recv()
            sent_ref[held_ref.shape[0] + group] = held_ref[group]

        return jnp.where(jnp.logical_or(remote, local), sent_ref[held_ref.shape[0] + group], 0.0)

    def send(self, slot, group, value):
        held_ref, sent_ref = self.refs[:2]
        sent_ref[held_ref.shape[0] + group] = value

        @pl.when(jnp.logical_and(self.has_target, slot == self.to_slot))
        def _():
            sent_ref[group] = value
            self.copy(group).start()

    def finish(self):
        @pl.when(self.has_target)
        def _():
            for g in range(self.refs[0].shape[0]):
                self.copy(g).wait_send()


class PairFill:
    def __init__(self, own_ref, both_ref, buffer_ref, sems):
        self.d, self.c, self.z = lax.axis_index("dp"), lax.axis_index("seq"), lax.axis_index("mp")
        own = own_ref.shape[1]
        mine = buffer_ref.at[:, pl.ds(pl.multiple_of(self.c * own, 16), own), :]
        theirs = buffer_ref.at[:, pl.ds(pl.multiple_of((1 - self.c) * own, 16), own), :]
        self.near = pltpu.make_async_copy(own_ref, mine, sems.at[0])
        self.far = pltpu.make_async_remote_copy(
            src_ref=own_ref, dst_ref=mine, send_sem=sems.at[1], recv_sem=sems.at[2], device_id=(self.d, 1 - self.c, self.z),
            device_id_type=MESH,
        )
        self.arrival = pltpu.make_async_copy(theirs, theirs, sems.at[2])
        self.keep = pltpu.make_async_copy(buffer_ref, both_ref, sems.at[3])

    def greet(self, barrier):
        pl.semaphore_signal(barrier, 1, device_id=(self.d, 1 - self.c, self.z), device_id_type=MESH)
        return 1

    def fill(self):
        self.far.start()
        self.near.start()
        self.near.wait()
        self.arrival.wait()
        self.keep.start()

    def finish(self):
        self.far.wait_send()
        self.keep.wait()


class PairSum:
    def __init__(self, part_ref, sum_ref, send_sem, recv_sem):
        self.refs = part_ref, sum_ref, send_sem, recv_sem
        self.d, self.c, self.z = lax.axis_index("dp"), lax.axis_index("seq"), lax.axis_index("mp")

    def greet(self, barrier):
        pl.semaphore_signal(barrier, 1, device_id=(self.d, 1 - self.c, self.z), device_id_type=MESH)
        return 1

    def rows(self, c):
        own = self.refs[1].shape[2]
        return pl.ds(pl.multiple_of(c * own, 16), own)

    def copy(self, step):
        part_ref, sum_ref, send_sem, recv_sem = self.refs
        return pltpu.make_async_remote_copy(
            src_ref=part_ref.at[lax.rem(step, 2), :, self.rows(1 - self.c), :], dst_ref=sum_ref.at[step],
            send_sem=send_sem.at[step], recv_sem=recv_sem.at[step], device_id=(self.d, 1 - self.c, self.z), device_id_type=MESH,
        )

    def free(self, step):
        @pl.when(step >= 2)
        def _():
            self.copy(step - 2).wait_send()

    def send(self, step):
        self.copy(step).start()

    def take(self, step):
        part_ref, sum_ref = self.refs[:2]
        self.copy(step).wait_recv()
        for m in range(sum_ref.shape[1]):
            sum_ref[step, m] += part_ref[lax.rem(step, 2), m, self.rows(self.c), :]

    def finish(self):
        steps = self.refs[1].shape[0]
        for step in (steps - 2, steps - 1):
            self.copy(step).wait_send()


def carried_by(kernel, count, first, to_rows, n_in, n_out, *refs):
    ins, src_ref, outs, dst_ref = refs[:n_in], refs[n_in], refs[n_in + 1 : n_in + 1 + n_out], refs[n_in + 1 + n_out]
    scratch, sems = refs[n_in + n_out + 2 : -2], refs[-2:]
    kernel(*ins, *outs, *scratch, mover=Mover(src_ref, dst_ref, *sems, count, first, to_rows))


def step_of(grid):
    return pl.program_id(0) * grid[1] + pl.program_id(1)


def begin(grid, *parties):
    parties = [p for p in parties if p is not None]
    if parties:
        @pl.when(step_of(grid) == 0)
        def _():
            barrier = pltpu.get_barrier_semaphore()
            waits = 0
            for party in parties:
                waits = waits + party.greet(barrier)
            pl.semaphore_wait(barrier, waits)
            for party in parties:
                if isinstance(party, PairFill):
                    party.fill()
    for party in parties:
        if isinstance(party, Mover):
            party.start_at(step_of(grid), grid[0] * grid[1])


def end(grid, *parties):
    parties = [p for p in parties if p is not None]
    if parties:
        @pl.when(step_of(grid) == grid[0] * grid[1] - 1)
        def _():
            for party in parties:
                party.finish()


def twice_split(v):
    hi, lo = split(v)
    lane = lax.broadcasted_iota(jnp.int32, v.shape, 1)
    return jnp.where(lane < v.shape[1] // 2, hi.astype(jnp.float32), lo.astype(jnp.float32)).astype(jnp.bfloat16)


def fold(v):
    half = v.shape[0] // 2
    return v[:half] + v[half:]


def twice(v):
    return jnp.concatenate([v, v], axis=0)


def pick_kernel(ids_ref, pack_ref, out_ref):
    out_ref[0, 0] = pack_ref[0, 0, 0]


def merge(ref):
    return ref[...].reshape(ref.shape[0] * ref.shape[1], ref.shape[2])


def project_kernel(
    grid, own_ref, w_ref, tailw_ref, down_ref, up_ref, xin_ref, z_ref, bcin_ref, rate_ref, lr_ref, both_ref, low_ref, sems,
    mover=None
):
    step = pl.program_id(1)
    pair = PairFill(own_ref, both_ref, low_ref, sems)
    begin(grid, pair, mover)
    slots, tokens = low_ref.shape[:2]

    @pl.when(step == 0)
    def _():
        for m in range(slots):
            tail = mm(low_ref[m], tailw_ref[...])
            bcin_ref[m] = tail[:, : 2 * NS].astype(jnp.bfloat16)
            rate_ref[m] = tail[:, 2 * NS :]
            lr_ref[m] = twice_split(mm_t(low_ref[m], twice(down_ref[0, m])))

    value = mm(merge(low_ref), w_ref[0])
    for m in range(slots):
        part = value[m * tokens : (m + 1) * tokens] + mm(lr_ref[m], twice(up_ref[m, 0]))

        @pl.when(step < grid[1] // 2)
        def _():
            xin_ref[m] = part.astype(jnp.bfloat16)

        @pl.when(step >= grid[1] // 2)
        def _():
            z_ref[m] = part

    end(grid, pair, mover)


def prep_kernel(rate_ref, bias_ref, decay_ref, mask_ref, bcin_ref, bchalo_ref, taps_ref, step_ref, cum_ref, lanes_ref, bc_ref):
    rows = rate_ref.shape[1]
    value = rate_ref[0] + bias_ref[...]
    step = (jnp.maximum(value, 0.0) + jnp.log1p(jnp.exp(-jnp.abs(value)))) * mask_ref[0]
    log = step * decay_ref[...]
    tri = lax.broadcasted_iota(jnp.int32, (Q, Q), 0) >= lax.broadcasted_iota(jnp.int32, (Q, Q), 1)
    tri = tri.astype(jnp.float32).astype(jnp.bfloat16)
    step_ref[0] = step
    cum = jnp.concatenate([ones_mm(tri, log[b * Q : (b + 1) * Q]) for b in range(rows // Q)], axis=0)
    cum_ref[0] = cum
    cum_t, step_t = cum.T, step.T
    for g in range(lanes_ref.shape[1]):
        lanes_ref[0, g, :HG] = cum_t[g * HG : (g + 1) * HG]
        lanes_ref[0, g, HG:] = step_t[g * HG : (g + 1) * HG]
    pre = conv_rows(bcin_ref[0], bchalo_ref[0], taps_ref[...])
    bc_ref[0] = pre * jax.nn.sigmoid(pre)


def forward_kernel(
    grid, xin_ref, halo_ref, taps_ref, bc_ref, cum_ref, step_ref, lanes_ref, skip_ref, z_ref, mixed_ref, square_ref, state_ref,
    end_ref, scores_ref, bt_ref, held_ref, sent_ref, send_sem, recv_sem, mover=None
):
    group = pl.program_id(1)
    rows = xin_ref.shape[1]
    blocks = rows // Q
    line = Line(held_ref, sent_ref, send_sem, recv_sem, lax.axis_size("mp"), 1)
    begin(grid, line, mover)

    @pl.when(step_of(grid) == 0)
    def _():
        sent_ref[...] = jnp.zeros(sent_ref.shape, jnp.float32)

    @pl.when(group == 0)
    def _():
        for b in range(blocks):
            part = bc_ref[0, b * Q : (b + 1) * Q]
            b_part = split(part[:, :NS])
            c_part = split(part[:, NS:])
            scores_ref[b] = mm3_t(c_part, b_part)
            hi, lo = split(part[:, :NS].T)
            bt_ref[0, b] = hi
            bt_ref[1, b] = lo

    pre = conv_rows(xin_ref[0], halo_ref[0], taps_ref[...])
    x = pre * jax.nn.sigmoid(pre)
    cums, decs, updates = [], [], []
    for b in range(blocks):
        at = slice(b * Q, (b + 1) * Q)
        cum = of_group(cum_ref[0, at], group)
        step = of_group(step_ref[0, at], group)
        total = cum[Q - 1 : Q]
        wx = x[at] * widen(jnp.exp(total - cum) * step)
        cums.append(cum)
        decs.append(widen(jnp.exp(total)))
        updates.append(mm3((bt_ref[0, b], bt_ref[1, b]), split(wx)))

    slot = pl.program_id(0)
    states = [line.receive(slot, group)]
    for b in range(blocks):
        states.append(decs[b] * states[b] + updates[b])
    state_ref[0] = states[0]
    end_ref[0] = states[blocks]
    line.send(slot, group, states[blocks])
    lane = lax.broadcasted_iota(jnp.int32, (Q, 2 * P_SIZE), 1)
    causal = lax.broadcasted_iota(jnp.int32, (Q, Q), 0) >= lax.broadcasted_iota(jnp.int32, (Q, Q), 1)
    square = []
    for b in range(blocks):
        at = slice(b * Q, (b + 1) * Q)
        scores = scores_ref[b]
        xb = x[at]
        carried = widen(jnp.exp(cums[b])) * mm3(split(bc_ref[0, at, NS:]), split(states[b]))
        parts = []
        for h in range(0, HG, 2):
            pair = xb[:, h * P_SIZE : (h + 2) * P_SIZE]
            x_hi, x_lo = split(pair)
            both = jnp.concatenate([x_hi, x_lo], axis=1)
            halves = []
            for k in (h, h + 1):
                spread = cums[b][:, k : k + 1] - lanes_ref[0, 0, k : k + 1, at]
                decay = jnp.exp(jnp.where(causal, spread, -10000.0))
                m_hi, m_lo = split(scores * decay * lanes_ref[0, 0, HG + k : HG + k + 1, at])
                first = mm(m_hi, both)
                halves.append(first[:, : 2 * P_SIZE] + first[:, 2 * P_SIZE :] + mm(m_lo, x_hi))
            parts.append(jnp.where(lane < P_SIZE, halves[0], halves[1]))
        mixed = jnp.concatenate(parts, axis=1) + skip_ref[0:1] * xb + carried
        mixed_ref[0, at] = mixed
        z = z_ref[0, at]
        gated = mixed * (z * jax.nn.sigmoid(z))
        square.append(lane_sum(gated * gated))
    add_up(square_ref, jnp.concatenate(square, axis=0), group)

    end(grid, line, mover)


def chunk_decay(cum_ref, group):
    rows = cum_ref.shape[1]
    before = jnp.zeros((1, 128), jnp.float32)
    parts = []
    for b in range(rows // Q):
        cum = of_group(cum_ref[0, b * Q : (b + 1) * Q], group)
        parts.append(jnp.exp(cum + before))
        before = before + cum[Q - 1 : Q]
    return widen(jnp.concatenate(parts, axis=0))


def gs_kernel(
    grid, own_ref, w_ref, up_ref, down_ref, mixed_ref, z_ref, gain_ref, gs_ref, dot_ref, rg_ref, both_ref, gb_ref, sems
):
    step = pl.program_id(1)
    pair = PairFill(own_ref, both_ref, gb_ref, sems)
    begin(grid, pair)
    slots, tokens = gb_ref.shape[:2]

    @pl.when(step == 0)
    def _():
        for m in range(slots):
            rg_ref[m] = twice_split(mm_t(gb_ref[m], twice(up_ref[0, m])))

    gb = merge(gb_ref)
    width = w_ref.shape[3]
    total = mm_t(gb[:, :width], w_ref[0, 0])
    for n in range(1, w_ref.shape[0]):
        total = total + mm_t(gb[:, n * width : (n + 1) * width], w_ref[n, 0])
    for m in range(slots):
        gs = total[m * tokens : (m + 1) * tokens] + mm(rg_ref[m], twice(down_ref[m, 0]))
        gs_ref[m] = gs
        z = z_ref[m]
        dots = lane_sum(gs * gain_ref[...] * (mixed_ref[m] * (z * jax.nn.sigmoid(z))))

        @pl.when(step == 0)
        def _():
            dot_ref[m] = dots

        @pl.when(step > 0)
        def _():
            dot_ref[m] += dots

    end(grid, pair)


def turned(v):
    return v.astype(jnp.float32).T.astype(jnp.bfloat16)


def rank_sum(rows_ref, m, factor_ref, first):
    width = factor_ref.shape[3]
    total = 0.0
    for n in range(factor_ref.shape[1]):
        factor = twice(factor_ref[m, n, first : first + R])
        total = total + mm_t(rows_ref[m, :, n * width : (n + 1) * width], factor)
    return total


def branch_kernel(
    grid, scaled_ref, w_ref, down_ref, up_ref, rg_ref, gb_ref, x_ref, mask_ref, out_ref, g_up_ref, g_down_ref, ro_ref, rot_ref,
    rgt_ref, part_ref, sum_ref, send_sem, recv_sem
):
    step = pl.program_id(1)
    pair = PairSum(part_ref, sum_ref, send_sem, recv_sem)
    begin(grid, pair)
    slots, tokens = scaled_ref.shape[:2]

    @pl.when(step == 0)
    def _():
        for m in range(slots):
            ro = twice_split(rank_sum(scaled_ref, m, down_ref, 0))
            ro_ref[m] = ro
            rot_ref[m] = turned(ro)
            rgt_ref[m] = turned(rg_ref[m])

    scaled = merge(scaled_ref)
    width = w_ref.shape[2]
    total = mm(scaled[:, :width], w_ref[0, 0])
    for n in range(1, w_ref.shape[1]):
        total = total + mm(scaled[:, n * width : (n + 1) * width], w_ref[0, n])
    cols = g_down_ref.shape[2]
    width = up_ref.shape[3]
    pair.free(step)
    for m in range(slots):
        part_ref[lax.rem(step, 2), m] = total[m * tokens : (m + 1) * tokens] + mm(ro_ref[m], twice(up_ref[0, m]))
    pair.send(step)
    for m in range(slots):
        g_up_ref[m] = fold(mm(rot_ref[m], gb_ref[m]))
        g_down_ref[m] = fold(mm(rgt_ref[m], scaled_ref[m, :, pl.ds(pl.multiple_of(step * cols, 128), cols)]))

    def put(n):
        pair.take(n)
        at = pl.ds(pl.multiple_of(n * width, 128), width)
        for m in range(slots):
            out_ref[m, :, at] = (x_ref[m, :, at].astype(jnp.float32) + mask_ref[m] * sum_ref[n, m]).astype(jnp.bfloat16)

    @pl.when(step > 0)
    def _():
        put(step - 1)

    @pl.when(step == grid[1] - 1)
    def _():
        put(step)

    end(grid, pair)


def unproject_kernel(
    grid, gz_ref, gx_ref, tail_ref, w_ref, tailw_ref, up_ref, down_ref, lr_ref, low_ref, x_ref, inv_ref, gain_ref, delta_ref,
    upz_ref, upx_ref, g_down_ref, ri_ref, rit_ref, lrt_ref, part_ref, sum_ref, send_sem, recv_sem, mover=None
):
    step = pl.program_id(1)
    pair = PairSum(part_ref, sum_ref, send_sem, recv_sem)
    begin(grid, pair, mover)
    slots, tokens = gz_ref.shape[:2]

    @pl.when(step == 0)
    def _():
        for m in range(slots):
            ri = twice_split(rank_sum(gz_ref, m, up_ref, 0) + rank_sum(gx_ref, m, up_ref, R))
            ri_ref[m] = ri
            rit_ref[m] = turned(ri)
            lrt_ref[m] = turned(lr_ref[m])

    total = mm_t(merge(gz_ref), w_ref[0]) + mm_t(merge(gx_ref), w_ref[1]) + mm_t(merge(tail_ref), tailw_ref[...])
    cols = upz_ref.shape[2]
    at = pl.ds(pl.multiple_of(step * cols, 128), cols)
    pair.free(step)
    for m in range(slots):
        part_ref[lax.rem(step, 2), m] = total[m * tokens : (m + 1) * tokens] + mm(ri_ref[m], twice(down_ref[0, m]))
    pair.send(step)
    for m in range(slots):
        upz_ref[m] = fold(mm(lrt_ref[m], gz_ref[m, :, at]))
        upx_ref[m] = fold(mm(lrt_ref[m], gx_ref[m, :, at]))
        g_down_ref[m] = fold(mm(rit_ref[m], low_ref[m]))

    @pl.when(step > 0)
    def _():
        pair.take(step - 1)

    @pl.when(step == grid[1] - 1)
    def _():
        pair.take(step)
        width = sum_ref.shape[3]
        for m in range(slots):
            spread = 0.0
            for n in range(sum_ref.shape[0]):
                at = slice(n * width, (n + 1) * width)
                gn = sum_ref[n, m] * gain_ref[:, at]
                sum_ref[n, m] = gn
                spread = spread + jnp.sum(gn * x_ref[m, :, at].astype(jnp.float32), axis=1, keepdims=True)
            inv = inv_ref[m]
            spread = spread * (inv * inv * inv / x_ref.shape[2])
            for n in range(sum_ref.shape[0]):
                at = slice(n * width, (n + 1) * width)
                delta_ref[m, :, at] = (inv * sum_ref[n, m] - x_ref[m, :, at].astype(jnp.float32) * spread).astype(jnp.bfloat16)

    end(grid, pair, mover)


def gate_back_kernel(
    grid, gs_ref, mixed_ref, z_ref, inv_ref, coef_ref, gain_ref, bc_ref, cum_ref, dy_ref, gz_ref, scaled_ref, lam_ref, q_ref, ct_ref,
    mover=None
):
    group = pl.program_id(1)
    begin(grid, mover)

    @pl.when(group == 0)
    def _():
        hi, lo = split(bc_ref[0, :, NS:].T)
        ct_ref[0] = hi
        ct_ref[1] = lo

    z = z_ref[0]
    mixed = mixed_ref[0]
    sig = jax.nn.sigmoid(z)
    act = z * sig
    gated = mixed * act
    inv = inv_ref[0]
    gain = gain_ref[...]
    scaled_ref[0] = (gated * inv * gain).astype(jnp.bfloat16)
    g_gated = gs_ref[0] * gain * inv - gated * coef_ref[0]
    dy = g_gated * act
    dy_ref[0] = dy
    gz_ref[0] = (g_gated * mixed * (sig * (1.0 + z * (1.0 - sig)))).astype(jnp.bfloat16)
    lam_ref[0] = mm3((ct_ref[0], ct_ref[1]), split(dy * chunk_decay(cum_ref, group)))
    add_up(q_ref, head_sums(dy * mixed, group), group)

    end(grid, mover)


def scan_back_kernel(
    grid, dy_ref, xin_ref, halo_ref, taps_ref, bc_ref, cum_ref, step_ref, lanes_ref, skip_ref, state_ref, lam_ref, end_ref,
    gx_ref, head_ref, tail_ref, gbc_ref, xu_ref, dx_ref, scorest_ref, dscorest_ref, bt_ref, ct_ref, held_ref, sent_ref, send_sem,
    recv_sem, mover=None
):
    group = pl.program_id(1)
    rows = xin_ref.shape[1]
    blocks = rows // Q
    line = Line(held_ref, sent_ref, send_sem, recv_sem, lax.axis_size("mp"), -1)
    begin(grid, line, mover)

    @pl.when(step_of(grid) == 0)
    def _():
        sent_ref[...] = jnp.zeros(sent_ref.shape, jnp.float32)

    @pl.when(group == 0)
    def _():
        for b in range(blocks):
            part = bc_ref[0, b * Q : (b + 1) * Q]
            scorest_ref[b] = mm3_t(split(part[:, :NS]), split(part[:, NS:]))
            dscorest_ref[b] = jnp.zeros((Q, Q), jnp.float32)
            hi, lo = split(part[:, :NS].T)
            bt_ref[0, b] = hi
            bt_ref[1, b] = lo
            hi, lo = split(part[:, NS:].T)
            ct_ref[0, b] = hi
            ct_ref[1, b] = lo
        gbc_ref[0] = jnp.zeros((rows, 2 * NS), jnp.float32)
        xu_ref[0] = jnp.zeros((rows, 128), jnp.float32)
        dx_ref[0] = jnp.zeros((rows, 128), jnp.float32)

    pre = conv_rows(xin_ref[0], halo_ref[0], taps_ref[...])
    sig = jax.nn.sigmoid(pre)
    x = pre * sig
    lane = lax.broadcasted_iota(jnp.int32, (Q, 2 * P_SIZE), 1)
    causal = lax.broadcasted_iota(jnp.int32, (Q, Q), 0) <= lax.broadcasted_iota(jnp.int32, (Q, Q), 1)
    cums, step_cols, decs, rests, wide_steps = [], [], [], [], []
    for b in range(blocks):
        at = slice(b * Q, (b + 1) * Q)
        cum = of_group(cum_ref[0, at], group)
        step = of_group(step_ref[0, at], group)
        total = cum[Q - 1 : Q]
        cums.append(cum)
        step_cols.append(step)
        decs.append(widen(jnp.exp(total)))
        rests.append(widen(jnp.exp(total - cum)))
        wide_steps.append(widen(step))
    states = [state_ref[0]]
    for b in range(blocks - 1):
        wx = x[b * Q : (b + 1) * Q] * rests[b] * wide_steps[b]
        states.append(decs[b] * states[b] + mm3((bt_ref[0, b], bt_ref[1, b]), split(wx)))
    slot = SLOTS - 1 - pl.program_id(0)
    lam = line.receive(slot, group)
    whole = decs[0]
    for dec in decs[1:]:
        whole = whole * dec
    line.send(slot, group, whole * lam + lam_ref[0])
    ends = jnp.sum(lam * end_ref[0], axis=0, keepdims=True)
    g_parts = [None] * blocks
    for b in reversed(range(blocks)):
        at = slice(b * Q, (b + 1) * Q)
        xb = x[at]
        dy = dy_ref[0, at]
        scores = scorest_ref[b]
        dscores = dscorest_ref[b]
        u_parts = []
        for h in range(0, HG, 2):
            pair = slice(h * P_SIZE, (h + 2) * P_SIZE)
            x_hi, x_lo = split(xb[:, pair])
            d_hi, d_lo = split(dy[:, pair])
            both = jnp.concatenate([d_hi, d_lo], axis=1)
            halves = []
            for k in (h, h + 1):
                mine = (lane < P_SIZE) if k == h else (lane >= P_SIZE)
                spread = lanes_ref[0, 0, k : k + 1, at] - cums[b][:, k : k + 1]
                decay = jnp.exp(jnp.where(causal, spread, -10000.0))
                zero = jnp.zeros_like(x_hi)
                xm_hi = jnp.where(mine, x_hi, zero)
                xm_lo = jnp.where(mine, x_lo, zero)
                dm = mm_t(xm_hi, d_hi) + mm_t(xm_hi, d_lo) + mm_t(xm_lo, d_hi)
                dscores = dscores + dm * decay * step_cols[b][:, k : k + 1]
                m_hi, m_lo = split(scores * decay)
                first = mm(m_hi, both)
                halves.append(first[:, : 2 * P_SIZE] + first[:, 2 * P_SIZE :] + mm(m_lo, d_hi))
            u_parts.append(jnp.where(lane < P_SIZE, halves[0], halves[1]))
        dscorest_ref[b] = dscores
        lam_s = split(lam)
        part = bc_ref[0, at]
        step = wide_steps[b]
        u = jnp.concatenate(u_parts, axis=1) + rests[b] * mm3(split(part[:, :NS]), lam_s)
        ev = split(widen(jnp.exp(cums[b])) * dy)
        gbc_ref[0, at, :NS] += mm3_t(split(rests[b] * step * xb), lam_s)
        gbc_ref[0, at, NS:] += mm3_t(ev, split(states[b]))
        if b > 0:
            lam = decs[b] * lam + mm3((ct_ref[0, b], ct_ref[1, b]), ev)
        xu_ref[0, at] += head_sums(xb * u, group)
        direct = xb * dy * skip_ref[0:1]
        if b == blocks - 1:
            row = lax.broadcasted_iota(jnp.int32, (Q, HG * P_SIZE), 0)
            direct = jnp.where(row == Q - 1, direct - ends, direct)
        dx_ref[0, at] += head_sums(direct, group)
        g_parts[b] = step * u + skip_ref[0:1] * dy
    g_pre = jnp.concatenate(g_parts, axis=0) * (sig * (1.0 + pre * (1.0 - sig)))
    g_ext = conv_rows_back(g_pre, taps_ref[...])
    gx_ref[0] = g_ext[8:].astype(jnp.bfloat16)
    head_ref[0] = g_ext[:8]
    tail_ref[0] = g_ext[rows:]

    @pl.when(group == pl.num_programs(1) - 1)
    def _():
        for b in range(blocks):
            at = slice(b * Q, (b + 1) * Q)
            part = bc_ref[0, at]
            ds = dscorest_ref[b]
            gbc_ref[0, at, :NS] += mm3(split(ds), split(part[:, NS:]))
            gbc_ref[0, at, NS:] += mm3(split(ds.T), split(part[:, :NS]))

    end(grid, line, mover)


def finish_kernel(
    count, out_ref, up_z_ref, up_x_ref, up_out_ref, down_ref, mine_ref, picks_ref, rows_ref, moved_ref, near_out_ref, far_out_ref,
    near_ref, far_ref, near1_ref, far1_ref, near2_ref,
    near2_in_ref, far2_ref, far2_in_ref, n1s, n1r, f1s, f1r, n2s, n2r, f2s, f2r, send_sem, recv_sem
):
    d, c, z = lax.axis_index("dp"), lax.axis_index("seq"), lax.axis_index("mp")
    mover = Mover(rows_ref, moved_ref, send_sem, recv_sem, count, tuple(range(SLOTS)), False)
    blocks = far2_ref.shape[0]
    barrier = pltpu.get_barrier_semaphore()
    waits = mover.greet(barrier)
    others = [(i, j) for i in range(blocks) for j in range(2) if i or j]
    for i, j in others:
        device = (lax.rem(d + i, blocks), lax.rem(c + j, 2), z)
        pl.semaphore_signal(barrier, 1, device_id=device, device_id_type=MESH)

    def by_sequence(ref, m):
        return sum(mine_ref[m, i] * ref[i] for i in range(SLOTS))

    pl.semaphore_wait(barrier, waits + len(others))
    for n in range(mover.pieces // 2):
        mover.start(n)

    part, each = near_ref.shape[4], far_ref.shape[5]
    for m in range(SLOTS):
        for kind, ref in enumerate((out_ref, up_z_ref, up_x_ref)):
            total = by_sequence(ref, m).astype(jnp.bfloat16)
            for n in range(count):
                near_ref[n, m, kind] = total[:, n * part : (n + 1) * part]
        for kind, ref in enumerate((up_out_ref, down_ref)):
            total = by_sequence(ref, m)
            for b in range(blocks):
                for n in range(2 * count):
                    at = (b * 2 * count + n) * each
                    far_ref[n, m, kind, b] = total[:, at : at + each].astype(jnp.bfloat16)

    def remote(src, dst, send, recv, *device):
        return pltpu.make_async_remote_copy(
            src_ref=src, dst_ref=dst, send_sem=send, recv_sem=recv, device_id=device, device_id_type=MESH
        )

    def arrival(ref, at, sem):
        pltpu.make_async_copy(ref.at[at], ref.at[at], sem.at[at]).wait()

    me = c * count + z
    copies = []
    for i in range(1, count):
        to = lax.rem(z + i, count)
        copies.append(remote(near_ref.at[to], near1_ref.at[z], n1s.at[i], n1r.at[z], d, c, to))
    column = [(j, i) for j in range(2) for i in range(count) if i or j]
    for j, i in column:
        to_c, to = lax.rem(c + j, 2), lax.rem(z + i, count)
        copies.append(remote(far_ref.at[to_c * count + to], far1_ref.at[me], f1s.at[j * count + i], f1r.at[me], d, to_c, to))
    for copy in copies:
        copy.start()
    for n in range(mover.pieces // 2, mover.pieces):
        mover.start(n)

    near = near_ref[z].astype(jnp.float32)
    for i in range(1, count):
        at = lax.rem(z + i, count)
        arrival(near1_ref, at, n1r)
        near = near + near1_ref[at].astype(jnp.float32)
    far = far_ref[me].astype(jnp.float32)
    for j, i in column:
        at = lax.rem(c + j, 2) * count + lax.rem(z + i, count)
        arrival(far1_ref, at, f1r)
        far = far + far1_ref[at].astype(jnp.float32)
    for a in range(ADAPT):
        near2_ref[a] = sum(picks_ref[m, a] * near[m] for m in range(SLOTS))
        for b in range(blocks):
            far2_ref[b, a] = sum(picks_ref[m, a] * far[m, :, b] for m in range(SLOTS))

    here = d * 2 + c
    copies2 = []
    for i, j in others:
        to_d, to_c = lax.rem(d + i, blocks), lax.rem(c + j, 2)
        copies2.append(
            remote(near2_ref.at[to_d * 2 + to_c], near2_in_ref.at[here], n2s.at[i * 2 + j], n2r.at[here], to_d, to_c, z)
        )
    for i in range(1, blocks):
        to = lax.rem(d + i, blocks)
        copies2.append(remote(far2_ref.at[to], far2_in_ref.at[d], f2s.at[i], f2r.at[d], to, c, z))
    for copy in copies2:
        copy.start()
    near2_in_ref[here] = near2_ref[here]
    far_sum = far2_ref[d]
    for i in range(1, blocks):
        at = lax.rem(d + i, blocks)
        arrival(far2_in_ref, at, f2r)
        far_sum = far_sum + far2_in_ref[at]
    far_out_ref[...] = far_sum
    for i, j in others:
        arrival(near2_in_ref, lax.rem(d + i, blocks) * 2 + lax.rem(c + j, 2), n2r)
    for half in range(2):
        near_out_ref[half] = sum(near2_in_ref[b * 2 + half] for b in range(blocks))
    for copy in copies + copies2:
        copy.wait_send()
    mover.finish()


def bc_back_kernel(
    g_ref, in_ref, halo_ref, taps_ref, q_ref, dx_ref, xu_ref, step_ref, rate_ref, bias_ref, decay_ref, mask_ref,
    out_ref, head_ref, tail_ref, g_rate_ref
):
    rows = in_ref.shape[1]
    pre = conv_rows(in_ref[0], halo_ref[0], taps_ref[...])
    sig = jax.nn.sigmoid(pre)
    g_ext = conv_rows_back(g_ref[0] * (sig * (1.0 + pre * (1.0 - sig))), taps_ref[...])
    out_ref[0] = g_ext[8:].astype(jnp.bfloat16)
    head_ref[0] = g_ext[:8]
    tail_ref[0] = g_ext[rows:]
    xu = xu_ref[0]
    flow = q_ref[0] - dx_ref[0] - step_ref[0] * xu
    later = lax.broadcasted_iota(jnp.int32, (rows, rows), 0) <= lax.broadcasted_iota(jnp.int32, (rows, rows), 1)
    g_log = ones_mm(later.astype(jnp.float32).astype(jnp.bfloat16), flow)
    sig = jax.nn.sigmoid(rate_ref[0] + bias_ref[...])
    g_rate_ref[0] = ((xu + g_log * decay_ref[...]) * mask_ref[0] * sig).astype(jnp.bfloat16)


def flip(v, mask, count):
    total = 0
    bit = 1
    while bit < count:
        b = lax.rem(v // bit, 2)
        total = total + (1 - b if mask & bit else b) * bit
        bit *= 2
    return total


def gather_kernel(
    nd, nz, wt_ref, x_ref, w_ref, rows_ref, local_sem, pair_sem, up_sem, down_sem, zrecv_sem, xsend_sem, xrecv_sem, ysend_sem,
    yrecv_sem, hsend_sem, hrecv_sem, asend_sem, arecv_sem
):
    d, c, z = lax.axis_index("dp"), lax.axis_index("seq"), lax.axis_index("mp")
    xn, yn = flip(d, 1, nd), flip(d, 2, nd)
    rows, part = wt_ref.shape[1], wt_ref.shape[2] // 2

    def remote(src, dst, send, recv, device):
        return pltpu.make_async_remote_copy(
            src_ref=src, dst_ref=dst, send_sem=send, recv_sem=recv, device_id=device, device_id_type=MESH
        )

    barrier = pltpu.get_barrier_semaphore()
    for cc in range(2):
        for r in range(nz):
            if cc or r:
                pl.semaphore_signal(barrier, 1, device_id=(d, flip(c, cc, 2), flip(z, r, nz)), device_id_type=MESH)
    for dd in (xn, yn):
        pl.semaphore_signal(barrier, 1, device_id=(dd, c, z), device_id_type=MESH)
    pl.semaphore_wait(barrier, 2 * nz - 1 + 2)

    def cols(s):
        return pl.ds(pl.multiple_of(s * part, 128), part)

    def area(dd, s):
        return w_ref.at[:, pl.ds(pl.multiple_of(dd * (2 * rows), 16), 2 * rows), cols(s)]

    def half_area(dd, s, h):
        return w_ref.at[:, pl.ds(pl.multiple_of(dd * (2 * rows) + h * rows, 16), rows), cols(s)]

    mine_area = w_ref.at[:, pl.ds(pl.multiple_of((2 * d + c) * rows, 16), rows), cols(z)]
    keep = pltpu.make_async_copy(wt_ref.at[:, :, cols(c)], mine_area, local_sem.at[0])
    pair = remote(wt_ref.at[:, :, cols(1 - c)], mine_area, pair_sem.at[0], pair_sem.at[1], (d, 1 - c, z))
    keep.start()
    pair.start()

    mover = Mover(x_ref, rows_ref, asend_sem, arecv_sem, nz, tuple(range(SLOTS)), True)
    for n in range(mover.pieces):
        mover.start(n)

    keep.wait()
    pair.wait()

    def spread(s):
        remote(area(d, s), area(d, s), xsend_sem.at[s], xrecv_sem.at[s], (xn, c, z)).start()
        remote(area(d, s), area(d, s), ysend_sem.at[s], yrecv_sem.at[s], (yn, c, z)).start()

    def send_up(s):
        @pl.when(z < nz - 1)
        def _():
            remote(area(d, s), area(d, s), up_sem.at[s], zrecv_sem.at[s], (d, c, z + 1)).start()

    def send_down(s):
        @pl.when(z > 0)
        def _():
            remote(area(d, s), area(d, s), down_sem.at[s], zrecv_sem.at[s], (d, c, z - 1)).start()

    def relay(s):
        remote(area(xn, s), area(xn, s), xsend_sem.at[s], xrecv_sem.at[s], (xn, c, z)).wait_recv()
        remote(half_area(xn, s, 0), half_area(xn, s, 0), hsend_sem.at[0, s], hrecv_sem.at[0, s], (yn, c, z)).start()
        remote(area(yn, s), area(yn, s), ysend_sem.at[s], yrecv_sem.at[s], (yn, c, z)).wait_recv()
        remote(half_area(yn, s, 1), half_area(yn, s, 1), hsend_sem.at[1, s], hrecv_sem.at[1, s], (xn, c, z)).start()

    send_up(z)
    send_down(z)
    spread(z)
    for r in range(1, nz + 1):
        if r < nz:
            @pl.when(z - r >= 0)
            def _():
                s = z - r
                remote(area(d, s), area(d, s), up_sem.at[s], zrecv_sem.at[s], (d, c, z)).wait_recv()
                send_up(s)
                spread(s)

            @pl.when(z + r < nz)
            def _():
                s = z + r
                remote(area(d, s), area(d, s), up_sem.at[s], zrecv_sem.at[s], (d, c, z)).wait_recv()
                send_down(s)
                spread(s)

        if r == 1:
            relay(z)
        else:
            @pl.when(z - r + 1 >= 0)
            def _():
                relay(z - r + 1)

            @pl.when(z + r - 1 < nz)
            def _():
                relay(z + r - 1)

    mover.finish()
    for s in range(nz):
        remote(half_area(d, s, 0), half_area(d, s, 0), hsend_sem.at[0, s], hrecv_sem.at[0, s], (yn, c, z)).wait()
        remote(half_area(d, s, 1), half_area(d, s, 1), hsend_sem.at[1, s], hrecv_sem.at[1, s], (xn, c, z)).wait()
        remote(area(d, s), area(d, s), xsend_sem.at[s], xrecv_sem.at[s], (xn, c, z)).wait_send()
        remote(area(d, s), area(d, s), ysend_sem.at[s], yrecv_sem.at[s], (yn, c, z)).wait_send()

        @pl.when(jnp.logical_and(s <= z, z < nz - 1))
        def _():
            remote(area(d, s), area(d, s), up_sem.at[s], zrecv_sem.at[s], (d, c, z)).wait_send()

        @pl.when(jnp.logical_and(s >= z, z > 0))
        def _():
            remote(area(d, s), area(d, s), down_sem.at[s], zrecv_sem.at[s], (d, c, z)).wait_send()


def gather(wt, x, nd, nz):
    half = wt.shape[2] // 2
    dma = pltpu.SemaphoreType.DMA
    anywhere = pl.BlockSpec(memory_space=pl.ANY)
    return pl.pallas_call(
        functools.partial(gather_kernel, nd, nz),
        name="gather",
        out_shape=(
            jax.ShapeDtypeStruct((2, wt.shape[1] * 2 * nd, half * nz), wt.dtype),
            jax.ShapeDtypeStruct((SLOTS, x.shape[1] // 4, x.shape[2] * nz), x.dtype),
        ),
        in_specs=[anywhere] * 2,
        out_specs=(anywhere,) * 2,
        scratch_shapes=[
            dma((1,)), dma((2,)), dma((nz,)), dma((nz,)), dma((nz,)), dma((nz,)), dma((nz,)), dma((nz,)), dma((nz,)),
            dma((2, nz)), dma((2, nz)), dma((4 * SLOTS,)), dma((SLOTS, nz)),
        ],
        compiler_params=pltpu.CompilerParams(collective_id=1, has_side_effects=True),
    )(wt, x)


def block(shape, index):
    return pl.BlockSpec(shape, index)


def call(kernel, name, grid, ins, outs, scratch, flops, size, comm=None, load=None):
    params = dict(vmem_limit_bytes=VMEM_LIMIT)
    kernel = functools.partial(kernel, grid)
    ins, outs, scratch = list(ins), list(outs), list(scratch)
    if load is not None:
        rows, result, first, to_rows = load
        count = lax.axis_size("mp")
        kernel = functools.partial(carried_by, kernel, count, first, to_rows, len(ins), len(outs))
        ins.append((rows, pl.BlockSpec(memory_space=pl.ANY)))
        outs.append((result, pl.BlockSpec(memory_space=pl.ANY)))
        sends = 4 * SLOTS if to_rows else count * len(first)
        scratch += [pltpu.SemaphoreType.DMA((sends,)), pltpu.SemaphoreType.DMA((SLOTS, 4))]
    if comm is not None:
        params.update(collective_id=comm, has_side_effects=True)
    return pl.pallas_call(
        kernel,
        name=name,
        grid=grid,
        in_specs=[s for _, s in ins],
        out_specs=[s for _, s in outs],
        out_shape=[s for s, _ in outs],
        scratch_shapes=scratch,
        compiler_params=pltpu.CompilerParams(**params),
        cost_estimate=pl.CostEstimate(flops=flops, bytes_accessed=size, transcendentals=0),
    )(*[a for a, _ in ins])


def skip_grid(kernel):
    return lambda grid, *refs: kernel(*refs)


def after(value, *deps):
    return lax.optimization_barrier((value,) + deps)[0]


def finish(grads, mine, picks, rows, moved, count, blocks):
    dma, f32, bf16 = pltpu.SemaphoreType.DMA, jnp.float32, jnp.bfloat16
    anywhere, vmem = pl.BlockSpec(memory_space=pl.ANY), pl.BlockSpec(memory_space=pltpu.VMEM)
    smem = pl.BlockSpec(memory_space=pltpu.SMEM)
    near_shape = (3, R, grads[0].shape[2] // count)
    far_shape = (2, R, D // (2 * blocks * count))
    near_all = (count, SLOTS) + near_shape
    far_all = (2 * count, SLOTS, 2, blocks) + far_shape[1:]
    return pl.pallas_call(
        functools.partial(finish_kernel, count),
        name="finish",
        in_specs=[vmem] * 5 + [smem, smem, anywhere],
        out_specs=[anywhere, vmem, vmem],
        out_shape=[moved, jax.ShapeDtypeStruct((2,) + near_shape, f32), jax.ShapeDtypeStruct((ADAPT,) + far_shape, f32)],
        scratch_shapes=[
            pltpu.VMEM(near_all, bf16), pltpu.VMEM(far_all, bf16), pltpu.VMEM(near_all, bf16), pltpu.VMEM(far_all, bf16),
            pltpu.VMEM((ADAPT,) + near_shape, f32), pltpu.VMEM((2 * blocks,) + near_shape, f32),
            pltpu.VMEM((blocks, ADAPT) + far_shape, f32), pltpu.VMEM((blocks, ADAPT) + far_shape, f32), dma((count,)), dma((count,)),
            dma((2 * count,)), dma((2 * count,)), dma((2 * blocks,)), dma((2 * blocks,)), dma((blocks,)), dma((blocks,)),
            dma((count * SLOTS,)), dma((SLOTS, 4)),
        ],
        compiler_params=pltpu.CompilerParams(vmem_limit_bytes=VMEM_LIMIT, collective_id=5, has_side_effects=True),
    )(*grads, mine, picks, rows)


def fast_body(
    x_in, cotangent, lengths, adapter_ids, norm_gain, w_zx, w_bc, w_dt, dt_bias, a_log, d_skip, conv_x, conv_bc,
    gate_gain, w_out, in_down, in_up, out_down, out_up
):
    bf16, f32 = jnp.bfloat16, jnp.float32
    micros, _, seg, feats = x_in.shape
    nz, nd = lax.axis_size("mp"), lax.axis_size("dp")
    core, z = lax.axis_index("seq"), lax.axis_index("mp")
    own = seg // nz
    tokens = 2 * own
    heads = dt_bias.shape[0] * nz // 2
    chan = heads * P_SIZE
    part = chan // nz
    groups = heads // HG
    wide = HG * P_SIZE
    blocks = tokens // Q
    each = D // (nd * 2 * nz)

    def other(v):
        return lax.ppermute(v, "seq", [(0, 1), (1, 0)])

    def pair_cat(mine, theirs, axis):
        return jnp.where(
            core == 0, jnp.concatenate([mine, theirs], axis), jnp.concatenate([theirs, mine], axis)
        )

    def halves(v, axis):
        v = v.reshape(v.shape[:axis] + (2, v.shape[axis] // 2) + v.shape[axis + 1 :])
        return (
            lax.dynamic_index_in_dim(v, core, axis, False),
            lax.dynamic_index_in_dim(v, 1 - core, axis, False),
        )

    line = part
    bc_piece = lax.dynamic_slice_in_dim(w_bc, z * (w_bc.shape[0] // nz), w_bc.shape[0] // nz, 0)
    pairs = jnp.stack([jnp.transpose(in_down, (0, 2, 1)), out_up.reshape(ADAPT, R, -1)], 1)
    same = [bc_piece, pairs]
    sized = [halves(jnp.transpose(in_up, (1, 0, 2)), 2), halves(out_down.T, 1), halves(w_dt.T, 0)]
    packs = []
    for k in range(2):
        packs.append(jnp.concatenate([v.reshape(-1, line) for v in [s[k] for s in sized] + same], 0))
    bounds = [0]
    for v in [s[0] for s in sized] + same:
        bounds.append(bounds[-1] + v.size // line)
    pack = pair_cat(packs[0][None], other(packs[1])[None], 0)
    params = jnp.concatenate([dt_bias, a_log, d_skip, gate_gain, conv_x.reshape(-1)])
    params = lax.all_gather(params, "mp")
    pack = lax.all_gather(pack, ("dp", "mp")).reshape((nd, nz) + pack.shape)
    zx_weight, x_rows = gather(jnp.transpose(w_zx, (1, 0, 2)), x_in[:, 0], nd, nz)
    out_mine, out_theirs = halves(after(w_out, x_rows), 0)
    out_pair = pair_cat(out_mine, other(out_theirs), 1)
    out_all = lax.all_gather(out_pair, ("dp", "mp")).reshape((nd, nz) + out_pair.shape)
    dt_rows = pack[:, :, :, bounds[2] : bounds[3]].reshape(nd, nz, 2, heads // nz, -1)
    dt_weight = jnp.transpose(dt_rows, (1, 3, 0, 2, 4)).reshape(heads, D)
    dt_weight = jnp.pad(dt_weight, ((0, 128 - heads), (0, 0)))
    bc_rows = pack[:, :, :, bounds[3] : bounds[4]].reshape(nd, nz, 2, -1, 2 * NS)
    bc_weight = jnp.transpose(bc_rows, (0, 2, 1, 3, 4)).reshape(D, 2 * NS)
    bc_half = lax.dynamic_slice_in_dim(bc_weight, core * NS, NS, 1)
    dt_weight = dt_weight.T
    tail_weight = jnp.concatenate([bc_half, dt_weight], 1)
    first_weight = jnp.concatenate([bc_weight, dt_weight], 1)

    hl = dt_bias.shape[0]

    def own_part(v):
        v = v.reshape(v.shape[0], 2, v.shape[1] // 2)
        return lax.dynamic_index_in_dim(v, core, 1, False).reshape(-1)

    bias = jnp.pad(own_part(params[:, :hl]), (0, 128 - heads))[None]
    rate = jnp.pad(-jnp.exp(own_part(params[:, hl : 2 * hl])), (0, 128 - heads))[None]
    skip = jnp.repeat(own_part(params[:, 2 * hl : 3 * hl]), P_SIZE)[None]
    width = gate_gain.shape[0]
    gain = own_part(params[:, 3 * hl : 3 * hl + width])[None]
    taps = params[:, 3 * hl + width :].reshape(nz, KC, 2, part)
    taps = jnp.transpose(lax.dynamic_index_in_dim(taps, core, 2, False), (1, 0, 2)).reshape(KC, chan)

    order = jnp.arange(micros)
    runs = run_of(order, z)
    sequence, chunk = runs // nz, lax.rem(runs, nz)
    lengths = jnp.take(lengths[:, 0], sequence)[:, None]
    ids = jnp.take(adapter_ids[:, 0], sequence)
    all_pos = (chunk * tokens)[:, None] + jnp.arange(tokens)
    own_pos = (chunk * tokens)[:, None] + core * own + jnp.arange(own)
    enters = (order == nz - 1 - z)[:, None, None]
    leaves = (order == nz - 2 - z)[:, None, None]
    forward_edge = [(i, i + 1) for i in range(nz - 1)]
    backward_edge = [(i + 1, i) for i in range(nz - 1)]

    m3 = lambda m, g: (m, 0, g)
    m0 = lambda m, g: (m, 0, 0)
    z2 = lambda m, g: (0, 0)
    shape = jax.ShapeDtypeStruct

    def per_token(width, index=m3):
        return block((1, tokens, width), index)

    chan_block = per_token(wide)
    halo_block = block((1, HALO, wide), m3)
    taps_block = block((KC, wide), lambda m, g: (0, g))
    line_block = block((1, wide), lambda m, g: (0, g))
    state_block = block((1, NS, wide), m3)
    bc_block = per_token(2 * NS, m0)
    bc_halo = block((1, HALO, 2 * NS), m0)
    bc_taps = block((KC, 2 * NS), z2)
    bc_edge = block((1, 8, 2 * NS), m0)
    one_col = per_token(1, m0)
    sums = per_token(128, m0)
    lanes_block = block((1, 1, 2 * HG, tokens), lambda m, g: (m, g, 0, 0))
    head_line = block((1, 128), z2)
    edge_block = block((1, 8, wide), m3)
    tok_f32 = shape((micros, tokens, chan), f32)
    tok_b16 = shape((micros, tokens, chan), bf16)
    state_f32 = shape((micros, NS, chan), f32)
    bc_f32 = shape((micros, tokens, 2 * NS), f32)
    sums_f32 = shape((micros, tokens, 128), f32)
    edge_f32 = shape((micros, 8, chan), f32)
    act_bytes = tokens * chan * 4
    dma = pltpu.SemaphoreType.DMA
    line_scratch = [pltpu.VMEM((groups, NS, wide), f32), pltpu.VMEM((2 * groups, NS, wide), f32)] + [dma((groups,))] * 2
    scan_grid = (micros, groups)

    x_low = x_rows
    x_rows = x_rows.astype(f32)
    inv_rms = lax.rsqrt(jnp.mean(x_rows * x_rows, axis=-1, keepdims=True) + eps)
    low_own = (x_rows * inv_rms * norm_gain).astype(bf16)
    mask_own = (own_pos < lengths).astype(f32)[..., None]
    mask = (all_pos < lengths).astype(f32)[..., None]
    picks = (adapter_ids == jnp.arange(ADAPT)).astype(f32)
    tall = bounds[2]
    factors = pl.pallas_call(
        pick_kernel,
        name="pick",
        grid_spec=pltpu.PrefetchScalarGridSpec(
            num_scalar_prefetch=1,
            grid=(micros, nz),
            in_specs=[block((1, 1, 1, tall, part), lambda m, n, k: (k[m] // 2, n, lax.rem(k[m], 2), 0, 0))],
            out_specs=block((1, 1, tall, part), lambda m, n, k: (m, n, 0, 0)),
        ),
        out_shape=shape((micros, nz, tall, part), bf16),
    )(ids, pack)
    per = 2 * R * each // line
    wide_rows = [lax.dynamic_slice_in_dim(pack, bounds[4] + per * ids[m], per, 3) for m in range(micros)]
    wide_rows = jnp.stack(wide_rows).reshape(micros, nd, nz, 2, 2, R, each)
    wide_rows = jnp.transpose(wide_rows, (4, 0, 5, 1, 3, 2, 6)).reshape(2, micros, R, D)

    def wide_block(kind, width, index):
        return block((1, micros, R, width), lambda m, g: (kind, 0, 0, index(g)))

    def every(width, index=None):
        if index is None:
            return pl.BlockSpec((micros, tokens, width), lambda m, g: (0, 0, 0), pipeline_mode=pl.Buffered(1))
        return block((micros, tokens, width), index)

    by_step = lambda m, g: (0, 0, g)
    rank_b16 = shape((micros, tokens, 2 * R), bf16)
    half_steps = chan // part
    steps = 2 * half_steps
    cot = cotangent[:, 0]
    early = 1
    hbm = pl.BlockSpec(memory_space=pl.ANY)
    pair_scratch = [pltpu.VMEM((micros, tokens, D), bf16), dma((4,))]
    xin, z_in, bcin, rate_in, lr, low, cot_early = call(
        project_kernel, "project", (1, steps),
        [(low_own, hbm), (zx_weight, block((1, D, part), lambda m, g: (1 - g // half_steps, 0, g % half_steps))),
         (first_weight, block((D, 2 * NS + 128), z2)), (wide_rows, wide_block(0, D, lambda g: 0)),
         (factors, block((micros, 1, R, part), lambda m, g: (0, g % half_steps, 1 - g // half_steps, 0)))],
        [(tok_b16, every(part, lambda m, g: (0, 0, jnp.minimum(g, half_steps - 1)))),
         (tok_f32, every(part, lambda m, g: (0, 0, jnp.maximum(g - half_steps, 0)))),
         (shape((micros, tokens, 2 * NS), bf16), every(2 * NS)), (sums_f32, every(128)), (rank_b16, every(2 * R)), (shape((micros, tokens, D), bf16), hbm)],
        pair_scratch, 4 * tokens * D * chan, act_bytes * 4, 2, (cot, shape((early, own, D), bf16), tuple(range(early)), True),
    )
    tail = jnp.concatenate([xin[:, tokens - HALO :], bcin[:, tokens - HALO :]], axis=2)
    goes = jnp.sum(jnp.where(leaves, tail, 0), axis=0, dtype=bf16)
    halo = jnp.where(enters, lax.ppermute(goes, "mp", forward_edge)[None], jnp.pad(tail[:-1], ((1, 0), (0, 0), (0, 0))))
    halo, bchalo = halo[..., :chan], halo[..., chan:]
    step, cum, lanes, bc = call(
        skip_grid(prep_kernel), "prep", (micros, 1),
        [(rate_in, sums), (bias, head_line), (rate, head_line), (mask, one_col), (bcin, bc_block), (bchalo, bc_halo),
         (conv_bc, bc_taps)],
        [(sums_f32, sums), (sums_f32, sums),
         (shape((micros, groups, 2 * HG, tokens), f32), block((1, groups, 2 * HG, tokens), lambda m, g: (m, 0, 0, 0))),
         (bc_f32, bc_block)],
        [], tokens * Q * 128 * 6, tokens * 128 * 24,
    )
    mixed, square, state, end_state, cot_late = call(
        forward_kernel, "ssd_forward", scan_grid,
        [(xin, chan_block), (halo, halo_block), (taps, taps_block), (bc, bc_block), (cum, sums), (step, sums),
         (lanes, lanes_block), (skip, line_block), (z_in, chan_block)],
        [(tok_f32, chan_block), (sums_f32, sums), (state_f32, state_block), (state_f32, state_block)],
        [pltpu.VMEM((blocks, Q, Q), f32), pltpu.VMEM((2, blocks, NS, Q), bf16), *line_scratch],
        6 * tokens * Q * chan * 2, act_bytes * 3, 3, (cot, shape((micros - early, own, D), bf16), tuple(range(early, micros)), True),
    )

    cols = out_all.shape[3]
    gb_own = jnp.concatenate([cot_early, cot_late], 0) * mask_own.astype(bf16)
    part_block = every(part, by_step)
    gs, dots, rg, gb = call(
        gs_kernel, "gs", (1, nz),
        [(gb_own, hbm), (out_all, block((nd, 1, part, cols), lambda m, g: (0, g, 0, 0))), (wide_rows, wide_block(1, D, lambda g: 0)),
         (factors, block((micros, 1, R, part), lambda m, g: (0, g, 2, 0))), (mixed, part_block), (z_in, part_block),
         (gain, block((1, part), lambda m, g: (0, g)))],
        [(tok_f32, part_block), (sums_f32, every(128)), (rank_b16, every(2 * R)), (shape((micros, tokens, D), bf16), hbm)],
        pair_scratch, 6 * tokens * D * chan, act_bytes * 15, 7,
    )
    both = jnp.stack([jnp.sum(square, axis=-1), jnp.sum(dots, axis=-1)])
    both = (both + other(both)) / DI
    inv_gate = lax.rsqrt(both[0] + eps)[..., None]
    coef = inv_gate**3 * both[1][..., None]
    dy, gz, scaled, lloc, q = call(
        gate_back_kernel, "gate_back", scan_grid,
        [(gs, chan_block), (mixed, chan_block), (z_in, chan_block), (inv_gate, one_col), (coef, one_col), (gain, line_block),
         (bc, bc_block), (cum, sums)],
        [(tok_f32, chan_block), (tok_b16, chan_block), (tok_b16, chan_block), (state_f32, state_block), (sums_f32, sums)],
        [pltpu.VMEM((2, NS, tokens), bf16)], 6 * tokens * NS * chan, act_bytes * 5,
    )
    step_cols = every(cols, by_step)
    rank_scratch = [pltpu.VMEM((micros, tokens, 2 * R), bf16)] + [pltpu.VMEM((micros, 2 * R, tokens), bf16)] * 2
    rank_cols = block((micros, R, cols), by_step)
    own_rows = pl.BlockSpec((micros, own, D), lambda m, g: (0, 0, 0), pipeline_mode=pl.Buffered(1))
    own_col = block((micros, own, 1), lambda m, g: (0, 0, 0))

    def pair_sum(steps):
        width = D // steps
        return [pltpu.VMEM((2, micros, tokens, width), f32), pltpu.VMEM((steps, micros, own, width), f32), dma((steps,)), dma((steps,))]

    out_rows, g_up_out, g_out = call(
        branch_kernel, "branch", (1, nd),
        [(scaled, every(chan)), (out_all, block((1,) + out_all.shape[1:], lambda m, g: (g, 0, 0, 0))),
         (factors, block((micros, nz, R, part), lambda m, g: (0, 0, 2, 0))), (wide_rows, wide_block(1, cols, lambda g: g)),
         (rg, every(2 * R)), (gb, step_cols), (x_low, own_rows), (mask_own, own_col)],
        [(shape((micros, own, D), bf16), own_rows), (shape((micros, R, D), f32), rank_cols),
         (shape((micros, R, chan), f32), block((micros, R, chan // nd), by_step))],
        rank_scratch + pair_sum(nd), 6 * tokens * D * chan, act_bytes * 12, 8,
    )

    first_slots, last_slots = tuple(range(micros - 1)), (micros - 1,)

    def last_first(spec):
        index = spec.index_map
        return block(spec.block_shape, lambda m, g: index(micros - 1 - m, g))

    ins = [(dy, chan_block), (xin, chan_block), (halo, halo_block), (taps, taps_block), (bc, bc_block), (cum, sums), (step, sums),
           (lanes, lanes_block), (skip, line_block), (state, state_block), (lloc, state_block), (end_state, state_block)]
    outs = [(tok_b16, chan_block), (edge_f32, edge_block), (edge_f32, edge_block), (bc_f32, bc_block), (sums_f32, sums),
            (sums_f32, sums)]
    gx, head, tail, gbc, xu, dx, out_first = call(
        scan_back_kernel, "ssd_back", scan_grid,
        [(a, last_first(s)) for a, s in ins], [(a, last_first(s)) for a, s in outs],
        [pltpu.VMEM((blocks, Q, Q), f32), pltpu.VMEM((blocks, Q, Q), f32), pltpu.VMEM((2, blocks, NS, Q), bf16),
         pltpu.VMEM((2, blocks, NS, Q), bf16), *line_scratch],
        12 * tokens * Q * chan * 2, act_bytes * 3, 4, (out_rows, shape((micros, seg, feats), bf16), first_slots, False),
    )
    gbc = gbc + other(gbc)
    edge_bc = shape((micros, 8, 2 * NS), f32)
    gbc, bhead, btail, g_rate = call(
        skip_grid(bc_back_kernel), "bc_back", (micros, 1),
        [(gbc, bc_block), (bcin, bc_block), (bchalo, bc_halo), (conv_bc, bc_taps), (q, sums), (dx, sums), (xu, sums),
         (step, sums), (rate_in, sums), (bias, head_line), (rate, head_line), (mask, one_col)],
        [(shape((micros, tokens, 2 * NS), bf16), bc_block), (edge_bc, bc_edge), (edge_bc, bc_edge),
         (shape((micros, tokens, 128), bf16), sums)],
        [], tokens * tokens * 128 * 6, tokens * 2 * NS * 8,
    )
    head = jnp.concatenate([head, bhead], 2)
    goes = lax.ppermute(jnp.sum(jnp.where(enters, head, 0), axis=0), "mp", backward_edge)
    back = jnp.pad(jnp.where(enters, 0, head)[1:], ((0, 1), (0, 0), (0, 0))) + jnp.where(leaves, goes[None], 0)
    tail = jnp.concatenate([tail, btail], 2).at[:, 8 - (KC - 1) :].add(back[:, 8 - (KC - 1) :]).astype(bf16)
    gx = lax.dynamic_update_slice_in_dim(gx, tail[..., :chan], tokens - 8, 1)
    gbc = lax.dynamic_update_slice_in_dim(gbc, tail[..., chan:], tokens - 8, 1)
    tail = jnp.concatenate([lax.dynamic_slice_in_dim(gbc, core * NS, NS, 2), g_rate], 2)
    back_steps = 2 * nz
    wide_cols, back_chan = D // back_steps, chan // back_steps
    delta, g_up_z, g_up_x, g_down, out_last = call(
        unproject_kernel, "unproject", (1, back_steps),
        [(gz, every(chan)), (gx, every(chan)), (tail, every(NS + 128)),
         (zx_weight, block((2, wide_cols, chan), lambda m, g: (0, g, 0))), (tail_weight, block((wide_cols, NS + 128), lambda m, g: (g, 0))),
         (factors, block((micros, nz, 2 * R, part), lambda m, g: (0, 0, 0, 0))), (wide_rows, wide_block(0, wide_cols, lambda g: g)),
         (lr, every(2 * R)), (low, every(wide_cols, by_step)), (x_low, own_rows), (inv_rms, own_col),
         (norm_gain[None], block((1, D), z2))],
        [(shape((micros, own, D), bf16), own_rows), (shape((micros, R, chan), f32), block((micros, R, back_chan), by_step)),
         (shape((micros, R, chan), f32), block((micros, R, back_chan), by_step)),
         (shape((micros, R, D), f32), block((micros, R, wide_cols), by_step))],
        rank_scratch + pair_sum(back_steps), 12 * tokens * D * chan, act_bytes * 9, 6, (out_rows[-1:], shape((micros, seg, feats), bf16), last_slots, False),
    )
    held_runs = jnp.arange(micros)[:, None] * nz + 2 * core + jnp.arange(2)
    in_last = place_of(held_runs)[1] == micros - 1
    in_last = jnp.repeat(in_last, tokens, axis=1)[..., None]
    out = jnp.where(in_last, out_last, out_first)[:, None]
    mine = (sequence == jnp.arange(micros)[:, None]).astype(f32)

    delta, near, far = finish(
        [g_out, g_up_z, g_up_x, g_up_out, g_down], mine, picks, delta, shape((micros, seg, feats), bf16), nz, nd
    )
    grad = cotangent.astype(f32) + delta[:, None].astype(f32)
    g_out_down = jnp.transpose(near[:, 0], (0, 2, 1)).reshape(2 * part, R)
    g_in_up = jnp.transpose(near[:, 1:], (2, 1, 0, 3)).reshape(R, 2, 2 * part)
    g_out_up = far[:, 0].reshape(ADAPT * R, each)
    g_in_down = jnp.transpose(far[:, 1], (0, 2, 1))
    return (out, grad, g_in_down, g_in_up, g_out_down, g_out_up)


def solution(mesh):
    in_specs = (
        P(None, "dp", "seq", "mp"),
        P(None, "dp", "seq", "mp"),
        P(None, "dp"),
        P(None, "dp"),
        P(),
        P(("dp", "seq"), None, "mp"),
        P(("dp", "seq"), None),
        P(("dp", "seq"), "mp"),
        P("mp"),
        P("mp"),
        P("mp"),
        P(None, "mp"),
        P(),
        P("mp"),
        P("mp", ("dp", "seq")),
        P(None, ("dp", "seq", "mp"), None),
        P(("dp", "seq"), None, "mp"),
        P("mp", ("dp", "seq")),
        P(None, ("dp", "seq", "mp")),
    )
    out_specs = (
        P(None, "dp", "seq", "mp"),
        P(None, "dp", "seq", "mp"),
        P(None, ("dp", "seq", "mp"), None),
        P(("dp", "seq"), None, "mp"),
        P("mp", ("dp", "seq")),
        P(None, ("dp", "seq", "mp")),
    )
    sizes = dict(mesh.shape)
    by_chip = (
        sizes["seq"] == 2
        and sizes["dp"] * 2 == ADAPT
        and sizes["mp"] == SLOTS + 1
    )
    return jax.shard_map(fast_body if by_chip else body, mesh=mesh, in_specs=in_specs, out_specs=out_specs, check_vma=False)
```
